32 devices in a mesh: dp: 16 (over z, x, core), fsdp: 2 (over y).
Axes of the slice: x: 2, y: 2, z: 4, core: 2. Of those that a mesh axis runs over, the one named last changes fastest.
Arguments:
- tokens: bfloat16 [32, 512, 1024], P(('dp', 'fsdp')), may hold values from -6 to 6
- memory: bfloat16 [32, 512, 1024], P(('dp', 'fsdp')), may hold values from -6 to 6
- compressed: bfloat16 [32, 512, 1024], P(('dp', 'fsdp')), may hold values from -6 to 6
- cotangent: bfloat16 [32, 512, 1024], P(('dp', 'fsdp')), may hold values from -6 to 6
- seg_len: int32 [32], P(('dp', 'fsdp')), may hold values from 128 to 512, as said below
- mem_fill: int32 [32], P(('dp', 'fsdp')), may hold values from 0 to 512
- cmem_fill: int32 [32], P(('dp', 'fsdp')), may hold values from 0 to 512
- w_qkv: bfloat16 [3, 1024, 1024], P(None, 'fsdp'), may hold values from -0.1875 to 0.1875
- w_rel: bfloat16 [1024, 1024], P('fsdp'), may hold values from -0.1875 to 0.1875
- w_out: bfloat16 [1024, 1024], P('fsdp'), may hold values from -0.75 to 0.75
- w_up: bfloat16 [1024, 4096], P('fsdp'), may hold values from -0.1875 to 0.1875
- w_down: bfloat16 [4096, 1024], P('fsdp'), may hold values from -0.09375 to 0.09375
- w_comp: bfloat16 [3, 1024, 1024], P(None, 'fsdp'), may hold values from -0.109375 to 0.109375
- norm_gain1: float32 [1024], replicated, may hold values from 0.5 to 1.5
- norm_gain2: float32 [1024], replicated, may hold values from 0.5 to 1.5
- bias_content: float32 [1024], replicated, may hold values from -3 to 3
- bias_position: float32 [1024], replicated, may hold values from -3 to 3
- bias_up: float32 [4096], replicated, may hold values from -3 to 3
Outputs:
- output: bfloat16 [32, 512, 1024], P(('dp', 'fsdp'))
- grad_tokens: bfloat16 [32, 512, 1024], P(('dp', 'fsdp'))
- new_memory: bfloat16 [32, 512, 1024], P(('dp', 'fsdp'))
- new_compressed: bfloat16 [32, 512, 1024], P(('dp', 'fsdp'))
- grad_qkv: float32 [3, 1024, 1024], P(None, 'fsdp', 'dp')
- grad_rel: float32 [1024, 1024], P('fsdp', 'dp')
- grad_out: float32 [1024, 1024], P('fsdp', 'dp')
- grad_up: float32 [1024, 4096], P('fsdp', 'dp')
- grad_down: float32 [4096, 1024], P('fsdp', 'dp')
- grad_comp: float32 [3, 1024, 1024], P(None, 'fsdp', 'dp')
- grad_gain1: float32 [1024], P(('dp', 'fsdp'))
- grad_gain2: float32 [1024], P(('dp', 'fsdp'))
- grad_content: float32 [1024], P(('dp', 'fsdp'))
- grad_position: float32 [1024], P(('dp', 'fsdp'))
- grad_bias_up: float32 [4096], P(('dp', 'fsdp'))
The draws below stay inside these ranges and needn't reach their ends.
Inputs may be any that keep to these rules, and one draw needn't show every extreme that they name: Each stream's segment length is 128, 256 or 512; rows from seg_len on are padding.
All inputs are finite; a program needn't handle non-finite values.
Results may differ from the reference program's by a relative error of at most 0.019.
Values may be sent and summed in bfloat16 or wider, within the bound.
No kernel may reach another device: no remote copies, remote signals or barrier semaphores. Data moves between devices by JAX's collectives and lax.ppermute only.
A program may use at most 320 MiB of HBM per device.

```python
import math
import jax
import jax.numpy as jnp
from jax import lax

D = 1024
H = 8
DH = 128
FF = 4096
M = 512
CM = 512
SEG = 512
KEYS = 1536
NCOMP = 170
STREAMS = 32


def pick_two(key):
    first = jax.random.randint(jax.random.fold_in(key, 1), (), 0, STREAMS)
    second = (first + 1 + jax.random.randint(jax.random.fold_in(key, 2), (), 0, STREAMS - 1)) % STREAMS
    return (first, second)


def draw_fill(key, top_fill):
    picks = jax.random.randint(key, (STREAMS,), 0, top_fill + 1)
    first, second = pick_two(key)
    return picks.at[first].set(top_fill).at[second].set(0).astype(jnp.int32)


def draw_seg_len(key, part):
    key = jax.random.fold_in(key, 11)
    picks = jax.random.randint(key, (STREAMS,), 0, 3)
    lengths = jnp.where(picks == 0, SEG // 4, jnp.where(picks == 1, SEG // 2, SEG))
    first, second = pick_two(key)
    return lengths.at[first].set(SEG).at[second].set(SEG // 4).astype(jnp.int32)


def draw_mem_fill(key, part):
    key = jax.random.fold_in(key, 23)
    return draw_fill(key, M)


def draw_cmem_fill(key, part):
    key = jax.random.fold_in(key, 37)
    return draw_fill(key, CM)


def with_spikes(result, own_key, source, target, parts, factor):
    owner, partner = [(jnp.arange(result.shape[axis_at]) // (result.shape[axis_at] // parts)).reshape([-1 if axis == axis_at else 1 for axis in range(result.ndim)]) for axis_at in (source, target)]
    chosen = jax.random.permutation(own_key, parts)[partner]
    strong = (owner == chosen) | (owner == (partner + parts // 2) % parts)
    return jnp.where(strong, factor * result, result)


def block_levels(key, shape, pieces, smallest, high):
    def one(dim, parts):
        steps = jax.random.uniform(jax.random.fold_in(jax.random.fold_in(key, 6), dim), (parts,), jnp.float32, smallest / len(pieces), high / len(pieces))
        return jnp.repeat(jnp.exp(steps), shape[dim] // parts).reshape((-1,) + (1,) * (len(shape) - dim - 1))

    gain = one(*pieces[0])
    for cut in pieces[1:]:
        gain = gain * one(*cut)
    return gain


def normal_values(rng, extent, scale, most, split=(), kind=jnp.bfloat16):
    drawn = jax.random.normal(rng, extent, jnp.float32) * scale
    if len(split) > 0:
        drawn = block_levels(rng, extent, split, -0.22, 0.18) * drawn
    return jnp.clip(drawn, min=-most, max=most).astype(kind)


def bell_draw_with(key, shape, scale, bound, pieces, heavy, held_as=jnp.bfloat16):
    result = scale * jax.random.normal(key, shape, jnp.float32)
    if pieces:
        result = result * block_levels(key, shape, pieces, -0.22, 0.18)
    return jnp.clip(with_spikes(result, jax.random.fold_in(key, 3), *heavy), -bound, bound).astype(held_as)


def setup_inputs(seed: int = 0) -> dict:
    arg_keys = jax.random.split(jax.random.key(seed), 19)
    tokens = normal_values(arg_keys[0], (STREAMS, SEG, D), 1.0, 6.0, ((0, 32),))
    memory = normal_values(arg_keys[1], (STREAMS, M, D), 1.0, 6.0, ((0, 32),))
    compressed = normal_values(arg_keys[2], (STREAMS, CM, D), 1.0, 6.0, ((0, 32),))
    cotangent = bell_draw_with(arg_keys[3], (STREAMS, SEG, D), 1.0, 6.0, ((0, 32),), (0, 2, 32, 2.75))
    seg_len = draw_seg_len(jax.random.fold_in(arg_keys[18], 71), 0)
    mem_fill = draw_mem_fill(jax.random.fold_in(arg_keys[18], 71), 0)
    cmem_fill = draw_cmem_fill(jax.random.fold_in(arg_keys[18], 71), 0)
    w_qkv = normal_values(arg_keys[7], (3, D, D), D ** -0.5, 0.1875, ((1, 2),))
    w_rel = normal_values(arg_keys[8], (D, D), D ** -0.5, 0.1875, ((0, 2),))
    w_out = normal_values(arg_keys[9], (D, D), (D // 16) ** -0.5, 0.75, ((0, 2),))
    w_up = normal_values(arg_keys[10], (D, FF), D ** -0.5, 0.1875, ((0, 2),))
    w_down = normal_values(arg_keys[11], (FF, D), FF ** -0.5, 0.09375, ((0, 2),))
    w_comp = normal_values(arg_keys[12], (3, D, D), (3 * D) ** -0.5, 0.109375, ((1, 2),))
    norm_gain1 = jnp.clip(1.0 + 0.1 * jax.random.normal(arg_keys[13], (D,), jnp.float32), 0.5, 1.5)
    norm_gain2 = jnp.clip(1.0 + 0.1 * jax.random.normal(arg_keys[14], (D,), jnp.float32), 0.5, 1.5)
    bias_content = normal_values(arg_keys[15], (D,), 0.5, 3.0, (), jnp.float32)
    bias_position = normal_values(arg_keys[16], (D,), 0.5, 3.0, (), jnp.float32)
    bias_up = normal_values(arg_keys[17], (FF,), 0.5, 3.0, (), jnp.float32)
    return dict(tokens=tokens, memory=memory, compressed=compressed, cotangent=cotangent, seg_len=seg_len, mem_fill=mem_fill, cmem_fill=cmem_fill, w_qkv=w_qkv, w_rel=w_rel, w_out=w_out, w_up=w_up, w_down=w_down, w_comp=w_comp, norm_gain1=norm_gain1, norm_gain2=norm_gain2, bias_content=bias_content, bias_position=bias_position, bias_up=bias_up)


@jax.custom_vjp
def low(v):
    return lax.optimization_barrier(v.astype(jnp.bfloat16)).astype(jnp.float32)

@jax.custom_vjp
def low_back(v):
    return v

def low_keep(v):
    return (low(v), None)

def low_pass(kept, grad):
    return (grad,)

def back_keep(v):
    return (v, None)

def back_low(kept, grad):
    return (low(grad),)
low.defvjp(low_keep, low_pass)
low_back.defvjp(back_keep, back_low)

def layer_norm(row_block, norm_gain):
    row_mean = lax.optimization_barrier(jnp.mean(row_block, axis=-1, keepdims=True))
    centred = row_block - row_mean
    spread = lax.optimization_barrier(jnp.mean(centred * centred, axis=-1, keepdims=True))
    return centred * lax.rsqrt(spread + 1e-05) * norm_gain

def sinusoid(table_rows, table_width):
    distance = (table_rows - 1 - jnp.arange(table_rows)).astype(jnp.float32)
    frequency = jnp.exp(jnp.arange(0, table_width, 2).astype(jnp.float32) * (-math.log(10000.0) / table_width))
    angles = distance[:, None] * frequency[None, :]
    return jnp.concatenate([jnp.sin(angles), jnp.cos(angles)], axis=1)

def rel_shift(scores):
    head_count, query_count, key_count = scores.shape
    padded = jnp.pad(scores, ((0, 0), (0, 0), (1, 0)))
    padded = padded.reshape(head_count, key_count + 1, query_count)[:, 1:]
    return padded.reshape(head_count, query_count, key_count)

def key_mask(query_count, comp_slots, mem_slots, mem_live, comp_live):
    row_index = jnp.arange(query_count)[:, None]
    col_index = jnp.arange(comp_slots + mem_slots + query_count)[None, :]
    seg_start = comp_slots + mem_slots
    live_comp = (col_index < comp_slots) & (col_index >= comp_slots - comp_live)
    live_mem = (col_index >= comp_slots) & (col_index < seg_start) & (col_index >= seg_start - mem_live)
    live_seg = (col_index >= seg_start) & (col_index - seg_start <= row_index)
    return live_comp | live_mem | live_seg

def masked_softmax(scores, key_live):
    masked = jnp.where(key_live, scores, -1e+30)
    top_score = lax.optimization_barrier(jnp.max(masked, axis=-1, keepdims=True))
    weights = jnp.exp(masked - top_score)
    return weights / lax.optimization_barrier(jnp.sum(weights, axis=-1, keepdims=True))

def matmul_high(lhs_operand, rhs_operand):
    return jnp.dot(lhs_operand, rhs_operand, precision=lax.Precision.HIGHEST, preferred_element_type=jnp.float32)

def einsum_high(pattern, lhs_operand, rhs_operand):
    return jnp.einsum(pattern, lhs_operand, rhs_operand, precision=lax.Precision.HIGHEST, preferred_element_type=jnp.float32)

def reference(tokens, memory, compressed, cotangent, seg_len, mem_fill, cmem_fill, w_qkv, w_rel, w_out, w_up, w_down, w_comp, norm_gain1, norm_gain2, bias_content, bias_position, bias_up):
    weights = tuple((weight_part.astype(jnp.float32) for weight_part in (w_qkv, w_rel, w_out, w_up, w_down, w_comp, norm_gain1, norm_gain2, bias_content, bias_position, bias_up)))
    sinus_table = low(sinusoid(KEYS, D))
    query_scale = DH ** (-0.5)

    def per_stream(running, stream_items):
        current, recent, distant, cot_rows, seg_length, mem_live, comp_live = stream_items
        recent_rows = recent.astype(jnp.float32)
        distant_rows = distant.astype(jnp.float32)
        key_live = key_mask(SEG, CM, M, mem_live, comp_live)
        comp_count = seg_length // 3
        old_live = jnp.arange(M)[None, :] < 3 * comp_count
        squeeze_live = jnp.arange(NCOMP)[None, :] < comp_count
        row_live = (jnp.arange(SEG) < seg_length).astype(jnp.float32)
        groups = recent_rows[:3 * NCOMP].reshape(NCOMP, 3 * D)

        def layer(segment_rows, wqkv_f, wrel_f, wout_f, wup_f, wdown_f, wcomp_f, gain_one, gain_two, content_bias, position_bias, up_bias, frozen_rows, frozen_gain, frozen_qkv):
            hidden = jnp.concatenate([distant_rows, recent_rows, segment_rows], axis=0)
            normed = low(layer_norm(hidden, gain_one))
            queries = low_back(matmul_high(normed[CM + M:], wqkv_f[0]))
            key_heads = low(low_back(matmul_high(normed, wqkv_f[1]))).reshape(KEYS, H, DH)
            value_heads = low(low_back(matmul_high(normed, wqkv_f[2]))).reshape(KEYS, H, DH)
            position = low(low_back(matmul_high(sinus_table, wrel_f))).reshape(KEYS, H, DH)
            query_content = low((queries + content_bias) * query_scale).reshape(SEG, H, DH)
            query_position = low((queries + position_bias) * query_scale).reshape(SEG, H, DH)
            content = einsum_high('qhd,khd->hqk', query_content, key_heads)
            relative = rel_shift(einsum_high('qhd,khd->hqk', query_position, position))
            scores = low_back(content + relative)
            probs = low(masked_softmax(scores, key_live))
            mixed_out = low(low_back(einsum_high('hqk,khd->qhd', probs, value_heads).reshape(SEG, D)))
            attended = segment_rows + low_back(matmul_high(mixed_out, wout_f))
            second = low(layer_norm(attended, gain_two))
            ffn_inner = low_back(matmul_high(second, wup_f) + up_bias)
            output = attended + matmul_high(low(jax.nn.gelu(ffn_inner)), wdown_f)
            frozen_seg = low(layer_norm(frozen_rows, frozen_gain))
            frozen_mem = low(layer_norm(recent_rows, frozen_gain))
            probe = low(matmul_high(frozen_seg, frozen_qkv[0]) * query_scale).reshape(SEG, H, DH)
            old_keys = low(matmul_high(frozen_mem, frozen_qkv[1])).reshape(M, H, DH)
            old_values = low(matmul_high(frozen_mem, frozen_qkv[2])).reshape(M, H, DH)
            old_probs = masked_softmax(einsum_high('qhd,khd->hqk', probe, old_keys), old_live)
            old_out = einsum_high('hqk,khd->qhd', low(old_probs), old_values)
            squeezed = low_back(matmul_high(groups, wcomp_f.reshape(3 * D, D)))
            squeezed_norm = low(layer_norm(squeezed, frozen_gain))
            comp_keys = low(low_back(matmul_high(squeezed_norm, frozen_qkv[1]))).reshape(NCOMP, H, DH)
            comp_values = low(low_back(matmul_high(squeezed_norm, frozen_qkv[2]))).reshape(NCOMP, H, DH)
            comp_scores = low_back(einsum_high('qhd,khd->hqk', probe, comp_keys))
            comp_probs = masked_softmax(comp_scores, squeeze_live)
            comp_out = low_back(einsum_high('hqk,khd->qhd', low(comp_probs), comp_values))
            recon_gap = (comp_out - old_out) * row_live[:, None, None]
            loss = jnp.sum(recon_gap * recon_gap) / seg_length.astype(jnp.float32)
            return ((output, loss), squeezed)
        segment_rows = current.astype(jnp.float32)
        primal_out, pullback, squeezed = jax.vjp(layer, segment_rows, weights[0], weights[1], weights[2], weights[3], weights[4], weights[5], weights[6], weights[7], weights[8], weights[9], weights[10], segment_rows, weights[6], weights[0], has_aux=True)
        output = primal_out[0]
        grads = pullback((cot_rows.astype(jnp.float32) * row_live[:, None], jnp.ones((), jnp.float32)))
        running = jax.tree.map(jnp.add, running, tuple(grads[1:12]))
        new_mem = lax.dynamic_slice_in_dim(jnp.concatenate([recent, current], axis=0), seg_length.astype(jnp.int32), M, 0)
        new_comp = lax.dynamic_slice_in_dim(jnp.concatenate([distant, squeezed.astype(jnp.bfloat16)], axis=0), comp_count.astype(jnp.int32), CM, 0)
        return (running, (output.astype(jnp.bfloat16), grads[0].astype(jnp.bfloat16), new_mem, new_comp))
    zeros = tuple((jnp.zeros(weight_part.shape, jnp.float32) for weight_part in weights))
    totals, stacked = lax.scan(per_stream, zeros, (tokens, memory, compressed, cotangent, seg_len, mem_fill, cmem_fill))
    return (stacked[0], stacked[1], stacked[2], stacked[3], totals[0], totals[1], totals[2], totals[3], totals[4], totals[5], totals[6], totals[7], totals[8], totals[9], totals[10])
```

```python
import functools
import math

import jax
import jax.numpy as jnp
from jax import lax
from jax.experimental import pallas as pl
from jax.experimental.pallas import tpu as pltpu
from jax.sharding import PartitionSpec as P

H = 8
BF = jnp.bfloat16
F32 = jnp.float32
VMEM = 60 * 1024 * 1024
GELU_C = math.sqrt(2.0 / math.pi)


def nn(a, b):
    return lax.dot_general(a, b, (((1,), (0,)), ((), ())), preferred_element_type=F32)


def nt(a, b):
    return lax.dot_general(a, b, (((1,), (1,)), ((), ())), preferred_element_type=F32)


def tn(a, b):
    return lax.dot_general(a, b, (((0,), (0,)), ((), ())), preferred_element_type=F32)


def call(kernel, name, grid, ins, outs, scratch, scal, args, flops):
    moved = sum(a.size * a.dtype.itemsize for a in args)
    moved += sum(math.prod(s.shape) * s.dtype.itemsize for s, _ in outs)
    return pl.pallas_call(
        kernel,
        name=name,
        out_shape=[s for s, _ in outs],
        grid_spec=pltpu.PrefetchScalarGridSpec(
            num_scalar_prefetch=1,
            grid=grid,
            in_specs=ins,
            out_specs=[b for _, b in outs],
            scratch_shapes=scratch,
        ),
        compiler_params=pltpu.CompilerParams(
            vmem_limit_bytes=VMEM, dimension_semantics=("arbitrary",) * len(grid)
        ),
        cost_estimate=pl.CostEstimate(flops=int(flops), bytes_accessed=int(moved), transcendentals=0),
    )(scal, *args)


def whole(shape):
    return pl.BlockSpec(shape, lambda i, s: (0,) * len(shape))


def out(shape, dtype, block, index):
    return (jax.ShapeDtypeStruct(shape, dtype), pl.BlockSpec(block, index))


def norm_rows(rows):
    centred = rows - jnp.mean(rows, axis=-1, keepdims=True)
    spread = jnp.mean(centred * centred, axis=-1, keepdims=True)
    scale = lax.rsqrt(spread + 1e-05)
    return centred * scale, scale


def norm_back(grad, gain, unit, scale):
    g = grad * gain
    inner = jnp.mean(g * unit, axis=-1, keepdims=True)
    return scale * (g - jnp.mean(g, axis=-1, keepdims=True) - unit * inner)


def place(dst, s_ref, own, mine, theirs, lead=()):
    half, quarter = own.shape[-2], mine.shape[-2]
    y, core = s_ref[0], s_ref[1]
    base = (1 - y) * half
    dst[lead + (pl.ds(pl.multiple_of(y * half, quarter), half),)] = own[...]
    dst[lead + (pl.ds(pl.multiple_of(base + core * quarter, quarter), quarter),)] = mine[...]
    dst[lead + (pl.ds(pl.multiple_of(base + (1 - core) * quarter, quarter), quarter),)] = theirs[...]


def qkv_kernel(s_ref, x_ref, o_ref, m_ref, t_ref, bc_ref, bp_ref, k_ref, v_ref, qc_ref, qp_ref,
               pr_ref, w_ref, *, first_query, scale):
    i = pl.program_id(0)

    @pl.when(i == 0)
    def _():
        for n in range(3):
            place(w_ref, s_ref, o_ref.at[n], m_ref.at[n], t_ref.at[n], (n,))

    x = x_ref[...]
    k_ref[...] = nn(x, w_ref[1]).astype(BF)
    v_ref[...] = nn(x, w_ref[2]).astype(BF)

    @pl.when(i >= first_query)
    def _():
        q = nn(x, w_ref[0])
        qc_ref[...] = ((q + bc_ref[...]) * scale).astype(BF)
        qp_ref[...] = ((q + bp_ref[...]) * scale).astype(BF)
        pr_ref[...] = (q * scale).astype(BF)


def project_qkv(scal, normed, parts, bias_content, bias_position, seg, scale):
    rows, width = normed.shape
    blk = 256
    first = (rows - seg) // blk
    keys = lambda: out((rows, width), BF, (blk, width), lambda i, s: (i, 0))
    quer = lambda: out((seg, width), BF, (blk, width), lambda i, s: (jnp.maximum(i - first, 0), 0))
    own, mine, theirs = parts
    return call(
        functools.partial(qkv_kernel, first_query=first, scale=scale), "project_qkv", (rows // blk,),
        [pl.BlockSpec((blk, width), lambda i, s: (i, 0)), whole(own.shape), whole(mine.shape),
         whole(theirs.shape), whole((1, width)), whole((1, width))],
        [keys(), keys(), quer(), quer(), quer(),
         out((3, width, width), BF, (3, width, width), lambda i, s: (0, 0, 0))],
        [], scal,
        (normed, own, mine, theirs, bias_content.reshape(1, -1), bias_position.reshape(1, -1)),
        2 * (2 * rows + seg) * width * width)


def position_kernel(s_ref, x_ref, o_ref, m_ref, t_ref, p_ref, w_ref):
    @pl.when(pl.program_id(0) == 0)
    def _():
        place(w_ref, s_ref, o_ref, m_ref, t_ref)

    p_ref[...] = nn(x_ref[...], w_ref[...]).astype(BF)


def project_position(scal, table, parts):
    rows, width = table.shape
    blk = 256
    own, mine, theirs = parts
    return call(
        position_kernel, "project_position", (rows // blk,),
        [pl.BlockSpec((blk, width), lambda i, s: (i, 0)), whole(own.shape), whole(mine.shape),
         whole(theirs.shape)],
        [out((rows, width), BF, (blk, width), lambda i, s: (i, 0))],
        [pltpu.VMEM((width, width), BF)], scal, (table, own, mine, theirs),
        2 * rows * width * width)[0]


RB = 256


def attention_kernel(s_ref, qc_ref, qp_ref, k_ref, v_ref, pos_ref, p_ref, mix_ref, *, comp, mem):
    seg, keys = qc_ref.shape[0], k_ref.shape[0]
    start = comp + mem
    mem_live, comp_live = s_ref[3], s_ref[4]
    flip = (lax.broadcasted_iota(jnp.int32, (RB, RB), 0)
            + lax.broadcasted_iota(jnp.int32, (RB, RB), 1) == RB - 1).astype(BF)
    for r in range(seg // RB):
        width = start + RB * (r + 1)
        rows = slice(r * RB, (r + 1) * RB)
        content = nt(qc_ref[rows], k_ref[:width])
        rel = nt(qp_ref[rows], pos_ref[keys - width:])
        rel = pltpu.roll(rel, width - RB + 1, 1, stride=1, stride_axis=0)
        col = lax.broadcasted_iota(jnp.int32, (RB, width), 1)
        row = lax.broadcasted_iota(jnp.int32, (RB, width), 0) + r * RB
        live = ((col >= comp - comp_live) & (col < comp)) | (
            (col >= start - mem_live) & (col - start <= row))
        masked = jnp.where(live, content + rel, -1e30)
        top = jnp.max(masked, axis=-1, keepdims=True)
        weights = jnp.exp(masked - top)
        probs = (weights / jnp.sum(weights, axis=-1, keepdims=True)).astype(BF)
        mix_ref[rows] = nn(probs, v_ref[:width]).astype(BF)
        p_ref[0, rows, :width] = nn(flip, probs).astype(BF)


def attention(scal, qc, qp, k, v, pos, comp, mem):
    seg, width = qc.shape
    keys = k.shape[0]
    dh = width // H
    q_spec = pl.BlockSpec((seg, dh), lambda h, s: (0, h))
    k_spec = pl.BlockSpec((keys, dh), lambda h, s: (0, h))
    return call(
        functools.partial(attention_kernel, comp=comp, mem=mem), "attention", (H,),
        [q_spec, q_spec, k_spec, k_spec, k_spec],
        [out((H, seg, keys), BF, (1, seg, keys), lambda h, s: (h, 0, 0)),
         out((seg, width), BF, (seg, dh), lambda h, s: (0, h))],
        [], scal, (qc, qp, k, v, pos), 16 * seg * keys * width)


def attention_back_kernel(s_ref, p_ref, gm_ref, qc_ref, qp_ref, k_ref, v_ref, pos_ref, gq_ref,
                          gk_ref, gv_ref, gp_ref, gc_ref, gb_ref, gs_ref, sh_ref, pr_ref, rev_ref,
                          *, start, scale):
    seg, keys = qc_ref.shape[0], k_ref.shape[0]
    flip = (lax.broadcasted_iota(jnp.int32, (RB, RB), 0)
            + lax.broadcasted_iota(jnp.int32, (RB, RB), 1) == RB - 1).astype(BF)
    sum_c = jnp.zeros((1, gc_ref.shape[1]), F32)
    sum_p = jnp.zeros((1, gc_ref.shape[1]), F32)
    for r in range(seg // RB):
        width = start + RB * (r + 1)
        rows = slice(r * RB, (r + 1) * RB)
        for n, ref in enumerate((gm_ref, qc_ref, qp_ref)):
            rev_ref[n, rows] = nn(flip, ref[rows]).astype(BF)
        low = p_ref[0, rows, :width]
        probs = low.astype(F32)
        weighted = probs * nt(rev_ref[0, rows], v_ref[:width])
        scores = (weighted - probs * jnp.sum(weighted, axis=-1, keepdims=True))
        low_scores = scores.astype(BF)
        moved = pltpu.roll(scores, 0, 1, stride=1, stride_axis=0).astype(BF)
        gs_ref[rows, :width] = low_scores
        sh_ref[rows, keys - width:] = moved
        pr_ref[rows, :width] = low
        if width < keys:
            gs_ref[rows, width:] = jnp.zeros((RB, keys - width), BF)
            pr_ref[rows, width:] = jnp.zeros((RB, keys - width), BF)
            sh_ref[rows, : keys - width] = jnp.zeros((RB, keys - width), BF)
        grad_c = nn(low_scores, k_ref[:width])
        grad_p = nn(moved, pos_ref[keys - width:])
        sum_c += jnp.sum(grad_c, axis=0, keepdims=True)
        sum_p += jnp.sum(grad_p, axis=0, keepdims=True)
        gq_ref[rows] = nn(flip, ((grad_c + grad_p) * scale).astype(BF)).astype(BF)
    gc_ref[...] = sum_c * scale
    gb_ref[...] = sum_p * scale
    gv_ref[...] = tn(rev_ref[0], pr_ref[...]).astype(BF)
    gk_ref[...] = tn(rev_ref[1], gs_ref[...]).astype(BF)
    gp_ref[...] = tn(rev_ref[2], sh_ref[...]).astype(BF)


def attention_back(scal, probs, gm, qc, qp, k, v, pos, start, scale):
    seg, width = qc.shape
    keys = k.shape[0]
    dh = width // H
    q_spec = pl.BlockSpec((seg, dh), lambda h, s: (0, h))
    k_spec = pl.BlockSpec((keys, dh), lambda h, s: (0, h))
    turned = lambda: out((width, keys), BF, (dh, keys), lambda h, s: (h, 0))
    sums = lambda: out((1, width), F32, (1, dh), lambda h, s: (0, h))
    big = pltpu.VMEM((seg, keys), BF)
    return call(
        functools.partial(attention_back_kernel, start=start, scale=scale), "attention_back", (H,),
        [pl.BlockSpec((1, seg, keys), lambda h, s: (h, 0, 0)), q_spec, q_spec, q_spec, k_spec,
         k_spec, k_spec],
        [out((seg, width), BF, (seg, dh), lambda h, s: (0, h)), turned(), turned(), turned(),
         sums(), sums()],
        [big, big, big, pltpu.VMEM((3, seg, dh), BF)], scal, (probs, gm, qc, qp, k, v, pos),
        24 * seg * keys * width)


def mixed_kernel(s_ref, tok_ref, mix_ref, o_ref, m_ref, t_ref, g_ref, att_ref, sec_ref, w_ref):
    @pl.when(pl.program_id(0) == 0)
    def _():
        place(w_ref, s_ref, o_ref, m_ref, t_ref)

    attended = tok_ref[...].astype(F32) + nn(mix_ref[...], w_ref[...])
    att_ref[...] = attended
    sec_ref[...] = (norm_rows(attended)[0] * g_ref[...]).astype(BF)


def mix_out(scal, tokens, mixed, parts, gain):
    seg, width = tokens.shape
    blk = 256
    own, mine, theirs = parts
    row = pl.BlockSpec((blk, width), lambda i, s: (i, 0))
    return call(
        mixed_kernel, "mix_out", (seg // blk,),
        [row, row, whole(own.shape), whole(mine.shape), whole(theirs.shape), whole((1, width))],
        [out((seg, width), F32, (blk, width), lambda i, s: (i, 0)),
         out((seg, width), BF, (blk, width), lambda i, s: (i, 0)),
         out((width, width), BF, (width, width), lambda i, s: (0, 0))],
        [], scal, (tokens, mixed, own, mine, theirs, gain), 2 * seg * width * width)


def part_shape(rows, cols, n_dp, extra=()):
    return (2, n_dp // 2) + extra + (rows // n_dp, cols // 2)


def put(keep, send, buf, values, core, width):
    rows, cols = values.shape
    pairs, _, chunk, _ = buf.shape
    buf[...] = values.reshape(pairs, 2, chunk, cols)
    mine, theirs = buf[:, core], buf[:, 1 - core]
    for y in range(cols // width):
        keep[y] = mine[:, :, y * width:(y + 1) * width].astype(BF)
        send[y] = theirs[:, :, y * width:(y + 1) * width].astype(BF)


def ffn_kernel(s_ref, sec_ref, cot_ref, att_ref, uo_ref, um_ref, ut_ref, do_ref, dm_ref, dt_ref,
               b_ref, g_ref, out_ref, gatt_ref, uk_ref, us_ref, dk_ref, ds_ref, gb_ref, gg_ref,
               gout_ref, wu_ref, wd_ref, acc_ref, gsec_ref, ubuf, dbuf):
    i, n = pl.program_id(0), pl.num_programs(0)
    y, core = s_ref[0], s_ref[1]

    @pl.when(i == 0)
    def _():
        row = lax.broadcasted_iota(jnp.int32, cot_ref.shape, 0)
        gout_ref[...] = jnp.where(row < s_ref[2], cot_ref[...], jnp.zeros((), BF))
        acc_ref[...] = att_ref[...]
        gsec_ref[...] = jnp.zeros_like(gsec_ref)

    place(wu_ref, s_ref, uo_ref, um_ref, ut_ref)
    half = i // (n // 2)
    side = (i % (n // 2)) // (n // 4)

    @pl.when(half == y)
    def _():
        wd_ref[...] = do_ref[...]

    @pl.when((half != y) & (side == core))
    def _():
        wd_ref[...] = dm_ref[...]

    @pl.when((half != y) & (side != core))
    def _():
        wd_ref[...] = dt_ref[...]

    second, gout = sec_ref[...], gout_ref[...]
    v = nn(second, wu_ref[...]) + b_ref[...]
    t = jnp.tanh(GELU_C * (v + 0.044715 * (v * v * v)))
    act = (0.5 * v * (1.0 + t)).astype(BF)
    slope = 0.5 * (1.0 + t) + 0.5 * v * (1.0 - t * t) * (GELU_C * (1.0 + 3 * 0.044715 * v * v))
    acc_ref[...] += nn(act, wd_ref[...])
    grad_inner = (nt(gout, wd_ref[...]) * slope).astype(BF)
    gb_ref[...] = jnp.sum(grad_inner.astype(F32), axis=0, keepdims=True)
    gsec_ref[...] += nt(grad_inner, wu_ref[...])
    put(dk_ref, ds_ref, dbuf, tn(gout, act), core, act.shape[1])
    put(uk_ref, us_ref, ubuf, tn(grad_inner, second), core, second.shape[1] // 2)

    @pl.when(i == n - 1)
    def _():
        out_ref[...] = acc_ref[...].astype(BF)
        unit, scale = norm_rows(att_ref[...])
        grad = gsec_ref[...]
        gg_ref[...] = jnp.sum(grad * unit, axis=0, keepdims=True)
        gatt_ref[...] = norm_back(grad, g_ref[...], unit, scale) + gout_ref[...].astype(F32)


def feed_forward(scal, second, cotangent, attended, up_parts, down_parts, bias_up, gain, n_dp):
    seg, width = second.shape
    inner = bias_up.shape[1]
    n = 8
    blk = inner // n
    uo, um, ut = up_parts
    do, dm, dt = down_parts
    uch, dch = inner // n_dp, width // n_dp
    pairs = blk // (2 * uch)
    col = lambda a: pl.BlockSpec((a.shape[0], blk), lambda i, s: (0, i))
    row = lambda m: pl.BlockSpec((blk, width), lambda i, s: (i % m, 0))
    up_shape, down_shape = part_shape(inner, width, n_dp), part_shape(width, inner, n_dp)
    up_out = lambda: out(up_shape, BF, (2, pairs, uch, width // 2), lambda i, s: (0, i, 0, 0))
    down_out = lambda: out(down_shape, BF, (1, n_dp // 2, dch, blk),
                           lambda i, s: (i // (n // 2), 0, 0, i % (n // 2)))
    full = (seg, width)
    return call(
        ffn_kernel, "feed_forward", (n,),
        [whole(full), whole(full), whole(full), col(uo), col(um), col(ut), row(n // 2),
         row(n // 4), row(n // 4), pl.BlockSpec((1, blk), lambda i, s: (0, i)), whole((1, width))],
        [out(full, BF, full, lambda i, s: (0, 0)), out(full, F32, full, lambda i, s: (0, 0)),
         up_out(), up_out(), down_out(), down_out(),
         out((1, inner), F32, (1, blk), lambda i, s: (0, i)),
         out((1, width), F32, (1, width), lambda i, s: (0, 0))],
        [pltpu.VMEM(full, BF), pltpu.VMEM((width, blk), BF), pltpu.VMEM((blk, width), BF),
         pltpu.VMEM(full, F32), pltpu.VMEM(full, F32), pltpu.VMEM((pairs, 2, uch, width), F32),
         pltpu.VMEM((n_dp // 2, 2, dch, blk), F32)],
        scal, (second, cotangent, attended, uo, um, ut, do, dm, dt, bias_up, gain),
        12 * seg * width * inner)


def mid_kernel(s_ref, ga_ref, mix_ref, w_ref, gm_ref, k_ref, x_ref, acc_ref, buf):
    i = pl.program_id(0)
    low = ga_ref[...].astype(BF)
    part = nt(low, w_ref[...])

    @pl.when(i == 0)
    def _():
        acc_ref[...] = part

    @pl.when(i > 0)
    def _():
        acc_ref[...] += part

    put(k_ref, x_ref, buf, tn(low, mix_ref[...]), s_ref[1], mix_ref.shape[1] // 2)

    @pl.when(i == pl.num_programs(0) - 1)
    def _():
        gm_ref[...] = acc_ref[...].astype(BF)


def mid(scal, grad_attended, mixed, w_out, n_dp):
    seg, width = mixed.shape
    blk = 256
    chunk = width // n_dp
    pairs = blk // (2 * chunk)
    shape = part_shape(width, width, n_dp)
    half = lambda: out(shape, BF, (2, pairs, chunk, width // 2), lambda i, s: (0, i, 0, 0))
    return call(
        mid_kernel, "grad_mixed", (width // blk,),
        [pl.BlockSpec((seg, blk), lambda i, s: (0, i)), whole((seg, width)),
         pl.BlockSpec((width, blk), lambda i, s: (0, i))],
        [out((seg, width), BF, (seg, width), lambda i, s: (0, 0)), half(), half()],
        [pltpu.VMEM((seg, width), F32), pltpu.VMEM((pairs, 2, chunk, width), F32)], scal,
        (grad_attended, mixed, w_out), 4 * seg * width * width)


def rel_kernel(s_ref, gp_ref, tab_ref, k_ref, x_ref, buf):
    put(k_ref, x_ref, buf, nn(gp_ref[...], tab_ref[...]), s_ref[1], tab_ref.shape[1] // 2)


def grad_rel(scal, gpos, table, n_dp):
    rows, width = table.shape
    blk = 256
    chunk = width // n_dp
    pairs = blk // (2 * chunk)
    shape = part_shape(width, width, n_dp)
    half = lambda: out(shape, BF, (2, pairs, chunk, width // 2), lambda i, s: (0, i, 0, 0))
    return call(
        rel_kernel, "grad_rel", (width // blk,),
        [pl.BlockSpec((blk, rows), lambda i, s: (i, 0)), whole((rows, width))],
        [half(), half()], [pltpu.VMEM((pairs, 2, chunk, width), F32)], scal, (gpos, table),
        2 * rows * width * width)


def grad_qkv_kernel(s_ref, gq_ref, gk_ref, gv_ref, x_ref, qk, qx, kk, kx, vk, vx, buf):
    core = s_ref[1]
    seg = gq_ref.shape[0]
    width = x_ref.shape[1] // 2
    put(kk, kx, buf, nn(gk_ref[...], x_ref[...]), core, width)
    put(vk, vx, buf, nn(gv_ref[...], x_ref[...]), core, width)
    put(qk, qx, buf, tn(gq_ref[...], x_ref[x_ref.shape[0] - seg:]), core, width)


def grad_qkv(scal, gq, gk, gv, normed, n_dp):
    rows, width = normed.shape
    seg = gq.shape[0]
    blk = 256
    chunk = width // n_dp
    pairs = blk // (2 * chunk)
    shape = part_shape(width, width, n_dp)
    half = lambda: out(shape, BF, (2, pairs, chunk, width // 2), lambda i, s: (0, i, 0, 0))
    turned = pl.BlockSpec((blk, rows), lambda i, s: (i, 0))
    return call(
        grad_qkv_kernel, "grad_qkv", (width // blk,),
        [pl.BlockSpec((seg, blk), lambda i, s: (0, i)), turned, turned, whole((rows, width))],
        [half() for _ in range(6)], [pltpu.VMEM((pairs, 2, chunk, width), F32)], scal,
        (gq, gk, gv, normed), 2 * (2 * rows + seg) * width * width)


def grad_tokens_kernel(s_ref, gq_ref, gk_ref, gv_ref, x_ref, tok_ref, ga_ref, w_ref, g_ref,
                       gt_ref, gg_ref, *, first):
    i = pl.program_id(0)
    grad = nt(gk_ref[...].T, w_ref[1]) + nt(gv_ref[...].T, w_ref[2])
    gain = g_ref[...]

    @pl.when(i == 0)
    def _():
        gg_ref[...] = jnp.zeros_like(gg_ref)

    @pl.when(i < first)
    def _():
        gg_ref[...] += jnp.sum(grad * x_ref[...].astype(F32), axis=0, keepdims=True) / gain

    @pl.when(i >= first)
    def _():
        total = grad + nt(gq_ref[...], w_ref[0])
        unit, scale = norm_rows(tok_ref[...].astype(F32))
        gg_ref[...] += jnp.sum(total * unit, axis=0, keepdims=True)
        gt_ref[...] = (ga_ref[...] + norm_back(total, gain, unit, scale)).astype(BF)


def grad_tokens(scal, gq, gk, gv, normed, tokens, grad_attended, w, gain):
    rows, width = normed.shape
    seg = tokens.shape[0]
    blk = 256
    first = (rows - seg) // blk
    turned = pl.BlockSpec((width, blk), lambda i, s: (0, i))
    late = pl.BlockSpec((blk, width), lambda i, s: (jnp.maximum(i - first, 0), 0))
    return call(
        functools.partial(grad_tokens_kernel, first=first), "grad_tokens", (rows // blk,),
        [late, turned, turned, pl.BlockSpec((blk, width), lambda i, s: (i, 0)), late, late,
         whole(w.shape), whole((1, width))],
        [out((seg, width), BF, (blk, width), lambda i, s: (jnp.maximum(i - first, 0), 0)),
         out((1, width), F32, (1, width), lambda i, s: (0, 0))],
        [], scal, (gq, gk, gv, normed, tokens, grad_attended, w, gain),
        2 * (2 * rows + seg) * width * width)


def squeeze_kernel(s_ref, gr_ref, o_ref, m_ref, t_ref, w_ref, g_ref, sq_ref, low_ref, k_ref, v_ref):
    y, core = s_ref[0], s_ref[1]
    half, quarter = o_ref.shape[1], m_ref.shape[1]
    base = (1 - y) * half
    total = jnp.zeros(sq_ref.shape, F32)
    for t in range(3):
        at = lambda off, size: gr_ref[t, :, pl.ds(pl.multiple_of(off, quarter), size)]
        total += nn(at(y * half, half), o_ref[t])
        total += nn(at(base + core * quarter, quarter), m_ref[t])
        total += nn(at(base + (1 - core) * quarter, quarter), t_ref[t])
    sq_ref[...] = total
    low_ref[...] = total.astype(BF)
    unit = (norm_rows(total)[0] * g_ref[...]).astype(BF)
    k_ref[...] = nn(unit, w_ref[1]).astype(BF)
    v_ref[...] = nn(unit, w_ref[2]).astype(BF)


def squeeze(scal, groups, parts, w, gain):
    _, rows, width = groups.shape
    own, mine, theirs = parts
    shape = (rows, width)
    here = lambda d: out(shape, d, shape, lambda i, s: (0, 0))
    return call(
        squeeze_kernel, "squeeze", (1,),
        [whole(groups.shape), whole(own.shape), whole(mine.shape), whole(theirs.shape),
         whole(w.shape), whole((1, width))],
        [here(F32), here(BF), here(BF), here(BF)], [], scal, (groups, own, mine, theirs, w, gain),
        10 * rows * width * width)


def masked_softmax(scores, live):
    masked = jnp.where(live, scores, -1e30)
    weights = jnp.exp(masked - jnp.max(masked, axis=-1, keepdims=True))
    return weights / jnp.sum(weights, axis=-1, keepdims=True)


def recon_kernel(s_ref, pr_ref, ok_ref, ov_ref, ck_ref, cv_ref, gk_ref, gv_ref):
    seg_len = s_ref[2]
    count = seg_len // 3
    probe = pr_ref[...]
    seg, mem, comp = probe.shape[0], ok_ref.shape[0], ck_ref.shape[0]
    old_live = lax.broadcasted_iota(jnp.int32, (seg, mem), 1) < 3 * count
    old = nn(masked_softmax(nt(probe, ok_ref[...]), old_live).astype(BF), ov_ref[...])
    live = lax.broadcasted_iota(jnp.int32, (seg, comp), 1) < count
    probs = masked_softmax(nt(probe, ck_ref[...]), live)
    low = probs.astype(BF)
    gap = nn(low, cv_ref[...]) - old
    row = lax.broadcasted_iota(jnp.int32, gap.shape, 0)
    grad_out = (jnp.where(row < seg_len, gap, 0.0) * (2.0 / seg_len.astype(F32))).astype(BF)
    gv_ref[...] = tn(low, grad_out).astype(BF)
    weighted = probs * nt(grad_out, cv_ref[...])
    scores = (weighted - probs * jnp.sum(weighted, axis=-1, keepdims=True)).astype(BF)
    gk_ref[...] = tn(scores, probe).astype(BF)


def reconstruct(scal, probe, k, v, ck, cv, mem):
    seg, width = probe.shape
    rows = ck.shape[0]
    dh = width // H
    at = lambda n, b: pl.BlockSpec((n, dh), lambda h, s: (b, h))
    grads = lambda: out((rows, width), BF, (rows, dh), lambda h, s: (0, h))
    return call(
        recon_kernel, "reconstruct", (H,),
        [at(seg, 0), at(mem, 1), at(mem, 1), at(rows, 0), at(rows, 0)], [grads(), grads()], [],
        scal, (probe, k, v, ck, cv), 4 * seg * width * mem + 12 * seg * width * rows)


def grad_comp_kernel(s_ref, sq_ref, gk_ref, gv_ref, w_ref, g_ref, gr_ref, k_ref, x_ref, low_ref, buf):
    @pl.when(pl.program_id(0) == 0)
    def _():
        grad = nt(gk_ref[...], w_ref[1]) + nt(gv_ref[...], w_ref[2])
        unit, scale = norm_rows(sq_ref[...])
        low_ref[...] = norm_back(grad, g_ref[...], unit, scale).astype(BF)

    part = tn(low_ref[...], gr_ref[0])
    put(k_ref.at[:, :, 0], x_ref.at[:, :, 0], buf, part, s_ref[1], part.shape[1] // 2)


def grad_comp(scal, squeezed, gk, gv, w, gain, groups, n_dp):
    taps, rows, width = groups.shape
    chunk = width // n_dp
    shape = part_shape(width, width, n_dp, (taps,))
    half = lambda: out(shape, BF, shape[:2] + (1,) + shape[3:], lambda i, s: (0, 0, i, 0, 0))
    here = whole((rows, width))
    return call(
        grad_comp_kernel, "grad_comp", (taps,),
        [here, here, here, whole(w.shape), whole((1, width)),
         pl.BlockSpec((1, rows, width), lambda i, s: (i, 0, 0))],
        [half(), half()],
        [pltpu.VMEM((rows, width), BF), pltpu.VMEM((n_dp // 2, 2, chunk, width), F32)], scal,
        (squeezed, gk, gv, w, gain, groups), 10 * rows * width * width)


class Links:
    def __init__(self):
        self.dp = lax.axis_index("dp")
        self.y = lax.axis_index("fsdp")
        self.n_dp = lax.axis_size("dp")
        self.bits = self.n_dp.bit_length() - 1

    def bit(self, axis):
        return self.y if axis == "y" else (self.dp >> axis) & 1

    def swap(self, value, axis):
        if axis == "y":
            return lax.ppermute(value, "fsdp", [(0, 1), (1, 0)])
        return lax.ppermute(value, "dp", [(i, i ^ (1 << axis)) for i in range(self.n_dp)])


def ordered(a, b, bit):
    shape = (a.shape[0], 2) + a.shape[1:]
    at = lax.broadcasted_iota(jnp.int32, shape, 1)
    return jnp.where(at == bit, a[:, None], b[:, None])


def gather(links, local, first, second):
    n, rows, cols = local.shape
    place_of = links.bit(0) * 4 + links.bit(second) * 2 + links.bit(first)
    piece = lax.dynamic_index_in_dim(local.reshape(n, 8, rows // 8, cols), place_of, 1, False)
    one = links.swap(piece, "y")
    two = ordered(one, links.swap(one, first), links.bit(first))
    two = two.reshape(n, rows // 4, cols)
    mine = ordered(two, links.swap(two, second), links.bit(second)).reshape(n, rows // 2, cols)
    return local, mine, links.swap(mine, 0)


def stage_kernel(s_ref, *refs, slots):
    n = len(slots)
    for c in range(n):
        keep, recv, held, send = refs[c], refs[n + c], refs[2 * n + c], refs[3 * n + c]
        bit = s_ref[slots[c]]
        total = lambda b: (keep[:, b].astype(F32) + recv[:, b].astype(F32)).astype(held.dtype)
        held[...] = total(bit)
        send[...] = total(1 - bit)


def stage(links, keeps, recvs, axes, places, steps):
    ins, outs = [], []
    args = [[], []]
    for keep, recv, where in zip(keeps, recvs, places):
        lead, tail = keep.shape[:-3], keep.shape[-3:]
        pre, post = math.prod(lead[:where]), math.prod(lead[where + 1:])
        view = (pre, 2, post * tail[0]) + tail[1:]
        rows = view[2]
        split = 1 if keep.dtype == F32 else steps
        bp = max(pre // split, 1)
        br = rows * bp * split // (pre * split) if split == 1 else rows * pre // (split * bp)
        br = min(max(br, 1), rows)
        nr = rows // br
        if split == 1:
            spec = lambda i, s: (0, 0, 0, 0, 0)
            held = lambda i, s: (0, 0, 0, 0)
            bp, br = pre, rows
        else:
            spec = functools.partial(lambda nr, i, s: (i // nr, 0, i % nr, 0, 0), nr)
            held = functools.partial(lambda nr, i, s: (i // nr, i % nr, 0, 0), nr)
        ins.append(pl.BlockSpec((bp, 2, br) + tail[1:], spec))
        shape = (pre, rows) + tail[1:]
        outs.append(out(shape, keep.dtype, (bp, br) + tail[1:], held))
        args[0].append(keep.reshape(view))
        args[1].append(recv.reshape(view))
    scal = jnp.stack([links.bit(a) for a in axes]).astype(jnp.int32)
    done = call(
        functools.partial(stage_kernel, slots=tuple(range(len(axes)))), "stage", (steps,),
        ins + ins, outs + outs, [], scal, args[0] + args[1], 0)
    n = len(keeps)
    shapes = [k.shape[:w] + k.shape[w + 1:] for k, w in zip(keeps, places)]
    held = [d.reshape(s) for d, s in zip(done[:n], shapes)]
    send = [d.reshape(s) for d, s in zip(done[n:], shapes)]
    return held, send


def final_kernel(s_ref, *refs):
    n = len(refs) // 3
    for c in range(n):
        total = refs[c][...].astype(F32) + refs[n + c][...].astype(F32)
        if total.shape[1] == 1:
            refs[2 * n + c][...] = total
        else:
            for t in range(total.shape[0]):
                refs[2 * n + c][t] = total[t].T


def final(keeps, recvs, scal):
    ins, outs = [], []
    for keep in keeps:
        taps, rows, cols = keep.shape
        ins.append(whole(keep.shape))
        shape = keep.shape if rows == 1 else (taps, cols, rows)
        outs.append(out(shape, F32, shape, lambda i, s: (0, 0, 0)))
    return call(final_kernel, "final", (1,), ins + ins, outs, [], scal, list(keeps) + list(recvs), 0)


def scatter(links, chains, orders, scal, steps):
    names = ["y"] + list(range(links.bits - 1, 0, -1))
    left = [list(names) for _ in chains]
    split = lambda a: a.reshape((2,) * len(names) + a.shape[2:])
    keeps = [split(k) for k, _ in chains]
    recvs = [links.swap(split(s), 0) for _, s in chains]
    for level in range(len(names)):
        axes = [o[level] for o in orders]
        places = [l.index(a) for l, a in zip(left, axes)]
        count = steps if level < 2 else 1
        keeps, sends = stage(links, keeps, recvs, axes, places, count)
        for l, a in zip(left, axes):
            l.remove(a)
        recvs = [links.swap(s, a) for s, a in zip(sends, axes)]
    return final(keeps, recvs, scal)


def turns(links):
    rest = list(range(3, links.bits))
    return [[1, "y", 2] + rest, ["y", 2, 1] + rest, [2, 1, "y"] + rest]


def sinusoid(table_rows, table_width):
    distance = (table_rows - 1 - jnp.arange(table_rows)).astype(F32)
    frequency = jnp.exp(
        jnp.arange(0, table_width, 2).astype(F32) * (-math.log(10000.0) / table_width)
    )
    angles = distance[:, None] * frequency[None, :]
    return jnp.concatenate([jnp.sin(angles), jnp.cos(angles)], axis=1)


def body(tokens, memory, compressed, cotangent, seg_len, mem_fill, cmem_fill, w_qkv, w_rel, w_out,
         w_up, w_down, w_comp, norm_gain1, norm_gain2, bias_content, bias_position, bias_up):
    streams = tokens.shape[0]
    assert streams == 1
    links = Links()
    n_dp = links.n_dp
    seg, width = tokens.shape[1:]
    mem, comp = memory.shape[1], compressed.shape[1]
    start = comp + mem
    keys = start + seg
    squeezed_rows = mem // 3
    scale = (width // H) ** (-0.5)
    current, recent, distant = tokens[0], memory[0], compressed[0]
    seg_length = seg_len[0]
    core = links.bit(0)
    scal = jnp.stack([links.y, core, seg_length, mem_fill[0], cmem_fill[0]]).astype(jnp.int32)
    gain1, gain2 = norm_gain1.reshape(1, -1), norm_gain2.reshape(1, -1)

    qkv_parts = gather(links, w_qkv, 2, 1)
    rel_parts = [p[0] for p in gather(links, w_rel[None], 1, 2)]
    comp_parts = gather(links, w_comp, 1, 2)
    out_parts = [p[0] for p in gather(links, w_out[None], 2, 1)]
    up_parts = [p[0] for p in gather(links, w_up[None], 2, 1)]
    down_parts = [p[0] for p in gather(links, w_down[None], 1, 2)]

    hidden = jnp.concatenate([distant, recent, current], axis=0).astype(F32)
    normed = (norm_rows(hidden)[0] * norm_gain1).astype(BF)
    table = sinusoid(keys, width).astype(BF)
    pad = -squeezed_rows % 64
    groups = jnp.stack([
        jnp.pad(recent[t:3 * squeezed_rows:3], ((0, pad), (0, 0))) for t in range(3)])

    k, v, qc, qp, probe, w_full = project_qkv(
        scal, normed, qkv_parts, bias_content, bias_position, seg, scale)
    pos = project_position(scal, table, rel_parts)
    probs, mixed = attention(scal, qc, qp, k, v, pos, comp, mem)

    squeezed, squeezed_low, ck, cv = squeeze(scal, groups, comp_parts, w_full, gain1)
    gck, gcv = reconstruct(scal, probe, k, v, ck, cv, mem)
    comp_chain = grad_comp(scal, squeezed, gck, gcv, w_full, gain1, groups, n_dp)

    attended, second, w_out_full = mix_out(scal, current, mixed, out_parts, gain2)
    (output, grad_attended, up_keep, up_send, down_keep, down_send, sum_bias, sum_gain2
     ) = feed_forward(scal, second, cotangent[0], attended, up_parts, down_parts,
                      bias_up.reshape(1, -1), gain2, n_dp)
    grad_mix, out_keep, out_send = mid(scal, grad_attended, mixed, w_out_full, n_dp)
    gq, gk, gv, gpos, sum_content, sum_position = attention_back(
        scal, probs, grad_mix, qc, qp, k, v, pos, start, scale)
    qkv_chains = grad_qkv(scal, gq, gk, gv, normed, n_dp)
    rel_chain = grad_rel(scal, gpos, table, n_dp)
    grad_rows, sum_gain1 = grad_tokens(
        scal, gq, gk, gv, normed, current, grad_attended, w_full, gain1)

    turn = turns(links)
    tap = lambda a: a[:, :, None]
    (grad_comp_t,) = scatter(links, [comp_chain], [turn[2]], scal, 4)
    grad_up_t, grad_down_t, grad_out_t = scatter(
        links, [(tap(up_keep), tap(up_send)), (tap(down_keep), tap(down_send)),
                (tap(out_keep), tap(out_send))],
        [turn[0], turn[1], turn[2]], scal, 4)
    small = jnp.concatenate(
        [s.reshape(n_dp, 2, -1) for s in
         (sum_gain1, sum_gain2, sum_content, sum_position, sum_bias)], axis=-1)
    small = small.reshape(n_dp // 2, 2, 2, 1, 1, -1).transpose(1, 2, 0, 3, 4, 5)
    small_keep = lax.dynamic_index_in_dim(small, core, 0, False)
    small_send = lax.dynamic_index_in_dim(small, 1 - core, 0, False)
    qk, qx, kk, kx, vk, vx = [tap(a) for a in qkv_chains]
    grad_q_t, grad_k_t, grad_v_t, grad_rel_t, vec = scatter(
        links, [(qk, qx), (kk, kx), (vk, vx), tuple(tap(a) for a in rel_chain),
                (small_keep, small_send)],
        [turn[0], turn[1], turn[2], turn[0], turn[1]], scal, 2)
    each = width // (2 * n_dp)
    vec = vec.reshape(-1)
    grad_gain1, grad_gain2, grad_content, grad_position = [
        vec[n * each:(n + 1) * each] for n in range(4)]

    new_memory = lax.dynamic_slice_in_dim(
        jnp.concatenate([recent, current], axis=0), seg_length, mem, 0)
    new_compressed = lax.dynamic_slice_in_dim(
        jnp.concatenate([distant, squeezed_low[:squeezed_rows]], axis=0), seg_length // 3, comp, 0)
    return (output[None], grad_rows[None], new_memory[None], new_compressed[None],
            jnp.concatenate([grad_q_t, grad_k_t, grad_v_t], axis=0), grad_rel_t[0], grad_out_t[0],
            grad_up_t[0], grad_down_t[0], grad_comp_t, grad_gain1, grad_gain2, grad_content,
            grad_position, vec[4 * each:])


def solution(mesh):
    rows = P(("dp", "fsdp"), None, None)
    one = P(("dp", "fsdp"))
    return jax.shard_map(
        body,
        mesh=mesh,
        in_specs=(rows, rows, rows, rows, one, one, one, P(None, "fsdp", None), P("fsdp", None),
                  P("fsdp", None), P("fsdp", None), P("fsdp", None), P(None, "fsdp", None), P(),
                  P(), P(), P(), P()),
        out_specs=(rows, rows, rows, rows, P(None, "fsdp", "dp"), P("fsdp", "dp"),
                   P("fsdp", "dp"), P("fsdp", "dp"), P("fsdp", "dp"), P(None, "fsdp", "dp"), one,
                   one, one, one, one),
        check_vma=False,
    )
```

```python
import functools
import math

import jax
import jax.numpy as jnp
from jax import lax
from jax.experimental import pallas as pl
from jax.experimental.pallas import tpu as pltpu
from jax.sharding import PartitionSpec as P

H = 8
BF = jnp.bfloat16
F32 = jnp.float32
VMEM = 60 * 1024 * 1024
GELU_C = math.sqrt(2.0 / math.pi)
COST = 1024
Y, CORE, SEG_LEN, MEM_LIVE, COMP_LIVE, PIECE_A, PIECE_B, BITS = range(8)


def nn(a, b):
    return lax.dot_general(a, b, (((1,), (0,)), ((), ())), preferred_element_type=F32)


def nt(a, b):
    return lax.dot_general(a, b, (((1,), (1,)), ((), ())), preferred_element_type=F32)


def tn(a, b):
    return lax.dot_general(a, b, (((0,), (0,)), ((), ())), preferred_element_type=F32)


class Steps:
    def __init__(self, scal):
        self.scal = scal
        self.token = None

    def __call__(self, kernel, name, grid, ins, outs, scratch, args, flops, aliases={}):
        before = [] if self.token is None else [self.token]
        n_in, n_out, extra = len(ins), len(outs), len(before)

        def ordered_kernel(s_ref, *refs):
            rest = refs[n_in + extra:]
            kernel(s_ref, *refs[:n_in], *rest[:n_out], *rest[n_out + 1:])

        anywhere = pl.BlockSpec(memory_space=pl.ANY)
        done = pl.pallas_call(
            ordered_kernel,
            name=name,
            out_shape=[s for s, _ in outs] + [jax.ShapeDtypeStruct((8, 128), F32)],
            grid_spec=pltpu.PrefetchScalarGridSpec(
                num_scalar_prefetch=1,
                grid=grid,
                in_specs=list(ins) + [anywhere] * extra,
                out_specs=[b for _, b in outs] + [anywhere],
                scratch_shapes=scratch,
            ),
            compiler_params=pltpu.CompilerParams(
                vmem_limit_bytes=VMEM, dimension_semantics=("arbitrary",) * len(grid)
            ),
            input_output_aliases=aliases,
            cost_estimate=pl.CostEstimate(flops=COST, bytes_accessed=COST, transcendentals=0),
        )(self.scal, *args, *before)
        *done, self.token = done
        return done


def follow(run, *values):
    anywhere = pl.BlockSpec(memory_space=pl.ANY)
    return run(
        lambda *refs: None, "follow", (1,), [anywhere] * len(values),
        [(jax.ShapeDtypeStruct(v.shape, v.dtype), anywhere) for v in values], [], values, 0,
        {n + 1: n for n in range(len(values))})


def whole(shape):
    return pl.BlockSpec(shape, lambda i, s: (0,) * len(shape))


def out(shape, dtype, block, index):
    return (jax.ShapeDtypeStruct(shape, dtype), pl.BlockSpec(block, index))


def fixed(shape, dtype):
    return out(shape, dtype, shape, lambda i, s: (0,) * len(shape))


def norm_rows(rows):
    centred = rows - jnp.mean(rows, axis=-1, keepdims=True)
    spread = jnp.mean(centred * centred, axis=-1, keepdims=True)
    scale = lax.rsqrt(spread + 1e-05)
    return centred * scale, scale


def norm_back(grad, gain, unit, scale):
    g = grad * gain
    inner = jnp.mean(g * unit, axis=-1, keepdims=True)
    return scale * (g - jnp.mean(g, axis=-1, keepdims=True) - unit * inner)


def place(dst, s_ref, own, mine, theirs, cols=slice(None)):
    half, quarter = own.shape[-2], mine.shape[-2]
    y, core = s_ref[Y], s_ref[CORE]
    base = (1 - y) * half
    at = lambda start, size: pl.ds(pl.multiple_of(start, quarter), size)
    dst[at(y * half, half), cols] = own[:, cols]
    dst[at(base + core * quarter, quarter), cols] = mine[...]
    dst[at(base + (1 - core) * quarter, quarter), cols] = theirs[...]


def pack_first_kernel(s_ref, rel, k, v, qa, qb, o_rel, o_a, o_b):
    width = rel.shape[-1]
    o_rel[...] = rel[...]
    o_a[0, :, :width] = k[0, 0]
    o_a[0, :, width:] = qa[0, 0]
    o_b[0, :, :width] = v[0, 0]
    o_b[0, :, width:] = qb[0, 0]


def pack_rest_kernel(s_ref, c0, c1, c2, ow, up, down, o_c, o_d, o_up, o_down):
    o_c[0] = c0[0, 0]
    o_c[1] = c1[0, 0]
    o_d[0] = c2[0, 0]
    o_d[1] = ow[0]
    o_up[...] = up[...]
    o_down[...] = down[...]


def eighths(a):
    lead = a.shape[:-2]
    return a.reshape(lead + (8, a.shape[-2] // 8, a.shape[-1]))


def part_of(a, where, n=0, cols=1, c=0):
    block = (1,) * (a.ndim - 2) + (a.shape[-2], a.shape[-1] // cols)
    if a.ndim == 3:
        return pl.BlockSpec(block, lambda i, s: (s[where], 0, c))
    return pl.BlockSpec(block, lambda i, s: (n, s[where], 0, c))


def pack_first(run, w_qkv, w_rel):
    qkv, rel = eighths(w_qkv), eighths(w_rel)
    part, width = rel.shape[1:]
    return run(
        pack_first_kernel, "pack_first", (1,),
        [part_of(rel, PIECE_A), part_of(qkv, PIECE_A, 1), part_of(qkv, PIECE_B, 2),
         part_of(qkv, PIECE_A, 0, 2, 0), part_of(qkv, PIECE_B, 0, 2, 1)],
        [fixed((1, part, width), BF), fixed((1, part, width * 3 // 2), BF),
         fixed((1, part, width * 3 // 2), BF)],
        [], (rel, qkv, qkv, qkv, qkv), 0)


def pack_rest(run, w_out, w_up, w_down, w_comp):
    comp, ow, up, down = eighths(w_comp), eighths(w_out), eighths(w_up), eighths(w_down)
    part, width = ow.shape[1:]
    return run(
        pack_rest_kernel, "pack_rest", (1,),
        [part_of(comp, PIECE_A, 0), part_of(comp, PIECE_A, 1), part_of(comp, PIECE_B, 2),
         part_of(ow, PIECE_B), part_of(up, PIECE_A), part_of(down, PIECE_B)],
        [fixed((2, part, width), BF), fixed((2, part, width), BF),
         fixed((1,) + up.shape[1:], BF), fixed((1,) + down.shape[1:], BF)],
        [], (comp, comp, comp, ow, up, down), 0)


def ordered(mine, theirs, bit):
    n, rows, cols = mine.shape
    at = lax.broadcasted_iota(jnp.int32, (n, 2, rows, cols), 1)
    return jnp.where(at == bit, mine[:, None], theirs[:, None]).reshape(n, 2 * rows, cols)


def normed_kernel(s_ref, d_ref, m_ref, t_ref, g_ref, x_ref):
    i = pl.program_id(0)
    for n, ref in enumerate((d_ref, m_ref, t_ref)):
        @pl.when(i // 2 == n)
        def _(ref=ref):
            x_ref[...] = (norm_rows(ref[...].astype(F32))[0] * g_ref[...]).astype(BF)


def norm_hidden(run, distant, recent, current, gain):
    mem, width = recent.shape
    blk = mem // 2
    part = lambda n: pl.BlockSpec((blk, width), lambda i, s: (jnp.clip(i - 2 * n, 0, 1), 0))
    return run(
        normed_kernel, "norm_hidden", (6,),
        [part(0), part(1), part(2), whole(gain.shape)],
        [out((3 * mem, width), BF, (blk, width), lambda i, s: (i, 0))],
        [], (distant, recent, current, gain), 0)[0]


def constants_kernel(s_ref, m_ref, sa_ref, ca_ref, sb_ref, cb_ref, tab_ref, gr_ref, wide_ref,
                     *, groups):
    i = pl.program_id(0)
    blk, width = tab_ref.shape
    half = width // 2
    fine = sb_ref.shape[0]
    for n in range(blk // fine):
        rows = slice(n * fine, (n + 1) * fine)
        a = i * (blk // fine) + n
        sa, ca = sa_ref[pl.ds(a, 1)], ca_ref[pl.ds(a, 1)]
        tab_ref[rows, :half] = (sa * cb_ref[...] + ca * sb_ref[...]).astype(BF)
        tab_ref[rows, half:] = (ca * cb_ref[...] - sa * sb_ref[...]).astype(BF)

    @pl.when(i == 0)
    def _():
        mem = m_ref.shape[0]
        lanes = wide_ref.shape[2]
        count = gr_ref.shape[1]
        live = lax.broadcasted_iota(jnp.int32, (count, 1), 0) < groups
        for n in range(width // lanes):
            cols = slice(n * lanes, (n + 1) * lanes)
            wide_ref[n, :mem] = m_ref[:, cols].astype(F32)
            wide_ref[n, mem:] = jnp.zeros((wide_ref.shape[1] - mem, lanes), F32)
            for t in range(3):
                rows = jnp.where(live, wide_ref[n, pl.ds(t, count, stride=3)], 0.0)
                gr_ref[t, :, cols] = rows.astype(BF)


def constants(run, recent, angles, groups):
    mem, width = recent.shape
    keys = 3 * mem
    blk = 512
    padded = groups + (-groups) % 64
    ins = (recent,) + angles
    return run(
        functools.partial(constants_kernel, groups=groups), "constants", (keys // blk,),
        [whole(a.shape) for a in ins],
        [out((keys, width), BF, (blk, width), lambda i, s: (i, 0)),
         fixed((3, padded, width), BF)],
        [pltpu.VMEM((width // 128, 3 * padded, 128), F32)], ins, 0)


def qkv_kernel(s_ref, x_ref, o_ref, am_ref, at_ref, bm_ref, bt_ref, bc_ref, bp_ref, kv_ref,
               qc_ref, qp_ref, pr_ref, w_ref, *, scale):
    i = pl.program_id(0)
    rows, width = x_ref.shape
    seg = qc_ref.shape[0]
    blk = 256
    lo, hi = slice(0, width // 2), slice(width // 2, width)
    own, dst = o_ref.at[0], w_ref.at[0]

    @pl.when(i == 0)
    def _():
        place(dst, s_ref, own, am_ref.at[0, :, :width], at_ref.at[0, :, :width])

    @pl.when(i == 1)
    def _():
        place(dst, s_ref, own, bm_ref.at[0, :, :width], bt_ref.at[0, :, :width])

    @pl.when(i == 2)
    def _():
        place(dst, s_ref, own, am_ref.at[0, :, width:], at_ref.at[0, :, width:], lo)
        place(dst, s_ref, own, bm_ref.at[0, :, width:], bt_ref.at[0, :, width:], hi)

    @pl.when(i < 2)
    def _():
        def some(n, _):
            at = pl.ds(pl.multiple_of(n * blk, blk), blk)
            kv_ref[0, at] = nn(x_ref[at], dst[...]).astype(BF)
            return 0

        lax.fori_loop(0, rows // blk, some, 0)

    @pl.when(i == 2)
    def _():
        for n in range(seg // blk):
            at = slice(n * blk, (n + 1) * blk)
            q = nn(x_ref[rows - seg + n * blk:rows - seg + (n + 1) * blk], dst[...])
            qc_ref[at] = ((q + bc_ref[...]) * scale).astype(BF)
            qp_ref[at] = ((q + bp_ref[...]) * scale).astype(BF)
            pr_ref[at] = (q * scale).astype(BF)


def project_qkv(run, normed, w_qkv, a_parts, b_parts, bias_content, bias_position, seg, scale):
    rows, width = normed.shape
    turn = lambda i, s: ((i + 1) % 3, 0, 0)
    parts = a_parts + b_parts
    return run(
        functools.partial(qkv_kernel, scale=scale), "project_qkv", (3,),
        [whole((rows, width)), pl.BlockSpec((1, width // 2, width), turn)]
        + [whole(p.shape) for p in parts] + [whole((1, width)), whole((1, width))],
        [out((2, rows, width), BF, (1, rows, width), lambda i, s: (jnp.minimum(i, 1), 0, 0)),
         fixed((seg, width), BF), fixed((seg, width), BF), fixed((seg, width), BF),
         out((3, width, width), BF, (1, width, width), turn)],
        [], (normed, w_qkv) + parts + (bias_content.reshape(1, -1), bias_position.reshape(1, -1)),
        2 * (2 * rows + seg) * width * width)


def position_kernel(s_ref, x_ref, o_ref, m_ref, t_ref, p_ref, w_ref):
    @pl.when(pl.program_id(0) == 0)
    def _():
        place(w_ref, s_ref, o_ref, m_ref.at[0], t_ref.at[0])

    p_ref[...] = nn(x_ref[...], w_ref[...]).astype(BF)


def project_position(run, table, own, parts):
    rows, width = table.shape
    blk = 512
    return run(
        position_kernel, "project_position", (rows // blk,),
        [pl.BlockSpec((blk, width), lambda i, s: (i, 0)), whole(own.shape)]
        + [whole(p.shape) for p in parts],
        [out((rows, width), BF, (blk, width), lambda i, s: (i, 0))],
        [pltpu.VMEM((width, width), BF)], (table, own) + parts,
        2 * rows * width * width)[0]


RB = 256


def flip_matrix():
    return (lax.broadcasted_iota(jnp.int32, (RB, RB), 0)
            + lax.broadcasted_iota(jnp.int32, (RB, RB), 1) == RB - 1).astype(BF)


def attention_kernel(s_ref, qc_ref, qp_ref, k_ref, v_ref, pos_ref, p_ref, mix_ref, bias_ref,
                     *, comp, mem):
    seg, keys = qc_ref.shape[0], k_ref.shape[1]
    start = comp + mem

    @pl.when(pl.program_id(0) == 0)
    def _():
        mem_live, comp_live = s_ref[MEM_LIVE], s_ref[COMP_LIVE]
        col = lax.broadcasted_iota(jnp.int32, bias_ref.shape, 1)
        row = lax.broadcasted_iota(jnp.int32, bias_ref.shape, 0)
        live = ((col >= comp - comp_live) & (col < comp)) | (
            (col >= start - mem_live) & (col - start <= row))
        bias_ref[...] = jnp.where(live, 0.0, -1e30)

    flip = flip_matrix()
    for r in range(seg // RB):
        width = start + RB * (r + 1)
        rows = slice(r * RB, (r + 1) * RB)
        content = nt(qc_ref[rows], k_ref[0, :width])
        rel = nt(qp_ref[rows], pos_ref[keys - width:])
        rel = pltpu.roll(rel, width - RB + 1, 1, stride=1, stride_axis=0)
        masked = content + rel + bias_ref[rows, :width]
        top = jnp.max(masked, axis=-1, keepdims=True)
        weights = jnp.exp(masked - top)
        probs = (weights * (1.0 / jnp.sum(weights, axis=-1, keepdims=True))).astype(BF)
        mix_ref[rows] = nn(probs, v_ref[0, :width]).astype(BF)
        p_ref[0, rows, :width] = nn(flip, probs).astype(BF)


def attention(run, qc, qp, kv, pos, comp, mem, half):
    seg, width = qc.shape
    keys = kv.shape[1]
    dh = width // H
    n = H // 2
    first = half * n
    q_spec = pl.BlockSpec((seg, dh), lambda h, s: (0, h + first))
    of = lambda m: pl.BlockSpec((1, keys, dh), lambda h, s: (m, 0, h + first))
    return run(
        functools.partial(attention_kernel, comp=comp, mem=mem), "attention", (n,),
        [q_spec, q_spec, of(0), of(1), pl.BlockSpec((keys, dh), lambda h, s: (0, h + first))],
        [out((n, seg, keys), BF, (1, seg, keys), lambda h, s: (h, 0, 0)),
         out((seg, width // 2), BF, (seg, dh), lambda h, s: (0, h))],
        [pltpu.VMEM((seg, keys), F32)], (qc, qp, kv, kv, pos), 16 * seg * keys * width)


def attention_back_kernel(s_ref, p_ref, gm_ref, qc_ref, qp_ref, k_ref, v_ref, pos_ref, gq_ref,
                          gk_ref, gv_ref, gp_ref, gc_ref, gb_ref, gs_ref, sh_ref, pr_ref, rev_ref,
                          *, start, scale):
    seg, keys = qc_ref.shape[0], k_ref.shape[1]
    flip = flip_matrix()
    sum_c = jnp.zeros((1, gc_ref.shape[1]), F32)
    sum_p = jnp.zeros((1, gc_ref.shape[1]), F32)
    for r in range(seg // RB):
        width = start + RB * (r + 1)
        rows = slice(r * RB, (r + 1) * RB)
        for n, ref in enumerate((gm_ref, qc_ref, qp_ref)):
            rev_ref[n, rows] = nn(flip, ref[rows]).astype(BF)
        low = p_ref[0, rows, :width]
        probs = low.astype(F32)
        weighted = probs * nt(rev_ref[0, rows], v_ref[0, :width])
        scores = (weighted - probs * jnp.sum(weighted, axis=-1, keepdims=True))
        low_scores = scores.astype(BF)
        moved = pltpu.roll(scores, 0, 1, stride=1, stride_axis=0).astype(BF)
        gs_ref[rows, :width] = low_scores
        sh_ref[rows, keys - width:] = moved
        pr_ref[rows, :width] = low
        if width < keys:
            gs_ref[rows, width:] = jnp.zeros((RB, keys - width), BF)
            pr_ref[rows, width:] = jnp.zeros((RB, keys - width), BF)
            sh_ref[rows, : keys - width] = jnp.zeros((RB, keys - width), BF)
        grad_c = nn(low_scores, k_ref[0, :width])
        grad_p = nn(moved, pos_ref[keys - width:])
        sum_c += jnp.sum(grad_c, axis=0, keepdims=True)
        sum_p += jnp.sum(grad_p, axis=0, keepdims=True)
        gq_ref[rows] = nn(flip, ((grad_c + grad_p) * scale).astype(BF)).astype(BF)
    gc_ref[...] = sum_c * scale
    gb_ref[...] = sum_p * scale
    gv_ref[...] = tn(rev_ref[0], pr_ref[...]).astype(BF)
    gk_ref[...] = tn(rev_ref[1], gs_ref[...]).astype(BF)
    gp_ref[...] = tn(rev_ref[2], sh_ref[...]).astype(BF)


def attention_back(run, probs, gm, qc, qp, kv, pos, start, scale, half):
    seg, width = qc.shape
    keys = kv.shape[1]
    dh = width // H
    n = H // 2
    first = half * n
    q_spec = pl.BlockSpec((seg, dh), lambda h, s: (0, h + first))
    of = lambda m: pl.BlockSpec((1, keys, dh), lambda h, s: (m, 0, h + first))
    turned = lambda: out((width // 2, keys), BF, (dh, keys), lambda h, s: (h, 0))
    sums = lambda: out((1, width // 2), F32, (1, dh), lambda h, s: (0, h))
    big = pltpu.VMEM((seg, keys), BF)
    return run(
        functools.partial(attention_back_kernel, start=start, scale=scale), "attention_back", (n,),
        [pl.BlockSpec((1, seg, keys), lambda h, s: (h, 0, 0)), q_spec, q_spec, q_spec,
         of(0), of(1), pl.BlockSpec((keys, dh), lambda h, s: (0, h + first))],
        [out((seg, width // 2), BF, (seg, dh), lambda h, s: (0, h)), turned(), turned(), turned(),
         sums(), sums()],
        [big, big, big, pltpu.VMEM((3, seg, dh), BF)], (probs[half], gm, qc, qp, kv, kv, pos),
        12 * seg * keys * width)


def mixed_kernel(s_ref, tok_ref, a_ref, b_ref, o_ref, m_ref, t_ref, g_ref, att_ref, sec_ref, w_ref):
    @pl.when(pl.program_id(0) == 0)
    def _():
        place(w_ref, s_ref, o_ref, m_ref.at[1], t_ref.at[1])

    mid = a_ref.shape[1]
    attended = (tok_ref[...].astype(F32) + nn(a_ref[...], w_ref[:mid])
                + nn(b_ref[...], w_ref[mid:]))
    att_ref[...] = attended
    sec_ref[...] = (norm_rows(attended)[0] * g_ref[...]).astype(BF)


def mix_out(run, tokens, mixed, own, parts, gain):
    seg, width = tokens.shape
    blk = 256
    row = pl.BlockSpec((blk, width), lambda i, s: (i, 0))
    side = pl.BlockSpec((blk, width // 2), lambda i, s: (i, 0))
    return run(
        mixed_kernel, "mix_out", (seg // blk,),
        [row, side, side, whole(own.shape)] + [whole(p.shape) for p in parts] + [whole((1, width))],
        [out((seg, width), F32, (blk, width), lambda i, s: (i, 0)),
         out((seg, width), BF, (blk, width), lambda i, s: (i, 0)),
         fixed((width, width), BF)],
        [], (tokens,) + mixed + (own,) + parts + (gain,), 2 * seg * width * width)


def part_shape(rows, cols, n_dp, taps, cut=1):
    return (2, n_dp // (2 * cut), taps, rows // n_dp, cols // 2)


def low_or_wide(chunk):
    return BF if chunk % 16 == 0 else F32


def by_core(buf, values, core):
    pairs, _, chunk, cols = buf.shape
    buf[...] = values.astype(buf.dtype).reshape(pairs, 2, chunk, cols)
    pick = lambda c: buf[:, c].reshape(pairs * chunk, cols)
    return jnp.concatenate([pick(core), pick(1 - core)], axis=0).astype(BF)


def put(keep, send, values):
    half = values.shape[0] // 2
    shape = keep.shape[:-1] + (values.shape[1],)
    keep[...] = values[:half].reshape(shape).astype(BF)
    send[...] = values[half:].reshape(shape).astype(BF)


def ffn_kernel(s_ref, sec_ref, cot_ref, att_ref, uo_ref, um_ref, ut_ref, do_ref, dm_ref, dt_ref,
               b_ref, g_ref, wo_ref, out_ref, gatt_ref, gm_ref, uk_ref, us_ref, dk_ref, ds_ref,
               gb_ref, gg_ref, gout_ref, turn_ref, wu_ref, wd_ref, acc_ref, gsec_ref, ubuf, dbuf):
    i, n = pl.program_id(0), pl.num_programs(0)
    y, core = s_ref[Y], s_ref[CORE]

    @pl.when(i == 0)
    def _():
        row = lax.broadcasted_iota(jnp.int32, cot_ref.shape, 0)
        live = jnp.where(row < s_ref[SEG_LEN], cot_ref[...], jnp.zeros((), BF))
        gout_ref[...] = live
        turn_ref[...] = by_core(dbuf, live.T, core)
        acc_ref[...] = att_ref[...]
        gsec_ref[...] = jnp.zeros_like(gsec_ref)

    place(wu_ref, s_ref, uo_ref, um_ref.at[0], ut_ref.at[0])
    half = i // (n // 2)
    side = (i % (n // 2)) // (n // 4)

    @pl.when(half == y)
    def _():
        wd_ref[...] = do_ref[...]

    @pl.when((half != y) & (side == core))
    def _():
        wd_ref[...] = dm_ref[0]

    @pl.when((half != y) & (side != core))
    def _():
        wd_ref[...] = dt_ref[0]

    second, gout = sec_ref[...], gout_ref[...]
    v = nn(second, wu_ref[...]) + b_ref[...]
    square = v * v
    gate = 0.5 + 0.5 * jnp.tanh(v * (GELU_C + (GELU_C * 0.044715) * square))
    act = (v * gate).astype(BF)
    slope = gate + (gate - gate * gate) * v * (2 * GELU_C + (6 * GELU_C * 0.044715) * square)
    acc_ref[...] += nn(act, wd_ref[...])
    grad_inner = nt(gout, wd_ref[...]) * slope
    low = grad_inner.astype(BF)
    gb_ref[...] = jnp.sum(low.astype(F32), axis=0, keepdims=True)
    gsec_ref[...] += nt(low, wu_ref[...])
    put(dk_ref.at[0, :, 0], ds_ref.at[0, :, 0], nn(turn_ref[...], act))
    part = nn(by_core(ubuf, low.T, core), second)
    width = part.shape[1] // 2
    for side in range(2):
        put(uk_ref.at[side, :, 0], us_ref.at[side, :, 0], part[:, side * width:(side + 1) * width])

    @pl.when(i == n - 1)
    def _():
        out_ref[...] = acc_ref[...].astype(BF)
        unit, scale = norm_rows(att_ref[...])
        grad = gsec_ref[...]
        gg_ref[...] = jnp.sum(grad * unit, axis=0, keepdims=True)
        gatt = norm_back(grad, g_ref[...], unit, scale) + gout_ref[...].astype(F32)
        gatt_ref[...] = gatt
        gm_ref[...] = nt(gatt.astype(BF), wo_ref[...]).astype(BF)


def feed_forward(run, second, cotangent, attended, w_up, up_parts, w_down, down_parts, bias_up,
                 gain, w_out, n_dp):
    seg, width = second.shape
    inner = bias_up.shape[1]
    n = 8
    blk = inner // n
    um, ut = up_parts
    dm, dt = down_parts
    uch, dch = inner // n_dp, width // n_dp
    pairs = blk // (2 * uch)
    col = lambda a: pl.BlockSpec((a.shape[0], blk), lambda i, s: (0, i))
    col3 = lambda a: pl.BlockSpec((1, a.shape[1], blk), lambda i, s: (0, 0, i))
    row3 = pl.BlockSpec((1, blk, width), lambda i, s: (0, i % (n // 4), 0))
    up_shape = part_shape(inner, width, n_dp, 1)
    down_shape = part_shape(width, inner, n_dp, n // 2)[:-1] + (blk,)
    up_out = lambda: out(up_shape, BF, (2, pairs, 1, uch, width // 2),
                         lambda i, s: (0, i, 0, 0, 0))
    down_out = lambda: out(down_shape, BF, (1, n_dp // 2, 1, dch, blk),
                           lambda i, s: (i // (n // 2), 0, i % (n // 2), 0, 0))
    full = (seg, width)
    return run(
        ffn_kernel, "feed_forward", (n,),
        [whole(full), whole(full), whole(full), col(w_up), col3(um), col3(ut),
         pl.BlockSpec((blk, width), lambda i, s: (i % (n // 2), 0)), row3, row3,
         pl.BlockSpec((1, blk), lambda i, s: (0, i)), whole((1, width)), whole((width, width))],
        [fixed(full, BF), fixed(full, F32), fixed(full, BF), up_out(), up_out(), down_out(),
         down_out(), out((1, inner), F32, (1, blk), lambda i, s: (0, i)), fixed((1, width), F32)],
        [pltpu.VMEM(full, BF), pltpu.VMEM((width, seg), BF), pltpu.VMEM((width, blk), BF),
         pltpu.VMEM((blk, width), BF), pltpu.VMEM(full, F32), pltpu.VMEM(full, F32),
         pltpu.VMEM((pairs, 2, uch, seg), low_or_wide(uch)),
         pltpu.VMEM((n_dp // 2, 2, dch, seg), low_or_wide(dch))],
        (second, cotangent, attended, w_up, um, ut, w_down, dm, dt, bias_up, gain, w_out),
        12 * seg * width * inner)


def grads_kernel(s_ref, gk_ref, gv_ref, gp_ref, gq_ref, ga_ref, x_ref, tab_ref, ma_ref, mb_ref, w_ref,
                 ak_ref, ax_ref, bk_ref, bx_ref, gg_ref, k_s, v_s, p_s, q_s, o_s, big, small):
    core = s_ref[CORE]
    rows = x_ref.shape[0]
    seg = gq_ref.shape[0]

    @pl.when(pl.program_id(0) == 0)
    def _():
        k_s[...] = by_core(big, gk_ref[...], core)
        v_s[...] = by_core(big, gv_ref[...], core)
        p_s[...] = by_core(big, gp_ref[...], core)
        q_s[...] = by_core(small, gq_ref[...].T, core)
        o_s[...] = by_core(small, ga_ref[...].astype(BF).T, core)

    x = x_ref[...]
    pairs, _, chunk, _ = small.shape
    n = pairs * chunk

    def both(a, b, tap, values):
        put(a.at[0, :, tap], b.at[0, :, tap], values)

    def gain(values, m):
        turned = w_ref[m].T.astype(F32)
        whole_ = turned.reshape(pairs, 2, chunk, turned.shape[1])
        even, odd = whole_[:, 0].reshape(n, -1), whole_[:, 1].reshape(n, -1)
        first = jnp.where(core == 0, even, odd)
        last = jnp.where(core == 0, odd, even)
        return (jnp.sum(values[:n] * first, axis=0, keepdims=True)
                + jnp.sum(values[n:] * last, axis=0, keepdims=True))

    part = nn(k_s[...], x)
    both(ak_ref, ax_ref, 0, part)
    total = gain(part, 1)
    part = nn(v_s[...], x)
    both(ak_ref, ax_ref, 1, part)
    total += gain(part, 2)
    part = nn(q_s[...], x[rows - seg:])
    both(bk_ref, bx_ref, 0, part)
    total += gain(part, 0)
    both(bk_ref, bx_ref, 1, nn(p_s[...], tab_ref[...]))
    gg_ref[...] = total
    i, n = pl.program_id(0), pl.num_programs(0)

    @pl.when(i < n // 2)
    def _():
        both(bk_ref, bx_ref, 2, nn(o_s[...], ma_ref[...]))

    @pl.when(i >= n // 2)
    def _():
        both(bk_ref, bx_ref, 2, nn(o_s[...], mb_ref[...]))


def projection_grads(run, turned, gq, gatt, normed, table, mixed, w, n_dp, half):
    rows, width = normed.shape
    seg = gq.shape[0]
    blk = 256
    chunk = width // n_dp
    mid = width // 2
    gk, gv, gpos = turned
    count = mid // blk
    col = lambda r: pl.BlockSpec((r, blk), lambda i, s: (0, i))
    shape = lambda taps: part_shape(width, width, n_dp, taps, 2)
    half_of = lambda taps: out(shape(taps), BF, (1,) + shape(taps)[1:4] + (blk,),
                               lambda i, s: (i // count, 0, 0, 0, i % count))
    side = pl.BlockSpec((seg, blk), lambda i, s: (0, i % count))
    kind = low_or_wide(chunk)
    pairs = mid // (2 * chunk)
    return run(
        grads_kernel, "projection_grads", (width // blk,),
        [whole(gk.shape), whole(gk.shape), whole(gk.shape), whole(gq.shape),
         pl.BlockSpec((seg, mid), lambda i, s: (0, half)), col(rows), col(rows), side, side,
         pl.BlockSpec((3, blk, mid), lambda i, s: (0, i, half))],
        [half_of(2), half_of(2), half_of(3), half_of(3),
         out((1, width), F32, (1, blk), lambda i, s: (0, i))],
        [pltpu.VMEM((mid, rows), BF)] * 3 + [pltpu.VMEM((mid, seg), BF)] * 2
        + [pltpu.VMEM((pairs, 2, chunk, rows), kind), pltpu.VMEM((pairs, 2, chunk, seg), kind)],
        (gk, gv, gpos, gq, gatt, normed, table) + mixed + (w,),
        (3 * rows + 2 * seg) * width * width)


def grad_tokens_kernel(s_ref, ka_ref, kb_ref, va_ref, vb_ref, qa_ref, qb_ref, tok_ref, ga_ref,
                       w_ref, g_ref, gt_ref, acc_ref):
    i = pl.program_id(0)
    mid = w_ref.shape[2] // 2
    left, right = w_ref[0, :, :mid], w_ref[0, :, mid:]

    @pl.when(i == 0)
    def _():
        acc_ref[...] = nn(left, ka_ref[...]) + nn(right, kb_ref[...])

    @pl.when(i == 1)
    def _():
        acc_ref[...] += nn(left, va_ref[...]) + nn(right, vb_ref[...])

    @pl.when(i == 2)
    def _():
        total = (acc_ref[...] + nt(left, qa_ref[...]) + nt(right, qb_ref[...])).T
        unit, scale = norm_rows(tok_ref[...].astype(F32))
        gt_ref[...] = (ga_ref[...] + norm_back(total, g_ref[...], unit, scale)).astype(BF)


def grad_tokens(run, gk, gv, gq, tokens, grad_attended, w, gain):
    seg, width = tokens.shape
    rows = gk[0].shape[1]
    late = pl.BlockSpec((width // 2, seg), lambda i, s: (0, rows // seg - 1))
    side = whole((seg, width // 2))
    return run(
        grad_tokens_kernel, "grad_tokens", (3,),
        [late] * 4 + [side] * 2 + [whole((seg, width)), whole((seg, width)),
         pl.BlockSpec((1, width, width), lambda i, s: ((i + 1) % 3, 0, 0)), whole((1, width))],
        [fixed((seg, width), BF)], [pltpu.VMEM((width, seg), F32)],
        tuple(gk) + tuple(gv) + tuple(gq) + (tokens, grad_attended, w, gain),
        6 * seg * width * width)[0]


def squeeze_kernel(s_ref, gr_ref, o_ref, am_ref, at_ref, bm_ref, bt_ref, w_ref, g_ref, sq_ref,
                   low_ref, k_ref, v_ref):
    y, core = s_ref[Y], s_ref[CORE]
    half, quarter = o_ref.shape[1], am_ref.shape[1]
    base = (1 - y) * half
    total = jnp.zeros(sq_ref.shape, F32)
    for t in range(3):
        m_ref, t_ref, n = (am_ref, at_ref, t) if t < 2 else (bm_ref, bt_ref, 0)
        at = lambda off, size: gr_ref[t, :, pl.ds(pl.multiple_of(off, quarter), size)]
        total += nn(at(y * half, half), o_ref[t])
        total += nn(at(base + core * quarter, quarter), m_ref[n])
        total += nn(at(base + (1 - core) * quarter, quarter), t_ref[n])
    sq_ref[...] = total
    low_ref[...] = total.astype(BF)
    unit = (norm_rows(total)[0] * g_ref[...]).astype(BF)
    k_ref[...] = nn(unit, w_ref[1]).astype(BF)
    v_ref[...] = nn(unit, w_ref[2]).astype(BF)


def squeeze(run, groups, own, a_parts, b_parts, w, gain):
    _, rows, width = groups.shape
    parts = a_parts + b_parts
    shape = (rows, width)
    return run(
        squeeze_kernel, "squeeze", (1,),
        [whole(groups.shape), whole(own.shape)] + [whole(p.shape) for p in parts]
        + [whole(w.shape), whole((1, width))],
        [fixed(shape, F32), fixed(shape, BF), fixed(shape, BF), fixed(shape, BF)], [],
        (groups, own) + parts + (w, gain), 10 * rows * width * width)


def masked_softmax(scores, live):
    masked = jnp.where(live, scores, -1e30)
    weights = jnp.exp(masked - jnp.max(masked, axis=-1, keepdims=True))
    return weights * (1.0 / jnp.sum(weights, axis=-1, keepdims=True))


def recon_kernel(s_ref, pr_ref, ok_ref, ov_ref, ck_ref, cv_ref, gk_ref, gv_ref):
    seg_len = s_ref[SEG_LEN]
    count = seg_len // 3
    probe = pr_ref[...]
    seg, mem, comp = probe.shape[0], ok_ref.shape[1], ck_ref.shape[0]
    old_live = lax.broadcasted_iota(jnp.int32, (1, mem), 1) < 3 * count
    old = nn(masked_softmax(nt(probe, ok_ref[0]), old_live).astype(BF), ov_ref[0])
    live = lax.broadcasted_iota(jnp.int32, (1, comp), 1) < count
    probs = masked_softmax(nt(probe, ck_ref[...]), live)
    low = probs.astype(BF)
    gap = nn(low, cv_ref[...]) - old
    row = lax.broadcasted_iota(jnp.int32, gap.shape, 0)
    grad_out = (jnp.where(row < seg_len, gap, 0.0) * (2.0 / seg_len.astype(F32))).astype(BF)
    gv_ref[...] = tn(low, grad_out).astype(BF)
    weighted = probs * nt(grad_out, cv_ref[...])
    scores = (weighted - probs * jnp.sum(weighted, axis=-1, keepdims=True)).astype(BF)
    gk_ref[...] = tn(scores, probe).astype(BF)


def reconstruct(run, probe, kv, ck, cv, mem):
    seg, width = probe.shape
    rows = ck.shape[0]
    dh = width // H
    at = lambda n, b: pl.BlockSpec((n, dh), lambda h, s: (b, h))
    old = lambda m: pl.BlockSpec((1, mem, dh), lambda h, s: (m, 1, h))
    grads = lambda: out((rows, width), BF, (rows, dh), lambda h, s: (0, h))
    return run(
        recon_kernel, "reconstruct", (H,),
        [at(seg, 0), old(0), old(1), at(rows, 0), at(rows, 0)], [grads(), grads()], [],
        (probe, kv, kv, ck, cv), 4 * seg * width * mem + 12 * seg * width * rows)


def grad_comp_kernel(s_ref, sq_ref, gk_ref, gv_ref, w_ref, g_ref, gr_ref, k_ref, x_ref, low_ref, buf):
    @pl.when(pl.program_id(0) == 0)
    def _():
        grad = nt(gk_ref[...], w_ref[1]) + nt(gv_ref[...], w_ref[2])
        unit, scale = norm_rows(sq_ref[...])
        low = norm_back(grad, g_ref[...], unit, scale).astype(BF)
        low_ref[...] = by_core(buf, low.astype(F32).T, s_ref[CORE])

    part = nn(low_ref[...], gr_ref[0])
    width = part.shape[1] // 2
    for y in range(2):
        put(k_ref.at[y, :, 0], x_ref.at[y, :, 0], part[:, y * width:(y + 1) * width])


def grad_comp(run, squeezed, gk, gv, w, gain, groups, n_dp):
    taps, rows, width = groups.shape
    chunk = width // n_dp
    shape = part_shape(width, width, n_dp, taps)
    half = lambda: out(shape, BF, shape[:2] + (1,) + shape[3:], lambda i, s: (0, 0, i, 0, 0))
    here = whole((rows, width))
    return run(
        grad_comp_kernel, "grad_comp", (taps,),
        [here, here, here, whole(w.shape), whole((1, width)),
         pl.BlockSpec((1, rows, width), lambda i, s: (i, 0, 0))],
        [half(), half()],
        [pltpu.VMEM((width, rows), BF), pltpu.VMEM((n_dp // 2, 2, chunk, rows), low_or_wide(chunk))],
        (squeezed, gk, gv, w, gain, groups), 10 * rows * width * width)


class Links:
    def __init__(self):
        self.dp = lax.axis_index("dp")
        self.y = lax.axis_index("fsdp")
        self.n_dp = lax.axis_size("dp")
        self.top = self.n_dp.bit_length() - 2

    def bit(self, axis):
        return self.y if axis == "y" else (self.dp >> axis) & 1

    def swap(self, value, axis):
        if axis == "y":
            return lax.ppermute(value, "fsdp", [(0, 1), (1, 0)])
        return lax.ppermute(value, "dp", [(i, i ^ (1 << axis)) for i in range(self.n_dp)])


class Chain:
    def __init__(self, links, keep, send, axes, order):
        self.links, self.axes, self.order = links, list(axes), list(order)
        lead = (2,) * len(self.axes)
        self.keep = keep.reshape(lead + keep.shape[2:])
        self.recv = links.swap(send.reshape(self.keep.shape), 0)

    def specs(self, steps):
        axis = self.order[0]
        where = self.axes.index(axis)
        lead, tail = self.keep.shape[:len(self.axes)], self.keep.shape[len(self.axes):]
        pre, post = math.prod(lead[:where]), math.prod(lead[where + 1:])
        rows = post * tail[0]
        view = (pre, 2, rows) + tail[1:]
        steps = math.gcd(steps, pre * post)
        bp = max(pre // steps, 1)
        nr = steps * bp // pre
        br = rows // nr
        last = steps - 1

        def read(i, s):
            i = jnp.minimum(i, last)
            return (i // nr, 0, i % nr, 0, 0)

        def write(i, s):
            i = jnp.minimum(i, last)
            return (i // nr, i % nr, 0, 0)

        args = [self.keep.reshape(view), self.recv.reshape(view)]
        ins = [pl.BlockSpec((bp, 2, br) + tail[1:], read)] * 2
        outs = [out((pre, rows) + tail[1:], BF, (bp, br) + tail[1:], write)] * 2
        slot = Y if axis == "y" else BITS + axis - 1

        def kernel(s_ref, keep, recv, held, send):
            @pl.when(pl.program_id(0) <= last)
            def _():
                bit = s_ref[slot]
                total = lambda b: (keep[:, b].astype(F32) + recv[:, b].astype(F32)).astype(BF)
                held[...] = total(bit)
                send[...] = total(1 - bit)

        def take(held, send):
            shape = lead[:where] + lead[where + 1:] + tail
            self.keep = held.reshape(shape)
            self.axes.pop(where)
            self.order.pop(0)
            self.recv = self.links.swap(send.reshape(shape), axis)

        return args, ins, outs, kernel, take


def chain_of(links, keep, recv, axes, order):
    chain = Chain.__new__(Chain)
    chain.links, chain.axes, chain.order = links, list(axes), list(order)
    chain.keep, chain.recv = keep, recv
    return chain


class Deal:
    def __init__(self, links, pairs, axes, orders, cuts):
        self.links, self.axes, self.orders, self.cuts = links, axes, orders, cuts
        self.keeps = [k for k, _ in pairs]
        self.sends = [x for _, x in pairs]
        self.rows, self.cols = self.keeps[0].shape[-2:]

    def start(self, sends):
        self.recvs = [self.links.swap(x, 0) for x in sends]

    def spans(self, c):
        lo, hi = self.cuts[c], self.cuts[c + 1]
        for n in range(2):
            a, b = max(lo - n * self.rows, 0), min(hi - n * self.rows, self.rows)
            if a < b:
                yield n, a, b

    def specs(self, steps):
        n = len(self.axes)
        lead = (2,) * n
        rows, cols = self.rows, self.cols
        firsts = [self.axes.index(o[0]) for o in self.orders]
        others = [a for a in range(n) if a not in firsts]
        split = max(steps >> len(others), 1)
        width = cols // split
        count = 2 ** len(others) * split

        def at(i):
            i = jnp.minimum(i, count - 1)
            places, rest = [0] * n, i // split
            for a in reversed(others):
                places[a] = rest % 2
                rest = rest // 2
            return places, i % split

        block = tuple(1 if a in others else 2 for a in range(n))

        def read(i, s):
            places, col = at(i)
            return (*places, 0, col)

        def write(first):
            def index(i, s):
                places, col = at(i)
                return (*places[:first], *places[first + 1:], 0, 0, col)
            return index

        args = [a.reshape(lead + (rows, cols)) for a in self.keeps + self.recvs]
        ins = [pl.BlockSpec(block + (rows, width), read)] * 4
        outs, slots = [], []
        for c, first in enumerate(firsts):
            size = self.cuts[c + 1] - self.cuts[c]
            shape = lead[1:] + (1, size, cols)
            less = block[:first] + block[first + 1:]
            outs += [out(shape, BF, less + (1, size, width), write(first))] * 2
            axis = self.axes[first]
            slots.append(Y if axis == "y" else BITS + axis - 1)

        def kernel(s_ref, *refs):
            held, sent = refs[4::2], refs[5::2]

            @pl.when(pl.program_id(0) < count)
            def _():
                for c, first in enumerate(firsts):
                    bit = s_ref[slots[c]]
                    row = 0
                    for m, a, b in self.spans(c):
                        keep, recv = refs[m], refs[2 + m]
                        for dst, side in ((held[c], bit), (sent[c], 1 - bit)):
                            pick = tuple(side if d == first else slice(None) for d in range(n))
                            pick += (slice(a, b), slice(None))
                            total = keep[pick].astype(F32) + recv[pick].astype(F32)
                            to = (slice(None),) * (n - 1) + (0, slice(row, row + b - a))
                            dst[to] = total.astype(BF)
                        row += b - a

        def take(*done):
            self.chains = []
            for c, order in enumerate(self.orders):
                axes = [a for a in self.axes if a != order[0]]
                recv = self.links.swap(done[2 * c + 1], order[0])
                self.chains.append(chain_of(self.links, done[2 * c], recv, axes, order[1:]))

        return args, ins, outs, kernel, take


class Dealt:
    def __init__(self, deal, blocks):
        self.deal, self.blocks = deal, blocks

    def specs(self, steps):
        deal = self.deal
        args = [a for c in deal.chains for a in (c.keep, c.recv)]
        rows, cols = deal.rows, deal.cols
        part = rows // self.blocks

        def kernel(s_ref, *refs):
            first, second = refs[-2:]

            @pl.when(pl.program_id(0) == 0)
            def _():
                halves = [[], []]
                for c in range(len(deal.chains)):
                    row = 0
                    for m, a, b in deal.spans(c):
                        pick = (0, slice(row, row + b - a))
                        halves[m].append(
                            refs[2 * c][pick].astype(F32) + refs[2 * c + 1][pick].astype(F32))
                        row += b - a
                one, two = [jnp.concatenate(h, axis=0) for h in halves]
                first[...] = one.T
                for n in range(self.blocks):
                    second[n * cols:(n + 1) * cols] = two[n * part:(n + 1) * part].T

        def take(*result):
            self.result = result

        outs = [fixed((cols, rows), F32), fixed((self.blocks * cols, part), F32)]
        return args, [whole(a.shape) for a in args], outs, kernel, take


class Join:
    def __init__(self, links, low, high):
        self.links, self.low, self.high = links, low, high

    def specs(self, steps):
        args = [self.low.keep, self.low.recv, self.high.keep, self.high.recv]
        shape = args[0].shape
        ins = [whole(shape)] * 4
        outs = [fixed(shape, BF)] * 2
        slot = BITS + self.links.top - 1

        def kernel(s_ref, lk, lr, hk, hr, held, send):
            @pl.when(pl.program_id(0) == 0)
            def _():
                low = (lk[...].astype(F32) + lr[...].astype(F32)).astype(BF)
                high = (hk[...].astype(F32) + hr[...].astype(F32)).astype(BF)
                upper = s_ref[slot] == 1
                held[...] = jnp.where(upper, high, low)
                send[...] = jnp.where(upper, low, high)

        def take(held, send):
            self.keep = held
            self.recv = self.links.swap(send, self.links.top)

        return args, ins, outs, kernel, take


class Small:
    def __init__(self, links, value):
        self.links, self.keep = links, value
        self.order = [0, "y"] + list(range(1, links.top + 1))
        self.send()

    def send(self):
        self.recv = self.links.swap(self.keep, self.order.pop(0)) if self.order else None

    def specs(self, steps):
        shape = self.keep.shape

        def kernel(s_ref, a, b, total):
            @pl.when(pl.program_id(0) == 0)
            def _():
                total[...] = a[...] + b[...]

        def take(total):
            self.keep = total
            self.send()

        return [self.keep, self.recv], [whole(shape)] * 2, [fixed(shape, F32)], kernel, take


class Last:
    def __init__(self, chain):
        self.chain = chain

    def specs(self, steps):
        keep, recv = self.chain.keep, self.chain.recv
        taps, rows, cols = keep.shape

        def kernel(s_ref, a, b, result):
            @pl.when(pl.program_id(0) == 0)
            def _():
                for t in range(taps):
                    result[t] = (a[t].astype(F32) + b[t].astype(F32)).T

        def take(result):
            self.result = result

        return ([keep, recv], [whole(keep.shape)] * 2, [fixed((taps, cols, rows), F32)], kernel, take)


class LastParts:
    def __init__(self, pair, rest):
        self.pair, self.rest = pair, rest

    def specs(self, steps):
        args = [self.pair.keep, self.pair.recv, self.rest.keep, self.rest.recv]
        _, rows, cols = args[0].shape

        def kernel(s_ref, a, b, c, d, qkv, rel, ow):
            @pl.when(pl.program_id(0) == 0)
            def _():
                total = lambda p, q, t: (p[t].astype(F32) + q[t].astype(F32)).T
                qkv[0] = total(c, d, 0)
                qkv[1] = total(a, b, 0)
                qkv[2] = total(a, b, 1)
                rel[...] = total(c, d, 1)
                ow[...] = total(c, d, 2)

        def take(*result):
            self.result = result

        outs = [fixed((3, cols, rows), F32), fixed((cols, rows), F32), fixed((cols, rows), F32)]
        return args, [whole(a.shape) for a in args], outs, kernel, take


class Carry:
    def __init__(self, *values):
        self.values = values

    def specs(self, steps):
        anywhere = pl.BlockSpec(memory_space=pl.ANY)
        outs = [(jax.ShapeDtypeStruct(v.shape, v.dtype), anywhere) for v in self.values]

        def take(*values):
            self.values = values

        return list(self.values), [anywhere] * len(outs), outs, lambda *refs: None, take


def advance(run, *items, steps=1):
    specs = [item.specs(steps) for item in items]
    n_in, n_out = [len(s[0]) for s in specs], [len(s[2]) for s in specs]
    aliases = {}
    for k, item in enumerate(items):
        if isinstance(item, Carry):
            aliases.update({1 + sum(n_in[:k]) + m: sum(n_out[:k]) + m for m in range(n_in[k])})

    def kernel(s_ref, *refs):
        a, b = 0, sum(n_in)
        for (_, _, _, part, _), i, o in zip(specs, n_in, n_out):
            part(s_ref, *refs[a:a + i], *refs[b:b + o])
            a, b = a + i, b + o

    done = list(run(
        kernel, "add", (steps,), [b for s in specs for b in s[1]], [o for s in specs for o in s[2]],
        [], [a for s in specs for a in s[0]], 0, aliases))
    for (_, _, outs, _, take) in specs:
        take(*done[:len(outs)])
        done = done[len(outs):]


def angle_parts(rows, width):
    fine = 32
    frequency = jnp.exp(
        jnp.arange(0, width, 2).astype(F32) * (-math.log(10000.0) / width))
    coarse = (fine * (rows // fine - 1 - jnp.arange(rows // fine))).astype(F32)
    near = (fine - 1 - jnp.arange(fine)).astype(F32)
    a, b = coarse[:, None] * frequency[None, :], near[:, None] * frequency[None, :]
    return (jnp.sin(a), jnp.cos(a), jnp.sin(b), jnp.cos(b))


def body(tokens, memory, compressed, cotangent, seg_len, mem_fill, cmem_fill, w_qkv, w_rel, w_out,
         w_up, w_down, w_comp, norm_gain1, norm_gain2, bias_content, bias_position, bias_up):
    streams = tokens.shape[0]
    assert streams == 1
    links = Links()
    n_dp, top = links.n_dp, links.top
    seg, width = tokens.shape[1:]
    mem, comp = memory.shape[1], compressed.shape[1]
    start = comp + mem
    keys = start + seg
    squeezed_rows = mem // 3
    scale = (width // H) ** (-0.5)
    current, recent, distant = tokens[0], memory[0], compressed[0]
    seg_length = seg_len[0]
    core, x, z = links.bit(0), links.bit(1), links.bit(2)
    run = Steps(jnp.stack(
        [links.y, core, seg_length, mem_fill[0], cmem_fill[0], core * 4 + x * 2 + z,
         core * 4 + z * 2 + x] + [links.bit(n) for n in range(1, top + 1)]).astype(jnp.int32))
    gain1, gain2 = norm_gain1.reshape(1, -1), norm_gain2.reshape(1, -1)

    swap = links.swap
    both = lambda value, axis: ordered(value, swap(value, axis), links.bit(axis))
    p_rel, p_a, p_b = pack_first(run, w_qkv, w_rel)
    rel, a, b = swap(p_rel, "y"), swap(p_a, "y"), swap(p_b, "y")
    normed = norm_hidden(run, distant, recent, current, gain1)
    c, d, up, down = [swap(p, "y") for p in pack_rest(run, w_out, w_up, w_down, w_comp)]
    table, groups = constants(run, recent, angle_parts(keys, width), squeezed_rows)
    rel = both(both(rel, 2), 1)
    a, b = both(a, 2), both(b, 1)
    a_far, b_far = swap(a, 1), swap(b, 2)
    pos = project_position(run, table, w_rel, (rel, swap(rel, 0)))
    a, a_far, b, b_far = follow(run, a, a_far, b, b_far)
    a, b = ordered(a, a_far, x), ordered(b, b_far, z)
    a_parts, b_parts = (a, swap(a, 0)), (b, swap(b, 0))
    c, d, up, down = follow(run, c, d, up, down)
    c_far, d_far, up_far, down_far = swap(c, 2), swap(d, 1), swap(up, 2), swap(down, 1)
    kv, qc, qp, probe, w_full = project_qkv(
        run, normed, w_qkv, a_parts, b_parts, bias_content, bias_position, seg, scale)
    c, c_far, d, d_far, up, up_far, down, down_far = follow(
        run, c, c_far, d, d_far, up, up_far, down, down_far)
    c, d, up, down = (ordered(c, c_far, z), ordered(d, d_far, x), ordered(up, up_far, z),
                      ordered(down, down_far, x))
    c_far, d_far, up_far, down_far = swap(c, 1), swap(d, 2), swap(up, 1), swap(down, 2)
    p0, m0 = attention(run, qc, qp, kv, pos, comp, mem, 0)
    p1, m1 = attention(run, qc, qp, kv, pos, comp, mem, 1)
    c, c_far, d, d_far = follow(run, c, c_far, d, d_far)
    c, d = ordered(c, c_far, x), ordered(d, d_far, z)
    c_parts, d_parts = (c, swap(c, 0)), (d, swap(d, 0))
    squeezed, squeezed_low, ck, cv = squeeze(run, groups, w_comp, c_parts, d_parts, w_full, gain1)
    far = list(range(3, top + 1))
    names, under = ["y"] + list(range(top, 0, -1)), ["y"] + list(range(top - 1, 0, -1))
    up, up_far, down, down_far = follow(run, up, up_far, down, down_far)
    up, down = ordered(up, up_far, x), ordered(down, down_far, z)
    up_parts, down_parts = (up, swap(up, 0)), (down, swap(down, 0))
    gck, gcv = reconstruct(run, probe, kv, ck, cv, mem)
    comp_chain = Chain(links, *grad_comp(run, squeezed, gck, gcv, w_full, gain1, groups, n_dp),
                       names, [2, 1, "y"] + far)

    attended, second, w_out_full = mix_out(run, current, (m0, m1), w_out, d_parts, gain2)
    advance(run, comp_chain, steps=2)
    (output, grad_attended, grad_mix, up_keep, up_send, down_keep, down_send, sum_bias, sum_gain2
     ) = feed_forward(run, second, cotangent[0], attended, w_up, up_parts, w_down, down_parts,
                      bias_up.reshape(1, -1), gain2, w_out_full, n_dp)
    rows, half = bias_up.shape[0] // n_dp, width // 2
    flat = lambda a: a.reshape(2, n_dp // 2, rows, half)
    third = max(2 * rows * 11 // 32 // 16 * 16, 8)
    deal = Deal(
        links, [(flat(up_keep), flat(up_send)), (flat(down_keep), flat(down_send))], names,
        [[1, "y", 2] + far, ["y", 2, 1] + far, [2, 1, "y"] + far],
        (0, third, 2 * third, 2 * rows))
    carry = Carry(*deal.sends)
    advance(run, comp_chain, carry)
    deal.start(carry.values)

    back = functools.partial(attention_back, run, (p0, p1), grad_mix, qc, qp, kv, pos, start, scale)
    grads = lambda turned, gq, half: projection_grads(
        run, turned, gq, grad_attended, normed, table, (m0, m1), w_full, n_dp, half)
    near = far[:-1]
    gq0, gk0, gv0, gpos0, content0, position0 = back(0)
    advance(run, deal, steps=4)
    *sent, gain_0 = grads((gk0, gv0, gpos0), gq0, 0)
    kv0, carry = sent[0], Carry(sent[1], sent[3])
    qro0 = sent[2]
    gq1, gk1, gv1, gpos1, content1, position1 = back(1)
    advance(run, *deal.chains, comp_chain, carry, steps=4)
    kv0 = Chain(links, kv0, carry.values[0], under, [2, "y", 1] + near)
    qro0 = Chain(links, qro0, carry.values[1], under, [1, 2, "y"] + near)
    *sent, gain_1 = grads((gk1, gv1, gpos1), gq1, 1)
    carry = Carry(sent[1], sent[3])
    advance(run, *deal.chains, comp_chain, kv0, qro0, carry, steps=2)
    kv1 = Chain(links, sent[0], carry.values[0], under, ["y", 2, 1] + near)
    qro1 = Chain(links, sent[2], carry.values[1], under, [1, "y", 2] + near)
    grad_rows = grad_tokens(run, (gk0, gk1), (gv0, gv1), (gq0, gq1), current, grad_attended,
                            w_full, gain1)
    row = lambda a, b: jnp.concatenate([a, b], axis=1)
    small = Small(links, jnp.concatenate(
        [(gain_0 + gain_1) / gain1, sum_gain2, row(content0, content1), row(position0, position1),
         sum_bias.reshape(-1, width)], axis=0))
    ready = [c for c in (*deal.chains, comp_chain, kv0, qro0) if c.order]
    advance(run, *ready, kv1, qro1, small, steps=2)
    new_memory = lax.dynamic_slice_in_dim(
        jnp.concatenate([recent, current], axis=0), seg_length, mem, 0)
    new_compressed = lax.dynamic_slice_in_dim(
        jnp.concatenate([distant, squeezed_low[:squeezed_rows]], axis=0), seg_length // 3, comp, 0)
    while kv1.order:
        ready = [c for c in (*deal.chains, comp_chain, kv0, qro0) if c.order]
        advance(run, *ready, kv1, qro1, small)
    last_comp = Last(comp_chain)
    dealt = Dealt(deal, bias_up.shape[0] // (2 * half))
    ends = [Join(links, kv0, kv1), Join(links, qro0, qro1)]
    advance(run, *ends, small, last_comp, dealt)
    tail = LastParts(*ends)
    advance(run, tail, small)
    while small.recv is not None:
        advance(run, small)
    grad_up, grad_down = dealt.result
    grad_qkv, grad_rel, grad_out = tail.result

    at = links.dp * 2 + links.y
    each, each_up = width // (2 * n_dp), bias_up.shape[0] // (2 * n_dp)
    vec = lax.dynamic_slice(small.keep[:4], (0, at * each), (4, each))
    vec_up = lax.dynamic_slice_in_dim(small.keep[4:].reshape(-1), at * each_up, each_up)
    return (output[None], grad_rows[None], new_memory[None], new_compressed[None],
            grad_qkv, grad_rel, grad_out,
            grad_up, grad_down, last_comp.result, vec[0], vec[1], vec[2], vec[3], vec_up)


def solution(mesh):
    rows = P(("dp", "fsdp"), None, None)
    one = P(("dp", "fsdp"))
    return jax.shard_map(
        body,
        mesh=mesh,
        in_specs=(rows, rows, rows, rows, one, one, one, P(None, "fsdp", None), P("fsdp", None),
                  P("fsdp", None), P("fsdp", None), P("fsdp", None), P(None, "fsdp", None), P(),
                  P(), P(), P(), P()),
        out_specs=(rows, rows, rows, rows, P(None, "fsdp", "dp"), P("fsdp", "dp"),
                   P("fsdp", "dp"), P("fsdp", "dp"), P("fsdp", "dp"), P(None, "fsdp", "dp"), one,
                   one, one, one, one),
        check_vma=False,
    )
```

```python
import functools
import math

import jax
import jax.numpy as jnp
from jax import lax
from jax.experimental import pallas as pl
from jax.experimental.pallas import tpu as pltpu
from jax.sharding import PartitionSpec as P

H = 8
BF = jnp.bfloat16
F32 = jnp.float32
VMEM = 60 * 1024 * 1024
GELU_C = math.sqrt(2.0 / math.pi)
COST = 0.0001
TEMPORARIES = 40 * 1024 * 1024
Y, CORE, SEG_LEN, MEM_LIVE, COMP_LIVE, PIECE_A, PIECE_B, BITS = range(8)


def nn(a, b):
    return lax.dot_general(a, b, (((1,), (0,)), ((), ())), preferred_element_type=F32)


def nt(a, b):
    return lax.dot_general(a, b, (((1,), (1,)), ((), ())), preferred_element_type=F32)


def tn(a, b):
    return lax.dot_general(a, b, (((0,), (0,)), ((), ())), preferred_element_type=F32)


class Steps:
    def __init__(self, scal):
        self.scal = scal
        self.token = None

    def __call__(self, kernel, name, grid, ins, outs, scratch, args, flops, aliases={}):
        before = [] if self.token is None else [self.token]
        n_in, n_out, extra = len(ins), len(outs), len(before)

        def ordered_kernel(s_ref, *refs):
            rest = refs[n_in + extra:]
            kernel(s_ref, *refs[:n_in], *rest[:n_out], *rest[n_out + 1:])

        anywhere = pl.BlockSpec(memory_space=pl.ANY)
        moved = sum(a.size * a.dtype.itemsize for a in args)
        need = TEMPORARIES
        for (block, array) in list(zip(ins, args)) + [(b, s) for s, b in outs]:
            if block.block_shape is not None:
                need += 2 * math.prod(block.block_shape) * array.dtype.itemsize
        for ref in scratch:
            need += math.prod(ref.shape) * jnp.dtype(ref.dtype).itemsize
        done = pl.pallas_call(
            ordered_kernel,
            name=name,
            out_shape=[s for s, _ in outs] + [jax.ShapeDtypeStruct((8, 128), F32)],
            grid_spec=pltpu.PrefetchScalarGridSpec(
                num_scalar_prefetch=1,
                grid=grid,
                in_specs=list(ins) + [anywhere] * extra,
                out_specs=[b for _, b in outs] + [anywhere],
                scratch_shapes=scratch,
            ),
            compiler_params=pltpu.CompilerParams(
                vmem_limit_bytes=min(need, VMEM), dimension_semantics=("arbitrary",) * len(grid)
            ),
            input_output_aliases=aliases,
            cost_estimate=pl.CostEstimate(
                flops=int(flops * COST), bytes_accessed=int(moved * COST), transcendentals=0),
        )(self.scal, *args, *before)
        *done, self.token = done
        return done


def follow(run, *values):
    anywhere = pl.BlockSpec(memory_space=pl.ANY)
    return run(
        lambda *refs: None, "follow", (1,), [anywhere] * len(values),
        [(jax.ShapeDtypeStruct(v.shape, v.dtype), anywhere) for v in values], [], values, 0,
        {n + 1: n for n in range(len(values))})


def whole(shape):
    return pl.BlockSpec(shape, lambda i, s: (0,) * len(shape))


def out(shape, dtype, block, index):
    return (jax.ShapeDtypeStruct(shape, dtype), pl.BlockSpec(block, index))


def fixed(shape, dtype):
    return out(shape, dtype, shape, lambda i, s: (0,) * len(shape))


def norm_rows(rows):
    centred = rows - jnp.mean(rows, axis=-1, keepdims=True)
    spread = jnp.mean(centred * centred, axis=-1, keepdims=True)
    scale = lax.rsqrt(spread + 1e-05)
    return centred * scale, scale


def norm_back(grad, gain, unit, scale):
    g = grad * gain
    inner = jnp.mean(g * unit, axis=-1, keepdims=True)
    return scale * (g - jnp.mean(g, axis=-1, keepdims=True) - unit * inner)


def place(dst, s_ref, own, mine, theirs, cols=slice(None)):
    half, quarter = own.shape[-2], mine.shape[-2]
    y, core = s_ref[Y], s_ref[CORE]
    base = (1 - y) * half
    at = lambda start, size: pl.ds(pl.multiple_of(start, quarter), size)
    dst[at(y * half, half), cols] = own[:, cols]
    dst[at(base + core * quarter, quarter), cols] = mine[...]
    dst[at(base + (1 - core) * quarter, quarter), cols] = theirs[...]


def pack_first_kernel(s_ref, rel, k, v, qa, qb, o_rel, o_a, o_b):
    width = rel.shape[-1]
    o_rel[...] = rel[...]
    o_a[0, :, :width] = k[0, 0]
    o_a[0, :, width:] = qa[0, 0]
    o_b[0, :, :width] = v[0, 0]
    o_b[0, :, width:] = qb[0, 0]


def pack_rest_kernel(s_ref, c0, c1, c2, ow, up, down, o_c, o_d, o_up, o_down):
    o_c[0] = c0[0, 0]
    o_c[1] = c1[0, 0]
    o_d[0] = c2[0, 0]
    o_d[1] = ow[0]
    o_up[...] = up[...]
    o_down[...] = down[...]


def quarters(a):
    lead = a.shape[:-2]
    return a.reshape(lead + (4, a.shape[-2] // 4, a.shape[-1]))


def part_of(a, where, n=0, cols=1, c=0):
    block = (1,) * (a.ndim - 2) + (a.shape[-2], a.shape[-1] // cols)
    if a.ndim == 3:
        return pl.BlockSpec(block, lambda i, s: (s[where], 0, c))
    return pl.BlockSpec(block, lambda i, s: (n, s[where], 0, c))


def pack_first(run, w_qkv, w_rel):
    qkv, rel = quarters(w_qkv), quarters(w_rel)
    part, width = rel.shape[1:]
    return run(
        pack_first_kernel, "pack_first", (1,),
        [part_of(rel, PIECE_A), part_of(qkv, PIECE_A, 1), part_of(qkv, PIECE_B, 2),
         part_of(qkv, PIECE_A, 0, 2, 0), part_of(qkv, PIECE_B, 0, 2, 1)],
        [fixed((1, part, width), BF), fixed((1, part, width * 3 // 2), BF),
         fixed((1, part, width * 3 // 2), BF)],
        [], (rel, qkv, qkv, qkv, qkv), 0)


def pack_rest(run, w_out, w_up, w_down, w_comp):
    comp, ow, up, down = quarters(w_comp), quarters(w_out), quarters(w_up), quarters(w_down)
    part, width = ow.shape[1:]
    return run(
        pack_rest_kernel, "pack_rest", (1,),
        [part_of(comp, PIECE_A, 0), part_of(comp, PIECE_A, 1), part_of(comp, PIECE_B, 2),
         part_of(ow, PIECE_B), part_of(up, PIECE_A), part_of(down, PIECE_B)],
        [fixed((2, part, width), BF), fixed((2, part, width), BF),
         fixed((1,) + up.shape[1:], BF), fixed((1,) + down.shape[1:], BF)],
        [], (comp, comp, comp, ow, up, down), 0)


def ordered(mine, theirs, bit):
    n, rows, cols = mine.shape
    at = lax.broadcasted_iota(jnp.int32, (n, 2, rows, cols), 1)
    return jnp.where(at == bit, mine[:, None], theirs[:, None]).reshape(n, 2 * rows, cols)


def normed_kernel(s_ref, d_ref, m_ref, t_ref, g_ref, x_ref):
    i = pl.program_id(0)
    for n, ref in enumerate((d_ref, m_ref, t_ref)):
        @pl.when(i // 2 == n)
        def _(ref=ref):
            x_ref[...] = (norm_rows(ref[...].astype(F32))[0] * g_ref[...]).astype(BF)


def norm_hidden(run, distant, recent, current, gain):
    mem, width = recent.shape
    blk = mem // 2
    part = lambda n: pl.BlockSpec((blk, width), lambda i, s: (jnp.clip(i - 2 * n, 0, 1), 0))
    return run(
        normed_kernel, "norm_hidden", (6,),
        [part(0), part(1), part(2), whole(gain.shape)],
        [out((3 * mem, width), BF, (blk, width), lambda i, s: (i, 0))],
        [], (distant, recent, current, gain), 0)[0]


def constants_kernel(s_ref, m_ref, sa_ref, ca_ref, sb_ref, cb_ref, tab_ref, gr_ref, wide_ref,
                     *, groups):
    i = pl.program_id(0)
    blk, width = tab_ref.shape
    half = width // 2
    fine = sb_ref.shape[0]
    for n in range(blk // fine):
        rows = slice(n * fine, (n + 1) * fine)
        a = i * (blk // fine) + n
        sa, ca = sa_ref[pl.ds(a, 1)], ca_ref[pl.ds(a, 1)]
        tab_ref[rows, :half] = (sa * cb_ref[...] + ca * sb_ref[...]).astype(BF)
        tab_ref[rows, half:] = (ca * cb_ref[...] - sa * sb_ref[...]).astype(BF)

    @pl.when(i == 0)
    def _():
        mem = m_ref.shape[0]
        lanes = wide_ref.shape[2]
        count = gr_ref.shape[1]
        live = lax.broadcasted_iota(jnp.int32, (count, 1), 0) < groups
        for n in range(width // lanes):
            cols = slice(n * lanes, (n + 1) * lanes)
            wide_ref[n, :mem] = m_ref[:, cols].astype(F32)
            wide_ref[n, mem:] = jnp.zeros((wide_ref.shape[1] - mem, lanes), F32)
            for t in range(3):
                rows = jnp.where(live, wide_ref[n, pl.ds(t, count, stride=3)], 0.0)
                gr_ref[t, :, cols] = rows.astype(BF)


def constants(run, recent, angles, groups):
    mem, width = recent.shape
    keys = 3 * mem
    blk = 512
    padded = groups + (-groups) % 64
    ins = (recent,) + angles
    return run(
        functools.partial(constants_kernel, groups=groups), "constants", (keys // blk,),
        [whole(a.shape) for a in ins],
        [out((keys, width), BF, (blk, width), lambda i, s: (i, 0)),
         fixed((3, padded, width), BF)],
        [pltpu.VMEM((width // 128, 3 * padded, 128), F32)], ins, 0)


def qkv_kernel(s_ref, x_ref, o_ref, am_ref, at_ref, bm_ref, bt_ref, bc_ref, bp_ref, kv_ref,
               qc_ref, qp_ref, pr_ref, w_ref, *, scale):
    i = pl.program_id(0)
    rows, width = x_ref.shape
    seg = qc_ref.shape[0]
    blk = 256
    lo, hi = slice(0, width // 2), slice(width // 2, width)
    own, dst = o_ref.at[0], w_ref.at[0]

    @pl.when(i == 0)
    def _():
        place(dst, s_ref, own, am_ref.at[0, :, :width], at_ref.at[0, :, :width])

    @pl.when(i == 1)
    def _():
        place(dst, s_ref, own, bm_ref.at[0, :, :width], bt_ref.at[0, :, :width])

    @pl.when(i == 2)
    def _():
        place(dst, s_ref, own, am_ref.at[0, :, width:], at_ref.at[0, :, width:], lo)
        place(dst, s_ref, own, bm_ref.at[0, :, width:], bt_ref.at[0, :, width:], hi)

    @pl.when(i < 2)
    def _():
        def some(n, _):
            at = pl.ds(pl.multiple_of(n * blk, blk), blk)
            kv_ref[0, at] = nn(x_ref[at], dst[...]).astype(BF)
            return 0

        lax.fori_loop(0, rows // blk, some, 0)

    @pl.when(i == 2)
    def _():
        for n in range(seg // blk):
            at = slice(n * blk, (n + 1) * blk)
            q = nn(x_ref[rows - seg + n * blk:rows - seg + (n + 1) * blk], dst[...])
            qc_ref[at] = ((q + bc_ref[...]) * scale).astype(BF)
            qp_ref[at] = ((q + bp_ref[...]) * scale).astype(BF)
            pr_ref[at] = (q * scale).astype(BF)


def project_qkv(run, normed, w_qkv, a_parts, b_parts, bias_content, bias_position, seg, scale):
    rows, width = normed.shape
    turn = lambda i, s: ((i + 1) % 3, 0, 0)
    parts = a_parts + b_parts
    return run(
        functools.partial(qkv_kernel, scale=scale), "project_qkv", (3,),
        [whole((rows, width)), pl.BlockSpec((1, width // 2, width), turn)]
        + [whole(p.shape) for p in parts] + [whole((1, width)), whole((1, width))],
        [out((2, rows, width), BF, (1, rows, width), lambda i, s: (jnp.minimum(i, 1), 0, 0)),
         fixed((seg, width), BF), fixed((seg, width), BF), fixed((seg, width), BF),
         out((3, width, width), BF, (1, width, width), turn)],
        [], (normed, w_qkv) + parts + (bias_content.reshape(1, -1), bias_position.reshape(1, -1)),
        2 * (2 * rows + seg) * width * width)


def position_kernel(s_ref, x_ref, o_ref, m_ref, t_ref, p_ref, w_ref):
    @pl.when(pl.program_id(0) == 0)
    def _():
        place(w_ref, s_ref, o_ref, m_ref.at[0], t_ref.at[0])

    p_ref[...] = nn(x_ref[...], w_ref[...]).astype(BF)


def project_position(run, table, own, parts):
    rows, width = table.shape
    blk = 512
    return run(
        position_kernel, "project_position", (rows // blk,),
        [pl.BlockSpec((blk, width), lambda i, s: (i, 0)), whole(own.shape)]
        + [whole(p.shape) for p in parts],
        [out((rows, width), BF, (blk, width), lambda i, s: (i, 0))],
        [pltpu.VMEM((width, width), BF)], (table, own) + parts,
        2 * rows * width * width)[0]


RB = 256


def flip_matrix():
    return (lax.broadcasted_iota(jnp.int32, (RB, RB), 0)
            + lax.broadcasted_iota(jnp.int32, (RB, RB), 1) == RB - 1).astype(BF)


def attention_kernel(s_ref, qc_ref, qp_ref, k_ref, v_ref, pos_ref, p_ref, mix_ref, bias_ref,
                     *, comp, mem):
    seg, keys = qc_ref.shape[0], k_ref.shape[1]
    start = comp + mem

    @pl.when(pl.program_id(0) == 0)
    def _():
        mem_live, comp_live = s_ref[MEM_LIVE], s_ref[COMP_LIVE]
        col = lax.broadcasted_iota(jnp.int32, bias_ref.shape, 1)
        row = lax.broadcasted_iota(jnp.int32, bias_ref.shape, 0)
        live = ((col >= comp - comp_live) & (col < comp)) | (
            (col >= start - mem_live) & (col - start <= row))
        bias_ref[...] = jnp.where(live, 0.0, -1e30)

    flip = flip_matrix()
    for r in range(seg // RB):
        width = start + RB * (r + 1)
        rows = slice(r * RB, (r + 1) * RB)
        content = nt(qc_ref[rows], k_ref[0, :width])
        rel = nt(qp_ref[rows], pos_ref[keys - width:])
        rel = pltpu.roll(rel, width - RB + 1, 1, stride=1, stride_axis=0)
        masked = content + rel + bias_ref[rows, :width]
        top = jnp.max(masked, axis=-1, keepdims=True)
        weights = jnp.exp(masked - top)
        probs = (weights * (1.0 / jnp.sum(weights, axis=-1, keepdims=True))).astype(BF)
        mix_ref[rows] = nn(probs, v_ref[0, :width]).astype(BF)
        p_ref[0, rows, :width] = nn(flip, probs).astype(BF)


def attention(run, qc, qp, kv, pos, comp, mem, half):
    seg, width = qc.shape
    keys = kv.shape[1]
    dh = width // H
    n = H // 2
    first = half * n
    q_spec = pl.BlockSpec((seg, dh), lambda h, s: (0, h + first))
    of = lambda m: pl.BlockSpec((1, keys, dh), lambda h, s: (m, 0, h + first))
    return run(
        functools.partial(attention_kernel, comp=comp, mem=mem), "attention", (n,),
        [q_spec, q_spec, of(0), of(1), pl.BlockSpec((keys, dh), lambda h, s: (0, h + first))],
        [out((n, seg, keys), BF, (1, seg, keys), lambda h, s: (h, 0, 0)),
         out((seg, width // 2), BF, (seg, dh), lambda h, s: (0, h))],
        [pltpu.VMEM((seg, keys), F32)], (qc, qp, kv, kv, pos), 16 * seg * keys * width)


def attention_back_kernel(s_ref, p_ref, gm_ref, qc_ref, qp_ref, k_ref, v_ref, pos_ref, gq_ref,
                          gk_ref, gv_ref, gp_ref, gc_ref, gb_ref, gs_ref, sh_ref, pr_ref, rev_ref,
                          *, start, scale):
    seg, keys = qc_ref.shape[0], k_ref.shape[1]
    flip = flip_matrix()
    sum_c = jnp.zeros((1, gc_ref.shape[1]), F32)
    sum_p = jnp.zeros((1, gc_ref.shape[1]), F32)
    for r in range(seg // RB):
        width = start + RB * (r + 1)
        rows = slice(r * RB, (r + 1) * RB)
        for n, ref in enumerate((gm_ref, qc_ref, qp_ref)):
            rev_ref[n, rows] = nn(flip, ref[rows]).astype(BF)
        low = p_ref[0, rows, :width]
        probs = low.astype(F32)
        weighted = probs * nt(rev_ref[0, rows], v_ref[0, :width])
        scores = (weighted - probs * jnp.sum(weighted, axis=-1, keepdims=True))
        low_scores = scores.astype(BF)
        moved = pltpu.roll(scores, 0, 1, stride=1, stride_axis=0).astype(BF)
        gs_ref[rows, :width] = low_scores
        sh_ref[rows, keys - width:] = moved
        pr_ref[rows, :width] = low
        if width < keys:
            gs_ref[rows, width:] = jnp.zeros((RB, keys - width), BF)
            pr_ref[rows, width:] = jnp.zeros((RB, keys - width), BF)
            sh_ref[rows, : keys - width] = jnp.zeros((RB, keys - width), BF)
        grad_c = nn(low_scores, k_ref[0, :width])
        grad_p = nn(moved, pos_ref[keys - width:])
        sum_c += jnp.sum(grad_c, axis=0, keepdims=True)
        sum_p += jnp.sum(grad_p, axis=0, keepdims=True)
        gq_ref[rows] = nn(flip, ((grad_c + grad_p) * scale).astype(BF)).astype(BF)
    gc_ref[...] = sum_c * scale
    gb_ref[...] = sum_p * scale
    gv_ref[...] = tn(rev_ref[0], pr_ref[...]).astype(BF)
    gk_ref[...] = tn(rev_ref[1], gs_ref[...]).astype(BF)
    gp_ref[...] = tn(rev_ref[2], sh_ref[...]).astype(BF)


def attention_back(run, probs, gm, qc, qp, kv, pos, start, scale, half):
    seg, width = qc.shape
    keys = kv.shape[1]
    dh = width // H
    n = H // 2
    first = half * n
    q_spec = pl.BlockSpec((seg, dh), lambda h, s: (0, h + first))
    of = lambda m: pl.BlockSpec((1, keys, dh), lambda h, s: (m, 0, h + first))
    turned = lambda: out((width // 2, keys), BF, (dh, keys), lambda h, s: (h, 0))
    sums = lambda: out((1, width // 2), F32, (1, dh), lambda h, s: (0, h))
    big = pltpu.VMEM((seg, keys), BF)
    return run(
        functools.partial(attention_back_kernel, start=start, scale=scale), "attention_back", (n,),
        [pl.BlockSpec((1, seg, keys), lambda h, s: (h, 0, 0)), q_spec, q_spec, q_spec,
         of(0), of(1), pl.BlockSpec((keys, dh), lambda h, s: (0, h + first))],
        [out((seg, width // 2), BF, (seg, dh), lambda h, s: (0, h)), turned(), turned(), turned(),
         sums(), sums()],
        [big, big, big, pltpu.VMEM((3, seg, dh), BF)], (probs[half], gm, qc, qp, kv, kv, pos),
        12 * seg * keys * width)


def mixed_kernel(s_ref, tok_ref, a_ref, b_ref, o_ref, m_ref, t_ref, g_ref, att_ref, sec_ref, w_ref):
    @pl.when(pl.program_id(0) == 0)
    def _():
        place(w_ref, s_ref, o_ref, m_ref.at[1], t_ref.at[1])

    mid = a_ref.shape[1]
    attended = (tok_ref[...].astype(F32) + nn(a_ref[...], w_ref[:mid])
                + nn(b_ref[...], w_ref[mid:]))
    att_ref[...] = attended
    sec_ref[...] = (norm_rows(attended)[0] * g_ref[...]).astype(BF)


def mix_out(run, tokens, mixed, own, parts, gain):
    seg, width = tokens.shape
    blk = 256
    row = pl.BlockSpec((blk, width), lambda i, s: (i, 0))
    side = pl.BlockSpec((blk, width // 2), lambda i, s: (i, 0))
    return run(
        mixed_kernel, "mix_out", (seg // blk,),
        [row, side, side, whole(own.shape)] + [whole(p.shape) for p in parts] + [whole((1, width))],
        [out((seg, width), F32, (blk, width), lambda i, s: (i, 0)),
         out((seg, width), BF, (blk, width), lambda i, s: (i, 0)),
         fixed((width, width), BF)],
        [], (tokens,) + mixed + (own,) + parts + (gain,), 2 * seg * width * width)


def part_shape(rows, cols, n_dp, taps, cut=1):
    return (2, n_dp // (2 * cut), taps, rows // n_dp, cols // 2)


def low_or_wide(chunk):
    return BF if chunk % 16 == 0 else F32


def by_core(buf, values, core):
    pairs, _, chunk, cols = buf.shape
    buf[...] = values.astype(buf.dtype).reshape(pairs, 2, chunk, cols)
    pick = lambda c: buf[:, c].reshape(pairs * chunk, cols)
    return jnp.concatenate([pick(core), pick(1 - core)], axis=0).astype(BF)


def put(keep, send, values):
    half = values.shape[0] // 2
    shape = keep.shape[:-1] + (values.shape[1],)
    keep[...] = values[:half].reshape(shape).astype(BF)
    send[...] = values[half:].reshape(shape).astype(BF)


def ffn_kernel(s_ref, sec_ref, cot_ref, att_ref, uo_ref, um_ref, ut_ref, do_ref, dm_ref, dt_ref,
               b_ref, g_ref, wo_ref, out_ref, gatt_ref, gm_ref, uk_ref, us_ref, dk_ref, ds_ref,
               gb_ref, gg_ref, gout_ref, turn_ref, wu_ref, wd_ref, acc_ref, gsec_ref, ubuf, dbuf):
    i, n = pl.program_id(0), pl.num_programs(0)
    y, core = s_ref[Y], s_ref[CORE]

    @pl.when(i == 0)
    def _():
        row = lax.broadcasted_iota(jnp.int32, cot_ref.shape, 0)
        live = jnp.where(row < s_ref[SEG_LEN], cot_ref[...], jnp.zeros((), BF))
        gout_ref[...] = live
        turn_ref[...] = by_core(dbuf, live.T, core)
        acc_ref[...] = att_ref[...]
        gsec_ref[...] = jnp.zeros_like(gsec_ref)

    place(wu_ref, s_ref, uo_ref, um_ref.at[0], ut_ref.at[0])
    half = i // (n // 2)
    side = (i % (n // 2)) // (n // 4)

    @pl.when(half == y)
    def _():
        wd_ref[...] = do_ref[...]

    @pl.when((half != y) & (side == core))
    def _():
        wd_ref[...] = dm_ref[0]

    @pl.when((half != y) & (side != core))
    def _():
        wd_ref[...] = dt_ref[0]

    second, gout = sec_ref[...], gout_ref[...]
    v = nn(second, wu_ref[...]) + b_ref[...]
    square = v * v
    gate = 0.5 + 0.5 * jnp.tanh(v * (GELU_C + (GELU_C * 0.044715) * square))
    act = (v * gate).astype(BF)
    slope = gate + (gate - gate * gate) * v * (2 * GELU_C + (6 * GELU_C * 0.044715) * square)
    acc_ref[...] += nn(act, wd_ref[...])
    grad_inner = nt(gout, wd_ref[...]) * slope
    low = grad_inner.astype(BF)
    gb_ref[...] = jnp.sum(low.astype(F32), axis=0, keepdims=True)
    gsec_ref[...] += nt(low, wu_ref[...])
    put(dk_ref.at[0, :, 0], ds_ref.at[0, :, 0], nn(turn_ref[...], act))
    part = nn(by_core(ubuf, low.T, core), second)
    width = part.shape[1] // 2
    for side in range(2):
        put(uk_ref.at[side, :, 0], us_ref.at[side, :, 0], part[:, side * width:(side + 1) * width])

    @pl.when(i == n - 1)
    def _():
        out_ref[...] = acc_ref[...].astype(BF)
        unit, scale = norm_rows(att_ref[...])
        grad = gsec_ref[...]
        gg_ref[...] = jnp.sum(grad * unit, axis=0, keepdims=True)
        gatt = norm_back(grad, g_ref[...], unit, scale) + gout_ref[...].astype(F32)
        gatt_ref[...] = gatt
        gm_ref[...] = nt(gatt.astype(BF), wo_ref[...]).astype(BF)


def feed_forward(run, second, cotangent, attended, w_up, up_parts, w_down, down_parts, bias_up,
                 gain, w_out, n_dp):
    seg, width = second.shape
    inner = bias_up.shape[1]
    n = 8
    blk = inner // n
    um, ut = up_parts
    dm, dt = down_parts
    uch, dch = inner // n_dp, width // n_dp
    pairs = blk // (2 * uch)
    col = lambda a: pl.BlockSpec((a.shape[0], blk), lambda i, s: (0, i))
    col3 = lambda a: pl.BlockSpec((1, a.shape[1], blk), lambda i, s: (0, 0, i))
    row3 = pl.BlockSpec((1, blk, width), lambda i, s: (0, i % (n // 4), 0))
    up_shape = part_shape(inner, width, n_dp, 1)
    down_shape = part_shape(width, inner, n_dp, n // 2)[:-1] + (blk,)
    up_out = lambda: out(up_shape, BF, (2, pairs, 1, uch, width // 2),
                         lambda i, s: (0, i, 0, 0, 0))
    down_out = lambda: out(down_shape, BF, (1, n_dp // 2, 1, dch, blk),
                           lambda i, s: (i // (n // 2), 0, i % (n // 2), 0, 0))
    full = (seg, width)
    return run(
        ffn_kernel, "feed_forward", (n,),
        [whole(full), whole(full), whole(full), col(w_up), col3(um), col3(ut),
         pl.BlockSpec((blk, width), lambda i, s: (i % (n // 2), 0)), row3, row3,
         pl.BlockSpec((1, blk), lambda i, s: (0, i)), whole((1, width)), whole((width, width))],
        [fixed(full, BF), fixed(full, F32), fixed(full, BF), up_out(), up_out(), down_out(),
         down_out(), out((1, inner), F32, (1, blk), lambda i, s: (0, i)), fixed((1, width), F32)],
        [pltpu.VMEM(full, BF), pltpu.VMEM((width, seg), BF), pltpu.VMEM((width, blk), BF),
         pltpu.VMEM((blk, width), BF), pltpu.VMEM(full, F32), pltpu.VMEM(full, F32),
         pltpu.VMEM((pairs, 2, uch, seg), low_or_wide(uch)),
         pltpu.VMEM((n_dp // 2, 2, dch, seg), low_or_wide(dch))],
        (second, cotangent, attended, w_up, um, ut, w_down, dm, dt, bias_up, gain, w_out),
        12 * seg * width * inner)


def grads_kernel(s_ref, gk_ref, gv_ref, gp_ref, gq_ref, ga_ref, x_ref, tab_ref, ma_ref, mb_ref, w_ref,
                 keep_ref, send_ref, gg_ref, k_s, v_s, p_s, q_s, o_s, big, small):
    core = s_ref[CORE]
    rows = x_ref.shape[0]
    seg = gq_ref.shape[0]

    @pl.when(pl.program_id(0) == 0)
    def _():
        k_s[...] = by_core(big, gk_ref[...], core)
        v_s[...] = by_core(big, gv_ref[...], core)
        p_s[...] = by_core(big, gp_ref[...], core)
        q_s[...] = by_core(small, gq_ref[...].T, core)
        o_s[...] = by_core(small, ga_ref[...].astype(BF).T, core)

    x = x_ref[...]
    pairs, _, chunk, _ = small.shape
    n = pairs * chunk

    def both(tap, values):
        put(keep_ref.at[0, :, tap], send_ref.at[0, :, tap], values)

    def gain(values, m):
        turned = w_ref[m].T.astype(F32)
        whole_ = turned.reshape(pairs, 2, chunk, turned.shape[1])
        even, odd = whole_[:, 0].reshape(n, -1), whole_[:, 1].reshape(n, -1)
        first = jnp.where(core == 0, even, odd)
        last = jnp.where(core == 0, odd, even)
        return (jnp.sum(values[:n] * first, axis=0, keepdims=True)
                + jnp.sum(values[n:] * last, axis=0, keepdims=True))

    part = nn(k_s[...], x)
    both(0, part)
    total = gain(part, 1)
    part = nn(v_s[...], x)
    both(1, part)
    total += gain(part, 2)
    part = nn(q_s[...], x[rows - seg:])
    both(2, part)
    total += gain(part, 0)
    both(3, nn(p_s[...], tab_ref[...]))
    gg_ref[...] = total
    i, n = pl.program_id(0), pl.num_programs(0)

    @pl.when(i < n // 2)
    def _():
        both(4, nn(o_s[...], ma_ref[...]))

    @pl.when(i >= n // 2)
    def _():
        both(4, nn(o_s[...], mb_ref[...]))


def projection_grads(run, turned, gq, gatt, normed, table, mixed, w, n_dp, half):
    rows, width = normed.shape
    seg = gq.shape[0]
    blk = 256
    chunk = width // n_dp
    mid = width // 2
    gk, gv, gpos = turned
    count = mid // blk
    col = lambda r: pl.BlockSpec((r, blk), lambda i, s: (0, i))
    shape = lambda taps: part_shape(width, width, n_dp, taps, 2)
    half_of = lambda taps: out(shape(taps), BF, (1,) + shape(taps)[1:4] + (blk,),
                               lambda i, s: (i // count, 0, 0, 0, i % count))
    side = pl.BlockSpec((seg, blk), lambda i, s: (0, i % count))
    kind = low_or_wide(chunk)
    pairs = mid // (2 * chunk)
    return run(
        grads_kernel, "projection_grads", (width // blk,),
        [whole(gk.shape), whole(gk.shape), whole(gk.shape), whole(gq.shape),
         pl.BlockSpec((seg, mid), lambda i, s: (0, half)), col(rows), col(rows), side, side,
         pl.BlockSpec((3, blk, mid), lambda i, s: (0, i, half))],
        [half_of(5), half_of(5),
         out((1, width), F32, (1, blk), lambda i, s: (0, i))],
        [pltpu.VMEM((mid, rows), BF)] * 3 + [pltpu.VMEM((mid, seg), BF)] * 2
        + [pltpu.VMEM((pairs, 2, chunk, rows), kind), pltpu.VMEM((pairs, 2, chunk, seg), kind)],
        (gk, gv, gpos, gq, gatt, normed, table) + mixed + (w,),
        (3 * rows + 2 * seg) * width * width)


def grad_tokens_kernel(s_ref, ka_ref, kb_ref, va_ref, vb_ref, qa_ref, qb_ref, tok_ref, ga_ref,
                       w_ref, g_ref, gt_ref, acc_ref):
    i = pl.program_id(0)
    mid = w_ref.shape[2] // 2
    left, right = w_ref[0, :, :mid], w_ref[0, :, mid:]

    @pl.when(i == 0)
    def _():
        acc_ref[...] = nn(left, ka_ref[...]) + nn(right, kb_ref[...])

    @pl.when(i == 1)
    def _():
        acc_ref[...] += nn(left, va_ref[...]) + nn(right, vb_ref[...])

    @pl.when(i == 2)
    def _():
        total = (acc_ref[...] + nt(left, qa_ref[...]) + nt(right, qb_ref[...])).T
        unit, scale = norm_rows(tok_ref[...].astype(F32))
        gt_ref[...] = (ga_ref[...] + norm_back(total, g_ref[...], unit, scale)).astype(BF)


def grad_tokens(run, gk, gv, gq, tokens, grad_attended, w, gain):
    seg, width = tokens.shape
    rows = gk[0].shape[1]
    late = pl.BlockSpec((width // 2, seg), lambda i, s: (0, rows // seg - 1))
    side = whole((seg, width // 2))
    return run(
        grad_tokens_kernel, "grad_tokens", (3,),
        [late] * 4 + [side] * 2 + [whole((seg, width)), whole((seg, width)),
         pl.BlockSpec((1, width, width), lambda i, s: ((i + 1) % 3, 0, 0)), whole((1, width))],
        [fixed((seg, width), BF)], [pltpu.VMEM((width, seg), F32)],
        tuple(gk) + tuple(gv) + tuple(gq) + (tokens, grad_attended, w, gain),
        6 * seg * width * width)[0]


def squeeze_kernel(s_ref, gr_ref, o_ref, am_ref, at_ref, bm_ref, bt_ref, w_ref, g_ref, sq_ref,
                   low_ref, k_ref, v_ref):
    y, core = s_ref[Y], s_ref[CORE]
    half, quarter = o_ref.shape[1], am_ref.shape[1]
    base = (1 - y) * half
    total = jnp.zeros(sq_ref.shape, F32)
    for t in range(3):
        m_ref, t_ref, n = (am_ref, at_ref, t) if t < 2 else (bm_ref, bt_ref, 0)
        at = lambda off, size: gr_ref[t, :, pl.ds(pl.multiple_of(off, quarter), size)]
        total += nn(at(y * half, half), o_ref[t])
        total += nn(at(base + core * quarter, quarter), m_ref[n])
        total += nn(at(base + (1 - core) * quarter, quarter), t_ref[n])
    sq_ref[...] = total
    low_ref[...] = total.astype(BF)
    unit = (norm_rows(total)[0] * g_ref[...]).astype(BF)
    k_ref[...] = nn(unit, w_ref[1]).astype(BF)
    v_ref[...] = nn(unit, w_ref[2]).astype(BF)


def squeeze(run, groups, own, a_parts, b_parts, w, gain):
    _, rows, width = groups.shape
    parts = a_parts + b_parts
    shape = (rows, width)
    return run(
        squeeze_kernel, "squeeze", (1,),
        [whole(groups.shape), whole(own.shape)] + [whole(p.shape) for p in parts]
        + [whole(w.shape), whole((1, width))],
        [fixed(shape, F32), fixed(shape, BF), fixed(shape, BF), fixed(shape, BF)], [],
        (groups, own) + parts + (w, gain), 10 * rows * width * width)


def masked_softmax(scores, live):
    masked = jnp.where(live, scores, -1e30)
    weights = jnp.exp(masked - jnp.max(masked, axis=-1, keepdims=True))
    return weights * (1.0 / jnp.sum(weights, axis=-1, keepdims=True))


def recon_kernel(s_ref, pr_ref, ok_ref, ov_ref, ck_ref, cv_ref, gk_ref, gv_ref):
    seg_len = s_ref[SEG_LEN]
    count = seg_len // 3
    probe = pr_ref[...]
    seg, mem, comp = probe.shape[0], ok_ref.shape[1], ck_ref.shape[0]
    old_live = lax.broadcasted_iota(jnp.int32, (1, mem), 1) < 3 * count
    old = nn(masked_softmax(nt(probe, ok_ref[0]), old_live).astype(BF), ov_ref[0])
    live = lax.broadcasted_iota(jnp.int32, (1, comp), 1) < count
    probs = masked_softmax(nt(probe, ck_ref[...]), live)
    low = probs.astype(BF)
    gap = nn(low, cv_ref[...]) - old
    row = lax.broadcasted_iota(jnp.int32, gap.shape, 0)
    grad_out = (jnp.where(row < seg_len, gap, 0.0) * (2.0 / seg_len.astype(F32))).astype(BF)
    gv_ref[...] = tn(low, grad_out).astype(BF)
    weighted = probs * nt(grad_out, cv_ref[...])
    scores = (weighted - probs * jnp.sum(weighted, axis=-1, keepdims=True)).astype(BF)
    gk_ref[...] = tn(scores, probe).astype(BF)


def reconstruct(run, probe, kv, ck, cv, mem):
    seg, width = probe.shape
    rows = ck.shape[0]
    dh = width // H
    at = lambda n, b: pl.BlockSpec((n, dh), lambda h, s: (b, h))
    old = lambda m: pl.BlockSpec((1, mem, dh), lambda h, s: (m, 1, h))
    grads = lambda: out((rows, width), BF, (rows, dh), lambda h, s: (0, h))
    return run(
        recon_kernel, "reconstruct", (H,),
        [at(seg, 0), old(0), old(1), at(rows, 0), at(rows, 0)], [grads(), grads()], [],
        (probe, kv, kv, ck, cv), 4 * seg * width * mem + 12 * seg * width * rows)


def grad_comp_kernel(s_ref, sq_ref, gk_ref, gv_ref, w_ref, g_ref, gr_ref, k_ref, x_ref, low_ref, buf):
    @pl.when(pl.program_id(0) == 0)
    def _():
        grad = nt(gk_ref[...], w_ref[1]) + nt(gv_ref[...], w_ref[2])
        unit, scale = norm_rows(sq_ref[...])
        low = norm_back(grad, g_ref[...], unit, scale).astype(BF)
        low_ref[...] = by_core(buf, low.astype(F32).T, s_ref[CORE])

    part = nn(low_ref[...], gr_ref[0])
    width = part.shape[1] // 2
    for y in range(2):
        put(k_ref.at[y, :, 0], x_ref.at[y, :, 0], part[:, y * width:(y + 1) * width])


def grad_comp(run, squeezed, gk, gv, w, gain, groups, n_dp):
    taps, rows, width = groups.shape
    chunk = width // n_dp
    shape = part_shape(width, width, n_dp, taps)
    half = lambda: out(shape, BF, shape[:2] + (1,) + shape[3:], lambda i, s: (0, 0, i, 0, 0))
    here = whole((rows, width))
    return run(
        grad_comp_kernel, "grad_comp", (taps,),
        [here, here, here, whole(w.shape), whole((1, width)),
         pl.BlockSpec((1, rows, width), lambda i, s: (i, 0, 0))],
        [half(), half()],
        [pltpu.VMEM((width, rows), BF), pltpu.VMEM((n_dp // 2, 2, chunk, rows), low_or_wide(chunk))],
        (squeezed, gk, gv, w, gain, groups), 10 * rows * width * width)


class Links:
    def __init__(self):
        self.dp = lax.axis_index("dp")
        self.y = lax.axis_index("fsdp")
        self.n_dp = lax.axis_size("dp")
        self.top = self.n_dp.bit_length() - 2

    def bit(self, axis):
        return self.y if axis == "y" else (self.dp >> axis) & 1

    def swap(self, value, axis):
        if axis == "y":
            return lax.ppermute(value, "fsdp", [(0, 1), (1, 0)])
        return lax.ppermute(value, "dp", [(i, i ^ (1 << axis)) for i in range(self.n_dp)])


class Part:
    def __init__(self, array, start):
        self.array, self.start = array, start


class Flow:
    def __init__(self, axes, order, rows):
        self.axes, self.order, self.rows = list(axes), list(order), rows

    def halves(self):
        axis = self.order[0]
        where = self.axes.index(axis)
        run = self.rows << (len(self.axes) - 1 - where)
        return axis, [(2 * p * run, (2 * p + 1) * run, p * run) for p in range(1 << where)], run

    def plan(self, take_in, give):
        axis, runs, length = self.halves()
        keep, recv = take_in(self.keep), take_in(self.recv.array)
        total = len(runs) * length
        held = give(fixed((total, self.keep.shape[1]), BF))
        place = give.send(axis, total, self)
        first = self.recv.start
        slot = Y if axis == "y" else BITS + axis - 1

        def kernel(s_ref, ins, outs, sends):
            bit = s_ref[slot]
            dst, base = sends(place)
            for low, high, to in runs:
                for side, ref, at in ((bit, outs[held], to), (1 - bit, dst, base + to)):
                    start = low + side * (high - low)
                    a = ins[keep][pl.ds(pl.multiple_of(start, 8), length)]
                    b = ins[recv][pl.ds(pl.multiple_of(first + start, 8), length)]
                    ref[at:at + length] = (a.astype(F32) + b.astype(F32)).astype(BF)

        def done(outs):
            self.keep = outs[held]
            self.axes.remove(axis)
            self.order.pop(0)

        return kernel, done


def cut_rows(rows, flows):
    if flows == 1:
        return (0, rows)
    unit = 16 if rows >= 96 else 8
    third = -(-rows // (3 * unit)) * unit
    return (0, third, 2 * third, rows)


class Source:
    def __init__(self, links, keep, send, axes, orders):
        self.axes, self.orders = axes, orders
        self.blocks = math.prod(keep.shape[:2])
        self.rows, self.cols = math.prod(keep.shape[2:4]), keep.shape[4]
        self.keep = keep.reshape(-1, self.cols)
        self.recv = links.swap(send, 0).reshape(-1, self.cols)
        self.cuts = cut_rows(self.rows, len(orders))

    def plan(self, take_in, give):
        keep, recv = take_in(self.keep), take_in(self.recv)
        rows, moves, self.flows = self.rows, [], []
        for c, order in enumerate(self.orders):
            lo, size = self.cuts[c], self.cuts[c + 1] - self.cuts[c]
            flow = Flow(self.axes, order, size)
            axis = order[0]
            where = self.axes.index(axis)
            post = 1 << (len(self.axes) - 1 - where)
            total = self.blocks // 2 * size
            held = give(fixed((total, self.cols), BF))
            moves.append((axis, where, post, lo, size, held, give.send(axis, total, flow)))
            self.flows.append(flow)

        def kernel(s_ref, ins, outs, sends):
            for axis, where, post, lo, size, held, place in moves:
                bit = s_ref[Y if axis == "y" else BITS + axis - 1]
                dst, base = sends(place)
                for p in range(1 << where):
                    for q in range(post):
                        to = (p * post + q) * size
                        for side, ref, at in ((bit, outs[held], to), (1 - bit, dst, base + to)):
                            start = ((2 * p + side) * post + q) * rows + lo
                            rng = pl.ds(pl.multiple_of(start, 8), size)
                            total = ins[keep][rng].astype(F32) + ins[recv][rng].astype(F32)
                            ref[at:at + size] = total.astype(BF)

        def done(outs):
            for flow, move in zip(self.flows, moves):
                flow.keep = outs[move[5]]
                flow.axes.remove(move[0])
                flow.order.pop(0)

        return kernel, done


class Join:
    def __init__(self, top, low, high):
        self.top, self.low, self.high = top, low, high
        self.rows = low.rows

    def plan(self, take_in, give):
        low, high = self.low, self.high
        refs = [take_in(low.keep), take_in(low.recv.array), take_in(high.keep),
                take_in(high.recv.array)]
        held = give(fixed(low.keep.shape, BF))
        place = give.send(self.top, self.rows, self)
        slot = BITS + self.top - 1
        rows = self.rows

        def kernel(s_ref, ins, outs, sends):
            dst, base = sends(place)
            part = lambda n, flow: (ins[refs[n]][...].astype(F32) + ins[refs[n + 1]][
                flow.recv.start:flow.recv.start + rows].astype(F32))
            a, b = part(0, low), part(2, high)
            upper = s_ref[slot] == 1
            outs[held][...] = jnp.where(upper, b, a).astype(BF)
            dst[base:base + rows] = jnp.where(upper, a, b).astype(BF)

        def done(outs):
            self.keep = outs[held]

        return kernel, done


class Small:
    def __init__(self, links, value):
        self.links, self.keep = links, value
        self.order = [0, "y"] + list(range(1, links.top + 1))
        self.send()

    def send(self):
        self.recv = self.links.swap(self.keep, self.order.pop(0)) if self.order else None

    def plan(self, take_in, give):
        a, b = take_in(self.keep), take_in(self.recv)
        total = give(fixed(self.keep.shape, F32))

        def kernel(s_ref, ins, outs, sends):
            outs[total][...] = ins[a][...] + ins[b][...]

        def done(outs):
            self.keep = outs[total]
            self.send()

        return kernel, done


class Finish:
    def __init__(self, flows, shapes, write):
        self.flows, self.shapes, self.write = flows, shapes, write

    def plan(self, take_in, give):
        refs = [(take_in(f.keep), take_in(f.recv.array), f.recv.start, f.rows) for f in self.flows]
        results = [give(fixed(shape, F32)) for shape in self.shapes]

        def kernel(s_ref, ins, outs, sends):
            rows = jnp.concatenate(
                [ins[k][...].astype(F32) + ins[r][first:first + n].astype(F32)
                 for k, r, first, n in refs], axis=0)
            self.write(rows, *[outs[n] for n in results])

        def done(outs):
            self.result = [outs[n] for n in results]

        return kernel, done


class Carry:
    def __init__(self, *values):
        self.values = values

    def plan(self, take_in, give):
        anywhere = pl.BlockSpec(memory_space=pl.ANY)
        at = []
        for v in self.values:
            n = give((jax.ShapeDtypeStruct(v.shape, v.dtype), anywhere))
            give.aliases[take_in(v, anywhere)] = n
            at.append(n)

        def done(outs):
            self.values = [outs[n] for n in at]

        return lambda *refs: None, done


class Gives:
    def __init__(self):
        self.outs, self.sizes, self.takers, self.aliases = [], {}, [], {}

    def __call__(self, spec):
        self.outs.append(spec)
        return len(self.outs) - 1

    def send(self, axis, rows, taker):
        start = self.sizes.get(axis, 0)
        self.sizes[axis] = start + rows
        self.takers.append((axis, start, taker))
        return axis, start


def advance(run, links, *items):
    args, ins, index = [], [], {}

    def take_in(array, spec=None):
        if id(array) not in index:
            index[id(array)] = len(args)
            args.append(array)
            ins.append(spec or whole(array.shape))
        return index[id(array)]

    give = Gives()
    plans = [item.plan(take_in, give) for item in items]
    n_out = len(give.outs)
    axes = sorted(give.sizes, key=lambda a: 0 if a == "y" else a)
    outs = give.outs + [fixed((give.sizes[a], args[0].shape[-1]), BF) for a in axes]

    def kernel(s_ref, *refs):
        in_refs, out_refs = refs[:len(args)], refs[len(args):]
        sends = lambda place: (out_refs[n_out + axes.index(place[0])], place[1])
        for part, _ in plans:
            part(s_ref, in_refs, out_refs, sends)

    done = run(kernel, "add", (1,), ins, outs, [], args, 0,
               {1 + a: b for a, b in give.aliases.items()})
    came = {a: links.swap(done[n_out + n], a) for n, a in enumerate(axes)}
    for axis, start, taker in give.takers:
        taker.recv = Part(came[axis], start)
    for _, take in plans:
        take(done)


class Deal:
    def __init__(self, links, pairs, axes, orders, cuts):
        self.links, self.axes, self.orders, self.cuts = links, axes, orders, cuts
        self.keeps = [k for k, _ in pairs]
        self.sends = [x for _, x in pairs]
        self.rows, self.cols = self.keeps[0].shape[-2:]

    def start(self, sends):
        self.recvs = [self.links.swap(x, 0) for x in sends]

    def spans(self, c):
        lo, hi = self.cuts[c], self.cuts[c + 1]
        for n in range(2):
            a, b = max(lo - n * self.rows, 0), min(hi - n * self.rows, self.rows)
            if a < b:
                yield n, a, b

    def add(self, run, steps):
        n = len(self.axes)
        lead = (2,) * n
        rows, cols = self.rows, self.cols
        firsts = [self.axes.index(o[0]) for o in self.orders]
        others = [a for a in range(n) if a not in firsts]
        split = max(steps >> len(others), 1)
        width = cols // split
        count = 2 ** len(others) * split

        def at(i):
            places, rest = [0] * n, i // split
            for a in reversed(others):
                places[a] = rest % 2
                rest = rest // 2
            return places, i % split

        block = tuple(1 if a in others else 2 for a in range(n))

        def read(i, s):
            places, col = at(i)
            return (*places, 0, col)

        def write(first):
            def index(i, s):
                places, col = at(i)
                return (*places[:first], *places[first + 1:], 0, col)
            return index

        args = [a.reshape(lead + (rows, cols)) for a in self.keeps + self.recvs]
        ins = [pl.BlockSpec(block + (rows, width), read)] * 4
        outs, slots = [], []
        for c, first in enumerate(firsts):
            size = self.cuts[c + 1] - self.cuts[c]
            shape = lead[1:] + (size, cols)
            less = block[:first] + block[first + 1:]
            outs += [out(shape, BF, less + (size, width), write(first))] * 2
            axis = self.axes[first]
            slots.append(Y if axis == "y" else BITS + axis - 1)

        def kernel(s_ref, *refs):
            held, sent = refs[4::2], refs[5::2]

            for c, first in enumerate(firsts):
                bit = s_ref[slots[c]]
                row = 0
                for m, a, b in self.spans(c):
                    keep, recv = refs[m], refs[2 + m]
                    for dst, side in ((held[c], bit), (sent[c], 1 - bit)):
                        pick = tuple(side if d == first else slice(None) for d in range(n))
                        pick += (slice(a, b), slice(None))
                        total = keep[pick].astype(F32) + recv[pick].astype(F32)
                        to = (slice(None),) * (n - 1) + (slice(row, row + b - a),)
                        dst[to] = total.astype(BF)
                    row += b - a

        def take(*done):
            self.chains = []
            for c, order in enumerate(self.orders):
                axes = [a for a in self.axes if a != order[0]]
                recv = self.links.swap(done[2 * c + 1], order[0])
                size = self.cuts[c + 1] - self.cuts[c]
                flow = Flow(axes, order[1:], size)
                flow.keep, flow.recv = done[2 * c].reshape(-1, self.cols), Part(
                    recv.reshape(-1, self.cols), 0)
                self.chains.append(flow)

        done = run(kernel, "deal", (count,), ins, outs, [], args, 0)
        take(*done)


def angle_parts(rows, width):
    fine = 32
    frequency = jnp.exp(
        jnp.arange(0, width, 2).astype(F32) * (-math.log(10000.0) / width))
    coarse = (fine * (rows // fine - 1 - jnp.arange(rows // fine))).astype(F32)
    near = (fine - 1 - jnp.arange(fine)).astype(F32)
    a, b = coarse[:, None] * frequency[None, :], near[:, None] * frequency[None, :]
    return (jnp.sin(a), jnp.cos(a), jnp.sin(b), jnp.cos(b))


def body(tokens, memory, compressed, cotangent, seg_len, mem_fill, cmem_fill, w_qkv, w_rel, w_out,
         w_up, w_down, w_comp, norm_gain1, norm_gain2, bias_content, bias_position, bias_up):
    streams = tokens.shape[0]
    assert streams == 1
    links = Links()
    n_dp, top = links.n_dp, links.top
    seg, width = tokens.shape[1:]
    mem, comp = memory.shape[1], compressed.shape[1]
    start = comp + mem
    keys = start + seg
    squeezed_rows = mem // 3
    scale = (width // H) ** (-0.5)
    current, recent, distant = tokens[0], memory[0], compressed[0]
    seg_length = seg_len[0]
    core, x, z = links.bit(0), links.bit(1), links.bit(2)
    run = Steps(jnp.stack(
        [links.y, core, seg_length, mem_fill[0], cmem_fill[0], core * 2 + z,
         core * 2 + x] + [links.bit(n) for n in range(1, top + 1)]).astype(jnp.int32))
    gain1, gain2 = norm_gain1.reshape(1, -1), norm_gain2.reshape(1, -1)

    swap = links.swap
    near_parts = lambda value: (value, swap(value, 0))
    p_rel, p_a, p_b = pack_first(run, w_qkv, w_rel)
    rel, a, b = swap(p_rel, "y"), swap(p_a, "y"), swap(p_b, "y")
    normed = norm_hidden(run, distant, recent, current, gain1)
    rel_far = swap(rel, 2)
    p_c, p_d, p_up, p_down = pack_rest(run, w_out, w_up, w_down, w_comp)
    c, d = swap(p_c, "y"), swap(p_d, "y")
    table, groups = constants(run, recent, angle_parts(keys, width), squeezed_rows)
    rel, rel_far = follow(run, rel, rel_far)
    rel_parts = near_parts(ordered(rel, rel_far, z))
    a_far, b_far = swap(a, 2), swap(b, 1)
    pos = project_position(run, table, w_rel, rel_parts)
    a, a_far, b, b_far, p_up, p_down = follow(run, a, a_far, b, b_far, p_up, p_down)
    a_parts, b_parts = near_parts(ordered(a, a_far, z)), near_parts(ordered(b, b_far, x))
    up, down = swap(p_up, "y"), swap(p_down, "y")
    kv, qc, qp, probe, w_full = project_qkv(
        run, normed, w_qkv, a_parts, b_parts, bias_content, bias_position, seg, scale)
    c, d = follow(run, c, d)
    c_far, d_far = swap(c, 2), swap(d, 1)
    p0, m0 = attention(run, qc, qp, kv, pos, comp, mem, 0)
    c, c_far, d, d_far = follow(run, c, c_far, d, d_far)
    c_parts, d_parts = near_parts(ordered(c, c_far, z)), near_parts(ordered(d, d_far, x))
    p1, m1 = attention(run, qc, qp, kv, pos, comp, mem, 1)
    up, down = follow(run, up, down)
    up_far, down_far = swap(up, 2), swap(down, 1)
    squeezed, squeezed_low, ck, cv = squeeze(run, groups, w_comp, c_parts, d_parts, w_full, gain1)
    gck, gcv = reconstruct(run, probe, kv, ck, cv, mem)
    up, up_far, down, down_far = follow(run, up, up_far, down, down_far)
    up_parts, down_parts = near_parts(ordered(up, up_far, z)), near_parts(ordered(down, down_far, x))
    comp_keep, comp_send = grad_comp(run, squeezed, gck, gcv, w_full, gain1, groups, n_dp)

    attended, second, w_out_full = mix_out(run, current, (m0, m1), w_out, d_parts, gain2)
    far = list(range(3, top + 1))
    names, under = ["y"] + list(range(top, 0, -1)), ["y"] + list(range(top - 1, 0, -1))
    turns = lambda rest: [[1, "y", 2] + rest, ["y", 2, 1] + rest, [2, 1, "y"] + rest]
    of_comp = Source(links, comp_keep, comp_send, names, [[2, 1, "y"] + far])
    advance(run, links, of_comp)
    (output, grad_attended, grad_mix, up_keep, up_send, down_keep, down_send, sum_bias, sum_gain2
     ) = feed_forward(run, second, cotangent[0], attended, w_up, up_parts, w_down, down_parts,
                      bias_up.reshape(1, -1), gain2, w_out_full, n_dp)
    inner = bias_up.shape[0]
    rows, half = inner // n_dp, width // 2
    flat = lambda a: a.reshape(2, n_dp // 2, rows, half)
    third = max(2 * rows * 11 // 32 // 16 * 16, 8)
    deal = Deal(
        links, [(flat(up_keep), flat(up_send)), (flat(down_keep), flat(down_send))], names,
        turns(far), (0, third, 2 * third, 2 * rows))
    carry = Carry(*deal.sends)
    advance(run, links, *of_comp.flows, carry)
    deal.start(carry.values)

    chunk = width // n_dp

    def write_ffn(rows, up, down):
        size = rows.shape[0] // 2
        up[...] = rows[:size].T
        for n in range(inner // (2 * half)):
            down[n * half:(n + 1) * half] = rows[size + n * chunk:size + (n + 1) * chunk].T

    def write_comp(rows, grad):
        for t in range(3):
            grad[t] = rows[t * chunk:(t + 1) * chunk].T

    def write_rest(rows, qkv, rel, ow):
        tap = lambda t: rows[t * chunk:(t + 1) * chunk].T
        qkv[0], qkv[1], qkv[2] = tap(2), tap(0), tap(1)
        rel[...], ow[...] = tap(3), tap(4)

    waiting = lambda *flows: [f for f in flows if f.order]
    back = functools.partial(attention_back, run, (p0, p1), grad_mix, qc, qp, kv, pos, start, scale)
    grads = lambda turned, gq, half: projection_grads(
        run, turned, gq, grad_attended, normed, table, (m0, m1), w_full, n_dp, half)
    gq0, gk0, gv0, gpos0, content0, position0 = back(0)
    advance(run, links, *of_comp.flows)
    deal.add(run, 4)
    keep_0, send_0, gain_0 = grads((gk0, gv0, gpos0), gq0, 0)
    gq1, gk1, gv1, gpos1, content1, position1 = back(1)
    carry = Carry(send_0)
    advance(run, links, *deal.chains, *of_comp.flows, carry)
    early = Source(links, keep_0, carry.values[0], under, turns(far[:-1]))
    keep_1, send_1, gain_1 = grads((gk1, gv1, gpos1), gq1, 1)
    carry = Carry(send_1)
    comp_end = Finish(of_comp.flows, [(3, half, chunk)], write_comp)
    comp_left = list(waiting(*of_comp.flows))
    advance(run, links, *deal.chains, *(comp_left or [comp_end]), early, carry)
    late = Source(links, keep_1, carry.values[0], under, turns(far[:-1]))
    row = lambda a, b: jnp.concatenate([a, b], axis=1)
    small = Small(links, jnp.concatenate(
        [(gain_0 + gain_1) / gain1, sum_gain2, row(content0, content1), row(position0, position1),
         sum_bias.reshape(-1, width)], axis=0))
    new_memory = lax.dynamic_slice_in_dim(
        jnp.concatenate([recent, current], axis=0), seg_length, mem, 0)
    new_compressed = lax.dynamic_slice_in_dim(
        jnp.concatenate([distant, squeezed_low[:squeezed_rows]], axis=0), seg_length // 3, comp, 0)
    advance(run, links, *waiting(*deal.chains, *comp_left), late, small)
    grad_rows = grad_tokens(run, (gk0, gk1), (gv0, gv1), (gq0, gq1), current, grad_attended,
                            w_full, gain1)
    while any(f.order for f in late.flows):
        advance(run, links, *waiting(*deal.chains, *comp_left, *early.flows, *late.flows),
                small)
    ends = [Join(top, a, b) for a, b in zip(early.flows, late.flows)]
    of_ffn = Finish(deal.chains, [(half, rows), (inner // 2, chunk)], write_ffn)
    advance(run, links, *ends, small, of_ffn, *([comp_end] if comp_left else []))
    rest = Finish(ends, [(3, half, chunk), (half, chunk), (half, chunk)], write_rest)
    last = [small] if small.recv is not None else []
    advance(run, links, rest, *last)
    while small.recv is not None:
        advance(run, links, small)
    (grad_up, grad_down), (grad_comp_,) = of_ffn.result, comp_end.result
    grad_qkv, grad_rel, grad_out = rest.result

    at = links.dp * 2 + links.y
    each, each_up = width // (2 * n_dp), bias_up.shape[0] // (2 * n_dp)
    vec = lax.dynamic_slice(small.keep[:4], (0, at * each), (4, each))
    vec_up = lax.dynamic_slice_in_dim(small.keep[4:].reshape(-1), at * each_up, each_up)
    return (output[None], grad_rows[None], new_memory[None], new_compressed[None],
            grad_qkv, grad_rel, grad_out,
            grad_up, grad_down, grad_comp_, vec[0], vec[1], vec[2], vec[3], vec_up)


def solution(mesh):
    rows = P(("dp", "fsdp"), None, None)
    one = P(("dp", "fsdp"))
    return jax.shard_map(
        body,
        mesh=mesh,
        in_specs=(rows, rows, rows, rows, one, one, one, P(None, "fsdp", None), P("fsdp", None),
                  P("fsdp", None), P("fsdp", None), P("fsdp", None), P(None, "fsdp", None), P(),
                  P(), P(), P(), P()),
        out_specs=(rows, rows, rows, rows, P(None, "fsdp", "dp"), P("fsdp", "dp"),
                   P("fsdp", "dp"), P("fsdp", "dp"), P("fsdp", "dp"), P(None, "fsdp", "dp"), one,
                   one, one, one, one),
        check_vma=False,
    )
```

```python
import functools
import math

import jax
import jax.numpy as jnp
from jax import lax
from jax.experimental import pallas as pl
from jax.experimental.pallas import tpu as pltpu
from jax.sharding import PartitionSpec as P

H = 8
BF = jnp.bfloat16
F32 = jnp.float32
VMEM = 60 * 1024 * 1024
GELU_C = math.sqrt(2.0 / math.pi)
COST = 0.0001
TEMPORARIES = 36 * 1024 * 1024
Y, CORE, SEG_LEN, MEM_LIVE, COMP_LIVE, PIECE_A, PIECE_B, BITS = range(8)


def nn(a, b):
    return lax.dot_general(a, b, (((1,), (0,)), ((), ())), preferred_element_type=F32)


def nt(a, b):
    return lax.dot_general(a, b, (((1,), (1,)), ((), ())), preferred_element_type=F32)


def tn(a, b):
    return lax.dot_general(a, b, (((0,), (0,)), ((), ())), preferred_element_type=F32)


class Steps:
    def __init__(self, scal):
        self.scal = scal
        self.token = None

    def __call__(self, kernel, name, grid, ins, outs, scratch, args, flops, aliases={}):
        before = [] if self.token is None else [self.token]
        n_in, n_out, extra = len(ins), len(outs), len(before)

        def ordered_kernel(s_ref, *refs):
            rest = refs[n_in + extra:]
            kernel(s_ref, *refs[:n_in], *rest[:n_out], *rest[n_out + 1:])

        anywhere = pl.BlockSpec(memory_space=pltpu.HBM)
        moved = sum(a.size * a.dtype.itemsize for a in args)
        need = TEMPORARIES
        for (block, array) in list(zip(ins, args)) + [(b, s) for s, b in outs]:
            if block.block_shape is not None:
                need += 2 * math.prod(block.block_shape) * array.dtype.itemsize
        for ref in (r for r in scratch if 'sem' not in str(r.dtype)):
            need += math.prod(ref.shape) * jnp.dtype(ref.dtype).itemsize
        done = pl.pallas_call(
            ordered_kernel,
            name=name,
            out_shape=[s for s, _ in outs] + [jax.ShapeDtypeStruct((8, 128), F32)],
            grid_spec=pltpu.PrefetchScalarGridSpec(
                num_scalar_prefetch=1,
                grid=grid,
                in_specs=list(ins) + [anywhere] * extra,
                out_specs=[b for _, b in outs] + [anywhere],
                scratch_shapes=scratch,
            ),
            compiler_params=pltpu.CompilerParams(
                vmem_limit_bytes=min(need, VMEM), dimension_semantics=("arbitrary",) * len(grid)
            ),
            input_output_aliases=aliases,
            cost_estimate=pl.CostEstimate(
                flops=int(flops * COST), bytes_accessed=int(moved * COST), transcendentals=0),
        )(self.scal, *args, *before)
        *done, self.token = done
        return done


def follow(run, *values):
    anywhere = pl.BlockSpec(memory_space=pltpu.HBM)
    return run(
        lambda *refs: None, "follow", (1,), [anywhere] * len(values),
        [(jax.ShapeDtypeStruct(v.shape, v.dtype), anywhere) for v in values], [], values, 0,
        {n + 1: n for n in range(len(values))})


def whole(shape):
    return pl.BlockSpec(shape, lambda i, s: (0,) * len(shape))


def out(shape, dtype, block, index):
    return (jax.ShapeDtypeStruct(shape, dtype), pl.BlockSpec(block, index))


def fixed(shape, dtype):
    return out(shape, dtype, shape, lambda i, s: (0,) * len(shape))


def norm_rows(rows):
    centred = rows - jnp.mean(rows, axis=-1, keepdims=True)
    spread = jnp.mean(centred * centred, axis=-1, keepdims=True)
    scale = lax.rsqrt(spread + 1e-05)
    return centred * scale, scale


def norm_back(grad, gain, unit, scale):
    g = grad * gain
    inner = jnp.mean(g * unit, axis=-1, keepdims=True)
    return scale * (g - jnp.mean(g, axis=-1, keepdims=True) - unit * inner)


def place(dst, s_ref, own, mine, theirs, cols=slice(None)):
    half, quarter = own.shape[-2], mine.shape[-2]
    y, core = s_ref[Y], s_ref[CORE]
    base = (1 - y) * half
    at = lambda start, size: pl.ds(pl.multiple_of(start, quarter), size)
    dst[at(y * half, half), cols] = own[:, cols]
    dst[at(base + core * quarter, quarter), cols] = mine[...]
    dst[at(base + (1 - core) * quarter, quarter), cols] = theirs[...]


def pack_first_kernel(s_ref, rel, k, v, qa, qb, o_rel, o_a, o_b):
    width = rel.shape[-1]
    o_rel[...] = rel[...]
    o_a[0, :, :width] = k[0, 0]
    o_a[0, :, width:] = qa[0, 0]
    o_b[0, :, :width] = v[0, 0]
    o_b[0, :, width:] = qb[0, 0]


def pack_rest_kernel(s_ref, c0, c1, c2, ow, up, down, o_c, o_d, o_up, o_down):
    o_c[0] = c0[0, 0]
    o_c[1] = c1[0, 0]
    o_d[0] = c2[0, 0]
    o_d[1] = ow[0]
    o_up[...] = up[...]
    o_down[...] = down[...]


def quarters(a):
    lead = a.shape[:-2]
    return a.reshape(lead + (4, a.shape[-2] // 4, a.shape[-1]))


def part_of(a, where, n=0, cols=1, c=0):
    block = (1,) * (a.ndim - 2) + (a.shape[-2], a.shape[-1] // cols)
    if a.ndim == 3:
        return pl.BlockSpec(block, lambda i, s: (s[where], 0, c))
    return pl.BlockSpec(block, lambda i, s: (n, s[where], 0, c))


def pack_first(run, w_qkv, w_rel):
    qkv, rel = quarters(w_qkv), quarters(w_rel)
    part, width = rel.shape[1:]
    return run(
        pack_first_kernel, "pack_first", (1,),
        [part_of(rel, PIECE_A), part_of(qkv, PIECE_A, 1), part_of(qkv, PIECE_B, 2),
         part_of(qkv, PIECE_A, 0, 2, 0), part_of(qkv, PIECE_B, 0, 2, 1)],
        [fixed((1, part, width), BF), fixed((1, part, width * 3 // 2), BF),
         fixed((1, part, width * 3 // 2), BF)],
        [], (rel, qkv, qkv, qkv, qkv), 0)


def pack_rest(run, w_out, w_up, w_down, w_comp):
    comp, ow, up, down = quarters(w_comp), quarters(w_out), quarters(w_up), quarters(w_down)
    part, width = ow.shape[1:]
    return run(
        pack_rest_kernel, "pack_rest", (1,),
        [part_of(comp, PIECE_A, 0), part_of(comp, PIECE_A, 1), part_of(comp, PIECE_B, 2),
         part_of(ow, PIECE_B), part_of(up, PIECE_A), part_of(down, PIECE_B)],
        [fixed((2, part, width), BF), fixed((2, part, width), BF),
         fixed((1,) + up.shape[1:], BF), fixed((1,) + down.shape[1:], BF)],
        [], (comp, comp, comp, ow, up, down), 0)


def order_kernel(s_ref, *refs, slots):
    n = len(slots)
    outs, sem = refs[2 * n:3 * n], refs[3 * n]
    copies = []
    for c, slot in enumerate(slots):
        bit = s_ref[slot]
        copies += [
            pltpu.make_async_copy(refs[c], outs[c].at[:, bit], sem.at[2 * c]),
            pltpu.make_async_copy(refs[n + c], outs[c].at[:, 1 - bit], sem.at[2 * c + 1])]
    for copy in copies:
        copy.start()
    for copy in copies:
        copy.wait()


def order(run, *pieces):
    args = [p[0] for p in pieces] + [p[1] for p in pieces]
    shapes = [(p[0].shape[0], 2) + p[0].shape[1:] for p in pieces]
    anywhere = pl.BlockSpec(memory_space=pltpu.HBM)
    done = run(
        functools.partial(order_kernel, slots=tuple(BITS + p[2] - 1 for p in pieces)), "order", (1,),
        [anywhere] * len(args), [(jax.ShapeDtypeStruct(s, BF), anywhere) for s in shapes],
        [pltpu.SemaphoreType.DMA((len(args),))], args, 0)
    return [d.reshape(s[0], 2 * s[2], s[3]) for d, s in zip(done, shapes)]


def normed_kernel(s_ref, d_ref, m_ref, t_ref, g_ref, x_ref):
    i = pl.program_id(0)
    for n, ref in enumerate((d_ref, m_ref, t_ref)):
        @pl.when(i // 2 == n)
        def _(ref=ref):
            x_ref[...] = (norm_rows(ref[...].astype(F32))[0] * g_ref[...]).astype(BF)


def norm_hidden(run, distant, recent, current, gain):
    mem, width = recent.shape
    blk = mem // 2
    part = lambda n: pl.BlockSpec((blk, width), lambda i, s: (jnp.clip(i - 2 * n, 0, 1), 0))
    return run(
        normed_kernel, "norm_hidden", (6,),
        [part(0), part(1), part(2), whole(gain.shape)],
        [out((3 * mem, width), BF, (blk, width), lambda i, s: (i, 0))],
        [], (distant, recent, current, gain), 0)[0]


def constants_kernel(s_ref, m_ref, sa_ref, ca_ref, sb_ref, cb_ref, tab_ref, gr_ref, wide_ref,
                     *, groups):
    i = pl.program_id(0)
    blk, width = tab_ref.shape
    half = width // 2
    fine = sb_ref.shape[0]
    for n in range(blk // fine):
        rows = slice(n * fine, (n + 1) * fine)
        a = i * (blk // fine) + n
        sa, ca = sa_ref[pl.ds(a, 1)], ca_ref[pl.ds(a, 1)]
        tab_ref[rows, :half] = (sa * cb_ref[...] + ca * sb_ref[...]).astype(BF)
        tab_ref[rows, half:] = (ca * cb_ref[...] - sa * sb_ref[...]).astype(BF)

    @pl.when(i == 0)
    def _():
        mem = m_ref.shape[0]
        lanes = wide_ref.shape[2]
        count = gr_ref.shape[1]
        live = lax.broadcasted_iota(jnp.int32, (count, 1), 0) < groups
        for n in range(width // lanes):
            cols = slice(n * lanes, (n + 1) * lanes)
            wide_ref[n, :mem] = m_ref[:, cols].astype(F32)
            wide_ref[n, mem:] = jnp.zeros((wide_ref.shape[1] - mem, lanes), F32)
            for t in range(3):
                rows = jnp.where(live, wide_ref[n, pl.ds(t, count, stride=3)], 0.0)
                gr_ref[t, :, cols] = rows.astype(BF)


def constants(run, recent, angles, groups):
    mem, width = recent.shape
    keys = 3 * mem
    blk = 512
    padded = groups + (-groups) % 64
    ins = (recent,) + angles
    return run(
        functools.partial(constants_kernel, groups=groups), "constants", (keys // blk,),
        [whole(a.shape) for a in ins],
        [out((keys, width), BF, (blk, width), lambda i, s: (i, 0)),
         fixed((3, padded, width), BF)],
        [pltpu.VMEM((width // 128, 3 * padded, 128), F32)], ins, 0)


def qkv_kernel(s_ref, x_ref, o_ref, am_ref, at_ref, bm_ref, bt_ref, bc_ref, bp_ref, kv_ref,
               qc_ref, qp_ref, pr_ref, w_ref, *, scale):
    i = pl.program_id(0)
    rows, width = x_ref.shape
    seg = qc_ref.shape[0]
    blk = 256
    lo, hi = slice(0, width // 2), slice(width // 2, width)
    own, dst = o_ref.at[0], w_ref.at[0]

    @pl.when(i == 0)
    def _():
        place(dst, s_ref, own, am_ref.at[0, :, :width], at_ref.at[0, :, :width])

    @pl.when(i == 1)
    def _():
        place(dst, s_ref, own, bm_ref.at[0, :, :width], bt_ref.at[0, :, :width])

    @pl.when(i == 2)
    def _():
        place(dst, s_ref, own, am_ref.at[0, :, width:], at_ref.at[0, :, width:], lo)
        place(dst, s_ref, own, bm_ref.at[0, :, width:], bt_ref.at[0, :, width:], hi)

    @pl.when(i < 2)
    def _():
        def some(n):
            at = slice(n * blk, (n + 1) * blk)
            kv_ref[0, at] = nn(x_ref[at], dst[...]).astype(BF)

        for n in range(rows // blk):
            some(n)

    @pl.when(i == 2)
    def _():
        for n in range(seg // blk):
            at = slice(n * blk, (n + 1) * blk)
            q = nn(x_ref[rows - seg + n * blk:rows - seg + (n + 1) * blk], dst[...])
            qc_ref[at] = ((q + bc_ref[...]) * scale).astype(BF)
            qp_ref[at] = ((q + bp_ref[...]) * scale).astype(BF)
            pr_ref[at] = (q * scale).astype(BF)


def project_qkv(run, normed, w_qkv, a_parts, b_parts, bias_content, bias_position, seg, scale):
    rows, width = normed.shape
    turn = lambda i, s: ((i + 1) % 3, 0, 0)
    parts = a_parts + b_parts
    return run(
        functools.partial(qkv_kernel, scale=scale), "project_qkv", (3,),
        [whole((rows, width)), pl.BlockSpec((1, width // 2, width), turn)]
        + [whole(p.shape) for p in parts] + [whole((1, width)), whole((1, width))],
        [out((2, rows, width), BF, (1, rows, width), lambda i, s: (jnp.minimum(i, 1), 0, 0)),
         fixed((seg, width), BF), fixed((seg, width), BF), fixed((seg, width), BF),
         out((3, width, width), BF, (1, width, width), turn)],
        [], (normed, w_qkv) + parts + (bias_content.reshape(1, -1), bias_position.reshape(1, -1)),
        2 * (2 * rows + seg) * width * width)


def position_kernel(s_ref, x_ref, o_ref, m_ref, t_ref, p_ref, w_ref):
    @pl.when(pl.program_id(0) == 0)
    def _():
        place(w_ref, s_ref, o_ref, m_ref.at[0], t_ref.at[0])

    p_ref[...] = nn(x_ref[...], w_ref[...]).astype(BF)


def project_position(run, table, own, parts):
    rows, width = table.shape
    blk = 512
    return run(
        position_kernel, "project_position", (rows // blk,),
        [pl.BlockSpec((blk, width), lambda i, s: (i, 0)), whole(own.shape)]
        + [whole(p.shape) for p in parts],
        [out((rows, width), BF, (blk, width), lambda i, s: (i, 0))],
        [pltpu.VMEM((width, width), BF)], (table, own) + parts,
        2 * rows * width * width)[0]


RB = 256


def flip_matrix():
    return (lax.broadcasted_iota(jnp.int32, (RB, RB), 0)
            + lax.broadcasted_iota(jnp.int32, (RB, RB), 1) == RB - 1).astype(BF)


def attention_kernel(s_ref, qc_ref, qp_ref, k_ref, v_ref, pos_ref, p_ref, mix_ref, bias_ref,
                     *, comp, mem):
    seg, keys = qc_ref.shape[0], k_ref.shape[1]
    start = comp + mem

    @pl.when(pl.program_id(0) == 0)
    def _():
        mem_live, comp_live = s_ref[MEM_LIVE], s_ref[COMP_LIVE]
        col = lax.broadcasted_iota(jnp.int32, bias_ref.shape, 1)
        row = lax.broadcasted_iota(jnp.int32, bias_ref.shape, 0)
        live = ((col >= comp - comp_live) & (col < comp)) | (
            (col >= start - mem_live) & (col - start <= row))
        bias_ref[...] = jnp.where(live, 0.0, -1e30)

    flip = flip_matrix()
    for r in range(seg // RB):
        width = start + RB * (r + 1)
        rows = slice(r * RB, (r + 1) * RB)
        content = nt(qc_ref[rows], k_ref[0, :width])
        rel = nt(qp_ref[rows], pos_ref[keys - width:])
        rel = pltpu.roll(rel, width - RB + 1, 1, stride=1, stride_axis=0)
        masked = content + rel + bias_ref[rows, :width]
        top = jnp.max(masked, axis=-1, keepdims=True)
        weights = jnp.exp(masked - top)
        probs = (weights * (1.0 / jnp.sum(weights, axis=-1, keepdims=True))).astype(BF)
        mix_ref[rows] = nn(probs, v_ref[0, :width]).astype(BF)
        p_ref[0, rows, :width] = nn(flip, probs).astype(BF)


def attention(run, qc, qp, kv, pos, comp, mem, half):
    seg, width = qc.shape
    keys = kv.shape[1]
    dh = width // H
    n = H // 2
    first = half * n
    q_spec = pl.BlockSpec((seg, dh), lambda h, s: (0, h + first))
    of = lambda m: pl.BlockSpec((1, keys, dh), lambda h, s: (m, 0, h + first))
    return run(
        functools.partial(attention_kernel, comp=comp, mem=mem), "attention", (n,),
        [q_spec, q_spec, of(0), of(1), pl.BlockSpec((keys, dh), lambda h, s: (0, h + first))],
        [out((n, seg, keys), BF, (1, seg, keys), lambda h, s: (h, 0, 0)),
         out((seg, width // 2), BF, (seg, dh), lambda h, s: (0, h))],
        [pltpu.VMEM((seg, keys), F32)], (qc, qp, kv, kv, pos), 16 * seg * keys * width)


def attention_back_kernel(s_ref, p_ref, gm_ref, qc_ref, qp_ref, k_ref, v_ref, pos_ref, gq_ref,
                          gk_ref, gv_ref, gp_ref, gc_ref, gb_ref, gs_ref, sh_ref, pr_ref, rev_ref,
                          *, start, scale):
    seg, keys = qc_ref.shape[0], k_ref.shape[1]
    flip = flip_matrix()
    sum_c = jnp.zeros((1, gc_ref.shape[1]), F32)
    sum_p = jnp.zeros((1, gc_ref.shape[1]), F32)
    for r in range(seg // RB):
        width = start + RB * (r + 1)
        rows = slice(r * RB, (r + 1) * RB)
        for n, ref in enumerate((gm_ref, qc_ref, qp_ref)):
            rev_ref[n, rows] = nn(flip, ref[rows]).astype(BF)
        low = p_ref[0, rows, :width]
        probs = low.astype(F32)
        weighted = probs * nt(rev_ref[0, rows], v_ref[0, :width])
        scores = (weighted - probs * jnp.sum(weighted, axis=-1, keepdims=True))
        low_scores = scores.astype(BF)
        moved = pltpu.roll(scores, 0, 1, stride=1, stride_axis=0).astype(BF)
        gs_ref[rows, :width] = low_scores
        sh_ref[rows, keys - width:] = moved
        pr_ref[rows, :width] = low
        if width < keys:
            gs_ref[rows, width:] = jnp.zeros((RB, keys - width), BF)
            pr_ref[rows, width:] = jnp.zeros((RB, keys - width), BF)
            sh_ref[rows, : keys - width] = jnp.zeros((RB, keys - width), BF)
        grad_c = nn(low_scores, k_ref[0, :width])
        grad_p = nn(moved, pos_ref[keys - width:])
        sum_c += jnp.sum(grad_c, axis=0, keepdims=True)
        sum_p += jnp.sum(grad_p, axis=0, keepdims=True)
        gq_ref[rows] = nn(flip, ((grad_c + grad_p) * scale).astype(BF)).astype(BF)
    gc_ref[...] = sum_c * scale
    gb_ref[...] = sum_p * scale
    gv_ref[...] = tn(rev_ref[0], pr_ref[...]).astype(BF)
    gk_ref[...] = tn(rev_ref[1], gs_ref[...]).astype(BF)
    gp_ref[...] = tn(rev_ref[2], sh_ref[...]).astype(BF)


def attention_back(run, probs, gm, qc, qp, kv, pos, start, scale, half):
    seg, width = qc.shape
    keys = kv.shape[1]
    dh = width // H
    n = H // 2
    first = half * n
    q_spec = pl.BlockSpec((seg, dh), lambda h, s: (0, h + first))
    of = lambda m: pl.BlockSpec((1, keys, dh), lambda h, s: (m, 0, h + first))
    turned = lambda: out((width // 2, keys), BF, (dh, keys), lambda h, s: (h, 0))
    sums = lambda: out((1, width // 2), F32, (1, dh), lambda h, s: (0, h))
    big = pltpu.VMEM((seg, keys), BF)
    return run(
        functools.partial(attention_back_kernel, start=start, scale=scale), "attention_back", (n,),
        [pl.BlockSpec((1, seg, keys), lambda h, s: (h, 0, 0)), q_spec, q_spec, q_spec,
         of(0), of(1), pl.BlockSpec((keys, dh), lambda h, s: (0, h + first))],
        [out((seg, width // 2), BF, (seg, dh), lambda h, s: (0, h)), turned(), turned(), turned(),
         sums(), sums()],
        [big, big, big, pltpu.VMEM((3, seg, dh), BF)], (probs[half], gm, qc, qp, kv, kv, pos),
        12 * seg * keys * width)


def mixed_kernel(s_ref, tok_ref, a_ref, b_ref, o_ref, m_ref, t_ref, g_ref, att_ref, sec_ref, w_ref):
    @pl.when(pl.program_id(0) == 0)
    def _():
        place(w_ref, s_ref, o_ref, m_ref.at[1], t_ref.at[1])

    mid = a_ref.shape[1]
    attended = (tok_ref[...].astype(F32) + nn(a_ref[...], w_ref[:mid])
                + nn(b_ref[...], w_ref[mid:]))
    att_ref[...] = attended
    sec_ref[...] = (norm_rows(attended)[0] * g_ref[...]).astype(BF)


def mix_out(run, tokens, mixed, own, parts, gain):
    seg, width = tokens.shape
    blk = 256
    row = pl.BlockSpec((blk, width), lambda i, s: (i, 0))
    side = pl.BlockSpec((blk, width // 2), lambda i, s: (i, 0))
    return run(
        mixed_kernel, "mix_out", (seg // blk,),
        [row, side, side, whole(own.shape)] + [whole(p.shape) for p in parts] + [whole((1, width))],
        [out((seg, width), F32, (blk, width), lambda i, s: (i, 0)),
         out((seg, width), BF, (blk, width), lambda i, s: (i, 0)),
         fixed((width, width), BF)],
        [], (tokens,) + mixed + (own,) + parts + (gain,), 2 * seg * width * width)


def part_shape(rows, cols, n_dp, taps, cut=1):
    return (2, n_dp // (2 * cut), taps, rows // n_dp, cols // 2)


def low_or_wide(chunk):
    return BF if chunk % 16 == 0 else F32


def by_core(buf, values, core):
    pairs, _, chunk, cols = buf.shape
    buf[...] = values.astype(buf.dtype).reshape(pairs, 2, chunk, cols)
    pick = lambda c: buf[:, c].reshape(pairs * chunk, cols)
    return jnp.concatenate([pick(core), pick(1 - core)], axis=0).astype(BF)


def put(keep, send, values):
    half = values.shape[0] // 2
    shape = keep.shape[:-1] + (values.shape[1],)
    keep[...] = values[:half].reshape(shape).astype(BF)
    send[...] = values[half:].reshape(shape).astype(BF)


def ffn_kernel(s_ref, sec_ref, cot_ref, att_ref, uo_ref, um_ref, ut_ref, do_ref, dm_ref, dt_ref,
               b_ref, g_ref, wo_ref, act_ref, gatt_ref, gm_ref, uk_ref, us_ref, dk_ref, ds_ref,
               gb_ref, gg_ref, gout_ref, turn_ref, wu_ref, wd_ref, gsec_ref, ubuf, dbuf):
    i, n = pl.program_id(0), pl.num_programs(0)
    y, core = s_ref[Y], s_ref[CORE]

    @pl.when(i == 0)
    def _():
        row = lax.broadcasted_iota(jnp.int32, cot_ref.shape, 0)
        live = jnp.where(row < s_ref[SEG_LEN], cot_ref[...], jnp.zeros((), BF))
        gout_ref[...] = live
        turn_ref[...] = by_core(dbuf, live.T, core)
        gsec_ref[...] = jnp.zeros_like(gsec_ref)

    place(wu_ref, s_ref, uo_ref, um_ref.at[0], ut_ref.at[0])
    half = i // (n // 2)
    side = (i % (n // 2)) // (n // 4)

    @pl.when(half == y)
    def _():
        wd_ref[...] = do_ref[...]

    @pl.when((half != y) & (side == core))
    def _():
        wd_ref[...] = dm_ref[0]

    @pl.when((half != y) & (side != core))
    def _():
        wd_ref[...] = dt_ref[0]

    second, gout = sec_ref[...], gout_ref[...]
    v = nn(second, wu_ref[...]) + b_ref[...]
    square = v * v
    gate = 0.5 + 0.5 * jnp.tanh(v * (GELU_C + (GELU_C * 0.044715) * square))
    act = (v * gate).astype(BF)
    slope = gate + (gate - gate * gate) * v * (2 * GELU_C + (6 * GELU_C * 0.044715) * square)
    act_ref[...] = act
    grad_inner = nt(gout, wd_ref[...]) * slope
    low = grad_inner.astype(BF)
    gb_ref[...] = jnp.sum(low.astype(F32), axis=0, keepdims=True)
    gsec_ref[...] += nt(low, wu_ref[...])
    put(dk_ref.at[0, :, 0], ds_ref.at[0, :, 0], nn(turn_ref[...], act))
    part = nn(by_core(ubuf, low.T, core), second)
    width = part.shape[1] // 2
    for side in range(2):
        put(uk_ref.at[side, :, 0], us_ref.at[side, :, 0], part[:, side * width:(side + 1) * width])

    @pl.when(i == n - 1)
    def _():
        unit, scale = norm_rows(att_ref[...])
        grad = gsec_ref[...]
        gg_ref[...] = jnp.sum(grad * unit, axis=0, keepdims=True)
        gatt = norm_back(grad, g_ref[...], unit, scale) + gout_ref[...].astype(F32)
        gatt_ref[...] = gatt
        gm_ref[...] = nt(gatt.astype(BF), wo_ref[...]).astype(BF)


def down_rows(n, blk, width):
    def own(i, s):
        return (jnp.clip(i - s[Y] * (n // 2), 0, n // 2 - 1), 0)

    def part(other):
        def index(i, s):
            side = s[CORE] if other == 0 else 1 - s[CORE]
            first = (1 - s[Y]) * (n // 2) + side * (n // 4)
            return (0, jnp.clip(i - first, 0, n // 4 - 1), 0)

        return pl.BlockSpec((1, blk, width), index)

    return pl.BlockSpec((blk, width), own), part(0), part(1)


def output_kernel(s_ref, act_ref, att_ref, do_ref, dm_ref, dt_ref, out_ref, acc_ref):
    i, n = pl.program_id(0), pl.num_programs(0)
    half, side = i // (n // 2), (i % (n // 2)) // (n // 4)
    y, core = s_ref[Y], s_ref[CORE]

    @pl.when(i == 0)
    def _():
        acc_ref[...] = att_ref[...]

    @pl.when(half == y)
    def _():
        acc_ref[...] += nn(act_ref[...], do_ref[...])

    @pl.when((half != y) & (side == core))
    def _():
        acc_ref[...] += nn(act_ref[...], dm_ref[0])

    @pl.when((half != y) & (side != core))
    def _():
        acc_ref[...] += nn(act_ref[...], dt_ref[0])

    @pl.when(i == n - 1)
    def _():
        out_ref[...] = acc_ref[...].astype(BF)


def layer_output(run, act, attended, w_down, down_parts):
    seg, inner = act.shape
    width = attended.shape[1]
    n = 4
    blk = inner // n
    dm, dt = down_parts
    return run(
        output_kernel, "output", (n,),
        [pl.BlockSpec((seg, blk), lambda i, s: (0, i)), whole((seg, width)),
         *down_rows(n, blk, width)],
        [fixed((seg, width), BF)], [pltpu.VMEM((seg, width), F32)],
        (act, attended, w_down, dm, dt), 2 * seg * width * inner)[0]


def feed_forward(run, second, cotangent, attended, w_up, up_parts, w_down, down_parts, bias_up,
                 gain, w_out, n_dp):
    seg, width = second.shape
    inner = bias_up.shape[1]
    n = 8
    blk = inner // n
    um, ut = up_parts
    dm, dt = down_parts
    uch, dch = inner // n_dp, width // n_dp
    pairs = blk // (2 * uch)
    col = lambda a: pl.BlockSpec((a.shape[0], blk), lambda i, s: (0, i))
    col3 = lambda a: pl.BlockSpec((1, a.shape[1], blk), lambda i, s: (0, 0, i))

    up_shape = part_shape(inner, width, n_dp, 1)
    down_shape = part_shape(width, inner, n_dp, n // 2)[:-1] + (blk,)
    up_out = lambda: out(up_shape, BF, (2, pairs, 1, uch, width // 2),
                         lambda i, s: (0, i, 0, 0, 0))
    down_out = lambda: out(down_shape, BF, (1, n_dp // 2, 1, dch, blk),
                           lambda i, s: (i // (n // 2), 0, i % (n // 2), 0, 0))
    full = (seg, width)
    return run(
        ffn_kernel, "feed_forward", (n,),
        [whole(full), whole(full), whole(full), col(w_up), col3(um), col3(ut),
         *down_rows(n, blk, width),
         pl.BlockSpec((1, blk), lambda i, s: (0, i)), whole((1, width)), whole((width, width))],
        [out((seg, inner), BF, (seg, blk), lambda i, s: (0, i)), fixed(full, F32),
         fixed(full, BF), up_out(), up_out(), down_out(),
         down_out(), out((1, inner), F32, (1, blk), lambda i, s: (0, i)), fixed((1, width), F32)],
        [pltpu.VMEM(full, BF), pltpu.VMEM((width, seg), BF), pltpu.VMEM((width, blk), BF),
         pltpu.VMEM((blk, width), BF), pltpu.VMEM(full, F32),
         pltpu.VMEM((pairs, 2, uch, seg), low_or_wide(uch)),
         pltpu.VMEM((n_dp // 2, 2, dch, seg), low_or_wide(dch))],
        (second, cotangent, attended, w_up, um, ut, w_down, dm, dt, bias_up, gain, w_out),
        12 * seg * width * inner)


def grads_kernel(s_ref, gk_ref, gv_ref, gp_ref, gq_ref, ga_ref, x_ref, tab_ref, ma_ref, mb_ref, w_ref,
                 keep_ref, send_ref, gg_ref, k_s, v_s, p_s, q_s, o_s, big, small):
    core = s_ref[CORE]
    rows = x_ref.shape[0]
    seg = gq_ref.shape[0]

    @pl.when(pl.program_id(0) == 0)
    def _():
        k_s[...] = by_core(big, gk_ref[...], core)
        v_s[...] = by_core(big, gv_ref[...], core)
        p_s[...] = by_core(big, gp_ref[...], core)
        q_s[...] = by_core(small, gq_ref[...].T, core)
        o_s[...] = by_core(small, ga_ref[...].astype(BF).T, core)

    x = x_ref[...]
    pairs, _, chunk, _ = small.shape
    n = pairs * chunk

    def both(tap, values):
        put(keep_ref.at[0, :, tap], send_ref.at[0, :, tap], values)

    def gain(values, m):
        turned = w_ref[m].T.astype(F32)
        whole_ = turned.reshape(pairs, 2, chunk, turned.shape[1])
        even, odd = whole_[:, 0].reshape(n, -1), whole_[:, 1].reshape(n, -1)
        first = jnp.where(core == 0, even, odd)
        last = jnp.where(core == 0, odd, even)
        return (jnp.sum(values[:n] * first, axis=0, keepdims=True)
                + jnp.sum(values[n:] * last, axis=0, keepdims=True))

    part = nn(k_s[...], x)
    both(0, part)
    total = gain(part, 1)
    part = nn(v_s[...], x)
    both(1, part)
    total += gain(part, 2)
    part = nn(q_s[...], x[rows - seg:])
    both(2, part)
    total += gain(part, 0)
    both(3, nn(p_s[...], tab_ref[...]))
    gg_ref[...] = total
    i, n = pl.program_id(0), pl.num_programs(0)

    @pl.when(i < n // 2)
    def _():
        both(4, nn(o_s[...], ma_ref[...]))

    @pl.when(i >= n // 2)
    def _():
        both(4, nn(o_s[...], mb_ref[...]))


def projection_grads(run, turned, gq, gatt, normed, table, mixed, w, n_dp, half):
    rows, width = normed.shape
    seg = gq.shape[0]
    blk = 256
    chunk = width // n_dp
    mid = width // 2
    gk, gv, gpos = turned
    count = mid // blk
    col = lambda r: pl.BlockSpec((r, blk), lambda i, s: (0, i))
    shape = lambda taps: part_shape(width, width, n_dp, taps, 2)
    half_of = lambda taps: out(shape(taps), BF, (1,) + shape(taps)[1:4] + (blk,),
                               lambda i, s: (i // count, 0, 0, 0, i % count))
    side = pl.BlockSpec((seg, blk), lambda i, s: (0, i % count))
    kind = low_or_wide(chunk)
    pairs = mid // (2 * chunk)
    return run(
        grads_kernel, "projection_grads", (width // blk,),
        [whole(gk.shape), whole(gk.shape), whole(gk.shape), whole(gq.shape),
         pl.BlockSpec((seg, mid), lambda i, s: (0, half)), col(rows), col(rows), side, side,
         pl.BlockSpec((3, blk, mid), lambda i, s: (0, i, half))],
        [half_of(5), half_of(5),
         out((1, width), F32, (1, blk), lambda i, s: (0, i))],
        [pltpu.VMEM((mid, rows), BF)] * 3 + [pltpu.VMEM((mid, seg), BF)] * 2
        + [pltpu.VMEM((pairs, 2, chunk, rows), kind), pltpu.VMEM((pairs, 2, chunk, seg), kind)],
        (gk, gv, gpos, gq, gatt, normed, table) + mixed + (w,),
        (3 * rows + 2 * seg) * width * width)


def grad_tokens_kernel(s_ref, ka_ref, kb_ref, va_ref, vb_ref, qa_ref, qb_ref, tok_ref, ga_ref,
                       w_ref, g_ref, gt_ref, acc_ref):
    i = pl.program_id(0)
    mid = w_ref.shape[2] // 2
    left, right = w_ref[0, :, :mid], w_ref[0, :, mid:]

    @pl.when(i == 0)
    def _():
        acc_ref[...] = nn(left, ka_ref[...]) + nn(right, kb_ref[...])

    @pl.when(i == 1)
    def _():
        acc_ref[...] += nn(left, va_ref[...]) + nn(right, vb_ref[...])

    @pl.when(i == 2)
    def _():
        total = (acc_ref[...] + nt(left, qa_ref[...]) + nt(right, qb_ref[...])).T
        unit, scale = norm_rows(tok_ref[...].astype(F32))
        gt_ref[...] = (ga_ref[...] + norm_back(total, g_ref[...], unit, scale)).astype(BF)


def grad_tokens(run, gk, gv, gq, tokens, grad_attended, w, gain):
    seg, width = tokens.shape
    rows = gk[0].shape[1]
    late = pl.BlockSpec((width // 2, seg), lambda i, s: (0, rows // seg - 1))
    side = whole((seg, width // 2))
    return run(
        grad_tokens_kernel, "grad_tokens", (3,),
        [late] * 4 + [side] * 2 + [whole((seg, width)), whole((seg, width)),
         pl.BlockSpec((1, width, width), lambda i, s: ((i + 1) % 3, 0, 0)), whole((1, width))],
        [fixed((seg, width), BF)], [pltpu.VMEM((width, seg), F32)],
        tuple(gk) + tuple(gv) + tuple(gq) + (tokens, grad_attended, w, gain),
        6 * seg * width * width)[0]


def squeeze_kernel(s_ref, gr_ref, o_ref, am_ref, at_ref, bm_ref, bt_ref, w_ref, g_ref, sq_ref,
                   low_ref, k_ref, v_ref):
    y, core = s_ref[Y], s_ref[CORE]
    half, quarter = o_ref.shape[1], am_ref.shape[1]
    base = (1 - y) * half
    total = jnp.zeros(sq_ref.shape, F32)
    for t in range(3):
        m_ref, t_ref, n = (am_ref, at_ref, t) if t < 2 else (bm_ref, bt_ref, 0)
        at = lambda off, size: gr_ref[t, :, pl.ds(pl.multiple_of(off, quarter), size)]
        total += nn(at(y * half, half), o_ref[t])
        total += nn(at(base + core * quarter, quarter), m_ref[n])
        total += nn(at(base + (1 - core) * quarter, quarter), t_ref[n])
    sq_ref[...] = total
    low_ref[...] = total.astype(BF)
    unit = (norm_rows(total)[0] * g_ref[...]).astype(BF)
    k_ref[...] = nn(unit, w_ref[1]).astype(BF)
    v_ref[...] = nn(unit, w_ref[2]).astype(BF)


def squeeze(run, groups, own, a_parts, b_parts, w, gain):
    _, rows, width = groups.shape
    parts = a_parts + b_parts
    shape = (rows, width)
    return run(
        squeeze_kernel, "squeeze", (1,),
        [whole(groups.shape), whole(own.shape)] + [whole(p.shape) for p in parts]
        + [whole(w.shape), whole((1, width))],
        [fixed(shape, F32), fixed(shape, BF), fixed(shape, BF), fixed(shape, BF)], [],
        (groups, own) + parts + (w, gain), 10 * rows * width * width)


def masked_softmax(scores, live):
    masked = jnp.where(live, scores, -1e30)
    weights = jnp.exp(masked - jnp.max(masked, axis=-1, keepdims=True))
    return weights * (1.0 / jnp.sum(weights, axis=-1, keepdims=True))


def recon_kernel(s_ref, pr_ref, ok_ref, ov_ref, ck_ref, cv_ref, gk_ref, gv_ref):
    seg_len = s_ref[SEG_LEN]
    count = seg_len // 3
    probe = pr_ref[...]
    seg, mem, comp = probe.shape[0], ok_ref.shape[1], ck_ref.shape[0]
    old_live = lax.broadcasted_iota(jnp.int32, (1, mem), 1) < 3 * count
    old = nn(masked_softmax(nt(probe, ok_ref[0]), old_live).astype(BF), ov_ref[0])
    live = lax.broadcasted_iota(jnp.int32, (1, comp), 1) < count
    probs = masked_softmax(nt(probe, ck_ref[...]), live)
    low = probs.astype(BF)
    gap = nn(low, cv_ref[...]) - old
    row = lax.broadcasted_iota(jnp.int32, gap.shape, 0)
    grad_out = (jnp.where(row < seg_len, gap, 0.0) * (2.0 / seg_len.astype(F32))).astype(BF)
    gv_ref[...] = tn(low, grad_out).astype(BF)
    weighted = probs * nt(grad_out, cv_ref[...])
    scores = (weighted - probs * jnp.sum(weighted, axis=-1, keepdims=True)).astype(BF)
    gk_ref[...] = tn(scores, probe).astype(BF)


def reconstruct(run, probe, kv, ck, cv, mem):
    seg, width = probe.shape
    rows = ck.shape[0]
    dh = width // H
    at = lambda n, b: pl.BlockSpec((n, dh), lambda h, s: (b, h))
    old = lambda m: pl.BlockSpec((1, mem, dh), lambda h, s: (m, 1, h))
    grads = lambda: out((rows, width), BF, (rows, dh), lambda h, s: (0, h))
    return run(
        recon_kernel, "reconstruct", (H,),
        [at(seg, 0), old(0), old(1), at(rows, 0), at(rows, 0)], [grads(), grads()], [],
        (probe, kv, kv, ck, cv), 4 * seg * width * mem + 12 * seg * width * rows)


def grad_comp_kernel(s_ref, sq_ref, gk_ref, gv_ref, w_ref, g_ref, gr_ref, k_ref, x_ref, low_ref, buf):
    @pl.when(pl.program_id(0) == 0)
    def _():
        grad = nt(gk_ref[...], w_ref[1]) + nt(gv_ref[...], w_ref[2])
        unit, scale = norm_rows(sq_ref[...])
        low = norm_back(grad, g_ref[...], unit, scale).astype(BF)
        low_ref[...] = by_core(buf, low.astype(F32).T, s_ref[CORE])

    part = nn(low_ref[...], gr_ref[0])
    width = part.shape[1] // 2
    for y in range(2):
        put(k_ref.at[y, :, 0], x_ref.at[y, :, 0], part[:, y * width:(y + 1) * width])


def grad_comp(run, squeezed, gk, gv, w, gain, groups, n_dp):
    taps, rows, width = groups.shape
    chunk = width // n_dp
    shape = part_shape(width, width, n_dp, taps)
    half = lambda: out(shape, BF, shape[:2] + (1,) + shape[3:], lambda i, s: (0, 0, i, 0, 0))
    here = whole((rows, width))
    return run(
        grad_comp_kernel, "grad_comp", (taps,),
        [here, here, here, whole(w.shape), whole((1, width)),
         pl.BlockSpec((1, rows, width), lambda i, s: (i, 0, 0))],
        [half(), half()],
        [pltpu.VMEM((width, rows), BF), pltpu.VMEM((n_dp // 2, 2, chunk, rows), low_or_wide(chunk))],
        (squeezed, gk, gv, w, gain, groups), 10 * rows * width * width)


class Links:
    def __init__(self):
        self.dp = lax.axis_index("dp")
        self.y = lax.axis_index("fsdp")
        self.n_dp = lax.axis_size("dp")
        self.top = self.n_dp.bit_length() - 2

    def bit(self, axis):
        return self.y if axis == "y" else (self.dp >> axis) & 1

    def swap(self, value, axis):
        if axis == "y":
            return lax.ppermute(value, "fsdp", [(0, 1), (1, 0)])
        return lax.ppermute(value, "dp", [(i, i ^ (1 << axis)) for i in range(self.n_dp)])


class Part:
    def __init__(self, array, start):
        self.array, self.start = array, start


class Flow:
    def __init__(self, axes, order, rows):
        self.axes, self.order, self.rows = list(axes), list(order), rows

    def halves(self):
        axis = self.order[0]
        where = self.axes.index(axis)
        run = self.rows << (len(self.axes) - 1 - where)
        return axis, [(2 * p * run, (2 * p + 1) * run, p * run) for p in range(1 << where)], run

    def plan(self, take_in, give):
        axis, runs, length = self.halves()
        keep, recv = take_in(self.keep), take_in(self.recv.array)
        total = len(runs) * length
        held = give(fixed((total, self.keep.shape[1]), BF))
        place = give.send(axis, total, self)
        first = self.recv.start
        slot = Y if axis == "y" else BITS + axis - 1

        def kernel(s_ref, ins, outs, sends):
            bit = s_ref[slot]
            dst, base = sends(place)
            for low, high, to in runs:
                for side, ref, at in ((bit, outs[held], to), (1 - bit, dst, base + to)):
                    start = low + side * (high - low)
                    a = ins[keep][pl.ds(pl.multiple_of(start, 8), length)]
                    b = ins[recv][pl.ds(pl.multiple_of(first + start, 8), length)]
                    ref[at:at + length] = (a.astype(F32) + b.astype(F32)).astype(BF)

        def done(outs):
            self.keep = outs[held]
            self.axes.remove(axis)
            self.order.pop(0)

        return kernel, done


def cut_rows(rows, flows):
    if flows == 1:
        return (0, rows)
    unit = 16 if rows >= 96 else 8
    third = -(-rows // (3 * unit)) * unit
    return (0, third, 2 * third, rows)


class Source:
    def __init__(self, links, keep, send, axes, orders):
        self.axes, self.orders = axes, orders
        self.blocks = math.prod(keep.shape[:2])
        self.rows, self.cols = math.prod(keep.shape[2:4]), keep.shape[4]
        self.keep = keep.reshape(-1, self.cols)
        self.recv = links.swap(send, 0).reshape(-1, self.cols)
        self.cuts = cut_rows(self.rows, len(orders))

    def plan(self, take_in, give):
        keep, recv = take_in(self.keep), take_in(self.recv)
        rows, moves, self.flows = self.rows, [], []
        for c, order in enumerate(self.orders):
            lo, size = self.cuts[c], self.cuts[c + 1] - self.cuts[c]
            flow = Flow(self.axes, order, size)
            axis = order[0]
            where = self.axes.index(axis)
            post = 1 << (len(self.axes) - 1 - where)
            total = self.blocks // 2 * size
            held = give(fixed((total, self.cols), BF))
            moves.append((axis, where, post, lo, size, held, give.send(axis, total, flow)))
            self.flows.append(flow)

        def kernel(s_ref, ins, outs, sends):
            for axis, where, post, lo, size, held, place in moves:
                bit = s_ref[Y if axis == "y" else BITS + axis - 1]
                dst, base = sends(place)
                for p in range(1 << where):
                    for q in range(post):
                        to = (p * post + q) * size
                        for side, ref, at in ((bit, outs[held], to), (1 - bit, dst, base + to)):
                            start = ((2 * p + side) * post + q) * rows + lo
                            rng = pl.ds(pl.multiple_of(start, 8), size)
                            total = ins[keep][rng].astype(F32) + ins[recv][rng].astype(F32)
                            ref[at:at + size] = total.astype(BF)

        def done(outs):
            for flow, move in zip(self.flows, moves):
                flow.keep = outs[move[5]]
                flow.axes.remove(move[0])
                flow.order.pop(0)

        return kernel, done


class Join:
    def __init__(self, top, low, high):
        self.top, self.low, self.high = top, low, high
        self.rows = low.rows

    def plan(self, take_in, give):
        low, high = self.low, self.high
        refs = [take_in(low.keep), take_in(low.recv.array), take_in(high.keep),
                take_in(high.recv.array)]
        held = give(fixed(low.keep.shape, BF))
        place = give.send(self.top, self.rows, self)
        slot = BITS + self.top - 1
        rows = self.rows

        def kernel(s_ref, ins, outs, sends):
            dst, base = sends(place)
            part = lambda n, flow: (ins[refs[n]][...].astype(F32) + ins[refs[n + 1]][
                flow.recv.start:flow.recv.start + rows].astype(F32))
            a, b = part(0, low), part(2, high)
            upper = s_ref[slot] == 1
            outs[held][...] = jnp.where(upper, b, a).astype(BF)
            dst[base:base + rows] = jnp.where(upper, a, b).astype(BF)

        def done(outs):
            self.keep = outs[held]

        return kernel, done


class Small:
    def __init__(self, links, value, order):
        self.keep, self.order = value, list(order)
        self.recv = Part(links.swap(value, 0), 0)

    def plan(self, take_in, give):
        a, b = take_in(self.keep), take_in(self.recv.array)
        first, wide = self.recv.start, self.recv.array.dtype == F32
        rows, cols = self.keep.shape
        half = cols // 2
        total = give(fixed(self.keep.shape, F32))
        place = give.send(self.order.pop(0), 4 * rows, self) if self.order else None

        def kernel(s_ref, ins, outs, sends):
            if wide:
                came = ins[b][...]
            else:
                part = lambda n: ins[b][first + n:first + n + 2 * rows].astype(F32)
                both = part(0) + part(2 * rows)
                came = jnp.concatenate([both[:rows], both[rows:]], axis=1)
            added = ins[a][...] + came
            outs[total][...] = added
            if place is not None:
                dst, base = sends(place)
                stacked = jnp.concatenate([added[:, :half], added[:, half:]], axis=0)
                high = stacked.astype(BF)
                dst[base:base + 2 * rows] = high
                dst[base + 2 * rows:base + 4 * rows] = (stacked - high.astype(F32)).astype(BF)

        def done(outs):
            self.keep = outs[total]
            if place is None:
                self.recv = None

        return kernel, done


class Finish:
    def __init__(self, flows, shapes, write):
        self.flows, self.shapes, self.write = flows, shapes, write

    def plan(self, take_in, give):
        refs = [(take_in(f.keep), take_in(f.recv.array), f.recv.start, f.rows) for f in self.flows]
        results = [give(fixed(shape, F32)) for shape in self.shapes]

        def kernel(s_ref, ins, outs, sends):
            rows = jnp.concatenate(
                [ins[k][...].astype(F32) + ins[r][first:first + n].astype(F32)
                 for k, r, first, n in refs], axis=0)
            self.write(rows, *[outs[n] for n in results])

        def done(outs):
            self.result = [outs[n] for n in results]

        return kernel, done


class Carry:
    def __init__(self, *values):
        self.values = values

    def plan(self, take_in, give):
        anywhere = pl.BlockSpec(memory_space=pltpu.HBM)
        at = []
        for v in self.values:
            n = give((jax.ShapeDtypeStruct(v.shape, v.dtype), anywhere))
            give.aliases[take_in(v, anywhere)] = n
            at.append(n)

        def done(outs):
            self.values = [outs[n] for n in at]

        return lambda *refs: None, done


class Gives:
    def __init__(self):
        self.outs, self.sizes, self.takers, self.aliases = [], {}, [], {}

    def __call__(self, spec):
        self.outs.append(spec)
        return len(self.outs) - 1

    def send(self, axis, rows, taker):
        start = self.sizes.get(axis, 0)
        self.sizes[axis] = start + rows
        self.takers.append((axis, start, taker))
        return axis, start


def advance(run, links, *items):
    args, ins, index = [], [], {}

    def take_in(array, spec=None):
        if id(array) not in index:
            index[id(array)] = len(args)
            args.append(array)
            ins.append(spec or whole(array.shape))
        return index[id(array)]

    give = Gives()
    plans = [item.plan(take_in, give) for item in items]
    n_out = len(give.outs)
    axes = sorted(give.sizes, key=lambda a: 0 if a == "y" else a)
    outs = give.outs + [fixed((give.sizes[a], args[0].shape[-1]), BF) for a in axes]

    def kernel(s_ref, *refs):
        in_refs, out_refs = refs[:len(args)], refs[len(args):]
        sends = lambda place: (out_refs[n_out + axes.index(place[0])], place[1])
        for part, _ in plans:
            part(s_ref, in_refs, out_refs, sends)

    done = run(kernel, "add", (1,), ins, outs, [], args, 0,
               {1 + a: b for a, b in give.aliases.items()})
    came = {a: links.swap(done[n_out + n], a) for n, a in enumerate(axes)}
    for axis, start, taker in give.takers:
        taker.recv = Part(came[axis], start)
    for _, take in plans:
        take(done)


class Deal:
    def __init__(self, links, pairs, axes, orders, cuts):
        self.links, self.axes, self.orders, self.cuts = links, axes, orders, cuts
        self.keeps = [k for k, _ in pairs]
        self.sends = [x for _, x in pairs]
        self.rows, self.cols = self.keeps[0].shape[-2:]

    def start(self, sends):
        self.recvs = [self.links.swap(x, 0) for x in sends]

    def spans(self, c):
        lo, hi = self.cuts[c], self.cuts[c + 1]
        for n in range(2):
            a, b = max(lo - n * self.rows, 0), min(hi - n * self.rows, self.rows)
            if a < b:
                yield n, a, b

    def add(self, run, steps):
        n = len(self.axes)
        lead = (2,) * n
        rows, cols = self.rows, self.cols
        firsts = [self.axes.index(o[0]) for o in self.orders]
        others = [a for a in range(n) if a not in firsts]
        split = max(steps >> len(others), 1)
        width = cols // split
        count = 2 ** len(others) * split

        def at(i):
            places, rest = [0] * n, i // split
            for a in reversed(others):
                places[a] = rest % 2
                rest = rest // 2
            return places, i % split

        block = tuple(1 if a in others else 2 for a in range(n))

        def read(i, s):
            places, col = at(i)
            return (*places, 0, col)

        def write(first):
            def index(i, s):
                places, col = at(i)
                return (*places[:first], *places[first + 1:], 0, col)
            return index

        args = [a.reshape(lead + (rows, cols)) for a in self.keeps + self.recvs]
        ins = [pl.BlockSpec(block + (rows, width), read)] * 4
        outs, slots = [], []
        for c, first in enumerate(firsts):
            size = self.cuts[c + 1] - self.cuts[c]
            shape = lead[1:] + (size, cols)
            less = block[:first] + block[first + 1:]
            outs += [out(shape, BF, less + (size, width), write(first))] * 2
            axis = self.axes[first]
            slots.append(Y if axis == "y" else BITS + axis - 1)

        def kernel(s_ref, *refs):
            held, sent = refs[4::2], refs[5::2]

            for c, first in enumerate(firsts):
                bit = s_ref[slots[c]]
                row = 0
                for m, a, b in self.spans(c):
                    keep, recv = refs[m], refs[2 + m]
                    for dst, side in ((held[c], bit), (sent[c], 1 - bit)):
                        pick = tuple(side if d == first else slice(None) for d in range(n))
                        pick += (slice(a, b), slice(None))
                        total = keep[pick].astype(F32) + recv[pick].astype(F32)
                        to = (slice(None),) * (n - 1) + (slice(row, row + b - a),)
                        dst[to] = total.astype(BF)
                    row += b - a

        def take(*done):
            self.chains = []
            for c, order in enumerate(self.orders):
                axes = [a for a in self.axes if a != order[0]]
                recv = self.links.swap(done[2 * c + 1], order[0])
                size = self.cuts[c + 1] - self.cuts[c]
                flow = Flow(axes, order[1:], size)
                flow.keep, flow.recv = done[2 * c].reshape(-1, self.cols), Part(
                    recv.reshape(-1, self.cols), 0)
                self.chains.append(flow)

        done = run(kernel, "deal", (count,), ins, outs, [], args, 0)
        take(*done)


def angle_parts(rows, width):
    fine = 32
    frequency = jnp.exp(
        jnp.arange(0, width, 2).astype(F32) * (-math.log(10000.0) / width))
    coarse = (fine * (rows // fine - 1 - jnp.arange(rows // fine))).astype(F32)
    near = (fine - 1 - jnp.arange(fine)).astype(F32)
    a, b = coarse[:, None] * frequency[None, :], near[:, None] * frequency[None, :]
    return (jnp.sin(a), jnp.cos(a), jnp.sin(b), jnp.cos(b))


def body(tokens, memory, compressed, cotangent, seg_len, mem_fill, cmem_fill, w_qkv, w_rel, w_out,
         w_up, w_down, w_comp, norm_gain1, norm_gain2, bias_content, bias_position, bias_up):
    streams = tokens.shape[0]
    assert streams == 1
    links = Links()
    n_dp, top = links.n_dp, links.top
    seg, width = tokens.shape[1:]
    mem, comp = memory.shape[1], compressed.shape[1]
    start = comp + mem
    keys = start + seg
    squeezed_rows = mem // 3
    scale = (width // H) ** (-0.5)
    current, recent, distant = tokens[0], memory[0], compressed[0]
    seg_length = seg_len[0]
    core, x, z = links.bit(0), links.bit(1), links.bit(2)
    run = Steps(jnp.stack(
        [links.y, core, seg_length, mem_fill[0], cmem_fill[0], core * 2 + z,
         core * 2 + x] + [links.bit(n) for n in range(1, top + 1)]).astype(jnp.int32))
    gain1, gain2 = norm_gain1.reshape(1, -1), norm_gain2.reshape(1, -1)

    swap = links.swap
    near_parts = lambda value: (value, swap(value, 0))
    p_rel, p_a, p_b = pack_first(run, w_qkv, w_rel)
    rel, a, b = swap(p_rel, "y"), swap(p_a, "y"), swap(p_b, "y")
    normed = norm_hidden(run, distant, recent, current, gain1)
    rel_far = swap(rel, 2)
    p_c, p_d, p_up, p_down = pack_rest(run, w_out, w_up, w_down, w_comp)
    c, d = swap(p_c, "y"), swap(p_d, "y")
    table, groups = constants(run, recent, angle_parts(keys, width), squeezed_rows)
    rel, = order(run, (rel, rel_far, 2))
    rel_parts = near_parts(rel)
    a_far, b_far = swap(a, 2), swap(b, 1)
    pos = project_position(run, table, w_rel, rel_parts)
    a, b = order(run, (a, a_far, 2), (b, b_far, 1))
    a_parts, b_parts = near_parts(a), near_parts(b)
    p_up, p_down = follow(run, p_up, p_down)
    up, down = swap(p_up, "y"), swap(p_down, "y")
    kv, qc, qp, probe, w_full = project_qkv(
        run, normed, w_qkv, a_parts, b_parts, bias_content, bias_position, seg, scale)
    c, d = follow(run, c, d)
    c_far, d_far = swap(c, 2), swap(d, 1)
    p0, m0 = attention(run, qc, qp, kv, pos, comp, mem, 0)
    c, d = order(run, (c, c_far, 2), (d, d_far, 1))
    c_parts, d_parts = near_parts(c), near_parts(d)
    p1, m1 = attention(run, qc, qp, kv, pos, comp, mem, 1)
    up, down = follow(run, up, down)
    up_far, down_far = swap(up, 2), swap(down, 1)
    squeezed, squeezed_low, ck, cv = squeeze(run, groups, w_comp, c_parts, d_parts, w_full, gain1)
    gck, gcv = reconstruct(run, probe, kv, ck, cv, mem)
    up, down = order(run, (up, up_far, 2), (down, down_far, 1))
    up_parts, down_parts = near_parts(up), near_parts(down)
    comp_keep, comp_send = grad_comp(run, squeezed, gck, gcv, w_full, gain1, groups, n_dp)

    attended, second, w_out_full = mix_out(run, current, (m0, m1), w_out, d_parts, gain2)
    far = list(range(3, top + 1))
    names, under = ["y"] + list(range(top, 0, -1)), ["y"] + list(range(top - 1, 0, -1))
    turns = lambda rest: [[1, "y", 2] + rest, ["y", 2, 1] + rest, [2, 1, "y"] + rest]
    of_comp = Source(links, comp_keep, comp_send, names, [[2, 1, "y"] + far])
    advance(run, links, of_comp)
    (act, grad_attended, grad_mix, up_keep, up_send, down_keep, down_send, sum_bias, sum_gain2
     ) = feed_forward(run, second, cotangent[0], attended, w_up, up_parts, w_down, down_parts,
                      bias_up.reshape(1, -1), gain2, w_out_full, n_dp)
    inner = bias_up.shape[0]
    rows, half = inner // n_dp, width // 2
    flat = lambda a: a.reshape(2, n_dp // 2, rows, half)
    third = max(2 * rows * 11 // 32 // 16 * 16, 8)
    deal = Deal(
        links, [(flat(up_keep), flat(up_send)), (flat(down_keep), flat(down_send))], names,
        turns(far), (0, third, 2 * third, 2 * rows))
    carry = Carry(*deal.sends)
    advance(run, links, *of_comp.flows, carry)
    deal.start(carry.values)

    chunk = width // n_dp

    def write_ffn(rows, up, down):
        size = rows.shape[0] // 2
        up[...] = rows[:size].T
        for n in range(inner // (2 * half)):
            down[n * half:(n + 1) * half] = rows[size + n * chunk:size + (n + 1) * chunk].T

    def write_comp(rows, grad):
        for t in range(3):
            grad[t] = rows[t * chunk:(t + 1) * chunk].T

    def write_rest(rows, qkv, rel, ow):
        tap = lambda t: rows[t * chunk:(t + 1) * chunk].T
        qkv[0], qkv[1], qkv[2] = tap(2), tap(0), tap(1)
        rel[...], ow[...] = tap(3), tap(4)

    waiting = lambda *flows: [f for f in flows if f.order]
    back = functools.partial(attention_back, run, (p0, p1), grad_mix, qc, qp, kv, pos, start, scale)
    grads = lambda turned, gq, half: projection_grads(
        run, turned, gq, grad_attended, normed, table, (m0, m1), w_full, n_dp, half)
    gq0, gk0, gv0, gpos0, content0, position0 = back(0)
    advance(run, links, *of_comp.flows)
    deal.add(run, 4)
    keep_0, send_0, gain_0 = grads((gk0, gv0, gpos0), gq0, 0)
    gq1, gk1, gv1, gpos1, content1, position1 = back(1)
    carry = Carry(send_0)
    advance(run, links, *deal.chains, *of_comp.flows, carry)
    early = Source(links, keep_0, carry.values[0], under, turns(far[:-1]))
    keep_1, send_1, gain_1 = grads((gk1, gv1, gpos1), gq1, 1)
    carry = Carry(send_1)
    comp_end = Finish(of_comp.flows, [(3, half, chunk)], write_comp)
    comp_left = list(waiting(*of_comp.flows))
    held = [Carry(f.recv.array) for f in of_comp.flows if not comp_left]
    advance(run, links, *deal.chains, *comp_left, early, carry, *held)
    for flow, kept in zip(of_comp.flows, held):
        flow.recv = Part(kept.values[0], flow.recv.start)
    late = Source(links, keep_1, carry.values[0], under, turns(far[:-1]))
    row = lambda a, b: jnp.concatenate([a, b], axis=1)
    small = Small(links, jnp.concatenate(
        [(gain_0 + gain_1) / gain1, sum_gain2, row(content0, content1), row(position0, position1),
         sum_bias.reshape(-1, width)], axis=0), ["y", 1, 2] + far)
    new_memory = lax.dynamic_slice_in_dim(
        jnp.concatenate([recent, current], axis=0), seg_length, mem, 0)
    new_compressed = lax.dynamic_slice_in_dim(
        jnp.concatenate([distant, squeezed_low[:squeezed_rows]], axis=0), seg_length // 3, comp, 0)
    output = layer_output(run, act, attended, w_down, down_parts)
    advance(run, links, *waiting(*deal.chains, *comp_left), late, small)
    grad_rows = grad_tokens(run, (gk0, gk1), (gv0, gv1), (gq0, gq1), current, grad_attended,
                            w_full, gain1)
    while any(f.order for f in late.flows):
        advance(run, links, *waiting(*deal.chains, *comp_left, *early.flows, *late.flows),
                small)
        if not comp_left and comp_end.flows[0].recv is not None and not hasattr(comp_end, 'result'):
            advance(run, links, comp_end)
    ends = [Join(top, a, b) for a, b in zip(early.flows, late.flows)]
    of_ffn = Finish(deal.chains, [(half, rows), (inner // 2, chunk)], write_ffn)
    advance(run, links, *ends, small, of_ffn, *([comp_end] if comp_left else []))
    rest = Finish(ends, [(3, half, chunk), (half, chunk), (half, chunk)], write_rest)
    advance(run, links, rest, small)
    assert small.recv is None
    (grad_up, grad_down), (grad_comp_,) = of_ffn.result, comp_end.result
    grad_qkv, grad_rel, grad_out = rest.result

    at = links.dp * 2 + links.y
    each, each_up = width // (2 * n_dp), bias_up.shape[0] // (2 * n_dp)
    vec = lax.dynamic_slice(small.keep[:4], (0, at * each), (4, each))
    vec_up = lax.dynamic_slice_in_dim(small.keep[4:].reshape(-1), at * each_up, each_up)
    return (output[None], grad_rows[None], new_memory[None], new_compressed[None],
            grad_qkv, grad_rel, grad_out,
            grad_up, grad_down, grad_comp_, vec[0], vec[1], vec[2], vec[3], vec_up)


def solution(mesh):
    rows = P(("dp", "fsdp"), None, None)
    one = P(("dp", "fsdp"))
    return jax.shard_map(
        body,
        mesh=mesh,
        in_specs=(rows, rows, rows, rows, one, one, one, P(None, "fsdp", None), P("fsdp", None),
                  P("fsdp", None), P("fsdp", None), P("fsdp", None), P(None, "fsdp", None), P(),
                  P(), P(), P(), P()),
        out_specs=(rows, rows, rows, rows, P(None, "fsdp", "dp"), P("fsdp", "dp"),
                   P("fsdp", "dp"), P("fsdp", "dp"), P("fsdp", "dp"), P(None, "fsdp", "dp"), one,
                   one, one, one, one),
        check_vma=False,
    )
```

```python
import functools
import math

import jax
import jax.numpy as jnp
from jax import lax
from jax.experimental import pallas as pl
from jax.experimental.pallas import tpu as pltpu
from jax.sharding import PartitionSpec as P

H = 8
BF = jnp.bfloat16
F32 = jnp.float32
VMEM = 60 * 1024 * 1024
GELU_C = math.sqrt(2.0 / math.pi)
COST = 0.0001
TEMPORARIES = 36 * 1024 * 1024
Y, CORE, SEG_LEN, MEM_LIVE, COMP_LIVE, PIECE_A, PIECE_B, BITS = range(8)


def nn(a, b):
    return lax.dot_general(a, b, (((1,), (0,)), ((), ())), preferred_element_type=F32)


def nt(a, b):
    return lax.dot_general(a, b, (((1,), (1,)), ((), ())), preferred_element_type=F32)


def tn(a, b):
    return lax.dot_general(a, b, (((0,), (0,)), ((), ())), preferred_element_type=F32)


class Steps:
    def __init__(self, scal):
        self.scal = scal
        self.token = None

    def __call__(self, kernel, name, grid, ins, outs, scratch, args, flops, aliases={}):
        before = [] if self.token is None else [self.token]
        n_in, n_out, extra = len(ins), len(outs), len(before)

        def ordered_kernel(s_ref, *refs):
            rest = refs[n_in + extra:]
            kernel(s_ref, *refs[:n_in], *rest[:n_out], *rest[n_out + 1:])

        anywhere = pl.BlockSpec(memory_space=pltpu.HBM)
        moved = sum(a.size * a.dtype.itemsize for a in args)
        need = TEMPORARIES
        for (block, array) in list(zip(ins, args)) + [(b, s) for s, b in outs]:
            if block.block_shape is not None:
                need += 2 * math.prod(block.block_shape) * array.dtype.itemsize
        for ref in (r for r in scratch if 'sem' not in str(r.dtype)):
            need += math.prod(ref.shape) * jnp.dtype(ref.dtype).itemsize
        done = pl.pallas_call(
            ordered_kernel,
            name=name,
            out_shape=[s for s, _ in outs] + [jax.ShapeDtypeStruct((8, 128), F32)],
            grid_spec=pltpu.PrefetchScalarGridSpec(
                num_scalar_prefetch=1,
                grid=grid,
                in_specs=list(ins) + [anywhere] * extra,
                out_specs=[b for _, b in outs] + [anywhere],
                scratch_shapes=scratch,
            ),
            compiler_params=pltpu.CompilerParams(
                vmem_limit_bytes=min(need, VMEM), dimension_semantics=("arbitrary",) * len(grid)
            ),
            input_output_aliases=aliases,
            cost_estimate=pl.CostEstimate(
                flops=int(flops * COST), bytes_accessed=int(moved * COST), transcendentals=0),
        )(self.scal, *args, *before)
        *done, self.token = done
        return done


def follow(run, *values):
    anywhere = pl.BlockSpec(memory_space=pltpu.HBM)
    return run(
        lambda *refs: None, "follow", (1,), [anywhere] * len(values),
        [(jax.ShapeDtypeStruct(v.shape, v.dtype), anywhere) for v in values], [], values, 0,
        {n + 1: n for n in range(len(values))})


def whole(shape):
    return pl.BlockSpec(shape, lambda i, s: (0,) * len(shape))


def out(shape, dtype, block, index):
    return (jax.ShapeDtypeStruct(shape, dtype), pl.BlockSpec(block, index))


def fixed(shape, dtype):
    return out(shape, dtype, shape, lambda i, s: (0,) * len(shape))


def norm_rows(rows):
    centred = rows - jnp.mean(rows, axis=-1, keepdims=True)
    spread = jnp.mean(centred * centred, axis=-1, keepdims=True)
    scale = lax.rsqrt(spread + 1e-05)
    return centred * scale, scale


def norm_back(grad, gain, unit, scale):
    g = grad * gain
    inner = jnp.mean(g * unit, axis=-1, keepdims=True)
    return scale * (g - jnp.mean(g, axis=-1, keepdims=True) - unit * inner)


def place(dst, s_ref, own, mine, theirs, cols=slice(None)):
    half, quarter = own.shape[-2], mine.shape[-2]
    y, core = s_ref[Y], s_ref[CORE]
    base = (1 - y) * half
    at = lambda start, size: pl.ds(pl.multiple_of(start, quarter), size)
    dst[at(y * half, half), cols] = own[:, cols]
    dst[at(base + core * quarter, quarter), cols] = mine[...]
    dst[at(base + (1 - core) * quarter, quarter), cols] = theirs[...]


def pack_first_kernel(s_ref, rel, k, v, qa, qb, o_rel, o_a, o_b):
    width = rel.shape[-1]
    o_rel[...] = rel[...]
    o_a[0, :, :width] = k[0, 0]
    o_a[0, :, width:] = qa[0, 0]
    o_b[0, :, :width] = v[0, 0]
    o_b[0, :, width:] = qb[0, 0]


def pack_rest_kernel(s_ref, c0, c1, c2, ow, up, down, o_c, o_d, o_up, o_down):
    o_c[0] = c0[0, 0]
    o_c[1] = c1[0, 0]
    o_d[0] = c2[0, 0]
    o_d[1] = ow[0]
    o_up[...] = up[...]
    o_down[...] = down[...]


def quarters(a):
    lead = a.shape[:-2]
    return a.reshape(lead + (4, a.shape[-2] // 4, a.shape[-1]))


def part_of(a, where, n=0, cols=1, c=0):
    block = (1,) * (a.ndim - 2) + (a.shape[-2], a.shape[-1] // cols)
    if a.ndim == 3:
        return pl.BlockSpec(block, lambda i, s: (s[where], 0, c))
    return pl.BlockSpec(block, lambda i, s: (n, s[where], 0, c))


def pack_first(run, w_qkv, w_rel):
    qkv, rel = quarters(w_qkv), quarters(w_rel)
    part, width = rel.shape[1:]
    return run(
        pack_first_kernel, "pack_first", (1,),
        [part_of(rel, PIECE_A), part_of(qkv, PIECE_A, 1), part_of(qkv, PIECE_B, 2),
         part_of(qkv, PIECE_A, 0, 2, 0), part_of(qkv, PIECE_B, 0, 2, 1)],
        [fixed((1, part, width), BF), fixed((1, part, width * 3 // 2), BF),
         fixed((1, part, width * 3 // 2), BF)],
        [], (rel, qkv, qkv, qkv, qkv), 0)


def pack_rest(run, w_out, w_up, w_down, w_comp):
    comp, ow, up, down = quarters(w_comp), quarters(w_out), quarters(w_up), quarters(w_down)
    part, width = ow.shape[1:]
    return run(
        pack_rest_kernel, "pack_rest", (1,),
        [part_of(comp, PIECE_A, 0), part_of(comp, PIECE_A, 1), part_of(comp, PIECE_B, 2),
         part_of(ow, PIECE_B), part_of(up, PIECE_A), part_of(down, PIECE_B)],
        [fixed((2, part, width), BF), fixed((2, part, width), BF),
         fixed((1,) + up.shape[1:], BF), fixed((1,) + down.shape[1:], BF)],
        [], (comp, comp, comp, ow, up, down), 0)


def order_kernel(s_ref, *refs, slots):
    n = len(slots)
    outs, sem = refs[2 * n:3 * n], refs[3 * n]
    copies = []
    for c, slot in enumerate(slots):
        bit = s_ref[slot]
        copies += [
            pltpu.make_async_copy(refs[c], outs[c].at[:, bit], sem.at[2 * c]),
            pltpu.make_async_copy(refs[n + c], outs[c].at[:, 1 - bit], sem.at[2 * c + 1])]
    for copy in copies:
        copy.start()
    for copy in copies:
        copy.wait()


def order(run, *pieces):
    args = [p[0] for p in pieces] + [p[1] for p in pieces]
    shapes = [(p[0].shape[0], 2) + p[0].shape[1:] for p in pieces]
    anywhere = pl.BlockSpec(memory_space=pltpu.HBM)
    done = run(
        functools.partial(order_kernel, slots=tuple(BITS + p[2] - 1 for p in pieces)), "order", (1,),
        [anywhere] * len(args), [(jax.ShapeDtypeStruct(s, BF), anywhere) for s in shapes],
        [pltpu.SemaphoreType.DMA((len(args),))], args, 0)
    return [d.reshape(s[0], 2 * s[2], s[3]) for d, s in zip(done, shapes)]


def normed_kernel(s_ref, d_ref, m_ref, t_ref, g_ref, x_ref):
    i = pl.program_id(0)
    for n, ref in enumerate((d_ref, m_ref, t_ref)):
        @pl.when(i // 2 == n)
        def _(ref=ref):
            x_ref[...] = (norm_rows(ref[...].astype(F32))[0] * g_ref[...]).astype(BF)


def norm_hidden(run, distant, recent, current, gain):
    mem, width = recent.shape
    blk = mem // 2
    part = lambda n: pl.BlockSpec((blk, width), lambda i, s: (jnp.clip(i - 2 * n, 0, 1), 0))
    return run(
        normed_kernel, "norm_hidden", (6,),
        [part(0), part(1), part(2), whole(gain.shape)],
        [out((3 * mem, width), BF, (blk, width), lambda i, s: (i, 0))],
        [], (distant, recent, current, gain), 0)[0]


def constants_kernel(s_ref, m_ref, sa_ref, ca_ref, sb_ref, cb_ref, tab_ref, gr_ref, wide_ref,
                     *, groups):
    i = pl.program_id(0)
    blk, width = tab_ref.shape
    half = width // 2
    fine = sb_ref.shape[0]
    for n in range(blk // fine):
        rows = slice(n * fine, (n + 1) * fine)
        a = i * (blk // fine) + n
        sa, ca = sa_ref[pl.ds(a, 1)], ca_ref[pl.ds(a, 1)]
        tab_ref[rows, :half] = (sa * cb_ref[...] + ca * sb_ref[...]).astype(BF)
        tab_ref[rows, half:] = (ca * cb_ref[...] - sa * sb_ref[...]).astype(BF)

    @pl.when(i == 0)
    def _():
        mem = m_ref.shape[0]
        lanes = wide_ref.shape[2]
        count = gr_ref.shape[1]
        live = lax.broadcasted_iota(jnp.int32, (count, 1), 0) < groups
        for n in range(width // lanes):
            cols = slice(n * lanes, (n + 1) * lanes)
            wide_ref[n, :mem] = m_ref[:, cols].astype(F32)
            wide_ref[n, mem:] = jnp.zeros((wide_ref.shape[1] - mem, lanes), F32)
            for t in range(3):
                rows = jnp.where(live, wide_ref[n, pl.ds(t, count, stride=3)], 0.0)
                gr_ref[t, :, cols] = rows.astype(BF)


def constants(run, recent, angles, groups):
    mem, width = recent.shape
    keys = 3 * mem
    blk = 512
    padded = groups + (-groups) % 64
    ins = (recent,) + angles
    return run(
        functools.partial(constants_kernel, groups=groups), "constants", (keys // blk,),
        [whole(a.shape) for a in ins],
        [out((keys, width), BF, (blk, width), lambda i, s: (i, 0)),
         fixed((3, padded, width), BF)],
        [pltpu.VMEM((width // 128, 3 * padded, 128), F32)], ins, 0)


def qkv_kernel(s_ref, x_ref, o_ref, am_ref, at_ref, bm_ref, bt_ref, bc_ref, bp_ref, kv_ref,
               qc_ref, qp_ref, pr_ref, w_ref, *, scale):
    i = pl.program_id(0)
    rows, width = x_ref.shape
    seg = qc_ref.shape[0]
    blk = 256
    lo, hi = slice(0, width // 2), slice(width // 2, width)
    own, dst = o_ref.at[0], w_ref.at[0]

    @pl.when(i == 0)
    def _():
        place(dst, s_ref, own, am_ref.at[0, :, :width], at_ref.at[0, :, :width])

    @pl.when(i == 1)
    def _():
        place(dst, s_ref, own, bm_ref.at[0, :, :width], bt_ref.at[0, :, :width])

    @pl.when(i == 2)
    def _():
        place(dst, s_ref, own, am_ref.at[0, :, width:], at_ref.at[0, :, width:], lo)
        place(dst, s_ref, own, bm_ref.at[0, :, width:], bt_ref.at[0, :, width:], hi)

    @pl.when(i < 2)
    def _():
        def some(n):
            at = slice(n * blk, (n + 1) * blk)
            kv_ref[0, at] = nn(x_ref[at], dst[...]).astype(BF)

        for n in range(rows // blk):
            some(n)

    @pl.when(i == 2)
    def _():
        for n in range(seg // blk):
            at = slice(n * blk, (n + 1) * blk)
            q = nn(x_ref[rows - seg + n * blk:rows - seg + (n + 1) * blk], dst[...])
            qc_ref[at] = ((q + bc_ref[...]) * scale).astype(BF)
            qp_ref[at] = ((q + bp_ref[...]) * scale).astype(BF)
            pr_ref[at] = (q * scale).astype(BF)


def project_qkv(run, normed, w_qkv, a_parts, b_parts, bias_content, bias_position, seg, scale):
    rows, width = normed.shape
    turn = lambda i, s: ((i + 1) % 3, 0, 0)
    parts = a_parts + b_parts
    return run(
        functools.partial(qkv_kernel, scale=scale), "project_qkv", (3,),
        [whole((rows, width)), pl.BlockSpec((1, width // 2, width), turn)]
        + [whole(p.shape) for p in parts] + [whole((1, width)), whole((1, width))],
        [out((2, rows, width), BF, (1, rows, width), lambda i, s: (jnp.minimum(i, 1), 0, 0)),
         fixed((seg, width), BF), fixed((seg, width), BF), fixed((seg, width), BF),
         out((3, width, width), BF, (1, width, width), turn)],
        [], (normed, w_qkv) + parts + (bias_content.reshape(1, -1), bias_position.reshape(1, -1)),
        2 * (2 * rows + seg) * width * width)


def position_kernel(s_ref, x_ref, o_ref, m_ref, t_ref, p_ref, w_ref):
    @pl.when(pl.program_id(0) == 0)
    def _():
        place(w_ref, s_ref, o_ref, m_ref.at[0], t_ref.at[0])

    p_ref[...] = nn(x_ref[...], w_ref[...]).astype(BF)


def project_position(run, table, own, parts):
    rows, width = table.shape
    blk = 512
    return run(
        position_kernel, "project_position", (rows // blk,),
        [pl.BlockSpec((blk, width), lambda i, s: (i, 0)), whole(own.shape)]
        + [whole(p.shape) for p in parts],
        [out((rows, width), BF, (blk, width), lambda i, s: (i, 0))],
        [pltpu.VMEM((width, width), BF)], (table, own) + parts,
        2 * rows * width * width)[0]


RB = 256


def flip_matrix():
    return (lax.broadcasted_iota(jnp.int32, (RB, RB), 0)
            + lax.broadcasted_iota(jnp.int32, (RB, RB), 1) == RB - 1).astype(BF)


def attention_kernel(s_ref, qc_ref, qp_ref, k_ref, v_ref, pos_ref, p_ref, mix_ref, bias_ref,
                     *, comp, mem):
    seg, keys = qc_ref.shape[0], k_ref.shape[1]
    start = comp + mem

    @pl.when(pl.program_id(0) == 0)
    def _():
        mem_live, comp_live = s_ref[MEM_LIVE], s_ref[COMP_LIVE]
        col = lax.broadcasted_iota(jnp.int32, bias_ref.shape, 1)
        row = lax.broadcasted_iota(jnp.int32, bias_ref.shape, 0)
        live = ((col >= comp - comp_live) & (col < comp)) | (
            (col >= start - mem_live) & (col - start <= row))
        bias_ref[...] = jnp.where(live, 0.0, -1e30)

    flip = flip_matrix()
    for r in range(seg // RB):
        width = start + RB * (r + 1)
        rows = slice(r * RB, (r + 1) * RB)
        content = nt(qc_ref[rows], k_ref[0, :width])
        rel = nt(qp_ref[rows], pos_ref[keys - width:])
        rel = pltpu.roll(rel, width - RB + 1, 1, stride=1, stride_axis=0)
        masked = content + rel + bias_ref[rows, :width]
        top = jnp.max(masked, axis=-1, keepdims=True)
        weights = jnp.exp(masked - top)
        probs = (weights * (1.0 / jnp.sum(weights, axis=-1, keepdims=True))).astype(BF)
        mix_ref[rows] = nn(probs, v_ref[0, :width]).astype(BF)
        p_ref[0, rows, :width] = nn(flip, probs).astype(BF)


def attention(run, qc, qp, kv, pos, comp, mem, half):
    seg, width = qc.shape
    keys = kv.shape[1]
    dh = width // H
    n = H // 2
    first = half * n
    q_spec = pl.BlockSpec((seg, dh), lambda h, s: (0, h + first))
    of = lambda m: pl.BlockSpec((1, keys, dh), lambda h, s: (m, 0, h + first))
    return run(
        functools.partial(attention_kernel, comp=comp, mem=mem), "attention", (n,),
        [q_spec, q_spec, of(0), of(1), pl.BlockSpec((keys, dh), lambda h, s: (0, h + first))],
        [out((n, seg, keys), BF, (1, seg, keys), lambda h, s: (h, 0, 0)),
         out((seg, width // 2), BF, (seg, dh), lambda h, s: (0, h))],
        [pltpu.VMEM((seg, keys), F32)], (qc, qp, kv, kv, pos), 16 * seg * keys * width)


def attention_back_kernel(s_ref, p_ref, gm_ref, mix_ref, qc_ref, qp_ref, k_ref, v_ref, pos_ref, gq_ref,
                          gk_ref, gv_ref, gp_ref, gc_ref, gb_ref, gs_ref, sh_ref, pr_ref, rev_ref,
                          *, start, scale):
    seg, keys = qc_ref.shape[0], k_ref.shape[1]
    flip = flip_matrix()
    sum_c = jnp.zeros((1, gc_ref.shape[1]), F32)
    sum_p = jnp.zeros((1, gc_ref.shape[1]), F32)
    for r in range(seg // RB):
        width = start + RB * (r + 1)
        rows = slice(r * RB, (r + 1) * RB)
        for n, ref in enumerate((gm_ref, qc_ref, qp_ref, mix_ref)):
            rev_ref[n, rows] = nn(flip, ref[rows]).astype(BF)
        low = p_ref[0, rows, :width]
        probs = low.astype(F32)
        total = jnp.sum(
            rev_ref[0, rows].astype(F32) * rev_ref[3, rows].astype(F32), axis=-1, keepdims=True)
        scores = probs * (nt(rev_ref[0, rows], v_ref[0, :width]) - total)
        low_scores = scores.astype(BF)
        moved = pltpu.roll(scores, 0, 1, stride=1, stride_axis=0).astype(BF)
        gs_ref[rows, :width] = low_scores
        sh_ref[rows, keys - width:] = moved
        pr_ref[rows, :width] = low
        if width < keys:
            gs_ref[rows, width:] = jnp.zeros((RB, keys - width), BF)
            pr_ref[rows, width:] = jnp.zeros((RB, keys - width), BF)
            sh_ref[rows, : keys - width] = jnp.zeros((RB, keys - width), BF)
        grad_c = nn(low_scores, k_ref[0, :width])
        grad_p = nn(moved, pos_ref[keys - width:])
        sum_c += jnp.sum(grad_c, axis=0, keepdims=True)
        sum_p += jnp.sum(grad_p, axis=0, keepdims=True)
        gq_ref[rows] = nn(flip, ((grad_c + grad_p) * scale).astype(BF)).astype(BF)
    gc_ref[...] = sum_c * scale
    gb_ref[...] = sum_p * scale
    gv_ref[...] = tn(rev_ref[0], pr_ref[...]).astype(BF)
    gk_ref[...] = tn(rev_ref[1], gs_ref[...]).astype(BF)
    gp_ref[...] = tn(rev_ref[2], sh_ref[...]).astype(BF)


def attention_back(run, probs, mixed, gm, qc, qp, kv, pos, start, scale, half):
    seg, width = qc.shape
    keys = kv.shape[1]
    dh = width // H
    n = H // 2
    first = half * n
    q_spec = pl.BlockSpec((seg, dh), lambda h, s: (0, h + first))
    of = lambda m: pl.BlockSpec((1, keys, dh), lambda h, s: (m, 0, h + first))
    turned = lambda: out((width // 2, keys), BF, (dh, keys), lambda h, s: (h, 0))
    sums = lambda: out((1, width // 2), F32, (1, dh), lambda h, s: (0, h))
    big = pltpu.VMEM((seg, keys), BF)
    return run(
        functools.partial(attention_back_kernel, start=start, scale=scale), "attention_back", (n,),
        [pl.BlockSpec((1, seg, keys), lambda h, s: (h, 0, 0)), q_spec,
         pl.BlockSpec((seg, dh), lambda h, s: (0, h)), q_spec, q_spec,
         of(0), of(1), pl.BlockSpec((keys, dh), lambda h, s: (0, h + first))],
        [out((seg, width // 2), BF, (seg, dh), lambda h, s: (0, h)), turned(), turned(), turned(),
         sums(), sums()],
        [big, big, big, pltpu.VMEM((4, seg, dh), BF)], (probs[half], gm, mixed[half], qc, qp, kv, kv, pos),
        12 * seg * keys * width)


def mixed_kernel(s_ref, tok_ref, a_ref, b_ref, o_ref, m_ref, t_ref, g_ref, att_ref, sec_ref, w_ref):
    @pl.when(pl.program_id(0) == 0)
    def _():
        place(w_ref, s_ref, o_ref, m_ref.at[1], t_ref.at[1])

    mid = a_ref.shape[1]
    attended = (tok_ref[...].astype(F32) + nn(a_ref[...], w_ref[:mid])
                + nn(b_ref[...], w_ref[mid:]))
    att_ref[...] = attended
    sec_ref[...] = (norm_rows(attended)[0] * g_ref[...]).astype(BF)


def mix_out(run, tokens, mixed, own, parts, gain):
    seg, width = tokens.shape
    blk = 256
    row = pl.BlockSpec((blk, width), lambda i, s: (i, 0))
    side = pl.BlockSpec((blk, width // 2), lambda i, s: (i, 0))
    return run(
        mixed_kernel, "mix_out", (seg // blk,),
        [row, side, side, whole(own.shape)] + [whole(p.shape) for p in parts] + [whole((1, width))],
        [out((seg, width), F32, (blk, width), lambda i, s: (i, 0)),
         out((seg, width), BF, (blk, width), lambda i, s: (i, 0)),
         fixed((width, width), BF)],
        [], (tokens,) + mixed + (own,) + parts + (gain,), 2 * seg * width * width)


def part_shape(rows, cols, n_dp, taps, cut=1):
    return (2, n_dp // (2 * cut), taps, rows // n_dp, cols // 2)


def low_or_wide(chunk):
    return BF if chunk % 16 == 0 else F32


def by_core(buf, values, core):
    pairs, _, chunk, cols = buf.shape
    buf[...] = values.astype(buf.dtype).reshape(pairs, 2, chunk, cols)
    pick = lambda c: buf[:, c].reshape(pairs * chunk, cols)
    return jnp.concatenate([pick(core), pick(1 - core)], axis=0).astype(BF)


def put(keep, send, values):
    half = values.shape[0] // 2
    shape = keep.shape[:-1] + (values.shape[1],)
    keep[...] = values[:half].reshape(shape).astype(BF)
    send[...] = values[half:].reshape(shape).astype(BF)


def ffn_kernel(s_ref, sec_ref, cot_ref, att_ref, uo_ref, um_ref, ut_ref, do_ref, dm_ref, dt_ref,
               b_ref, g_ref, wo_ref, act_ref, gatt_ref, gm_ref, uk_ref, us_ref, dk_ref, ds_ref,
               gb_ref, gg_ref, gout_ref, turn_ref, wu_ref, wd_ref, gsec_ref, ubuf, dbuf):
    i, n = pl.program_id(0), pl.num_programs(0)
    y, core = s_ref[Y], s_ref[CORE]

    @pl.when(i == 0)
    def _():
        row = lax.broadcasted_iota(jnp.int32, cot_ref.shape, 0)
        live = jnp.where(row < s_ref[SEG_LEN], cot_ref[...], jnp.zeros((), BF))
        gout_ref[...] = live
        turn_ref[...] = by_core(dbuf, live.T, core)
        gsec_ref[...] = jnp.zeros_like(gsec_ref)

    place(wu_ref, s_ref, uo_ref, um_ref.at[0], ut_ref.at[0])
    half = i // (n // 2)
    side = (i % (n // 2)) // (n // 4)

    @pl.when(half == y)
    def _():
        wd_ref[...] = do_ref[...]

    @pl.when((half != y) & (side == core))
    def _():
        wd_ref[...] = dm_ref[0]

    @pl.when((half != y) & (side != core))
    def _():
        wd_ref[...] = dt_ref[0]

    second, gout = sec_ref[...], gout_ref[...]
    v = nn(second, wu_ref[...]) + b_ref[...]
    square = v * v
    gate = 0.5 + 0.5 * jnp.tanh(v * (GELU_C + (GELU_C * 0.044715) * square))
    act = (v * gate).astype(BF)
    slope = gate + (gate - gate * gate) * v * (2 * GELU_C + (6 * GELU_C * 0.044715) * square)
    act_ref[...] = act
    grad_inner = nt(gout, wd_ref[...]) * slope
    low = grad_inner.astype(BF)
    gb_ref[...] = jnp.sum(low.astype(F32), axis=0, keepdims=True)
    gsec_ref[...] += nt(low, wu_ref[...])
    put(dk_ref.at[0, :, 0], ds_ref.at[0, :, 0], nn(turn_ref[...], act))
    part = nn(by_core(ubuf, low.T, core), second)
    width = part.shape[1] // 2
    for side in range(2):
        put(uk_ref.at[side, :, 0], us_ref.at[side, :, 0], part[:, side * width:(side + 1) * width])

    @pl.when(i == n - 1)
    def _():
        unit, scale = norm_rows(att_ref[...])
        grad = gsec_ref[...]
        gg_ref[...] = jnp.sum(grad * unit, axis=0, keepdims=True)
        gatt = norm_back(grad, g_ref[...], unit, scale) + gout_ref[...].astype(F32)
        gatt_ref[...] = gatt
        gm_ref[...] = nt(gatt.astype(BF), wo_ref[...]).astype(BF)


def down_rows(n, blk, width):
    def own(i, s):
        return (jnp.clip(i - s[Y] * (n // 2), 0, n // 2 - 1), 0)

    def part(other):
        def index(i, s):
            side = s[CORE] if other == 0 else 1 - s[CORE]
            first = (1 - s[Y]) * (n // 2) + side * (n // 4)
            return (0, jnp.clip(i - first, 0, n // 4 - 1), 0)

        return pl.BlockSpec((1, blk, width), index)

    return pl.BlockSpec((blk, width), own), part(0), part(1)


def output_kernel(s_ref, act_ref, att_ref, do_ref, dm_ref, dt_ref, out_ref, acc_ref):
    i, n = pl.program_id(0), pl.num_programs(0)
    half, side = i // (n // 2), (i % (n // 2)) // (n // 4)
    y, core = s_ref[Y], s_ref[CORE]

    @pl.when(i == 0)
    def _():
        acc_ref[...] = att_ref[...]

    @pl.when(half == y)
    def _():
        acc_ref[...] += nn(act_ref[...], do_ref[...])

    @pl.when((half != y) & (side == core))
    def _():
        acc_ref[...] += nn(act_ref[...], dm_ref[0])

    @pl.when((half != y) & (side != core))
    def _():
        acc_ref[...] += nn(act_ref[...], dt_ref[0])

    @pl.when(i == n - 1)
    def _():
        out_ref[...] = acc_ref[...].astype(BF)


def layer_output(run, act, attended, w_down, down_parts):
    seg, inner = act.shape
    width = attended.shape[1]
    n = 4
    blk = inner // n
    dm, dt = down_parts
    return run(
        output_kernel, "output", (n,),
        [pl.BlockSpec((seg, blk), lambda i, s: (0, i)), whole((seg, width)),
         *down_rows(n, blk, width)],
        [fixed((seg, width), BF)], [pltpu.VMEM((seg, width), F32)],
        (act, attended, w_down, dm, dt), 2 * seg * width * inner)[0]


def feed_forward(run, second, cotangent, attended, w_up, up_parts, w_down, down_parts, bias_up,
                 gain, w_out, n_dp):
    seg, width = second.shape
    inner = bias_up.shape[1]
    n = 8
    blk = inner // n
    um, ut = up_parts
    dm, dt = down_parts
    uch, dch = inner // n_dp, width // n_dp
    pairs = blk // (2 * uch)
    col = lambda a: pl.BlockSpec((a.shape[0], blk), lambda i, s: (0, i))
    col3 = lambda a: pl.BlockSpec((1, a.shape[1], blk), lambda i, s: (0, 0, i))

    up_shape = part_shape(inner, width, n_dp, 1)
    down_shape = part_shape(width, inner, n_dp, n // 2)[:-1] + (blk,)
    up_out = lambda: out(up_shape, BF, (2, pairs, 1, uch, width // 2),
                         lambda i, s: (0, i, 0, 0, 0))
    down_out = lambda: out(down_shape, BF, (1, n_dp // 2, 1, dch, blk),
                           lambda i, s: (i // (n // 2), 0, i % (n // 2), 0, 0))
    full = (seg, width)
    return run(
        ffn_kernel, "feed_forward", (n,),
        [whole(full), whole(full), whole(full), col(w_up), col3(um), col3(ut),
         *down_rows(n, blk, width),
         pl.BlockSpec((1, blk), lambda i, s: (0, i)), whole((1, width)), whole((width, width))],
        [out((seg, inner), BF, (seg, blk), lambda i, s: (0, i)), fixed(full, F32),
         fixed(full, BF), up_out(), up_out(), down_out(),
         down_out(), out((1, inner), F32, (1, blk), lambda i, s: (0, i)), fixed((1, width), F32)],
        [pltpu.VMEM(full, BF), pltpu.VMEM((width, seg), BF), pltpu.VMEM((width, blk), BF),
         pltpu.VMEM((blk, width), BF), pltpu.VMEM(full, F32),
         pltpu.VMEM((pairs, 2, uch, seg), low_or_wide(uch)),
         pltpu.VMEM((n_dp // 2, 2, dch, seg), low_or_wide(dch))],
        (second, cotangent, attended, w_up, um, ut, w_down, dm, dt, bias_up, gain, w_out),
        12 * seg * width * inner)


def grads_kernel(s_ref, gk_ref, gv_ref, gp_ref, gq_ref, ga_ref, x_ref, tab_ref, ma_ref, mb_ref, w_ref,
                 keep_ref, send_ref, gg_ref, k_s, v_s, p_s, q_s, o_s, big, small):
    core = s_ref[CORE]
    rows = x_ref.shape[0]
    seg = gq_ref.shape[0]

    @pl.when(pl.program_id(0) == 0)
    def _():
        k_s[...] = by_core(big, gk_ref[...], core)
        v_s[...] = by_core(big, gv_ref[...], core)
        p_s[...] = by_core(big, gp_ref[...], core)
        q_s[...] = by_core(small, gq_ref[...].T, core)
        o_s[...] = by_core(small, ga_ref[...].astype(BF).T, core)

    x = x_ref[...]
    pairs, _, chunk, _ = small.shape
    n = pairs * chunk

    def both(tap, values):
        put(keep_ref.at[0, :, tap], send_ref.at[0, :, tap], values)

    def gain(values, m):
        turned = w_ref[m].T.astype(F32)
        whole_ = turned.reshape(pairs, 2, chunk, turned.shape[1])
        even, odd = whole_[:, 0].reshape(n, -1), whole_[:, 1].reshape(n, -1)
        first = jnp.where(core == 0, even, odd)
        last = jnp.where(core == 0, odd, even)
        return (jnp.sum(values[:n] * first, axis=0, keepdims=True)
                + jnp.sum(values[n:] * last, axis=0, keepdims=True))

    part = nn(k_s[...], x)
    both(0, part)
    total = gain(part, 1)
    part = nn(v_s[...], x)
    both(1, part)
    total += gain(part, 2)
    part = nn(q_s[...], x[rows - seg:])
    both(2, part)
    total += gain(part, 0)
    both(3, nn(p_s[...], tab_ref[...]))
    gg_ref[...] = total
    i, n = pl.program_id(0), pl.num_programs(0)

    @pl.when(i < n // 2)
    def _():
        both(4, nn(o_s[...], ma_ref[...]))

    @pl.when(i >= n // 2)
    def _():
        both(4, nn(o_s[...], mb_ref[...]))


def projection_grads(run, turned, gq, gatt, normed, table, mixed, w, n_dp, half):
    rows, width = normed.shape
    seg = gq.shape[0]
    blk = 256
    chunk = width // n_dp
    mid = width // 2
    gk, gv, gpos = turned
    count = mid // blk
    col = lambda r: pl.BlockSpec((r, blk), lambda i, s: (0, i))
    shape = lambda taps: part_shape(width, width, n_dp, taps, 2)
    half_of = lambda taps: out(shape(taps), BF, (1,) + shape(taps)[1:4] + (blk,),
                               lambda i, s: (i // count, 0, 0, 0, i % count))
    side = pl.BlockSpec((seg, blk), lambda i, s: (0, i % count))
    kind = low_or_wide(chunk)
    pairs = mid // (2 * chunk)
    return run(
        grads_kernel, "projection_grads", (width // blk,),
        [whole(gk.shape), whole(gk.shape), whole(gk.shape), whole(gq.shape),
         pl.BlockSpec((seg, mid), lambda i, s: (0, half)), col(rows), col(rows), side, side,
         pl.BlockSpec((3, blk, mid), lambda i, s: (0, i, half))],
        [half_of(5), half_of(5),
         out((1, width), F32, (1, blk), lambda i, s: (0, i))],
        [pltpu.VMEM((mid, rows), BF)] * 3 + [pltpu.VMEM((mid, seg), BF)] * 2
        + [pltpu.VMEM((pairs, 2, chunk, rows), kind), pltpu.VMEM((pairs, 2, chunk, seg), kind)],
        (gk, gv, gpos, gq, gatt, normed, table) + mixed + (w,),
        (3 * rows + 2 * seg) * width * width)


def grad_tokens_kernel(s_ref, ka_ref, kb_ref, va_ref, vb_ref, qa_ref, qb_ref, tok_ref, ga_ref,
                       w_ref, g_ref, gt_ref, acc_ref):
    i = pl.program_id(0)
    mid = w_ref.shape[2] // 2
    left, right = w_ref[0, :, :mid], w_ref[0, :, mid:]

    @pl.when(i == 0)
    def _():
        acc_ref[...] = nn(left, ka_ref[...]) + nn(right, kb_ref[...])

    @pl.when(i == 1)
    def _():
        acc_ref[...] += nn(left, va_ref[...]) + nn(right, vb_ref[...])

    @pl.when(i == 2)
    def _():
        total = (acc_ref[...] + nt(left, qa_ref[...]) + nt(right, qb_ref[...])).T
        unit, scale = norm_rows(tok_ref[...].astype(F32))
        gt_ref[...] = (ga_ref[...] + norm_back(total, g_ref[...], unit, scale)).astype(BF)


def grad_tokens(run, gk, gv, gq, tokens, grad_attended, w, gain):
    seg, width = tokens.shape
    rows = gk[0].shape[1]
    late = pl.BlockSpec((width // 2, seg), lambda i, s: (0, rows // seg - 1))
    side = whole((seg, width // 2))
    return run(
        grad_tokens_kernel, "grad_tokens", (3,),
        [late] * 4 + [side] * 2 + [whole((seg, width)), whole((seg, width)),
         pl.BlockSpec((1, width, width), lambda i, s: ((i + 1) % 3, 0, 0)), whole((1, width))],
        [fixed((seg, width), BF)], [pltpu.VMEM((width, seg), F32)],
        tuple(gk) + tuple(gv) + tuple(gq) + (tokens, grad_attended, w, gain),
        6 * seg * width * width)[0]


def squeeze_kernel(s_ref, gr_ref, o_ref, am_ref, at_ref, bm_ref, bt_ref, wk_ref, wv_ref, g_ref,
                   sq_ref, low_ref, k_ref, v_ref):
    y, core = s_ref[Y], s_ref[CORE]
    half, quarter = o_ref.shape[1], am_ref.shape[1]
    base = (1 - y) * half
    total = jnp.zeros(sq_ref.shape, F32)
    for t in range(3):
        m_ref, t_ref, n = (am_ref, at_ref, t) if t < 2 else (bm_ref, bt_ref, 0)
        at = lambda off, size: gr_ref[t, :, pl.ds(pl.multiple_of(off, quarter), size)]
        total += nn(at(y * half, half), o_ref[t])
        total += nn(at(base + core * quarter, quarter), m_ref[n])
        total += nn(at(base + (1 - core) * quarter, quarter), t_ref[n])
    sq_ref[...] = total
    low_ref[...] = total.astype(BF)
    unit = (norm_rows(total)[0] * g_ref[...]).astype(BF)
    k_ref[...] = nn(unit, wk_ref[0]).astype(BF)
    v_ref[...] = nn(unit, wv_ref[0]).astype(BF)


def key_value(width):
    return [pl.BlockSpec((1, width, width), lambda i, s: (1, 0, 0)),
            pl.BlockSpec((1, width, width), lambda i, s: (2, 0, 0))]


def squeeze(run, groups, own, a_parts, b_parts, w, gain):
    _, rows, width = groups.shape
    parts = a_parts + b_parts
    shape = (rows, width)
    return run(
        squeeze_kernel, "squeeze", (1,),
        [whole(groups.shape), whole(own.shape)] + [whole(p.shape) for p in parts]
        + [*key_value(width), whole((1, width))],
        [fixed(shape, F32), fixed(shape, BF), fixed(shape, BF), fixed(shape, BF)], [],
        (groups, own) + parts + (w, w, gain), 10 * rows * width * width)


def masked_softmax(scores, live):
    masked = jnp.where(live, scores, -1e30)
    weights = jnp.exp(masked - jnp.max(masked, axis=-1, keepdims=True))
    return weights * (1.0 / jnp.sum(weights, axis=-1, keepdims=True))


def recon_kernel(s_ref, *refs):
    dh = refs[0].shape[-1] // 2
    for n in range(2):
        cols = slice(n * dh, (n + 1) * dh)
        recon_head(s_ref, *[
            r.at[0, :, cols] if len(r.shape) == 3 else r.at[:, cols] for r in refs])


def recon_head(s_ref, pr_ref, ok_ref, ov_ref, ck_ref, cv_ref, gk_ref, gv_ref):
    seg_len = s_ref[SEG_LEN]
    count = seg_len // 3
    probe = pr_ref[...]
    seg, mem, comp = probe.shape[0], ok_ref.shape[0], ck_ref.shape[0]
    old_live = lax.broadcasted_iota(jnp.int32, (1, mem), 1) < 3 * count
    old = nn(masked_softmax(nt(probe, ok_ref[...]), old_live).astype(BF), ov_ref[...])
    live = lax.broadcasted_iota(jnp.int32, (1, comp), 1) < count
    probs = masked_softmax(nt(probe, ck_ref[...]), live)
    low = probs.astype(BF)
    gap = nn(low, cv_ref[...]) - old
    row = lax.broadcasted_iota(jnp.int32, gap.shape, 0)
    grad_out = (jnp.where(row < seg_len, gap, 0.0) * (2.0 / seg_len.astype(F32))).astype(BF)
    gv_ref[...] = tn(low, grad_out).astype(BF)
    weighted = probs * nt(grad_out, cv_ref[...])
    scores = (weighted - probs * jnp.sum(weighted, axis=-1, keepdims=True)).astype(BF)
    gk_ref[...] = tn(scores, probe).astype(BF)


def reconstruct(run, probe, kv, ck, cv, mem):
    seg, width = probe.shape
    rows = ck.shape[0]
    dh = 2 * width // H
    at = lambda n, b: pl.BlockSpec((n, dh), lambda h, s: (b, h))
    old = lambda m: pl.BlockSpec((1, mem, dh), lambda h, s: (m, 1, h))
    grads = lambda: out((rows, width), BF, (rows, dh), lambda h, s: (0, h))
    return run(
        recon_kernel, "reconstruct", (H // 2,),
        [at(seg, 0), old(0), old(1), at(rows, 0), at(rows, 0)], [grads(), grads()], [],
        (probe, kv, kv, ck, cv), 4 * seg * width * mem + 12 * seg * width * rows)


def grad_comp_kernel(s_ref, sq_ref, gk_ref, gv_ref, wk_ref, wv_ref, g_ref, gr_ref, k_ref, x_ref, low_ref, buf):
    @pl.when(pl.program_id(0) == 0)
    def _():
        grad = nt(gk_ref[...], wk_ref[0]) + nt(gv_ref[...], wv_ref[0])
        unit, scale = norm_rows(sq_ref[...])
        low = norm_back(grad, g_ref[...], unit, scale).astype(BF)
        low_ref[...] = by_core(buf, low.astype(F32).T, s_ref[CORE])

    part = nn(low_ref[...], gr_ref[0])
    width = part.shape[1] // 2
    for y in range(2):
        put(k_ref.at[y, :, 0], x_ref.at[y, :, 0], part[:, y * width:(y + 1) * width])


def grad_comp(run, squeezed, gk, gv, w, gain, groups, n_dp):
    taps, rows, width = groups.shape
    chunk = width // n_dp
    shape = part_shape(width, width, n_dp, taps)
    half = lambda: out(shape, BF, shape[:2] + (1,) + shape[3:], lambda i, s: (0, 0, i, 0, 0))
    here = whole((rows, width))
    return run(
        grad_comp_kernel, "grad_comp", (taps,),
        [here, here, here, *key_value(width), whole((1, width)),
         pl.BlockSpec((1, rows, width), lambda i, s: (i, 0, 0))],
        [half(), half()],
        [pltpu.VMEM((width, rows), BF), pltpu.VMEM((n_dp // 2, 2, chunk, rows), low_or_wide(chunk))],
        (squeezed, gk, gv, w, w, gain, groups), 10 * rows * width * width)


class Links:
    def __init__(self):
        self.dp = lax.axis_index("dp")
        self.y = lax.axis_index("fsdp")
        self.n_dp = lax.axis_size("dp")
        self.top = self.n_dp.bit_length() - 2

    def bit(self, axis):
        return self.y if axis == "y" else (self.dp >> axis) & 1

    def swap(self, value, axis):
        if axis == "y":
            return lax.ppermute(value, "fsdp", [(0, 1), (1, 0)])
        return lax.ppermute(value, "dp", [(i, i ^ (1 << axis)) for i in range(self.n_dp)])


class Part:
    def __init__(self, array, start):
        self.array, self.start = array, start


class Flow:
    def __init__(self, axes, order, rows):
        self.axes, self.order, self.rows = list(axes), list(order), rows

    def halves(self):
        axis = self.order[0]
        where = self.axes.index(axis)
        run = self.rows << (len(self.axes) - 1 - where)
        return axis, [(2 * p * run, (2 * p + 1) * run, p * run) for p in range(1 << where)], run

    def plan(self, take_in, give):
        axis, runs, length = self.halves()
        keep, recv = take_in(self.keep), take_in(self.recv.array)
        total = len(runs) * length
        held = give(fixed((total, self.keep.shape[1]), BF))
        place = give.send(axis, total, self)
        first = self.recv.start
        slot = Y if axis == "y" else BITS + axis - 1

        def kernel(s_ref, ins, outs, sends):
            bit = s_ref[slot]
            dst, base = sends(place)
            for low, high, to in runs:
                for side, ref, at in ((bit, outs[held], to), (1 - bit, dst, base + to)):
                    start = low + side * (high - low)
                    a = ins[keep][pl.ds(pl.multiple_of(start, 8), length)]
                    b = ins[recv][pl.ds(pl.multiple_of(first + start, 8), length)]
                    ref[at:at + length] = (a.astype(F32) + b.astype(F32)).astype(BF)

        def done(outs):
            self.keep = outs[held]
            self.axes.remove(axis)
            self.order.pop(0)

        return kernel, done


def cut_rows(rows, flows):
    if flows == 1:
        return (0, rows)
    unit = 16 if rows >= 96 else 8
    third = -(-rows // (3 * unit)) * unit
    return (0, third, 2 * third, rows)


class Source:
    def __init__(self, links, keep, send, axes, orders):
        self.axes, self.orders = axes, orders
        self.blocks = math.prod(keep.shape[:2])
        self.rows, self.cols = math.prod(keep.shape[2:4]), keep.shape[4]
        self.keep = keep.reshape(-1, self.cols)
        self.recv = links.swap(send, 0).reshape(-1, self.cols)
        self.cuts = cut_rows(self.rows, len(orders))

    def plan(self, take_in, give):
        keep, recv = take_in(self.keep), take_in(self.recv)
        rows, moves, self.flows = self.rows, [], []
        for c, order in enumerate(self.orders):
            lo, size = self.cuts[c], self.cuts[c + 1] - self.cuts[c]
            flow = Flow(self.axes, order, size)
            axis = order[0]
            where = self.axes.index(axis)
            post = 1 << (len(self.axes) - 1 - where)
            total = self.blocks // 2 * size
            held = give(fixed((total, self.cols), BF))
            moves.append((axis, where, post, lo, size, held, give.send(axis, total, flow)))
            self.flows.append(flow)

        def kernel(s_ref, ins, outs, sends):
            for axis, where, post, lo, size, held, place in moves:
                bit = s_ref[Y if axis == "y" else BITS + axis - 1]
                dst, base = sends(place)
                for p in range(1 << where):
                    for q in range(post):
                        to = (p * post + q) * size
                        for side, ref, at in ((bit, outs[held], to), (1 - bit, dst, base + to)):
                            start = ((2 * p + side) * post + q) * rows + lo
                            rng = pl.ds(pl.multiple_of(start, 8), size)
                            total = ins[keep][rng].astype(F32) + ins[recv][rng].astype(F32)
                            ref[at:at + size] = total.astype(BF)

        def done(outs):
            for flow, move in zip(self.flows, moves):
                flow.keep = outs[move[5]]
                flow.axes.remove(move[0])
                flow.order.pop(0)

        return kernel, done


class Join:
    def __init__(self, top, low, high):
        self.top, self.low, self.high = top, low, high
        self.rows = low.rows

    def plan(self, take_in, give):
        low, high = self.low, self.high
        refs = [take_in(low.keep), take_in(low.recv.array), take_in(high.keep),
                take_in(high.recv.array)]
        held = give(fixed(low.keep.shape, BF))
        place = give.send(self.top, self.rows, self)
        slot = BITS + self.top - 1
        rows = self.rows

        def kernel(s_ref, ins, outs, sends):
            dst, base = sends(place)
            part = lambda n, flow: (ins[refs[n]][...].astype(F32) + ins[refs[n + 1]][
                flow.recv.start:flow.recv.start + rows].astype(F32))
            a, b = part(0, low), part(2, high)
            upper = s_ref[slot] == 1
            outs[held][...] = jnp.where(upper, b, a).astype(BF)
            dst[base:base + rows] = jnp.where(upper, a, b).astype(BF)

        def done(outs):
            self.keep = outs[held]

        return kernel, done


class Small:
    def __init__(self, links, value, order):
        self.keep, self.order = value, list(order)
        self.recv = Part(links.swap(value, 0), 0)

    def plan(self, take_in, give):
        a, b = take_in(self.keep), take_in(self.recv.array)
        first, wide = self.recv.start, self.recv.array.dtype == F32
        rows, cols = self.keep.shape
        half = cols // 2
        total = give(fixed(self.keep.shape, F32))
        place = give.send(self.order.pop(0), 4 * rows, self) if self.order else None

        def kernel(s_ref, ins, outs, sends):
            if wide:
                came = ins[b][...]
            else:
                part = lambda n: ins[b][first + n:first + n + 2 * rows].astype(F32)
                both = part(0) + part(2 * rows)
                came = jnp.concatenate([both[:rows], both[rows:]], axis=1)
            added = ins[a][...] + came
            outs[total][...] = added
            if place is not None:
                dst, base = sends(place)
                stacked = jnp.concatenate([added[:, :half], added[:, half:]], axis=0)
                high = stacked.astype(BF)
                dst[base:base + 2 * rows] = high
                dst[base + 2 * rows:base + 4 * rows] = (stacked - high.astype(F32)).astype(BF)

        def done(outs):
            self.keep = outs[total]
            if place is None:
                self.recv = None

        return kernel, done


class Finish:
    def __init__(self, flows, shapes, write):
        self.flows, self.shapes, self.write = flows, shapes, write

    def plan(self, take_in, give):
        refs = [(take_in(f.keep), take_in(f.recv.array), f.recv.start, f.rows) for f in self.flows]
        results = [give(fixed(shape, F32)) for shape in self.shapes]

        def kernel(s_ref, ins, outs, sends):
            rows = jnp.concatenate(
                [ins[k][...].astype(F32) + ins[r][first:first + n].astype(F32)
                 for k, r, first, n in refs], axis=0)
            self.write(rows, *[outs[n] for n in results])

        def done(outs):
            self.result = [outs[n] for n in results]

        return kernel, done


class Carry:
    def __init__(self, *values):
        self.values = values

    def plan(self, take_in, give):
        anywhere = pl.BlockSpec(memory_space=pltpu.HBM)
        at = []
        for v in self.values:
            n = give((jax.ShapeDtypeStruct(v.shape, v.dtype), anywhere))
            give.aliases[take_in(v, anywhere)] = n
            at.append(n)

        def done(outs):
            self.values = [outs[n] for n in at]

        return lambda *refs: None, done


class Gives:
    def __init__(self):
        self.outs, self.sizes, self.takers, self.aliases = [], {}, [], {}

    def __call__(self, spec):
        self.outs.append(spec)
        return len(self.outs) - 1

    def send(self, axis, rows, taker):
        start = self.sizes.get(axis, 0)
        self.sizes[axis] = start + rows
        self.takers.append((axis, start, taker))
        return axis, start


def advance(run, links, *items):
    args, ins, index = [], [], {}

    def take_in(array, spec=None):
        if id(array) not in index:
            index[id(array)] = len(args)
            args.append(array)
            ins.append(spec or whole(array.shape))
        return index[id(array)]

    give = Gives()
    plans = [item.plan(take_in, give) for item in items]
    n_out = len(give.outs)
    axes = sorted(give.sizes, key=lambda a: 0 if a == "y" else a)
    outs = give.outs + [fixed((give.sizes[a], args[0].shape[-1]), BF) for a in axes]

    def kernel(s_ref, *refs):
        in_refs, out_refs = refs[:len(args)], refs[len(args):]
        sends = lambda place: (out_refs[n_out + axes.index(place[0])], place[1])
        for part, _ in plans:
            part(s_ref, in_refs, out_refs, sends)

    done = run(kernel, "add", (1,), ins, outs, [], args, 0,
               {1 + a: b for a, b in give.aliases.items()})
    came = {a: links.swap(done[n_out + n], a) for n, a in enumerate(axes)}
    for axis, start, taker in give.takers:
        taker.recv = Part(came[axis], start)
    for _, take in plans:
        take(done)


class Deal:
    def __init__(self, links, pairs, axes, orders, cuts):
        self.links, self.axes, self.orders, self.cuts = links, axes, orders, cuts
        self.keeps = [k for k, _ in pairs]
        self.sends = [x for _, x in pairs]
        self.rows, self.cols = self.keeps[0].shape[-2:]

    def start(self, sends):
        self.recvs = [self.links.swap(x, 0) for x in sends]

    def spans(self, c):
        lo, hi = self.cuts[c], self.cuts[c + 1]
        for n in range(2):
            a, b = max(lo - n * self.rows, 0), min(hi - n * self.rows, self.rows)
            if a < b:
                yield n, a, b

    def add(self, run, steps):
        n = len(self.axes)
        lead = (2,) * n
        rows, cols = self.rows, self.cols
        firsts = [self.axes.index(o[0]) for o in self.orders]
        others = [a for a in range(n) if a not in firsts]
        split = max(steps >> len(others), 1)
        width = cols // split
        count = 2 ** len(others) * split

        def at(i):
            places, rest = [0] * n, i // split
            for a in reversed(others):
                places[a] = rest % 2
                rest = rest // 2
            return places, i % split

        block = tuple(1 if a in others else 2 for a in range(n))

        def read(i, s):
            places, col = at(i)
            return (*places, 0, col)

        def write(first):
            def index(i, s):
                places, col = at(i)
                return (*places[:first], *places[first + 1:], 0, col)
            return index

        args = [a.reshape(lead + (rows, cols)) for a in self.keeps + self.recvs]
        ins = [pl.BlockSpec(block + (rows, width), read)] * 4
        outs, slots = [], []
        for c, first in enumerate(firsts):
            size = self.cuts[c + 1] - self.cuts[c]
            shape = lead[1:] + (size, cols)
            less = block[:first] + block[first + 1:]
            outs += [out(shape, BF, less + (size, width), write(first))] * 2
            axis = self.axes[first]
            slots.append(Y if axis == "y" else BITS + axis - 1)

        def kernel(s_ref, *refs):
            held, sent = refs[4::2], refs[5::2]

            for c, first in enumerate(firsts):
                bit = s_ref[slots[c]]
                row = 0
                for m, a, b in self.spans(c):
                    keep, recv = refs[m], refs[2 + m]
                    for dst, side in ((held[c], bit), (sent[c], 1 - bit)):
                        pick = tuple(side if d == first else slice(None) for d in range(n))
                        pick += (slice(a, b), slice(None))
                        total = keep[pick].astype(F32) + recv[pick].astype(F32)
                        to = (slice(None),) * (n - 1) + (slice(row, row + b - a),)
                        dst[to] = total.astype(BF)
                    row += b - a

        def take(*done):
            self.chains = []
            for c, order in enumerate(self.orders):
                axes = [a for a in self.axes if a != order[0]]
                recv = self.links.swap(done[2 * c + 1], order[0])
                size = self.cuts[c + 1] - self.cuts[c]
                flow = Flow(axes, order[1:], size)
                flow.keep, flow.recv = done[2 * c].reshape(-1, self.cols), Part(
                    recv.reshape(-1, self.cols), 0)
                self.chains.append(flow)

        done = run(kernel, "deal", (count,), ins, outs, [], args, 0)
        take(*done)


def angle_parts(rows, width):
    fine = 32
    frequency = jnp.exp(
        jnp.arange(0, width, 2).astype(F32) * (-math.log(10000.0) / width))
    coarse = (fine * (rows // fine - 1 - jnp.arange(rows // fine))).astype(F32)
    near = (fine - 1 - jnp.arange(fine)).astype(F32)
    a, b = coarse[:, None] * frequency[None, :], near[:, None] * frequency[None, :]
    return (jnp.sin(a), jnp.cos(a), jnp.sin(b), jnp.cos(b))


def body(tokens, memory, compressed, cotangent, seg_len, mem_fill, cmem_fill, w_qkv, w_rel, w_out,
         w_up, w_down, w_comp, norm_gain1, norm_gain2, bias_content, bias_position, bias_up):
    streams = tokens.shape[0]
    assert streams == 1
    links = Links()
    n_dp, top = links.n_dp, links.top
    seg, width = tokens.shape[1:]
    mem, comp = memory.shape[1], compressed.shape[1]
    start = comp + mem
    keys = start + seg
    squeezed_rows = mem // 3
    scale = (width // H) ** (-0.5)
    current, recent, distant = tokens[0], memory[0], compressed[0]
    seg_length = seg_len[0]
    core, x, z = links.bit(0), links.bit(1), links.bit(2)
    run = Steps(jnp.stack(
        [links.y, core, seg_length, mem_fill[0], cmem_fill[0], core * 2 + z,
         core * 2 + x] + [links.bit(n) for n in range(1, top + 1)]).astype(jnp.int32))
    gain1, gain2 = norm_gain1.reshape(1, -1), norm_gain2.reshape(1, -1)

    swap = links.swap
    near_parts = lambda value: (value, swap(value, 0))
    p_rel, p_a, p_b = pack_first(run, w_qkv, w_rel)
    rel, a, b = swap(p_rel, "y"), swap(p_a, "y"), swap(p_b, "y")
    normed = norm_hidden(run, distant, recent, current, gain1)
    rel_far = swap(rel, 2)
    p_c, p_d, p_up, p_down = pack_rest(run, w_out, w_up, w_down, w_comp)
    c, d = swap(p_c, "y"), swap(p_d, "y")
    table, groups = constants(run, recent, angle_parts(keys, width), squeezed_rows)
    rel, = order(run, (rel, rel_far, 2))
    rel_parts = near_parts(rel)
    a_far, b_far = swap(a, 2), swap(b, 1)
    pos = project_position(run, table, w_rel, rel_parts)
    a, b = order(run, (a, a_far, 2), (b, b_far, 1))
    a_parts, b_parts = near_parts(a), near_parts(b)
    p_up, p_down = follow(run, p_up, p_down)
    up, down = swap(p_up, "y"), swap(p_down, "y")
    kv, qc, qp, probe, w_full = project_qkv(
        run, normed, w_qkv, a_parts, b_parts, bias_content, bias_position, seg, scale)
    c, d = follow(run, c, d)
    c_far, d_far = swap(c, 2), swap(d, 1)
    p0, m0 = attention(run, qc, qp, kv, pos, comp, mem, 0)
    c, d = order(run, (c, c_far, 2), (d, d_far, 1))
    c_parts, d_parts = near_parts(c), near_parts(d)
    p1, m1 = attention(run, qc, qp, kv, pos, comp, mem, 1)
    up, down = follow(run, up, down)
    up_far, down_far = swap(up, 2), swap(down, 1)
    squeezed, squeezed_low, ck, cv = squeeze(run, groups, w_comp, c_parts, d_parts, w_full, gain1)
    gck, gcv = reconstruct(run, probe, kv, ck, cv, mem)
    up, down = order(run, (up, up_far, 2), (down, down_far, 1))
    up_parts, down_parts = near_parts(up), near_parts(down)
    comp_keep, comp_send = grad_comp(run, squeezed, gck, gcv, w_full, gain1, groups, n_dp)

    attended, second, w_out_full = mix_out(run, current, (m0, m1), w_out, d_parts, gain2)
    far = list(range(3, top + 1))
    names, under = ["y"] + list(range(top, 0, -1)), ["y"] + list(range(top - 1, 0, -1))
    turns = lambda rest: [[1, "y", 2] + rest, ["y", 2, 1] + rest, [2, 1, "y"] + rest]
    of_comp = Source(links, comp_keep, comp_send, names, [[2, 1, "y"] + far])
    advance(run, links, of_comp)
    (act, grad_attended, grad_mix, up_keep, up_send, down_keep, down_send, sum_bias, sum_gain2
     ) = feed_forward(run, second, cotangent[0], attended, w_up, up_parts, w_down, down_parts,
                      bias_up.reshape(1, -1), gain2, w_out_full, n_dp)
    inner = bias_up.shape[0]
    rows, half = inner // n_dp, width // 2
    flat = lambda a: a.reshape(2, n_dp // 2, rows, half)
    third = max(2 * rows * 11 // 32 // 16 * 16, 8)
    deal = Deal(
        links, [(flat(up_keep), flat(up_send)), (flat(down_keep), flat(down_send))], names,
        turns(far), (0, third, 2 * third, 2 * rows))
    carry = Carry(*deal.sends)
    advance(run, links, *of_comp.flows, carry)
    deal.start(carry.values)

    chunk = width // n_dp

    def write_ffn(rows, up, down):
        size = rows.shape[0] // 2
        up[...] = rows[:size].T
        for n in range(inner // (2 * half)):
            down[n * half:(n + 1) * half] = rows[size + n * chunk:size + (n + 1) * chunk].T

    def write_comp(rows, grad):
        for t in range(3):
            grad[t] = rows[t * chunk:(t + 1) * chunk].T

    def write_rest(rows, qkv, rel, ow):
        tap = lambda t: rows[t * chunk:(t + 1) * chunk].T
        qkv[0], qkv[1], qkv[2] = tap(2), tap(0), tap(1)
        rel[...], ow[...] = tap(3), tap(4)

    waiting = lambda *flows: [f for f in flows if f.order]
    back = functools.partial(attention_back, run, (p0, p1), (m0, m1), grad_mix, qc, qp, kv, pos, start, scale)
    grads = lambda turned, gq, half: projection_grads(
        run, turned, gq, grad_attended, normed, table, (m0, m1), w_full, n_dp, half)
    gq0, gk0, gv0, gpos0, content0, position0 = back(0)
    advance(run, links, *of_comp.flows)
    deal.add(run, 4)
    keep_0, send_0, gain_0 = grads((gk0, gv0, gpos0), gq0, 0)
    gq1, gk1, gv1, gpos1, content1, position1 = back(1)
    carry = Carry(send_0)
    advance(run, links, *deal.chains, *of_comp.flows, carry)
    early = Source(links, keep_0, carry.values[0], under, turns(far[:-1]))
    keep_1, send_1, gain_1 = grads((gk1, gv1, gpos1), gq1, 1)
    carry = Carry(send_1)
    comp_end = Finish(of_comp.flows, [(3, half, chunk)], write_comp)
    comp_left = list(waiting(*of_comp.flows))
    held = [Carry(f.recv.array) for f in of_comp.flows if not comp_left]
    advance(run, links, *deal.chains, *comp_left, early, carry, *held)
    for flow, kept in zip(of_comp.flows, held):
        flow.recv = Part(kept.values[0], flow.recv.start)
    late = Source(links, keep_1, carry.values[0], under, turns(far[:-1]))
    row = lambda a, b: jnp.concatenate([a, b], axis=1)
    small = Small(links, jnp.concatenate(
        [(gain_0 + gain_1) / gain1, sum_gain2, row(content0, content1), row(position0, position1),
         sum_bias.reshape(-1, width)], axis=0), ["y", 1, 2] + far)
    new_memory = lax.dynamic_slice_in_dim(
        jnp.concatenate([recent, current], axis=0), seg_length, mem, 0)
    new_compressed = lax.dynamic_slice_in_dim(
        jnp.concatenate([distant, squeezed_low[:squeezed_rows]], axis=0), seg_length // 3, comp, 0)
    output = layer_output(run, act, attended, w_down, down_parts)
    advance(run, links, *waiting(*deal.chains, *comp_left), late, small)
    grad_rows = grad_tokens(run, (gk0, gk1), (gv0, gv1), (gq0, gq1), current, grad_attended,
                            w_full, gain1)
    while any(f.order for f in late.flows):
        advance(run, links, *waiting(*deal.chains, *comp_left, *early.flows, *late.flows),
                small)
        if not comp_left and comp_end.flows[0].recv is not None and not hasattr(comp_end, 'result'):
            advance(run, links, comp_end)
    ends = [Join(top, a, b) for a, b in zip(early.flows, late.flows)]
    of_ffn = Finish(deal.chains, [(half, rows), (inner // 2, chunk)], write_ffn)
    advance(run, links, *ends, small, of_ffn, *([comp_end] if comp_left else []))
    rest = Finish(ends, [(3, half, chunk), (half, chunk), (half, chunk)], write_rest)
    advance(run, links, rest, small)
    assert small.recv is None
    (grad_up, grad_down), (grad_comp_,) = of_ffn.result, comp_end.result
    grad_qkv, grad_rel, grad_out = rest.result

    at = links.dp * 2 + links.y
    each, each_up = width // (2 * n_dp), bias_up.shape[0] // (2 * n_dp)
    vec = lax.dynamic_slice(small.keep[:4], (0, at * each), (4, each))
    vec_up = lax.dynamic_slice_in_dim(small.keep[4:].reshape(-1), at * each_up, each_up)
    return (output[None], grad_rows[None], new_memory[None], new_compressed[None],
            grad_qkv, grad_rel, grad_out,
            grad_up, grad_down, grad_comp_, vec[0], vec[1], vec[2], vec[3], vec_up)


def solution(mesh):
    rows = P(("dp", "fsdp"), None, None)
    one = P(("dp", "fsdp"))
    return jax.shard_map(
        body,
        mesh=mesh,
        in_specs=(rows, rows, rows, rows, one, one, one, P(None, "fsdp", None), P("fsdp", None),
                  P("fsdp", None), P("fsdp", None), P("fsdp", None), P(None, "fsdp", None), P(),
                  P(), P(), P(), P()),
        out_specs=(rows, rows, rows, rows, P(None, "fsdp", "dp"), P("fsdp", "dp"),
                   P("fsdp", "dp"), P("fsdp", "dp"), P("fsdp", "dp"), P(None, "fsdp", "dp"), one,
                   one, one, one, one),
        check_vma=False,
    )
```

```python
import functools
import math

import jax
import jax.numpy as jnp
from jax import lax
from jax.experimental import pallas as pl
from jax.experimental.pallas import tpu as pltpu
from jax.sharding import PartitionSpec as P

H = 8
BF = jnp.bfloat16
F32 = jnp.float32
VMEM = 60 * 1024 * 1024
GELU_C = math.sqrt(2.0 / math.pi)
COST = 0.0001
TEMPORARIES = 36 * 1024 * 1024
Y, CORE, SEG_LEN, MEM_LIVE, COMP_LIVE, PIECE_A, PIECE_B, BITS = range(8)


def nn(a, b):
    return lax.dot_general(a, b, (((1,), (0,)), ((), ())), preferred_element_type=F32)


def nt(a, b):
    return lax.dot_general(a, b, (((1,), (1,)), ((), ())), preferred_element_type=F32)


def tn(a, b):
    return lax.dot_general(a, b, (((0,), (0,)), ((), ())), preferred_element_type=F32)


class Steps:
    def __init__(self, scal):
        self.scal = scal
        self.token = None

    def __call__(self, kernel, name, grid, ins, outs, scratch, args, flops, aliases={}):
        before = [] if self.token is None else [self.token]
        n_in, n_out, extra = len(ins), len(outs), len(before)

        def ordered_kernel(s_ref, *refs):
            rest = refs[n_in + extra:]
            kernel(s_ref, *refs[:n_in], *rest[:n_out], *rest[n_out + 1:])

        anywhere = pl.BlockSpec(memory_space=pltpu.HBM)
        moved = sum(a.size * a.dtype.itemsize for a in args)
        need = TEMPORARIES
        for (block, array) in list(zip(ins, args)) + [(b, s) for s, b in outs]:
            if block.block_shape is not None:
                need += 2 * math.prod(block.block_shape) * array.dtype.itemsize
        for ref in (r for r in scratch if 'sem' not in str(r.dtype)):
            need += math.prod(ref.shape) * jnp.dtype(ref.dtype).itemsize
        done = pl.pallas_call(
            ordered_kernel,
            name=name,
            out_shape=[s for s, _ in outs] + [jax.ShapeDtypeStruct((8, 128), F32)],
            grid_spec=pltpu.PrefetchScalarGridSpec(
                num_scalar_prefetch=1,
                grid=grid,
                in_specs=list(ins) + [anywhere] * extra,
                out_specs=[b for _, b in outs] + [anywhere],
                scratch_shapes=scratch,
            ),
            compiler_params=pltpu.CompilerParams(
                vmem_limit_bytes=min(need, VMEM), dimension_semantics=("arbitrary",) * len(grid)
            ),
            input_output_aliases=aliases,
            cost_estimate=pl.CostEstimate(
                flops=int(flops * COST), bytes_accessed=int(moved * COST), transcendentals=0),
        )(self.scal, *args, *before)
        *done, self.token = done
        return done


def follow(run, *values):
    anywhere = pl.BlockSpec(memory_space=pltpu.HBM)
    return run(
        lambda *refs: None, "follow", (1,), [anywhere] * len(values),
        [(jax.ShapeDtypeStruct(v.shape, v.dtype), anywhere) for v in values], [], values, 0,
        {n + 1: n for n in range(len(values))})


def whole(shape):
    return pl.BlockSpec(shape, lambda i, s: (0,) * len(shape))


def out(shape, dtype, block, index):
    return (jax.ShapeDtypeStruct(shape, dtype), pl.BlockSpec(block, index))


def fixed(shape, dtype):
    return out(shape, dtype, shape, lambda i, s: (0,) * len(shape))


def norm_rows(rows):
    centred = rows - jnp.mean(rows, axis=-1, keepdims=True)
    spread = jnp.mean(centred * centred, axis=-1, keepdims=True)
    scale = lax.rsqrt(spread + 1e-05)
    return centred * scale, scale


def norm_back(grad, gain, unit, scale):
    g = grad * gain
    inner = jnp.mean(g * unit, axis=-1, keepdims=True)
    return scale * (g - jnp.mean(g, axis=-1, keepdims=True) - unit * inner)


def place(dst, s_ref, own, mine, theirs, cols=slice(None)):
    half, quarter = own.shape[-2], mine.shape[-2]
    y, core = s_ref[Y], s_ref[CORE]
    base = (1 - y) * half
    at = lambda start, size: pl.ds(pl.multiple_of(start, quarter), size)
    dst[at(y * half, half), cols] = own[:, cols]
    dst[at(base + core * quarter, quarter), cols] = mine[...]
    dst[at(base + (1 - core) * quarter, quarter), cols] = theirs[...]


def pack_first_kernel(s_ref, rel, k, v, qa, qb, o_rel, o_a, o_b):
    width = rel.shape[-1]
    o_rel[...] = rel[...]
    o_a[0, :, :width] = k[0, 0]
    o_a[0, :, width:] = qa[0, 0]
    o_b[0, :, :width] = v[0, 0]
    o_b[0, :, width:] = qb[0, 0]


def pack_rest_kernel(s_ref, c0, c1, c2, ow, up, down, o_c, o_d, o_up, o_down):
    o_c[0] = c0[0, 0]
    o_c[1] = c1[0, 0]
    o_d[0] = c2[0, 0]
    o_d[1] = ow[0]
    o_up[...] = up[...]
    o_down[...] = down[...]


def quarters(a):
    lead = a.shape[:-2]
    return a.reshape(lead + (4, a.shape[-2] // 4, a.shape[-1]))


def part_of(a, where, n=0, cols=1, c=0):
    block = (1,) * (a.ndim - 2) + (a.shape[-2], a.shape[-1] // cols)
    if a.ndim == 3:
        return pl.BlockSpec(block, lambda i, s: (s[where], 0, c))
    return pl.BlockSpec(block, lambda i, s: (n, s[where], 0, c))


def pack_first(run, w_qkv, w_rel):
    qkv, rel = quarters(w_qkv), quarters(w_rel)
    part, width = rel.shape[1:]
    return run(
        pack_first_kernel, "pack_first", (1,),
        [part_of(rel, PIECE_A), part_of(qkv, PIECE_A, 1), part_of(qkv, PIECE_B, 2),
         part_of(qkv, PIECE_A, 0, 2, 0), part_of(qkv, PIECE_B, 0, 2, 1)],
        [fixed((1, part, width), BF), fixed((1, part, width * 3 // 2), BF),
         fixed((1, part, width * 3 // 2), BF)],
        [], (rel, qkv, qkv, qkv, qkv), 0)


def pack_rest(run, w_out, w_up, w_down, w_comp):
    comp, ow, up, down = quarters(w_comp), quarters(w_out), quarters(w_up), quarters(w_down)
    part, width = ow.shape[1:]
    return run(
        pack_rest_kernel, "pack_rest", (1,),
        [part_of(comp, PIECE_A, 0), part_of(comp, PIECE_A, 1), part_of(comp, PIECE_B, 2),
         part_of(ow, PIECE_B), part_of(up, PIECE_A), part_of(down, PIECE_B)],
        [fixed((2, part, width), BF), fixed((2, part, width), BF),
         fixed((1,) + up.shape[1:], BF), fixed((1,) + down.shape[1:], BF)],
        [], (comp, comp, comp, ow, up, down), 0)


def order_kernel(s_ref, *refs, slots):
    n = len(slots)
    outs, sem = refs[2 * n:3 * n], refs[3 * n]
    copies = []
    for c, slot in enumerate(slots):
        bit = s_ref[slot]
        copies += [
            pltpu.make_async_copy(refs[c], outs[c].at[:, bit], sem.at[2 * c]),
            pltpu.make_async_copy(refs[n + c], outs[c].at[:, 1 - bit], sem.at[2 * c + 1])]
    for copy in copies:
        copy.start()
    for copy in copies:
        copy.wait()


def order(run, *pieces):
    args = [p[0] for p in pieces] + [p[1] for p in pieces]
    shapes = [(p[0].shape[0], 2) + p[0].shape[1:] for p in pieces]
    anywhere = pl.BlockSpec(memory_space=pltpu.HBM)
    done = run(
        functools.partial(order_kernel, slots=tuple(BITS + p[2] - 1 for p in pieces)), "order", (1,),
        [anywhere] * len(args), [(jax.ShapeDtypeStruct(s, BF), anywhere) for s in shapes],
        [pltpu.SemaphoreType.DMA((len(args),))], args, 0)
    return [d.reshape(s[0], 2 * s[2], s[3]) for d, s in zip(done, shapes)]


def normed_kernel(s_ref, d_ref, m_ref, t_ref, g_ref, x_ref):
    i = pl.program_id(0)
    for n, ref in enumerate((d_ref, m_ref, t_ref)):
        @pl.when(i // 2 == n)
        def _(ref=ref):
            x_ref[...] = (norm_rows(ref[...].astype(F32))[0] * g_ref[...]).astype(BF)


def norm_hidden(run, distant, recent, current, gain):
    mem, width = recent.shape
    blk = mem // 2
    part = lambda n: pl.BlockSpec((blk, width), lambda i, s: (jnp.clip(i - 2 * n, 0, 1), 0))
    return run(
        normed_kernel, "norm_hidden", (6,),
        [part(0), part(1), part(2), whole(gain.shape)],
        [out((3 * mem, width), BF, (blk, width), lambda i, s: (i, 0))],
        [], (distant, recent, current, gain), 0)[0]


def constants_kernel(s_ref, m_ref, sa_ref, ca_ref, sb_ref, cb_ref, tab_ref, gr_ref, wide_ref,
                     *, groups):
    i = pl.program_id(0)
    blk, width = tab_ref.shape
    half = width // 2
    fine = sb_ref.shape[0]
    for n in range(blk // fine):
        rows = slice(n * fine, (n + 1) * fine)
        a = i * (blk // fine) + n
        sa, ca = sa_ref[pl.ds(a, 1)], ca_ref[pl.ds(a, 1)]
        tab_ref[rows, :half] = (sa * cb_ref[...] + ca * sb_ref[...]).astype(BF)
        tab_ref[rows, half:] = (ca * cb_ref[...] - sa * sb_ref[...]).astype(BF)

    @pl.when(i == 0)
    def _():
        mem = m_ref.shape[0]
        lanes = wide_ref.shape[2]
        count = gr_ref.shape[1]
        live = lax.broadcasted_iota(jnp.int32, (count, 1), 0) < groups
        for n in range(width // lanes):
            cols = slice(n * lanes, (n + 1) * lanes)
            wide_ref[n, :mem] = m_ref[:, cols].astype(F32)
            wide_ref[n, mem:] = jnp.zeros((wide_ref.shape[1] - mem, lanes), F32)
            for t in range(3):
                rows = jnp.where(live, wide_ref[n, pl.ds(t, count, stride=3)], 0.0)
                gr_ref[t, :, cols] = rows.astype(BF)


def constants(run, recent, angles, groups):
    mem, width = recent.shape
    keys = 3 * mem
    blk = 512
    padded = groups + (-groups) % 64
    ins = (recent,) + angles
    return run(
        functools.partial(constants_kernel, groups=groups), "constants", (keys // blk,),
        [whole(a.shape) for a in ins],
        [out((keys, width), BF, (blk, width), lambda i, s: (i, 0)),
         fixed((3, padded, width), BF)],
        [pltpu.VMEM((width // 128, 3 * padded, 128), F32)], ins, 0)


def qkv_kernel(s_ref, x_ref, o_ref, am_ref, at_ref, bm_ref, bt_ref, bc_ref, bp_ref, kv_ref,
               qc_ref, qp_ref, pr_ref, w_ref, *, scale):
    i = pl.program_id(0)
    rows, width = x_ref.shape
    seg = qc_ref.shape[0]
    blk = 256
    lo, hi = slice(0, width // 2), slice(width // 2, width)
    own, dst = o_ref.at[0], w_ref.at[0]

    @pl.when(i == 0)
    def _():
        place(dst, s_ref, own, am_ref.at[0, :, :width], at_ref.at[0, :, :width])

    @pl.when(i == 1)
    def _():
        place(dst, s_ref, own, bm_ref.at[0, :, :width], bt_ref.at[0, :, :width])

    @pl.when(i == 2)
    def _():
        place(dst, s_ref, own, am_ref.at[0, :, width:], at_ref.at[0, :, width:], lo)
        place(dst, s_ref, own, bm_ref.at[0, :, width:], bt_ref.at[0, :, width:], hi)

    @pl.when(i < 2)
    def _():
        def some(n):
            at = slice(n * blk, (n + 1) * blk)
            kv_ref[0, at] = nn(x_ref[at], dst[...]).astype(BF)

        for n in range(rows // blk):
            some(n)

    @pl.when(i == 2)
    def _():
        for n in range(seg // blk):
            at = slice(n * blk, (n + 1) * blk)
            q = nn(x_ref[rows - seg + n * blk:rows - seg + (n + 1) * blk], dst[...])
            qc_ref[at] = ((q + bc_ref[...]) * scale).astype(BF)
            qp_ref[at] = ((q + bp_ref[...]) * scale).astype(BF)
            pr_ref[at] = (q * scale).astype(BF)


def project_qkv(run, normed, w_qkv, a_parts, b_parts, bias_content, bias_position, seg, scale):
    rows, width = normed.shape
    turn = lambda i, s: ((i + 1) % 3, 0, 0)
    parts = a_parts + b_parts
    return run(
        functools.partial(qkv_kernel, scale=scale), "project_qkv", (3,),
        [whole((rows, width)), pl.BlockSpec((1, width // 2, width), turn)]
        + [whole(p.shape) for p in parts] + [whole((1, width)), whole((1, width))],
        [out((2, rows, width), BF, (1, rows, width), lambda i, s: (jnp.minimum(i, 1), 0, 0)),
         fixed((seg, width), BF), fixed((seg, width), BF), fixed((seg, width), BF),
         out((3, width, width), BF, (1, width, width), turn)],
        [], (normed, w_qkv) + parts + (bias_content.reshape(1, -1), bias_position.reshape(1, -1)),
        2 * (2 * rows + seg) * width * width)


def position_kernel(s_ref, x_ref, o_ref, m_ref, t_ref, p_ref, w_ref):
    @pl.when(pl.program_id(0) == 0)
    def _():
        place(w_ref, s_ref, o_ref, m_ref.at[0], t_ref.at[0])

    p_ref[...] = nn(x_ref[...], w_ref[...]).astype(BF)


def project_position(run, table, own, parts):
    rows, width = table.shape
    blk = 512
    return run(
        position_kernel, "project_position", (rows // blk,),
        [pl.BlockSpec((blk, width), lambda i, s: (i, 0)), whole(own.shape)]
        + [whole(p.shape) for p in parts],
        [out((rows, width), BF, (blk, width), lambda i, s: (i, 0))],
        [pltpu.VMEM((width, width), BF)], (table, own) + parts,
        2 * rows * width * width)[0]


RB = 256


def flip_matrix():
    return (lax.broadcasted_iota(jnp.int32, (RB, RB), 0)
            + lax.broadcasted_iota(jnp.int32, (RB, RB), 1) == RB - 1).astype(BF)


def attention_kernel(s_ref, qc_ref, qp_ref, k_ref, v_ref, pos_ref, p_ref, mix_ref, bias_ref,
                     *, comp, mem):
    seg, keys = qc_ref.shape[0], k_ref.shape[1]
    start = comp + mem

    @pl.when(pl.program_id(0) == 0)
    def _():
        mem_live, comp_live = s_ref[MEM_LIVE], s_ref[COMP_LIVE]
        col = lax.broadcasted_iota(jnp.int32, bias_ref.shape, 1)
        row = lax.broadcasted_iota(jnp.int32, bias_ref.shape, 0)
        live = ((col >= comp - comp_live) & (col < comp)) | (
            (col >= start - mem_live) & (col - start <= row))
        bias_ref[...] = jnp.where(live, 0.0, -1e30)

    for r in range(seg // RB):
        width = start + RB * (r + 1)
        rows = slice(r * RB, (r + 1) * RB)
        content = nt(qc_ref[rows], k_ref[0, :width])
        rel = nt(qp_ref[rows], pos_ref[keys - width:])
        rel = pltpu.roll(rel, width - RB + 1, 1, stride=1, stride_axis=0)
        masked = content + rel + bias_ref[rows, :width]
        top = jnp.max(masked, axis=-1, keepdims=True)
        weights = jnp.exp(masked - top)
        probs = (weights * (1.0 / jnp.sum(weights, axis=-1, keepdims=True))).astype(BF)
        mix_ref[rows] = nn(probs, v_ref[0, :width]).astype(BF)
        p_ref[0, rows, :width] = probs
        if width < keys:
            p_ref[0, rows, width:] = jnp.zeros((RB, keys - width), BF)


def attention(run, qc, qp, kv, pos, comp, mem, half):
    seg, width = qc.shape
    keys = kv.shape[1]
    dh = width // H
    n = H // 2
    first = half * n
    q_spec = pl.BlockSpec((seg, dh), lambda h, s: (0, h + first))
    of = lambda m: pl.BlockSpec((1, keys, dh), lambda h, s: (m, 0, h + first))
    return run(
        functools.partial(attention_kernel, comp=comp, mem=mem), "attention", (n,),
        [q_spec, q_spec, of(0), of(1), pl.BlockSpec((keys, dh), lambda h, s: (0, h + first))],
        [out((n, seg, keys), BF, (1, seg, keys), lambda h, s: (h, 0, 0)),
         out((seg, width // 2), BF, (seg, dh), lambda h, s: (0, h))],
        [pltpu.VMEM((seg, keys), F32)], (qc, qp, kv, kv, pos), 16 * seg * keys * width)


def attention_back_kernel(s_ref, p_ref, gm_ref, mix_ref, qc_ref, qp_ref, k_ref, v_ref, pos_ref, gq_ref,
                          gk_ref, gv_ref, gp_ref, gc_ref, gb_ref, gs_ref, sh_ref, rev_ref,
                          *, start, scale):
    seg, keys = qc_ref.shape[0], k_ref.shape[1]
    flip = flip_matrix()
    sum_c = jnp.zeros((1, gc_ref.shape[1]), F32)
    sum_p = jnp.zeros((1, gc_ref.shape[1]), F32)
    for r in range(seg // RB):
        width = start + RB * (r + 1)
        rows = slice(r * RB, (r + 1) * RB)
        rev_ref[rows] = nn(flip, qp_ref[rows]).astype(BF)
        grad = gm_ref[rows]
        total = jnp.sum(
            grad.astype(F32) * mix_ref[rows].astype(F32), axis=-1, keepdims=True)
        probs = p_ref[0, rows, :width].astype(F32)
        scores = (probs * (nt(grad, v_ref[0, :width]) - total)).astype(BF)
        moved = pltpu.roll(nn(flip, scores), 0, 1, stride=1, stride_axis=0).astype(BF)
        gs_ref[rows, :width] = scores
        sh_ref[rows, keys - width:] = moved
        if width < keys:
            gs_ref[rows, width:] = jnp.zeros((RB, keys - width), BF)
            sh_ref[rows, : keys - width] = jnp.zeros((RB, keys - width), BF)
        grad_c = nn(scores, k_ref[0, :width])
        turned = nn(moved, pos_ref[keys - width:])
        high = turned.astype(BF)
        grad_p = nn(flip, high) + nn(flip, (turned - high.astype(F32)).astype(BF))
        sum_c += jnp.sum(grad_c, axis=0, keepdims=True)
        sum_p += jnp.sum(turned, axis=0, keepdims=True)
        gq_ref[rows] = ((grad_c + grad_p) * scale).astype(BF)
    gc_ref[...] = sum_c * scale
    gb_ref[...] = sum_p * scale
    gv_ref[...] = tn(gm_ref[...], p_ref[0]).astype(BF)
    gk_ref[...] = tn(qc_ref[...], gs_ref[...]).astype(BF)
    gp_ref[...] = tn(rev_ref[...], sh_ref[...]).astype(BF)


def attention_back(run, probs, mixed, gm, qc, qp, kv, pos, start, scale, half):
    seg, width = qc.shape
    keys = kv.shape[1]
    dh = width // H
    n = H // 2
    first = half * n
    q_spec = pl.BlockSpec((seg, dh), lambda h, s: (0, h + first))
    of = lambda m: pl.BlockSpec((1, keys, dh), lambda h, s: (m, 0, h + first))
    turned = lambda: out((width // 2, keys), BF, (dh, keys), lambda h, s: (h, 0))
    sums = lambda: out((1, width // 2), F32, (1, dh), lambda h, s: (0, h))
    big = pltpu.VMEM((seg, keys), BF)
    return run(
        functools.partial(attention_back_kernel, start=start, scale=scale), "attention_back", (n,),
        [pl.BlockSpec((1, seg, keys), lambda h, s: (h, 0, 0)), q_spec,
         pl.BlockSpec((seg, dh), lambda h, s: (0, h)), q_spec, q_spec,
         of(0), of(1), pl.BlockSpec((keys, dh), lambda h, s: (0, h + first))],
        [out((seg, width // 2), BF, (seg, dh), lambda h, s: (0, h)), turned(), turned(), turned(),
         sums(), sums()],
        [big, big, pltpu.VMEM((seg, dh), BF)], (probs[half], gm, mixed[half], qc, qp, kv, kv, pos),
        12 * seg * keys * width)


def mixed_kernel(s_ref, tok_ref, a_ref, b_ref, o_ref, m_ref, t_ref, g_ref, att_ref, sec_ref, w_ref):
    @pl.when(pl.program_id(0) == 0)
    def _():
        place(w_ref, s_ref, o_ref, m_ref.at[1], t_ref.at[1])

    mid = a_ref.shape[1]
    attended = (tok_ref[...].astype(F32) + nn(a_ref[...], w_ref[:mid])
                + nn(b_ref[...], w_ref[mid:]))
    att_ref[...] = attended
    sec_ref[...] = (norm_rows(attended)[0] * g_ref[...]).astype(BF)


def mix_out(run, tokens, mixed, own, parts, gain):
    seg, width = tokens.shape
    blk = 256
    row = pl.BlockSpec((blk, width), lambda i, s: (i, 0))
    side = pl.BlockSpec((blk, width // 2), lambda i, s: (i, 0))
    return run(
        mixed_kernel, "mix_out", (seg // blk,),
        [row, side, side, whole(own.shape)] + [whole(p.shape) for p in parts] + [whole((1, width))],
        [out((seg, width), F32, (blk, width), lambda i, s: (i, 0)),
         out((seg, width), BF, (blk, width), lambda i, s: (i, 0)),
         fixed((width, width), BF)],
        [], (tokens,) + mixed + (own,) + parts + (gain,), 2 * seg * width * width)


def part_shape(rows, cols, n_dp, taps, cut=1):
    return (2, n_dp // (2 * cut), taps, rows // n_dp, cols // 2)


def low_or_wide(chunk):
    return BF if chunk % 16 == 0 else F32


def by_core(buf, values, core):
    pairs, _, chunk, cols = buf.shape
    buf[...] = values.astype(buf.dtype).reshape(pairs, 2, chunk, cols)
    pick = lambda c: buf[:, c].reshape(pairs * chunk, cols)
    return jnp.concatenate([pick(core), pick(1 - core)], axis=0).astype(BF)


def put(keep, send, values):
    half = values.shape[0] // 2
    shape = keep.shape[:-1] + (values.shape[1],)
    keep[...] = values[:half].reshape(shape).astype(BF)
    send[...] = values[half:].reshape(shape).astype(BF)


def ffn_kernel(s_ref, sec_ref, cot_ref, att_ref, uo_ref, um_ref, ut_ref, do_ref, dm_ref, dt_ref,
               b_ref, g_ref, wo_ref, act_ref, gatt_ref, gm_ref, uk_ref, us_ref, dk_ref, ds_ref,
               gb_ref, gg_ref, gout_ref, turn_ref, wu_ref, wd_ref, gsec_ref, ubuf, dbuf):
    i, n = pl.program_id(0), pl.num_programs(0)
    y, core = s_ref[Y], s_ref[CORE]

    @pl.when(i == 0)
    def _():
        row = lax.broadcasted_iota(jnp.int32, cot_ref.shape, 0)
        live = jnp.where(row < s_ref[SEG_LEN], cot_ref[...], jnp.zeros((), BF))
        gout_ref[...] = live
        turn_ref[...] = by_core(dbuf, live.T, core)
        gsec_ref[...] = jnp.zeros_like(gsec_ref)

    place(wu_ref, s_ref, uo_ref, um_ref.at[0], ut_ref.at[0])
    half = i // (n // 2)
    side = (i % (n // 2)) // (n // 4)

    @pl.when(half == y)
    def _():
        wd_ref[...] = do_ref[...]

    @pl.when((half != y) & (side == core))
    def _():
        wd_ref[...] = dm_ref[0]

    @pl.when((half != y) & (side != core))
    def _():
        wd_ref[...] = dt_ref[0]

    second, gout = sec_ref[...], gout_ref[...]
    v = nn(second, wu_ref[...]) + b_ref[...]
    square = v * v
    gate = 0.5 + 0.5 * jnp.tanh(v * (GELU_C + (GELU_C * 0.044715) * square))
    act = (v * gate).astype(BF)
    slope = gate + (gate - gate * gate) * v * (2 * GELU_C + (6 * GELU_C * 0.044715) * square)
    act_ref[...] = act
    grad_inner = nt(gout, wd_ref[...]) * slope
    low = grad_inner.astype(BF)
    gb_ref[...] = jnp.sum(low.astype(F32), axis=0, keepdims=True)
    gsec_ref[...] += nt(low, wu_ref[...])
    put(dk_ref.at[0, :, 0], ds_ref.at[0, :, 0], nn(turn_ref[...], act))
    part = nn(by_core(ubuf, low.T, core), second)
    width = part.shape[1] // 2
    for side in range(2):
        put(uk_ref.at[side, :, 0], us_ref.at[side, :, 0], part[:, side * width:(side + 1) * width])

    @pl.when(i == n - 1)
    def _():
        unit, scale = norm_rows(att_ref[...])
        grad = gsec_ref[...]
        gg_ref[...] = jnp.sum(grad * unit, axis=0, keepdims=True)
        gatt = norm_back(grad, g_ref[...], unit, scale) + gout_ref[...].astype(F32)
        gatt_ref[...] = gatt
        gm_ref[...] = nt(gatt.astype(BF), wo_ref[...]).astype(BF)


def down_rows(n, blk, width):
    def own(i, s):
        return (jnp.clip(i - s[Y] * (n // 2), 0, n // 2 - 1), 0)

    def part(other):
        def index(i, s):
            side = s[CORE] if other == 0 else 1 - s[CORE]
            first = (1 - s[Y]) * (n // 2) + side * (n // 4)
            return (0, jnp.clip(i - first, 0, n // 4 - 1), 0)

        return pl.BlockSpec((1, blk, width), index)

    return pl.BlockSpec((blk, width), own), part(0), part(1)


def output_kernel(s_ref, act_ref, att_ref, do_ref, dm_ref, dt_ref, out_ref, acc_ref):
    i, n = pl.program_id(0), pl.num_programs(0)
    half, side = i // (n // 2), (i % (n // 2)) // (n // 4)
    y, core = s_ref[Y], s_ref[CORE]

    @pl.when(i == 0)
    def _():
        acc_ref[...] = att_ref[...]

    @pl.when(half == y)
    def _():
        acc_ref[...] += nn(act_ref[...], do_ref[...])

    @pl.when((half != y) & (side == core))
    def _():
        acc_ref[...] += nn(act_ref[...], dm_ref[0])

    @pl.when((half != y) & (side != core))
    def _():
        acc_ref[...] += nn(act_ref[...], dt_ref[0])

    @pl.when(i == n - 1)
    def _():
        out_ref[...] = acc_ref[...].astype(BF)


def layer_output(run, act, attended, w_down, down_parts):
    seg, inner = act.shape
    width = attended.shape[1]
    n = 4
    blk = inner // n
    dm, dt = down_parts
    return run(
        output_kernel, "output", (n,),
        [pl.BlockSpec((seg, blk), lambda i, s: (0, i)), whole((seg, width)),
         *down_rows(n, blk, width)],
        [fixed((seg, width), BF)], [pltpu.VMEM((seg, width), F32)],
        (act, attended, w_down, dm, dt), 2 * seg * width * inner)[0]


def feed_forward(run, second, cotangent, attended, w_up, up_parts, w_down, down_parts, bias_up,
                 gain, w_out, n_dp):
    seg, width = second.shape
    inner = bias_up.shape[1]
    n = 8
    blk = inner // n
    um, ut = up_parts
    dm, dt = down_parts
    uch, dch = inner // n_dp, width // n_dp
    pairs = blk // (2 * uch)
    col = lambda a: pl.BlockSpec((a.shape[0], blk), lambda i, s: (0, i))
    col3 = lambda a: pl.BlockSpec((1, a.shape[1], blk), lambda i, s: (0, 0, i))

    up_shape = part_shape(inner, width, n_dp, 1)
    down_shape = part_shape(width, inner, n_dp, n // 2)[:-1] + (blk,)
    up_out = lambda: out(up_shape, BF, (2, pairs, 1, uch, width // 2),
                         lambda i, s: (0, i, 0, 0, 0))
    down_out = lambda: out(down_shape, BF, (1, n_dp // 2, 1, dch, blk),
                           lambda i, s: (i // (n // 2), 0, i % (n // 2), 0, 0))
    full = (seg, width)
    return run(
        ffn_kernel, "feed_forward", (n,),
        [whole(full), whole(full), whole(full), col(w_up), col3(um), col3(ut),
         *down_rows(n, blk, width),
         pl.BlockSpec((1, blk), lambda i, s: (0, i)), whole((1, width)), whole((width, width))],
        [out((seg, inner), BF, (seg, blk), lambda i, s: (0, i)), fixed(full, F32),
         fixed(full, BF), up_out(), up_out(), down_out(),
         down_out(), out((1, inner), F32, (1, blk), lambda i, s: (0, i)), fixed((1, width), F32)],
        [pltpu.VMEM(full, BF), pltpu.VMEM((width, seg), BF), pltpu.VMEM((width, blk), BF),
         pltpu.VMEM((blk, width), BF), pltpu.VMEM(full, F32),
         pltpu.VMEM((pairs, 2, uch, seg), low_or_wide(uch)),
         pltpu.VMEM((n_dp // 2, 2, dch, seg), low_or_wide(dch))],
        (second, cotangent, attended, w_up, um, ut, w_down, dm, dt, bias_up, gain, w_out),
        12 * seg * width * inner)


def grads_kernel(s_ref, gk_ref, gv_ref, gp_ref, gq_ref, ga_ref, x_ref, tab_ref, ma_ref, mb_ref, w_ref,
                 keep_ref, send_ref, gg_ref, k_s, v_s, p_s, q_s, o_s, big, small):
    core = s_ref[CORE]
    rows = x_ref.shape[0]
    seg = gq_ref.shape[0]

    @pl.when(pl.program_id(0) == 0)
    def _():
        k_s[...] = by_core(big, gk_ref[...], core)
        v_s[...] = by_core(big, gv_ref[...], core)
        p_s[...] = by_core(big, gp_ref[...], core)
        q_s[...] = by_core(small, gq_ref[...].T, core)
        o_s[...] = by_core(small, ga_ref[...].astype(BF).T, core)

    x = x_ref[...]
    pairs, _, chunk, _ = small.shape
    n = pairs * chunk

    def both(tap, values):
        put(keep_ref.at[0, :, tap], send_ref.at[0, :, tap], values)

    def gain(values, m):
        turned = w_ref[m].T.astype(F32)
        whole_ = turned.reshape(pairs, 2, chunk, turned.shape[1])
        even, odd = whole_[:, 0].reshape(n, -1), whole_[:, 1].reshape(n, -1)
        first = jnp.where(core == 0, even, odd)
        last = jnp.where(core == 0, odd, even)
        return (jnp.sum(values[:n] * first, axis=0, keepdims=True)
                + jnp.sum(values[n:] * last, axis=0, keepdims=True))

    part = nn(k_s[...], x)
    both(0, part)
    total = gain(part, 1)
    part = nn(v_s[...], x)
    both(1, part)
    total += gain(part, 2)
    part = nn(q_s[...], x[rows - seg:])
    both(2, part)
    total += gain(part, 0)
    both(3, nn(p_s[...], tab_ref[...]))
    gg_ref[...] = total
    i, n = pl.program_id(0), pl.num_programs(0)

    @pl.when(i < n // 2)
    def _():
        both(4, nn(o_s[...], ma_ref[...]))

    @pl.when(i >= n // 2)
    def _():
        both(4, nn(o_s[...], mb_ref[...]))


def projection_grads(run, turned, gq, gatt, normed, table, mixed, w, n_dp, half):
    rows, width = normed.shape
    seg = gq.shape[0]
    blk = 256
    chunk = width // n_dp
    mid = width // 2
    gk, gv, gpos = turned
    count = mid // blk
    col = lambda r: pl.BlockSpec((r, blk), lambda i, s: (0, i))
    shape = lambda taps: part_shape(width, width, n_dp, taps, 2)
    half_of = lambda taps: out(shape(taps), BF, (1,) + shape(taps)[1:4] + (blk,),
                               lambda i, s: (i // count, 0, 0, 0, i % count))
    side = pl.BlockSpec((seg, blk), lambda i, s: (0, i % count))
    kind = low_or_wide(chunk)
    pairs = mid // (2 * chunk)
    return run(
        grads_kernel, "projection_grads", (width // blk,),
        [whole(gk.shape), whole(gk.shape), whole(gk.shape), whole(gq.shape),
         pl.BlockSpec((seg, mid), lambda i, s: (0, half)), col(rows), col(rows), side, side,
         pl.BlockSpec((3, blk, mid), lambda i, s: (0, i, half))],
        [half_of(5), half_of(5),
         out((1, width), F32, (1, blk), lambda i, s: (0, i))],
        [pltpu.VMEM((mid, rows), BF)] * 3 + [pltpu.VMEM((mid, seg), BF)] * 2
        + [pltpu.VMEM((pairs, 2, chunk, rows), kind), pltpu.VMEM((pairs, 2, chunk, seg), kind)],
        (gk, gv, gpos, gq, gatt, normed, table) + mixed + (w,),
        (3 * rows + 2 * seg) * width * width)


def grad_tokens_kernel(s_ref, ka_ref, kb_ref, va_ref, vb_ref, qa_ref, qb_ref, tok_ref, ga_ref,
                       w_ref, g_ref, gt_ref, acc_ref):
    i = pl.program_id(0)
    mid = w_ref.shape[2] // 2
    left, right = w_ref[0, :, :mid], w_ref[0, :, mid:]

    @pl.when(i == 0)
    def _():
        acc_ref[...] = nn(left, ka_ref[...]) + nn(right, kb_ref[...])

    @pl.when(i == 1)
    def _():
        acc_ref[...] += nn(left, va_ref[...]) + nn(right, vb_ref[...])

    @pl.when(i == 2)
    def _():
        total = (acc_ref[...] + nt(left, qa_ref[...]) + nt(right, qb_ref[...])).T
        unit, scale = norm_rows(tok_ref[...].astype(F32))
        gt_ref[...] = (ga_ref[...] + norm_back(total, g_ref[...], unit, scale)).astype(BF)


def grad_tokens(run, gk, gv, gq, tokens, grad_attended, w, gain):
    seg, width = tokens.shape
    rows = gk[0].shape[1]
    late = pl.BlockSpec((width // 2, seg), lambda i, s: (0, rows // seg - 1))
    side = whole((seg, width // 2))
    return run(
        grad_tokens_kernel, "grad_tokens", (3,),
        [late] * 4 + [side] * 2 + [whole((seg, width)), whole((seg, width)),
         pl.BlockSpec((1, width, width), lambda i, s: ((i + 1) % 3, 0, 0)), whole((1, width))],
        [fixed((seg, width), BF)], [pltpu.VMEM((width, seg), F32)],
        tuple(gk) + tuple(gv) + tuple(gq) + (tokens, grad_attended, w, gain),
        6 * seg * width * width)[0]


def squeeze_kernel(s_ref, gr_ref, o_ref, am_ref, at_ref, bm_ref, bt_ref, wk_ref, wv_ref, g_ref,
                   sq_ref, low_ref, k_ref, v_ref):
    y, core = s_ref[Y], s_ref[CORE]
    half, quarter = o_ref.shape[1], am_ref.shape[1]
    base = (1 - y) * half
    total = jnp.zeros(sq_ref.shape, F32)
    for t in range(3):
        m_ref, t_ref, n = (am_ref, at_ref, t) if t < 2 else (bm_ref, bt_ref, 0)
        at = lambda off, size: gr_ref[t, :, pl.ds(pl.multiple_of(off, quarter), size)]
        total += nn(at(y * half, half), o_ref[t])
        total += nn(at(base + core * quarter, quarter), m_ref[n])
        total += nn(at(base + (1 - core) * quarter, quarter), t_ref[n])
    sq_ref[...] = total
    low_ref[...] = total.astype(BF)
    unit = (norm_rows(total)[0] * g_ref[...]).astype(BF)
    k_ref[...] = nn(unit, wk_ref[0]).astype(BF)
    v_ref[...] = nn(unit, wv_ref[0]).astype(BF)


def key_value(width):
    return [pl.BlockSpec((1, width, width), lambda i, s: (1, 0, 0)),
            pl.BlockSpec((1, width, width), lambda i, s: (2, 0, 0))]


def squeeze(run, groups, own, a_parts, b_parts, w, gain):
    _, rows, width = groups.shape
    parts = a_parts + b_parts
    shape = (rows, width)
    return run(
        squeeze_kernel, "squeeze", (1,),
        [whole(groups.shape), whole(own.shape)] + [whole(p.shape) for p in parts]
        + [*key_value(width), whole((1, width))],
        [fixed(shape, F32), fixed(shape, BF), fixed(shape, BF), fixed(shape, BF)], [],
        (groups, own) + parts + (w, w, gain), 10 * rows * width * width)


def masked_softmax(scores, live):
    masked = jnp.where(live, scores, -1e30)
    weights = jnp.exp(masked - jnp.max(masked, axis=-1, keepdims=True))
    return weights * (1.0 / jnp.sum(weights, axis=-1, keepdims=True))


def recon_kernel(s_ref, *refs):
    dh = refs[0].shape[-1] // 2
    for n in range(2):
        cols = slice(n * dh, (n + 1) * dh)
        recon_head(s_ref, *[
            r.at[0, :, cols] if len(r.shape) == 3 else r.at[:, cols] for r in refs])


def recon_head(s_ref, pr_ref, ok_ref, ov_ref, ck_ref, cv_ref, gk_ref, gv_ref):
    seg_len = s_ref[SEG_LEN]
    count = seg_len // 3
    probe = pr_ref[...]
    seg, mem, comp = probe.shape[0], ok_ref.shape[0], ck_ref.shape[0]
    old_live = lax.broadcasted_iota(jnp.int32, (1, mem), 1) < 3 * count
    old = nn(masked_softmax(nt(probe, ok_ref[...]), old_live).astype(BF), ov_ref[...])
    live = lax.broadcasted_iota(jnp.int32, (1, comp), 1) < count
    probs = masked_softmax(nt(probe, ck_ref[...]), live)
    low = probs.astype(BF)
    gap = nn(low, cv_ref[...]) - old
    row = lax.broadcasted_iota(jnp.int32, gap.shape, 0)
    grad_out = (jnp.where(row < seg_len, gap, 0.0) * (2.0 / seg_len.astype(F32))).astype(BF)
    gv_ref[...] = tn(low, grad_out).astype(BF)
    weighted = probs * nt(grad_out, cv_ref[...])
    scores = (weighted - probs * jnp.sum(weighted, axis=-1, keepdims=True)).astype(BF)
    gk_ref[...] = tn(scores, probe).astype(BF)


def reconstruct(run, probe, kv, ck, cv, mem):
    seg, width = probe.shape
    rows = ck.shape[0]
    dh = 2 * width // H
    at = lambda n, b: pl.BlockSpec((n, dh), lambda h, s: (b, h))
    old = lambda m: pl.BlockSpec((1, mem, dh), lambda h, s: (m, 1, h))
    grads = lambda: out((rows, width), BF, (rows, dh), lambda h, s: (0, h))
    return run(
        recon_kernel, "reconstruct", (H // 2,),
        [at(seg, 0), old(0), old(1), at(rows, 0), at(rows, 0)], [grads(), grads()], [],
        (probe, kv, kv, ck, cv), 4 * seg * width * mem + 12 * seg * width * rows)


def grad_comp_kernel(s_ref, sq_ref, gk_ref, gv_ref, wk_ref, wv_ref, g_ref, gr_ref, k_ref, x_ref, low_ref, buf):
    @pl.when(pl.program_id(0) == 0)
    def _():
        grad = nt(gk_ref[...], wk_ref[0]) + nt(gv_ref[...], wv_ref[0])
        unit, scale = norm_rows(sq_ref[...])
        low = norm_back(grad, g_ref[...], unit, scale).astype(BF)
        low_ref[...] = by_core(buf, low.astype(F32).T, s_ref[CORE])

    part = nn(low_ref[...], gr_ref[0])
    width = part.shape[1] // 2
    for y in range(2):
        put(k_ref.at[y, :, 0], x_ref.at[y, :, 0], part[:, y * width:(y + 1) * width])


def grad_comp(run, squeezed, gk, gv, w, gain, groups, n_dp):
    taps, rows, width = groups.shape
    chunk = width // n_dp
    shape = part_shape(width, width, n_dp, taps)
    half = lambda: out(shape, BF, shape[:2] + (1,) + shape[3:], lambda i, s: (0, 0, i, 0, 0))
    here = whole((rows, width))
    return run(
        grad_comp_kernel, "grad_comp", (taps,),
        [here, here, here, *key_value(width), whole((1, width)),
         pl.BlockSpec((1, rows, width), lambda i, s: (i, 0, 0))],
        [half(), half()],
        [pltpu.VMEM((width, rows), BF), pltpu.VMEM((n_dp // 2, 2, chunk, rows), low_or_wide(chunk))],
        (squeezed, gk, gv, w, w, gain, groups), 10 * rows * width * width)


class Links:
    def __init__(self):
        self.dp = lax.axis_index("dp")
        self.y = lax.axis_index("fsdp")
        self.n_dp = lax.axis_size("dp")
        self.top = self.n_dp.bit_length() - 2

    def bit(self, axis):
        return self.y if axis == "y" else (self.dp >> axis) & 1

    def swap(self, value, axis):
        if axis == "y":
            return lax.ppermute(value, "fsdp", [(0, 1), (1, 0)])
        return lax.ppermute(value, "dp", [(i, i ^ (1 << axis)) for i in range(self.n_dp)])


class Part:
    def __init__(self, array, start):
        self.array, self.start = array, start


class Flow:
    def __init__(self, axes, order, rows):
        self.axes, self.order, self.rows = list(axes), list(order), rows

    def halves(self):
        axis = self.order[0]
        where = self.axes.index(axis)
        run = self.rows << (len(self.axes) - 1 - where)
        return axis, [(2 * p * run, (2 * p + 1) * run, p * run) for p in range(1 << where)], run

    def plan(self, take_in, give):
        axis, runs, length = self.halves()
        keep, recv = take_in(self.keep), take_in(self.recv.array)
        total = len(runs) * length
        held = give(fixed((total, self.keep.shape[1]), BF))
        place = give.send(axis, total, self)
        first = self.recv.start
        slot = Y if axis == "y" else BITS + axis - 1

        def kernel(s_ref, ins, outs, sends):
            bit = s_ref[slot]
            dst, base = sends(place)
            for low, high, to in runs:
                for side, ref, at in ((bit, outs[held], to), (1 - bit, dst, base + to)):
                    start = low + side * (high - low)
                    a = ins[keep][pl.ds(pl.multiple_of(start, 8), length)]
                    b = ins[recv][pl.ds(pl.multiple_of(first + start, 8), length)]
                    ref[at:at + length] = (a.astype(F32) + b.astype(F32)).astype(BF)

        def done(outs):
            self.keep = outs[held]
            self.axes.remove(axis)
            self.order.pop(0)

        return kernel, done


def cut_rows(rows, flows):
    if flows == 1:
        return (0, rows)
    unit = 16 if rows >= 96 else 8
    third = -(-rows // (3 * unit)) * unit
    return (0, third, 2 * third, rows)


class Source:
    def __init__(self, links, keep, send, axes, orders):
        self.axes, self.orders = axes, orders
        self.blocks = math.prod(keep.shape[:2])
        self.rows, self.cols = math.prod(keep.shape[2:4]), keep.shape[4]
        self.keep = keep.reshape(-1, self.cols)
        self.recv = links.swap(send, 0).reshape(-1, self.cols)
        self.cuts = cut_rows(self.rows, len(orders))

    def plan(self, take_in, give):
        keep, recv = take_in(self.keep), take_in(self.recv)
        rows, moves, self.flows = self.rows, [], []
        for c, order in enumerate(self.orders):
            lo, size = self.cuts[c], self.cuts[c + 1] - self.cuts[c]
            flow = Flow(self.axes, order, size)
            axis = order[0]
            where = self.axes.index(axis)
            post = 1 << (len(self.axes) - 1 - where)
            total = self.blocks // 2 * size
            held = give(fixed((total, self.cols), BF))
            moves.append((axis, where, post, lo, size, held, give.send(axis, total, flow)))
            self.flows.append(flow)

        def kernel(s_ref, ins, outs, sends):
            for axis, where, post, lo, size, held, place in moves:
                bit = s_ref[Y if axis == "y" else BITS + axis - 1]
                dst, base = sends(place)
                for p in range(1 << where):
                    for q in range(post):
                        to = (p * post + q) * size
                        for side, ref, at in ((bit, outs[held], to), (1 - bit, dst, base + to)):
                            start = ((2 * p + side) * post + q) * rows + lo
                            rng = pl.ds(pl.multiple_of(start, 8), size)
                            total = ins[keep][rng].astype(F32) + ins[recv][rng].astype(F32)
                            ref[at:at + size] = total.astype(BF)

        def done(outs):
            for flow, move in zip(self.flows, moves):
                flow.keep = outs[move[5]]
                flow.axes.remove(move[0])
                flow.order.pop(0)

        return kernel, done


class Join:
    def __init__(self, top, low, high):
        self.top, self.low, self.high = top, low, high
        self.rows = low.rows

    def plan(self, take_in, give):
        low, high = self.low, self.high
        refs = [take_in(low.keep), take_in(low.recv.array), take_in(high.keep),
                take_in(high.recv.array)]
        held = give(fixed(low.keep.shape, BF))
        place = give.send(self.top, self.rows, self)
        slot = BITS + self.top - 1
        rows = self.rows

        def kernel(s_ref, ins, outs, sends):
            dst, base = sends(place)
            part = lambda n, flow: (ins[refs[n]][...].astype(F32) + ins[refs[n + 1]][
                flow.recv.start:flow.recv.start + rows].astype(F32))
            a, b = part(0, low), part(2, high)
            upper = s_ref[slot] == 1
            outs[held][...] = jnp.where(upper, b, a).astype(BF)
            dst[base:base + rows] = jnp.where(upper, a, b).astype(BF)

        def done(outs):
            self.keep = outs[held]

        return kernel, done


class Small:
    def __init__(self, links, value, order):
        self.keep, self.order = value, list(order)
        self.recv = Part(links.swap(value, 0), 0)

    def plan(self, take_in, give):
        a, b = take_in(self.keep), take_in(self.recv.array)
        first, wide = self.recv.start, self.recv.array.dtype == F32
        rows, cols = self.keep.shape
        half = cols // 2
        total = give(fixed(self.keep.shape, F32))
        place = give.send(self.order.pop(0), 4 * rows, self) if self.order else None

        def kernel(s_ref, ins, outs, sends):
            if wide:
                came = ins[b][...]
            else:
                part = lambda n: ins[b][first + n:first + n + 2 * rows].astype(F32)
                both = part(0) + part(2 * rows)
                came = jnp.concatenate([both[:rows], both[rows:]], axis=1)
            added = ins[a][...] + came
            outs[total][...] = added
            if place is not None:
                dst, base = sends(place)
                stacked = jnp.concatenate([added[:, :half], added[:, half:]], axis=0)
                high = stacked.astype(BF)
                dst[base:base + 2 * rows] = high
                dst[base + 2 * rows:base + 4 * rows] = (stacked - high.astype(F32)).astype(BF)

        def done(outs):
            self.keep = outs[total]
            if place is None:
                self.recv = None

        return kernel, done


class Finish:
    def __init__(self, flows, shapes, write):
        self.flows, self.shapes, self.write = flows, shapes, write

    def plan(self, take_in, give):
        refs = [(take_in(f.keep), take_in(f.recv.array), f.recv.start, f.rows) for f in self.flows]
        results = [give(fixed(shape, F32)) for shape in self.shapes]

        def kernel(s_ref, ins, outs, sends):
            rows = jnp.concatenate(
                [ins[k][...].astype(F32) + ins[r][first:first + n].astype(F32)
                 for k, r, first, n in refs], axis=0)
            self.write(rows, *[outs[n] for n in results])

        def done(outs):
            self.result = [outs[n] for n in results]

        return kernel, done


class Carry:
    def __init__(self, *values):
        self.values = values

    def plan(self, take_in, give):
        anywhere = pl.BlockSpec(memory_space=pltpu.HBM)
        at = []
        for v in self.values:
            n = give((jax.ShapeDtypeStruct(v.shape, v.dtype), anywhere))
            give.aliases[take_in(v, anywhere)] = n
            at.append(n)

        def done(outs):
            self.values = [outs[n] for n in at]

        return lambda *refs: None, done


class Gives:
    def __init__(self):
        self.outs, self.sizes, self.takers, self.aliases = [], {}, [], {}

    def __call__(self, spec):
        self.outs.append(spec)
        return len(self.outs) - 1

    def send(self, axis, rows, taker):
        start = self.sizes.get(axis, 0)
        self.sizes[axis] = start + rows
        self.takers.append((axis, start, taker))
        return axis, start


def advance(run, links, *items):
    args, ins, index = [], [], {}

    def take_in(array, spec=None):
        if id(array) not in index:
            index[id(array)] = len(args)
            args.append(array)
            ins.append(spec or whole(array.shape))
        return index[id(array)]

    give = Gives()
    plans = [item.plan(take_in, give) for item in items]
    n_out = len(give.outs)
    axes = sorted(give.sizes, key=lambda a: 0 if a == "y" else a)
    outs = give.outs + [fixed((give.sizes[a], args[0].shape[-1]), BF) for a in axes]

    def kernel(s_ref, *refs):
        in_refs, out_refs = refs[:len(args)], refs[len(args):]
        sends = lambda place: (out_refs[n_out + axes.index(place[0])], place[1])
        for part, _ in plans:
            part(s_ref, in_refs, out_refs, sends)

    done = run(kernel, "add", (1,), ins, outs, [], args, 0,
               {1 + a: b for a, b in give.aliases.items()})
    came = {a: links.swap(done[n_out + n], a) for n, a in enumerate(axes)}
    for axis, start, taker in give.takers:
        taker.recv = Part(came[axis], start)
    for _, take in plans:
        take(done)


class Deal:
    def __init__(self, links, pairs, axes, orders, cuts):
        self.links, self.axes, self.orders, self.cuts = links, axes, orders, cuts
        self.keeps = [k for k, _ in pairs]
        self.sends = [x for _, x in pairs]
        self.rows, self.cols = self.keeps[0].shape[-2:]

    def start(self, sends):
        self.recvs = [self.links.swap(x, 0) for x in sends]

    def spans(self, c):
        lo, hi = self.cuts[c], self.cuts[c + 1]
        for n in range(2):
            a, b = max(lo - n * self.rows, 0), min(hi - n * self.rows, self.rows)
            if a < b:
                yield n, a, b

    def add(self, run, steps):
        n = len(self.axes)
        lead = (2,) * n
        rows, cols = self.rows, self.cols
        firsts = [self.axes.index(o[0]) for o in self.orders]
        others = [a for a in range(n) if a not in firsts]
        split = max(steps >> len(others), 1)
        width = cols // split
        count = 2 ** len(others) * split

        def at(i):
            places, rest = [0] * n, i // split
            for a in reversed(others):
                places[a] = rest % 2
                rest = rest // 2
            return places, i % split

        block = tuple(1 if a in others else 2 for a in range(n))

        def read(i, s):
            places, col = at(i)
            return (*places, 0, col)

        def write(first):
            def index(i, s):
                places, col = at(i)
                return (*places[:first], *places[first + 1:], 0, col)
            return index

        args = [a.reshape(lead + (rows, cols)) for a in self.keeps + self.recvs]
        ins = [pl.BlockSpec(block + (rows, width), read)] * 4
        outs, slots = [], []
        for c, first in enumerate(firsts):
            size = self.cuts[c + 1] - self.cuts[c]
            shape = lead[1:] + (size, cols)
            less = block[:first] + block[first + 1:]
            outs += [out(shape, BF, less + (size, width), write(first))] * 2
            axis = self.axes[first]
            slots.append(Y if axis == "y" else BITS + axis - 1)

        def kernel(s_ref, *refs):
            held, sent = refs[4::2], refs[5::2]

            for c, first in enumerate(firsts):
                bit = s_ref[slots[c]]
                row = 0
                for m, a, b in self.spans(c):
                    keep, recv = refs[m], refs[2 + m]
                    for dst, side in ((held[c], bit), (sent[c], 1 - bit)):
                        pick = tuple(side if d == first else slice(None) for d in range(n))
                        pick += (slice(a, b), slice(None))
                        total = keep[pick].astype(F32) + recv[pick].astype(F32)
                        to = (slice(None),) * (n - 1) + (slice(row, row + b - a),)
                        dst[to] = total.astype(BF)
                    row += b - a

        def take(*done):
            self.chains = []
            for c, order in enumerate(self.orders):
                axes = [a for a in self.axes if a != order[0]]
                recv = self.links.swap(done[2 * c + 1], order[0])
                size = self.cuts[c + 1] - self.cuts[c]
                flow = Flow(axes, order[1:], size)
                flow.keep, flow.recv = done[2 * c].reshape(-1, self.cols), Part(
                    recv.reshape(-1, self.cols), 0)
                self.chains.append(flow)

        done = run(kernel, "deal", (count,), ins, outs, [], args, 0)
        take(*done)


def angle_parts(rows, width):
    fine = 32
    frequency = jnp.exp(
        jnp.arange(0, width, 2).astype(F32) * (-math.log(10000.0) / width))
    coarse = (fine * (rows // fine - 1 - jnp.arange(rows // fine))).astype(F32)
    near = (fine - 1 - jnp.arange(fine)).astype(F32)
    a, b = coarse[:, None] * frequency[None, :], near[:, None] * frequency[None, :]
    return (jnp.sin(a), jnp.cos(a), jnp.sin(b), jnp.cos(b))


def body(tokens, memory, compressed, cotangent, seg_len, mem_fill, cmem_fill, w_qkv, w_rel, w_out,
         w_up, w_down, w_comp, norm_gain1, norm_gain2, bias_content, bias_position, bias_up):
    streams = tokens.shape[0]
    assert streams == 1
    links = Links()
    n_dp, top = links.n_dp, links.top
    seg, width = tokens.shape[1:]
    mem, comp = memory.shape[1], compressed.shape[1]
    start = comp + mem
    keys = start + seg
    squeezed_rows = mem // 3
    scale = (width // H) ** (-0.5)
    current, recent, distant = tokens[0], memory[0], compressed[0]
    seg_length = seg_len[0]
    core, x, z = links.bit(0), links.bit(1), links.bit(2)
    run = Steps(jnp.stack(
        [links.y, core, seg_length, mem_fill[0], cmem_fill[0], core * 2 + z,
         core * 2 + x] + [links.bit(n) for n in range(1, top + 1)]).astype(jnp.int32))
    gain1, gain2 = norm_gain1.reshape(1, -1), norm_gain2.reshape(1, -1)

    swap = links.swap
    near_parts = lambda value: (value, swap(value, 0))
    p_rel, p_a, p_b = pack_first(run, w_qkv, w_rel)
    rel, a, b = swap(p_rel, "y"), swap(p_a, "y"), swap(p_b, "y")
    normed = norm_hidden(run, distant, recent, current, gain1)
    rel_far = swap(rel, 2)
    p_c, p_d, p_up, p_down = pack_rest(run, w_out, w_up, w_down, w_comp)
    c, d = swap(p_c, "y"), swap(p_d, "y")
    table, groups = constants(run, recent, angle_parts(keys, width), squeezed_rows)
    rel, = order(run, (rel, rel_far, 2))
    rel_parts = near_parts(rel)
    a_far, b_far = swap(a, 2), swap(b, 1)
    pos = project_position(run, table, w_rel, rel_parts)
    a, b = order(run, (a, a_far, 2), (b, b_far, 1))
    a_parts, b_parts = near_parts(a), near_parts(b)
    p_up, p_down = follow(run, p_up, p_down)
    up, down = swap(p_up, "y"), swap(p_down, "y")
    kv, qc, qp, probe, w_full = project_qkv(
        run, normed, w_qkv, a_parts, b_parts, bias_content, bias_position, seg, scale)
    c, d = follow(run, c, d)
    c_far, d_far = swap(c, 2), swap(d, 1)
    p0, m0 = attention(run, qc, qp, kv, pos, comp, mem, 0)
    c, d = order(run, (c, c_far, 2), (d, d_far, 1))
    c_parts, d_parts = near_parts(c), near_parts(d)
    p1, m1 = attention(run, qc, qp, kv, pos, comp, mem, 1)
    up, down = follow(run, up, down)
    up_far, down_far = swap(up, 2), swap(down, 1)
    squeezed, squeezed_low, ck, cv = squeeze(run, groups, w_comp, c_parts, d_parts, w_full, gain1)
    gck, gcv = reconstruct(run, probe, kv, ck, cv, mem)
    up, down = order(run, (up, up_far, 2), (down, down_far, 1))
    up_parts, down_parts = near_parts(up), near_parts(down)
    comp_keep, comp_send = grad_comp(run, squeezed, gck, gcv, w_full, gain1, groups, n_dp)

    attended, second, w_out_full = mix_out(run, current, (m0, m1), w_out, d_parts, gain2)
    far = list(range(3, top + 1))
    names, under = ["y"] + list(range(top, 0, -1)), ["y"] + list(range(top - 1, 0, -1))
    turns = lambda rest: [[1, "y", 2] + rest, ["y", 2, 1] + rest, [2, 1, "y"] + rest]
    of_comp = Source(links, comp_keep, comp_send, names, [[2, 1, "y"] + far])
    advance(run, links, of_comp)
    (act, grad_attended, grad_mix, up_keep, up_send, down_keep, down_send, sum_bias, sum_gain2
     ) = feed_forward(run, second, cotangent[0], attended, w_up, up_parts, w_down, down_parts,
                      bias_up.reshape(1, -1), gain2, w_out_full, n_dp)
    inner = bias_up.shape[0]
    rows, half = inner // n_dp, width // 2
    flat = lambda a: a.reshape(2, n_dp // 2, rows, half)
    third = max(2 * rows * 11 // 32 // 16 * 16, 8)
    deal = Deal(
        links, [(flat(up_keep), flat(up_send)), (flat(down_keep), flat(down_send))], names,
        turns(far), (0, third, 2 * third, 2 * rows))
    carry = Carry(*deal.sends)
    advance(run, links, *of_comp.flows, carry)
    deal.start(carry.values)

    chunk = width // n_dp

    def write_ffn(rows, up, down):
        size = rows.shape[0] // 2
        up[...] = rows[:size].T
        for n in range(inner // (2 * half)):
            down[n * half:(n + 1) * half] = rows[size + n * chunk:size + (n + 1) * chunk].T

    def write_comp(rows, grad):
        for t in range(3):
            grad[t] = rows[t * chunk:(t + 1) * chunk].T

    def write_rest(rows, qkv, rel, ow):
        tap = lambda t: rows[t * chunk:(t + 1) * chunk].T
        qkv[0], qkv[1], qkv[2] = tap(2), tap(0), tap(1)
        rel[...], ow[...] = tap(3), tap(4)

    waiting = lambda *flows: [f for f in flows if f.order]
    back = functools.partial(attention_back, run, (p0, p1), (m0, m1), grad_mix, qc, qp, kv, pos, start, scale)
    grads = lambda turned, gq, half: projection_grads(
        run, turned, gq, grad_attended, normed, table, (m0, m1), w_full, n_dp, half)
    gq0, gk0, gv0, gpos0, content0, position0 = back(0)
    advance(run, links, *of_comp.flows)
    deal.add(run, 4)
    keep_0, send_0, gain_0 = grads((gk0, gv0, gpos0), gq0, 0)
    gq1, gk1, gv1, gpos1, content1, position1 = back(1)
    carry = Carry(send_0)
    advance(run, links, *deal.chains, *of_comp.flows, carry)
    early = Source(links, keep_0, carry.values[0], under, turns(far[:-1]))
    keep_1, send_1, gain_1 = grads((gk1, gv1, gpos1), gq1, 1)
    carry = Carry(send_1)
    comp_end = Finish(of_comp.flows, [(3, half, chunk)], write_comp)
    comp_left = list(waiting(*of_comp.flows))
    held = [Carry(f.recv.array) for f in of_comp.flows if not comp_left]
    advance(run, links, *deal.chains, *comp_left, early, carry, *held)
    for flow, kept in zip(of_comp.flows, held):
        flow.recv = Part(kept.values[0], flow.recv.start)
    late = Source(links, keep_1, carry.values[0], under, turns(far[:-1]))
    row = lambda a, b: jnp.concatenate([a, b], axis=1)
    small = Small(links, jnp.concatenate(
        [(gain_0 + gain_1) / gain1, sum_gain2, row(content0, content1), row(position0, position1),
         sum_bias.reshape(-1, width)], axis=0), ["y", 1, 2] + far)
    new_memory = lax.dynamic_slice_in_dim(
        jnp.concatenate([recent, current], axis=0), seg_length, mem, 0)
    new_compressed = lax.dynamic_slice_in_dim(
        jnp.concatenate([distant, squeezed_low[:squeezed_rows]], axis=0), seg_length // 3, comp, 0)
    output = layer_output(run, act, attended, w_down, down_parts)
    advance(run, links, *waiting(*deal.chains, *comp_left), late, small)
    grad_rows = grad_tokens(run, (gk0, gk1), (gv0, gv1), (gq0, gq1), current, grad_attended,
                            w_full, gain1)
    while any(f.order for f in late.flows):
        advance(run, links, *waiting(*deal.chains, *comp_left, *early.flows, *late.flows),
                small)
        if not comp_left and comp_end.flows[0].recv is not None and not hasattr(comp_end, 'result'):
            advance(run, links, comp_end)
    ends = [Join(top, a, b) for a, b in zip(early.flows, late.flows)]
    of_ffn = Finish(deal.chains, [(half, rows), (inner // 2, chunk)], write_ffn)
    advance(run, links, *ends, small, of_ffn, *([comp_end] if comp_left else []))
    rest = Finish(ends, [(3, half, chunk), (half, chunk), (half, chunk)], write_rest)
    advance(run, links, rest, small)
    assert small.recv is None
    (grad_up, grad_down), (grad_comp_,) = of_ffn.result, comp_end.result
    grad_qkv, grad_rel, grad_out = rest.result

    at = links.dp * 2 + links.y
    each, each_up = width // (2 * n_dp), bias_up.shape[0] // (2 * n_dp)
    vec = lax.dynamic_slice(small.keep[:4], (0, at * each), (4, each))
    vec_up = lax.dynamic_slice_in_dim(small.keep[4:].reshape(-1), at * each_up, each_up)
    return (output[None], grad_rows[None], new_memory[None], new_compressed[None],
            grad_qkv, grad_rel, grad_out,
            grad_up, grad_down, grad_comp_, vec[0], vec[1], vec[2], vec[3], vec_up)


def solution(mesh):
    rows = P(("dp", "fsdp"), None, None)
    one = P(("dp", "fsdp"))
    return jax.shard_map(
        body,
        mesh=mesh,
        in_specs=(rows, rows, rows, rows, one, one, one, P(None, "fsdp", None), P("fsdp", None),
                  P("fsdp", None), P("fsdp", None), P("fsdp", None), P(None, "fsdp", None), P(),
                  P(), P(), P(), P()),
        out_specs=(rows, rows, rows, rows, P(None, "fsdp", "dp"), P("fsdp", "dp"),
                   P("fsdp", "dp"), P("fsdp", "dp"), P("fsdp", "dp"), P(None, "fsdp", "dp"), one,
                   one, one, one, one),
        check_vma=False,
    )
```

```python
import functools
import math

import jax
import jax.numpy as jnp
from jax import lax
from jax.experimental import pallas as pl
from jax.experimental.pallas import tpu as pltpu
from jax.sharding import PartitionSpec as P

H = 8
BF = jnp.bfloat16
F32 = jnp.float32
VMEM = 60 * 1024 * 1024
GELU_C = math.sqrt(2.0 / math.pi)
COST = 0.0001
TEMPORARIES = 32 * 1024 * 1024
Y, CORE, SEG_LEN, MEM_LIVE, COMP_LIVE, PIECE_A, PIECE_B, BITS = range(8)


def nn(a, b):
    return lax.dot_general(a, b, (((1,), (0,)), ((), ())), preferred_element_type=F32)


def nt(a, b):
    return lax.dot_general(a, b, (((1,), (1,)), ((), ())), preferred_element_type=F32)


def tn(a, b):
    return lax.dot_general(a, b, (((0,), (0,)), ((), ())), preferred_element_type=F32)


class Steps:
    def __init__(self, scal):
        self.scal = scal
        self.token = None

    def __call__(self, kernel, name, grid, ins, outs, scratch, args, flops, aliases={}):
        before = [] if self.token is None else [self.token]
        n_in, n_out, extra = len(ins), len(outs), len(before)

        def ordered_kernel(s_ref, *refs):
            rest = refs[n_in + extra:]
            kernel(s_ref, *refs[:n_in], *rest[:n_out], *rest[n_out + 1:])

        anywhere = pl.BlockSpec(memory_space=pltpu.HBM)
        moved = sum(a.size * a.dtype.itemsize for a in args)
        need = TEMPORARIES
        for (block, array) in list(zip(ins, args)) + [(b, s) for s, b in outs]:
            if block.block_shape is not None:
                need += 2 * math.prod(block.block_shape) * array.dtype.itemsize
        for ref in (r for r in scratch if 'sem' not in str(r.dtype)):
            need += math.prod(ref.shape) * jnp.dtype(ref.dtype).itemsize
        done = pl.pallas_call(
            ordered_kernel,
            name=name,
            out_shape=[s for s, _ in outs] + [jax.ShapeDtypeStruct((8, 128), F32)],
            grid_spec=pltpu.PrefetchScalarGridSpec(
                num_scalar_prefetch=1,
                grid=grid,
                in_specs=list(ins) + [anywhere] * extra,
                out_specs=[b for _, b in outs] + [anywhere],
                scratch_shapes=scratch,
            ),
            compiler_params=pltpu.CompilerParams(
                vmem_limit_bytes=min(need, VMEM), dimension_semantics=("arbitrary",) * len(grid)
            ),
            input_output_aliases=aliases,
            cost_estimate=pl.CostEstimate(
                flops=int(flops * COST), bytes_accessed=int(moved * COST), transcendentals=0),
        )(self.scal, *args, *before)
        *done, self.token = done
        return done


def follow(run, *values):
    anywhere = pl.BlockSpec(memory_space=pltpu.HBM)
    return run(
        lambda *refs: None, "follow", (1,), [anywhere] * len(values),
        [(jax.ShapeDtypeStruct(v.shape, v.dtype), anywhere) for v in values], [], values, 0,
        {n + 1: n for n in range(len(values))})


def whole(shape):
    return pl.BlockSpec(shape, lambda i, s: (0,) * len(shape))


def out(shape, dtype, block, index):
    return (jax.ShapeDtypeStruct(shape, dtype), pl.BlockSpec(block, index))


def fixed(shape, dtype):
    return out(shape, dtype, shape, lambda i, s: (0,) * len(shape))


def norm_rows(rows):
    centred = rows - jnp.mean(rows, axis=-1, keepdims=True)
    spread = jnp.mean(centred * centred, axis=-1, keepdims=True)
    scale = lax.rsqrt(spread + 1e-05)
    return centred * scale, scale


def norm_back(grad, gain, unit, scale):
    g = grad * gain
    inner = jnp.mean(g * unit, axis=-1, keepdims=True)
    return scale * (g - jnp.mean(g, axis=-1, keepdims=True) - unit * inner)


def place(dst, s_ref, own, mine, theirs, cols=slice(None)):
    half, quarter = own.shape[-2], mine.shape[-2]
    y, core = s_ref[Y], s_ref[CORE]
    base = (1 - y) * half
    at = lambda start, size: pl.ds(pl.multiple_of(start, quarter), size)
    dst[at(y * half, half), cols] = own[:, cols]
    dst[at(base + core * quarter, quarter), cols] = mine[...]
    dst[at(base + (1 - core) * quarter, quarter), cols] = theirs[...]


def pack_first_kernel(s_ref, rel, k, v, qa, qb, o_rel, o_a, o_b):
    width = rel.shape[-1]
    o_rel[...] = rel[...]
    o_a[0, :, :width] = k[0, 0]
    o_a[0, :, width:] = qa[0, 0]
    o_b[0, :, :width] = v[0, 0]
    o_b[0, :, width:] = qb[0, 0]


def pack_rest_kernel(s_ref, c0, c1, c2, ow, up, down, o_c, o_d, o_up, o_down):
    o_c[0] = c0[0, 0]
    o_c[1] = c1[0, 0]
    o_d[0] = c2[0, 0]
    o_d[1] = ow[0]
    o_up[...] = up[...]
    o_down[...] = down[...]


def quarters(a):
    lead = a.shape[:-2]
    return a.reshape(lead + (4, a.shape[-2] // 4, a.shape[-1]))


def part_of(a, where, n=0, cols=1, c=0):
    block = (1,) * (a.ndim - 2) + (a.shape[-2], a.shape[-1] // cols)
    if a.ndim == 3:
        return pl.BlockSpec(block, lambda i, s: (s[where], 0, c))
    return pl.BlockSpec(block, lambda i, s: (n, s[where], 0, c))


def pack_first(run, w_qkv, w_rel):
    qkv, rel = quarters(w_qkv), quarters(w_rel)
    part, width = rel.shape[1:]
    return run(
        pack_first_kernel, "pack_first", (1,),
        [part_of(rel, PIECE_A), part_of(qkv, PIECE_A, 1), part_of(qkv, PIECE_B, 2),
         part_of(qkv, PIECE_A, 0, 2, 0), part_of(qkv, PIECE_B, 0, 2, 1)],
        [fixed((1, part, width), BF), fixed((1, part, width * 3 // 2), BF),
         fixed((1, part, width * 3 // 2), BF)],
        [], (rel, qkv, qkv, qkv, qkv), 0)


def pack_rest(run, w_out, w_up, w_down, w_comp):
    comp, ow, up, down = quarters(w_comp), quarters(w_out), quarters(w_up), quarters(w_down)
    part, width = ow.shape[1:]
    return run(
        pack_rest_kernel, "pack_rest", (1,),
        [part_of(comp, PIECE_A, 0), part_of(comp, PIECE_A, 1), part_of(comp, PIECE_B, 2),
         part_of(ow, PIECE_B), part_of(up, PIECE_A), part_of(down, PIECE_B)],
        [fixed((2, part, width), BF), fixed((2, part, width), BF),
         fixed((1,) + up.shape[1:], BF), fixed((1,) + down.shape[1:], BF)],
        [], (comp, comp, comp, ow, up, down), 0)


def order_kernel(s_ref, *refs, slots):
    n = len(slots)
    outs, sem = refs[2 * n:3 * n], refs[3 * n]
    copies = []
    for c, slot in enumerate(slots):
        bit = s_ref[slot]
        copies += [
            pltpu.make_async_copy(refs[c], outs[c].at[:, bit], sem.at[2 * c]),
            pltpu.make_async_copy(refs[n + c], outs[c].at[:, 1 - bit], sem.at[2 * c + 1])]
    for copy in copies:
        copy.start()
    for copy in copies:
        copy.wait()


def order(run, *pieces):
    args = [p[0] for p in pieces] + [p[1] for p in pieces]
    shapes = [(p[0].shape[0], 2) + p[0].shape[1:] for p in pieces]
    anywhere = pl.BlockSpec(memory_space=pltpu.HBM)
    done = run(
        functools.partial(order_kernel, slots=tuple(BITS + p[2] - 1 for p in pieces)), "order", (1,),
        [anywhere] * len(args), [(jax.ShapeDtypeStruct(s, BF), anywhere) for s in shapes],
        [pltpu.SemaphoreType.DMA((len(args),))], args, 0)
    return [d.reshape(s[0], 2 * s[2], s[3]) for d, s in zip(done, shapes)]


def normed_kernel(s_ref, d_ref, m_ref, t_ref, g_ref, x_ref):
    i = pl.program_id(0)
    for n, ref in enumerate((d_ref, m_ref, t_ref)):
        @pl.when(i // 2 == n)
        def _(ref=ref):
            x_ref[...] = (norm_rows(ref[...].astype(F32))[0] * g_ref[...]).astype(BF)


def norm_hidden(run, distant, recent, current, gain):
    mem, width = recent.shape
    blk = mem // 2
    part = lambda n: pl.BlockSpec((blk, width), lambda i, s: (jnp.clip(i - 2 * n, 0, 1), 0))
    return run(
        normed_kernel, "norm_hidden", (6,),
        [part(0), part(1), part(2), whole(gain.shape)],
        [out((3 * mem, width), BF, (blk, width), lambda i, s: (i, 0))],
        [], (distant, recent, current, gain), 0)[0]


def constants_kernel(s_ref, m_ref, sa_ref, ca_ref, sb_ref, cb_ref, tab_ref, gr_ref, wide_ref,
                     *, groups):
    i = pl.program_id(0)
    blk, width = tab_ref.shape
    half = width // 2
    fine = sb_ref.shape[0]
    for n in range(blk // fine):
        rows = slice(n * fine, (n + 1) * fine)
        a = i * (blk // fine) + n
        sa, ca = sa_ref[pl.ds(a, 1)], ca_ref[pl.ds(a, 1)]
        tab_ref[rows, :half] = (sa * cb_ref[...] + ca * sb_ref[...]).astype(BF)
        tab_ref[rows, half:] = (ca * cb_ref[...] - sa * sb_ref[...]).astype(BF)

    @pl.when(i == 0)
    def _():
        mem = m_ref.shape[0]
        lanes = wide_ref.shape[2]
        count = gr_ref.shape[1]
        live = lax.broadcasted_iota(jnp.int32, (count, 1), 0) < groups
        for n in range(width // lanes):
            cols = slice(n * lanes, (n + 1) * lanes)
            wide_ref[n, :mem] = m_ref[:, cols].astype(F32)
            wide_ref[n, mem:] = jnp.zeros((wide_ref.shape[1] - mem, lanes), F32)
            for t in range(3):
                rows = jnp.where(live, wide_ref[n, pl.ds(t, count, stride=3)], 0.0)
                gr_ref[t, :, cols] = rows.astype(BF)


def constants(run, recent, angles, groups):
    mem, width = recent.shape
    keys = 3 * mem
    blk = 512
    padded = groups + (-groups) % 64
    ins = (recent,) + angles
    return run(
        functools.partial(constants_kernel, groups=groups), "constants", (keys // blk,),
        [whole(a.shape) for a in ins],
        [out((keys, width), BF, (blk, width), lambda i, s: (i, 0)),
         fixed((3, padded, width), BF)],
        [pltpu.VMEM((width // 128, 3 * padded, 128), F32)], ins, 0)


def qkv_kernel(s_ref, x_ref, o_ref, am_ref, at_ref, bm_ref, bt_ref, bc_ref, bp_ref, kv_ref,
               qc_ref, qp_ref, pr_ref, w_ref, *, scale):
    i = pl.program_id(0)
    rows, width = x_ref.shape
    seg = qc_ref.shape[0]
    blk = 256
    lo, hi = slice(0, width // 2), slice(width // 2, width)
    own, dst = o_ref.at[0], w_ref.at[0]

    @pl.when(i == 0)
    def _():
        place(dst, s_ref, own, am_ref.at[0, :, :width], at_ref.at[0, :, :width])

    @pl.when(i == 1)
    def _():
        place(dst, s_ref, own, bm_ref.at[0, :, :width], bt_ref.at[0, :, :width])

    @pl.when(i == 2)
    def _():
        place(dst, s_ref, own, am_ref.at[0, :, width:], at_ref.at[0, :, width:], lo)
        place(dst, s_ref, own, bm_ref.at[0, :, width:], bt_ref.at[0, :, width:], hi)

    @pl.when(i < 2)
    def _():
        def some(n):
            at = slice(n * blk, (n + 1) * blk)
            kv_ref[0, at] = nn(x_ref[at], dst[...]).astype(BF)

        for n in range(rows // blk):
            some(n)

    @pl.when(i == 2)
    def _():
        for n in range(seg // blk):
            at = slice(n * blk, (n + 1) * blk)
            q = nn(x_ref[rows - seg + n * blk:rows - seg + (n + 1) * blk], dst[...])
            qc_ref[at] = ((q + bc_ref[...]) * scale).astype(BF)
            qp_ref[at] = ((q + bp_ref[...]) * scale).astype(BF)
            pr_ref[at] = (q * scale).astype(BF)


def project_qkv(run, normed, w_qkv, a_parts, b_parts, bias_content, bias_position, seg, scale):
    rows, width = normed.shape
    turn = lambda i, s: ((i + 1) % 3, 0, 0)
    parts = a_parts + b_parts
    return run(
        functools.partial(qkv_kernel, scale=scale), "project_qkv", (3,),
        [whole((rows, width)), pl.BlockSpec((1, width // 2, width), turn)]
        + [whole(p.shape) for p in parts] + [whole((1, width)), whole((1, width))],
        [out((2, rows, width), BF, (1, rows, width), lambda i, s: (jnp.minimum(i, 1), 0, 0)),
         fixed((seg, width), BF), fixed((seg, width), BF), fixed((seg, width), BF),
         out((3, width, width), BF, (1, width, width), turn)],
        [], (normed, w_qkv) + parts + (bias_content.reshape(1, -1), bias_position.reshape(1, -1)),
        2 * (2 * rows + seg) * width * width)


def position_kernel(s_ref, x_ref, o_ref, m_ref, t_ref, p_ref, w_ref):
    @pl.when(pl.program_id(0) == 0)
    def _():
        place(w_ref, s_ref, o_ref, m_ref.at[0], t_ref.at[0])

    p_ref[...] = nn(x_ref[...], w_ref[...]).astype(BF)


def project_position(run, table, own, parts):
    rows, width = table.shape
    blk = 512
    return run(
        position_kernel, "project_position", (rows // blk,),
        [pl.BlockSpec((blk, width), lambda i, s: (i, 0)), whole(own.shape)]
        + [whole(p.shape) for p in parts],
        [out((rows, width), BF, (blk, width), lambda i, s: (i, 0))],
        [pltpu.VMEM((width, width), BF)], (table, own) + parts,
        2 * rows * width * width)[0]


RB = 256


def flip_matrix():
    return (lax.broadcasted_iota(jnp.int32, (RB, RB), 0)
            + lax.broadcasted_iota(jnp.int32, (RB, RB), 1) == RB - 1).astype(BF)


def attention_kernel(s_ref, qc_ref, qp_ref, k_ref, v_ref, pos_ref, p_ref, mix_ref, bias_ref,
                     *, comp, mem):
    seg, keys = qc_ref.shape[0], k_ref.shape[1]
    start = comp + mem

    @pl.when(pl.program_id(0) == 0)
    def _():
        mem_live, comp_live = s_ref[MEM_LIVE], s_ref[COMP_LIVE]
        col = lax.broadcasted_iota(jnp.int32, bias_ref.shape, 1)
        row = lax.broadcasted_iota(jnp.int32, bias_ref.shape, 0)
        live = ((col >= comp - comp_live) & (col < comp)) | (
            (col >= start - mem_live) & (col - start <= row))
        bias_ref[...] = jnp.where(live, 0.0, -1e30)

    for r in range(seg // RB):
        width = start + RB * (r + 1)
        rows = slice(r * RB, (r + 1) * RB)
        content = nt(qc_ref[rows], k_ref[0, :width])
        rel = nt(qp_ref[rows], pos_ref[keys - width:])
        rel = pltpu.roll(rel, width - RB + 1, 1, stride=1, stride_axis=0)
        masked = content + rel + bias_ref[rows, :width]
        top = jnp.max(masked, axis=-1, keepdims=True)
        weights = jnp.exp(masked - top)
        probs = (weights * (1.0 / jnp.sum(weights, axis=-1, keepdims=True))).astype(BF)
        mix_ref[rows] = nn(probs, v_ref[0, :width]).astype(BF)
        p_ref[0, rows, :width] = probs
        if width < keys:
            p_ref[0, rows, width:] = jnp.zeros((RB, keys - width), BF)


def attention(run, qc, qp, kv, pos, comp, mem, half):
    seg, width = qc.shape
    keys = kv.shape[1]
    dh = width // H
    n = H // 2
    first = half * n
    q_spec = pl.BlockSpec((seg, dh), lambda h, s: (0, h + first))
    of = lambda m: pl.BlockSpec((1, keys, dh), lambda h, s: (m, 0, h + first))
    return run(
        functools.partial(attention_kernel, comp=comp, mem=mem), "attention", (n,),
        [q_spec, q_spec, of(0), of(1), pl.BlockSpec((keys, dh), lambda h, s: (0, h + first))],
        [out((n, seg, keys), BF, (1, seg, keys), lambda h, s: (h, 0, 0)),
         out((seg, width // 2), BF, (seg, dh), lambda h, s: (0, h))],
        [pltpu.VMEM((seg, keys), F32)], (qc, qp, kv, kv, pos), 16 * seg * keys * width)


def attention_back_kernel(s_ref, p_ref, gm_ref, mix_ref, qc_ref, qp_ref, k_ref, v_ref, pos_ref, gq_ref,
                          gk_ref, gv_ref, gp_ref, gc_ref, gb_ref, gs_ref, sh_ref, rev_ref,
                          *, start, scale):
    seg, keys = qc_ref.shape[0], k_ref.shape[1]
    flip = flip_matrix()
    sum_c = jnp.zeros((1, gc_ref.shape[1]), F32)
    sum_p = jnp.zeros((1, gc_ref.shape[1]), F32)
    for r in range(seg // RB):
        width = start + RB * (r + 1)
        rows = slice(r * RB, (r + 1) * RB)
        rev_ref[rows] = nn(flip, qp_ref[rows]).astype(BF)
        grad = gm_ref[rows]
        total = jnp.sum(
            grad.astype(F32) * mix_ref[rows].astype(F32), axis=-1, keepdims=True)
        probs = p_ref[0, rows, :width].astype(F32)
        scores = (probs * (nt(grad, v_ref[0, :width]) - total)).astype(BF)
        moved = pltpu.roll(nn(flip, scores), 0, 1, stride=1, stride_axis=0).astype(BF)
        gs_ref[rows, :width] = scores
        sh_ref[rows, keys - width:] = moved
        if width < keys:
            gs_ref[rows, width:] = jnp.zeros((RB, keys - width), BF)
            sh_ref[rows, : keys - width] = jnp.zeros((RB, keys - width), BF)
        grad_c = nn(scores, k_ref[0, :width])
        turned = nn(moved, pos_ref[keys - width:])
        high = turned.astype(BF)
        grad_p = nn(flip, high) + nn(flip, (turned - high.astype(F32)).astype(BF))
        sum_c += jnp.sum(grad_c, axis=0, keepdims=True)
        sum_p += jnp.sum(turned, axis=0, keepdims=True)
        gq_ref[rows] = ((grad_c + grad_p) * scale).astype(BF)
    gc_ref[...] = sum_c * scale
    gb_ref[...] = sum_p * scale
    gv_ref[...] = tn(gm_ref[...], p_ref[0]).astype(BF)
    gk_ref[...] = tn(qc_ref[...], gs_ref[...]).astype(BF)
    gp_ref[...] = tn(rev_ref[...], sh_ref[...]).astype(BF)


def attention_back(run, probs, mixed, gm, qc, qp, kv, pos, start, scale, half):
    seg, width = qc.shape
    keys = kv.shape[1]
    dh = width // H
    n = H // 2
    first = half * n
    q_spec = pl.BlockSpec((seg, dh), lambda h, s: (0, h + first))
    of = lambda m: pl.BlockSpec((1, keys, dh), lambda h, s: (m, 0, h + first))
    turned = lambda: out((width // 2, keys), BF, (dh, keys), lambda h, s: (h, 0))
    sums = lambda: out((1, width // 2), F32, (1, dh), lambda h, s: (0, h))
    big = pltpu.VMEM((seg, keys), BF)
    return run(
        functools.partial(attention_back_kernel, start=start, scale=scale), "attention_back", (n,),
        [pl.BlockSpec((1, seg, keys), lambda h, s: (h, 0, 0)), q_spec,
         pl.BlockSpec((seg, dh), lambda h, s: (0, h)), q_spec, q_spec,
         of(0), of(1), pl.BlockSpec((keys, dh), lambda h, s: (0, h + first))],
        [out((seg, width // 2), BF, (seg, dh), lambda h, s: (0, h)), turned(), turned(), turned(),
         sums(), sums()],
        [big, big, pltpu.VMEM((seg, dh), BF)], (probs[half], gm, mixed[half], qc, qp, kv, kv, pos),
        12 * seg * keys * width)


def mixed_kernel(s_ref, tok_ref, a_ref, b_ref, o_ref, m_ref, t_ref, g_ref, att_ref, sec_ref, w_ref):
    @pl.when(pl.program_id(0) == 0)
    def _():
        place(w_ref, s_ref, o_ref, m_ref.at[1], t_ref.at[1])

    mid = a_ref.shape[1]
    attended = (tok_ref[...].astype(F32) + nn(a_ref[...], w_ref[:mid])
                + nn(b_ref[...], w_ref[mid:]))
    att_ref[...] = attended
    sec_ref[...] = (norm_rows(attended)[0] * g_ref[...]).astype(BF)


def mix_out(run, tokens, mixed, own, parts, gain):
    seg, width = tokens.shape
    blk = 256
    row = pl.BlockSpec((blk, width), lambda i, s: (i, 0))
    side = pl.BlockSpec((blk, width // 2), lambda i, s: (i, 0))
    return run(
        mixed_kernel, "mix_out", (seg // blk,),
        [row, side, side, whole(own.shape)] + [whole(p.shape) for p in parts] + [whole((1, width))],
        [out((seg, width), F32, (blk, width), lambda i, s: (i, 0)),
         out((seg, width), BF, (blk, width), lambda i, s: (i, 0)),
         fixed((width, width), BF)],
        [], (tokens,) + mixed + (own,) + parts + (gain,), 2 * seg * width * width)


def part_shape(rows, cols, n_dp, taps, cut=1):
    return (2, n_dp // (2 * cut), taps, rows // n_dp, cols // 2)


def low_or_wide(chunk):
    return BF if chunk % 16 == 0 else F32


def by_core(buf, values, core):
    pairs, _, chunk, cols = buf.shape
    buf[...] = values.astype(buf.dtype).reshape(pairs, 2, chunk, cols)
    pick = lambda c: buf[:, c].reshape(pairs * chunk, cols)
    return jnp.concatenate([pick(core), pick(1 - core)], axis=0).astype(BF)


def put(keep, send, values):
    half = values.shape[0] // 2
    shape = keep.shape[:-1] + (values.shape[1],)
    keep[...] = values[:half].reshape(shape).astype(BF)
    send[...] = values[half:].reshape(shape).astype(BF)


def ffn_kernel(s_ref, sec_ref, cot_ref, att_ref, uo_ref, um_ref, ut_ref, do_ref, dm_ref, dt_ref,
               b_ref, g_ref, wo_ref, act_ref, gatt_ref, gm_ref, uk_ref, us_ref, dk_ref, ds_ref,
               gb_ref, gg_ref, gout_ref, turn_ref, wu_ref, wd_ref, gsec_ref, ubuf, dbuf):
    i, n = pl.program_id(0), pl.num_programs(0)
    y, core = s_ref[Y], s_ref[CORE]

    @pl.when(i == 0)
    def _():
        row = lax.broadcasted_iota(jnp.int32, cot_ref.shape, 0)
        live = jnp.where(row < s_ref[SEG_LEN], cot_ref[...], jnp.zeros((), BF))
        gout_ref[...] = live
        turn_ref[...] = by_core(dbuf, live.T, core)
        gsec_ref[...] = jnp.zeros_like(gsec_ref)

    place(wu_ref, s_ref, uo_ref, um_ref.at[0], ut_ref.at[0])
    half = i // (n // 2)
    side = (i % (n // 2)) // (n // 4)

    @pl.when(half == y)
    def _():
        wd_ref[...] = do_ref[...]

    @pl.when((half != y) & (side == core))
    def _():
        wd_ref[...] = dm_ref[0]

    @pl.when((half != y) & (side != core))
    def _():
        wd_ref[...] = dt_ref[0]

    second, gout = sec_ref[...], gout_ref[...]
    v = nn(second, wu_ref[...]) + b_ref[...]
    square = v * v
    gate = 0.5 + 0.5 * jnp.tanh(v * (GELU_C + (GELU_C * 0.044715) * square))
    act = (v * gate).astype(BF)
    slope = gate + (gate - gate * gate) * v * (2 * GELU_C + (6 * GELU_C * 0.044715) * square)
    act_ref[...] = act
    grad_inner = nt(gout, wd_ref[...]) * slope
    low = grad_inner.astype(BF)
    gb_ref[...] = jnp.sum(low.astype(F32), axis=0, keepdims=True)
    gsec_ref[...] += nt(low, wu_ref[...])
    put(dk_ref.at[0, :, 0], ds_ref.at[0, :, 0], nn(turn_ref[...], act))
    part = nn(by_core(ubuf, low.T, core), second)
    width = part.shape[1] // 2
    for side in range(2):
        put(uk_ref.at[side, :, 0], us_ref.at[side, :, 0], part[:, side * width:(side + 1) * width])

    @pl.when(i == n - 1)
    def _():
        unit, scale = norm_rows(att_ref[...])
        grad = gsec_ref[...]
        gg_ref[...] = jnp.sum(grad * unit, axis=0, keepdims=True)
        gatt = norm_back(grad, g_ref[...], unit, scale) + gout_ref[...].astype(F32)
        gatt_ref[...] = gatt
        gm_ref[...] = nt(gatt.astype(BF), wo_ref[...]).astype(BF)


def down_rows(n, blk, width):
    def own(i, s):
        return (jnp.clip(i - s[Y] * (n // 2), 0, n // 2 - 1), 0)

    def part(other):
        def index(i, s):
            side = s[CORE] if other == 0 else 1 - s[CORE]
            first = (1 - s[Y]) * (n // 2) + side * (n // 4)
            return (0, jnp.clip(i - first, 0, n // 4 - 1), 0)

        return pl.BlockSpec((1, blk, width), index)

    return pl.BlockSpec((blk, width), own), part(0), part(1)


def output_kernel(s_ref, act_ref, att_ref, do_ref, dm_ref, dt_ref, out_ref, acc_ref):
    i, n = pl.program_id(0), pl.num_programs(0)
    half, side = i // (n // 2), (i % (n // 2)) // (n // 4)
    y, core = s_ref[Y], s_ref[CORE]

    @pl.when(i == 0)
    def _():
        acc_ref[...] = att_ref[...]

    @pl.when(half == y)
    def _():
        acc_ref[...] += nn(act_ref[...], do_ref[...])

    @pl.when((half != y) & (side == core))
    def _():
        acc_ref[...] += nn(act_ref[...], dm_ref[0])

    @pl.when((half != y) & (side != core))
    def _():
        acc_ref[...] += nn(act_ref[...], dt_ref[0])

    @pl.when(i == n - 1)
    def _():
        out_ref[...] = acc_ref[...].astype(BF)


def layer_output(run, act, attended, w_down, down_parts):
    seg, inner = act.shape
    width = attended.shape[1]
    n = 4
    blk = inner // n
    dm, dt = down_parts
    return run(
        output_kernel, "output", (n,),
        [pl.BlockSpec((seg, blk), lambda i, s: (0, i)), whole((seg, width)),
         *down_rows(n, blk, width)],
        [fixed((seg, width), BF)], [pltpu.VMEM((seg, width), F32)],
        (act, attended, w_down, dm, dt), 2 * seg * width * inner)[0]


def feed_forward(run, second, cotangent, attended, w_up, up_parts, w_down, down_parts, bias_up,
                 gain, w_out, n_dp):
    seg, width = second.shape
    inner = bias_up.shape[1]
    n = 8
    blk = inner // n
    um, ut = up_parts
    dm, dt = down_parts
    uch, dch = inner // n_dp, width // n_dp
    pairs = blk // (2 * uch)
    col = lambda a: pl.BlockSpec((a.shape[0], blk), lambda i, s: (0, i))
    col3 = lambda a: pl.BlockSpec((1, a.shape[1], blk), lambda i, s: (0, 0, i))

    up_shape = part_shape(inner, width, n_dp, 1)
    down_shape = part_shape(width, inner, n_dp, n // 2)[:-1] + (blk,)
    up_out = lambda: out(up_shape, BF, (2, pairs, 1, uch, width // 2),
                         lambda i, s: (0, i, 0, 0, 0))
    down_out = lambda: out(down_shape, BF, (1, n_dp // 2, 1, dch, blk),
                           lambda i, s: (i // (n // 2), 0, i % (n // 2), 0, 0))
    full = (seg, width)
    return run(
        ffn_kernel, "feed_forward", (n,),
        [whole(full), whole(full), whole(full), col(w_up), col3(um), col3(ut),
         *down_rows(n, blk, width),
         pl.BlockSpec((1, blk), lambda i, s: (0, i)), whole((1, width)), whole((width, width))],
        [out((seg, inner), BF, (seg, blk), lambda i, s: (0, i)), fixed(full, F32),
         fixed(full, BF), up_out(), up_out(), down_out(),
         down_out(), out((1, inner), F32, (1, blk), lambda i, s: (0, i)), fixed((1, width), F32)],
        [pltpu.VMEM(full, BF), pltpu.VMEM((width, seg), BF), pltpu.VMEM((width, blk), BF),
         pltpu.VMEM((blk, width), BF), pltpu.VMEM(full, F32),
         pltpu.VMEM((pairs, 2, uch, seg), low_or_wide(uch)),
         pltpu.VMEM((n_dp // 2, 2, dch, seg), low_or_wide(dch))],
        (second, cotangent, attended, w_up, um, ut, w_down, dm, dt, bias_up, gain, w_out),
        12 * seg * width * inner)


def grads_kernel(s_ref, gk_ref, gv_ref, gp_ref, gq_ref, ga_ref, x_ref, tab_ref, ma_ref, mb_ref, w_ref,
                 keep_ref, send_ref, gg_ref, k_s, v_s, p_s, q_s, o_s, big, small):
    core = s_ref[CORE]
    rows = x_ref.shape[0]
    seg = gq_ref.shape[0]

    @pl.when(pl.program_id(0) == 0)
    def _():
        k_s[...] = by_core(big, gk_ref[...], core)
        v_s[...] = by_core(big, gv_ref[...], core)
        p_s[...] = by_core(big, gp_ref[...], core)
        q_s[...] = by_core(small, gq_ref[...].T, core)
        o_s[...] = by_core(small, ga_ref[...].astype(BF).T, core)

    x = x_ref[...]
    pairs, _, chunk, _ = small.shape
    n = pairs * chunk

    def both(tap, values):
        put(keep_ref.at[0, :, tap], send_ref.at[0, :, tap], values)

    def gain(values, m):
        turned = w_ref[m].T.astype(F32)
        whole_ = turned.reshape(pairs, 2, chunk, turned.shape[1])
        even, odd = whole_[:, 0].reshape(n, -1), whole_[:, 1].reshape(n, -1)
        first = jnp.where(core == 0, even, odd)
        last = jnp.where(core == 0, odd, even)
        return (jnp.sum(values[:n] * first, axis=0, keepdims=True)
                + jnp.sum(values[n:] * last, axis=0, keepdims=True))

    part = nn(k_s[...], x)
    both(0, part)
    total = gain(part, 1)
    part = nn(v_s[...], x)
    both(1, part)
    total += gain(part, 2)
    part = nn(q_s[...], x[rows - seg:])
    both(2, part)
    total += gain(part, 0)
    both(3, nn(p_s[...], tab_ref[...]))
    gg_ref[...] = total
    i, n = pl.program_id(0), pl.num_programs(0)

    @pl.when(i < n // 2)
    def _():
        both(4, nn(o_s[...], ma_ref[...]))

    @pl.when(i >= n // 2)
    def _():
        both(4, nn(o_s[...], mb_ref[...]))


def projection_grads(run, turned, gq, gatt, normed, table, mixed, w, n_dp, half):
    rows, width = normed.shape
    seg = gq.shape[0]
    blk = 256
    chunk = width // n_dp
    mid = width // 2
    gk, gv, gpos = turned
    count = mid // blk
    col = lambda r: pl.BlockSpec((r, blk), lambda i, s: (0, i))
    shape = lambda taps: part_shape(width, width, n_dp, taps, 2)
    half_of = lambda taps: out(shape(taps), BF, (1,) + shape(taps)[1:4] + (blk,),
                               lambda i, s: (i // count, 0, 0, 0, i % count))
    side = pl.BlockSpec((seg, blk), lambda i, s: (0, i % count))
    kind = low_or_wide(chunk)
    pairs = mid // (2 * chunk)
    return run(
        grads_kernel, "projection_grads", (width // blk,),
        [whole(gk.shape), whole(gk.shape), whole(gk.shape), whole(gq.shape),
         pl.BlockSpec((seg, mid), lambda i, s: (0, half)), col(rows), col(rows), side, side,
         pl.BlockSpec((3, blk, mid), lambda i, s: (0, i, half))],
        [half_of(5), half_of(5),
         out((1, width), F32, (1, blk), lambda i, s: (0, i))],
        [pltpu.VMEM((mid, rows), BF)] * 3 + [pltpu.VMEM((mid, seg), BF)] * 2
        + [pltpu.VMEM((pairs, 2, chunk, rows), kind), pltpu.VMEM((pairs, 2, chunk, seg), kind)],
        (gk, gv, gpos, gq, gatt, normed, table) + mixed + (w,),
        (3 * rows + 2 * seg) * width * width)


def grad_tokens_kernel(s_ref, ka_ref, kb_ref, va_ref, vb_ref, qa_ref, qb_ref, tok_ref, ga_ref,
                       w_ref, g_ref, gt_ref, acc_ref):
    i = pl.program_id(0)
    mid = w_ref.shape[2] // 2
    left, right = w_ref[0, :, :mid], w_ref[0, :, mid:]

    @pl.when(i == 0)
    def _():
        acc_ref[...] = nn(left, ka_ref[...]) + nn(right, kb_ref[...])

    @pl.when(i == 1)
    def _():
        acc_ref[...] += nn(left, va_ref[...]) + nn(right, vb_ref[...])

    @pl.when(i == 2)
    def _():
        total = (acc_ref[...] + nt(left, qa_ref[...]) + nt(right, qb_ref[...])).T
        unit, scale = norm_rows(tok_ref[...].astype(F32))
        gt_ref[...] = (ga_ref[...] + norm_back(total, g_ref[...], unit, scale)).astype(BF)


def grad_tokens(run, gk, gv, gq, tokens, grad_attended, w, gain):
    seg, width = tokens.shape
    rows = gk[0].shape[1]
    late = pl.BlockSpec((width // 2, seg), lambda i, s: (0, rows // seg - 1))
    side = whole((seg, width // 2))
    return run(
        grad_tokens_kernel, "grad_tokens", (3,),
        [late] * 4 + [side] * 2 + [whole((seg, width)), whole((seg, width)),
         pl.BlockSpec((1, width, width), lambda i, s: ((i + 1) % 3, 0, 0)), whole((1, width))],
        [fixed((seg, width), BF)], [pltpu.VMEM((width, seg), F32)],
        tuple(gk) + tuple(gv) + tuple(gq) + (tokens, grad_attended, w, gain),
        6 * seg * width * width)[0]


def squeeze_kernel(s_ref, gr_ref, o_ref, am_ref, at_ref, bm_ref, bt_ref, wk_ref, wv_ref, g_ref,
                   sq_ref, low_ref, k_ref, v_ref):
    y, core = s_ref[Y], s_ref[CORE]
    half, quarter = o_ref.shape[1], am_ref.shape[1]
    base = (1 - y) * half
    total = jnp.zeros(sq_ref.shape, F32)
    for t in range(3):
        m_ref, t_ref, n = (am_ref, at_ref, t) if t < 2 else (bm_ref, bt_ref, 0)
        at = lambda off, size: gr_ref[t, :, pl.ds(pl.multiple_of(off, quarter), size)]
        total += nn(at(y * half, half), o_ref[t])
        total += nn(at(base + core * quarter, quarter), m_ref[n])
        total += nn(at(base + (1 - core) * quarter, quarter), t_ref[n])
    sq_ref[...] = total
    low_ref[...] = total.astype(BF)
    unit = (norm_rows(total)[0] * g_ref[...]).astype(BF)
    k_ref[...] = nn(unit, wk_ref[0]).astype(BF)
    v_ref[...] = nn(unit, wv_ref[0]).astype(BF)


def key_value(width):
    return [pl.BlockSpec((1, width, width), lambda i, s: (1, 0, 0)),
            pl.BlockSpec((1, width, width), lambda i, s: (2, 0, 0))]


def squeeze(run, groups, own, a_parts, b_parts, w, gain):
    _, rows, width = groups.shape
    parts = a_parts + b_parts
    shape = (rows, width)
    return run(
        squeeze_kernel, "squeeze", (1,),
        [whole(groups.shape), whole(own.shape)] + [whole(p.shape) for p in parts]
        + [*key_value(width), whole((1, width))],
        [fixed(shape, F32), fixed(shape, BF), fixed(shape, BF), fixed(shape, BF)], [],
        (groups, own) + parts + (w, w, gain), 10 * rows * width * width)


def masked_softmax(scores, live):
    masked = jnp.where(live, scores, -1e30)
    weights = jnp.exp(masked - jnp.max(masked, axis=-1, keepdims=True))
    return weights * (1.0 / jnp.sum(weights, axis=-1, keepdims=True))


def recon_kernel(s_ref, *refs):
    dh = refs[0].shape[-1] // 2
    for n in range(2):
        cols = slice(n * dh, (n + 1) * dh)
        recon_head(s_ref, *[
            r.at[0, :, cols] if len(r.shape) == 3 else r.at[:, cols] for r in refs])


def recon_head(s_ref, pr_ref, ok_ref, ov_ref, ck_ref, cv_ref, gk_ref, gv_ref):
    seg_len = s_ref[SEG_LEN]
    count = seg_len // 3
    probe = pr_ref[...]
    seg, mem, comp = probe.shape[0], ok_ref.shape[0], ck_ref.shape[0]
    old_live = lax.broadcasted_iota(jnp.int32, (1, mem), 1) < 3 * count
    old = nn(masked_softmax(nt(probe, ok_ref[...]), old_live).astype(BF), ov_ref[...])
    live = lax.broadcasted_iota(jnp.int32, (1, comp), 1) < count
    probs = masked_softmax(nt(probe, ck_ref[...]), live)
    low = probs.astype(BF)
    gap = nn(low, cv_ref[...]) - old
    row = lax.broadcasted_iota(jnp.int32, gap.shape, 0)
    grad_out = (jnp.where(row < seg_len, gap, 0.0) * (2.0 / seg_len.astype(F32))).astype(BF)
    gv_ref[...] = tn(low, grad_out).astype(BF)
    weighted = probs * nt(grad_out, cv_ref[...])
    scores = (weighted - probs * jnp.sum(weighted, axis=-1, keepdims=True)).astype(BF)
    gk_ref[...] = tn(scores, probe).astype(BF)


def reconstruct(run, probe, kv, ck, cv, mem):
    seg, width = probe.shape
    rows = ck.shape[0]
    dh = 2 * width // H
    at = lambda n, b: pl.BlockSpec((n, dh), lambda h, s: (b, h))
    old = lambda m: pl.BlockSpec((1, mem, dh), lambda h, s: (m, 1, h))
    grads = lambda: out((rows, width), BF, (rows, dh), lambda h, s: (0, h))
    return run(
        recon_kernel, "reconstruct", (H // 2,),
        [at(seg, 0), old(0), old(1), at(rows, 0), at(rows, 0)], [grads(), grads()], [],
        (probe, kv, kv, ck, cv), 4 * seg * width * mem + 12 * seg * width * rows)


def grad_comp_kernel(s_ref, sq_ref, gk_ref, gv_ref, wk_ref, wv_ref, g_ref, gr_ref, k_ref, x_ref, low_ref, buf):
    @pl.when(pl.program_id(0) == 0)
    def _():
        grad = nt(gk_ref[...], wk_ref[0]) + nt(gv_ref[...], wv_ref[0])
        unit, scale = norm_rows(sq_ref[...])
        low = norm_back(grad, g_ref[...], unit, scale).astype(BF)
        low_ref[...] = by_core(buf, low.astype(F32).T, s_ref[CORE])

    part = nn(low_ref[...], gr_ref[0])
    width = part.shape[1] // 2
    for y in range(2):
        put(k_ref.at[y, :, 0], x_ref.at[y, :, 0], part[:, y * width:(y + 1) * width])


def grad_comp(run, squeezed, gk, gv, w, gain, groups, n_dp):
    taps, rows, width = groups.shape
    chunk = width // n_dp
    shape = part_shape(width, width, n_dp, taps)
    half = lambda: out(shape, BF, shape[:2] + (1,) + shape[3:], lambda i, s: (0, 0, i, 0, 0))
    here = whole((rows, width))
    return run(
        grad_comp_kernel, "grad_comp", (taps,),
        [here, here, here, *key_value(width), whole((1, width)),
         pl.BlockSpec((1, rows, width), lambda i, s: (i, 0, 0))],
        [half(), half()],
        [pltpu.VMEM((width, rows), BF), pltpu.VMEM((n_dp // 2, 2, chunk, rows), low_or_wide(chunk))],
        (squeezed, gk, gv, w, w, gain, groups), 10 * rows * width * width)


class Links:
    def __init__(self):
        self.dp = lax.axis_index("dp")
        self.y = lax.axis_index("fsdp")
        self.n_dp = lax.axis_size("dp")
        self.top = self.n_dp.bit_length() - 2

    def bit(self, axis):
        return self.y if axis == "y" else (self.dp >> axis) & 1

    def swap(self, value, axis):
        if axis == "y":
            return lax.ppermute(value, "fsdp", [(0, 1), (1, 0)])
        return lax.ppermute(value, "dp", [(i, i ^ (1 << axis)) for i in range(self.n_dp)])


class Part:
    def __init__(self, array, start):
        self.array, self.start = array, start


class Flow:
    def __init__(self, axes, order, rows):
        self.axes, self.order, self.rows = list(axes), list(order), rows

    def halves(self):
        axis = self.order[0]
        where = self.axes.index(axis)
        run = self.rows << (len(self.axes) - 1 - where)
        return axis, [(2 * p * run, (2 * p + 1) * run, p * run) for p in range(1 << where)], run

    def plan(self, take_in, give):
        axis, runs, length = self.halves()
        keep, recv = take_in(self.keep), take_in(self.recv.array)
        total = len(runs) * length
        held = give(fixed((total, self.keep.shape[1]), BF))
        place = give.send(axis, total, self)
        first = self.recv.start
        slot = Y if axis == "y" else BITS + axis - 1

        def kernel(s_ref, ins, outs, sends):
            bit = s_ref[slot]
            dst, base = sends(place)
            for low, high, to in runs:
                for side, ref, at in ((bit, outs[held], to), (1 - bit, dst, base + to)):
                    start = low + side * (high - low)
                    a = ins[keep][pl.ds(pl.multiple_of(start, 8), length)]
                    b = ins[recv][pl.ds(pl.multiple_of(first + start, 8), length)]
                    ref[at:at + length] = (a.astype(F32) + b.astype(F32)).astype(BF)

        def done(outs):
            self.keep = outs[held]
            self.axes.remove(axis)
            self.order.pop(0)

        return kernel, done


def cut_rows(rows, flows):
    if flows == 1:
        return (0, rows)
    unit = 16 if rows >= 96 else 8
    third = -(-rows // (3 * unit)) * unit
    return (0, third, 2 * third, rows)


class Source:
    def __init__(self, links, keep, send, axes, orders):
        self.axes, self.orders = axes, orders
        self.blocks = math.prod(keep.shape[:2])
        self.rows, self.cols = math.prod(keep.shape[2:4]), keep.shape[4]
        self.keep = keep.reshape(-1, self.cols)
        self.recv = links.swap(send, 0).reshape(-1, self.cols)
        self.cuts = cut_rows(self.rows, len(orders))

    def plan(self, take_in, give):
        keep, recv = take_in(self.keep), take_in(self.recv)
        rows, moves, self.flows = self.rows, [], []
        for c, order in enumerate(self.orders):
            lo, size = self.cuts[c], self.cuts[c + 1] - self.cuts[c]
            flow = Flow(self.axes, order, size)
            axis = order[0]
            where = self.axes.index(axis)
            post = 1 << (len(self.axes) - 1 - where)
            total = self.blocks // 2 * size
            held = give(fixed((total, self.cols), BF))
            moves.append((axis, where, post, lo, size, held, give.send(axis, total, flow)))
            self.flows.append(flow)

        def kernel(s_ref, ins, outs, sends):
            for axis, where, post, lo, size, held, place in moves:
                bit = s_ref[Y if axis == "y" else BITS + axis - 1]
                dst, base = sends(place)
                for p in range(1 << where):
                    for q in range(post):
                        to = (p * post + q) * size
                        for side, ref, at in ((bit, outs[held], to), (1 - bit, dst, base + to)):
                            start = ((2 * p + side) * post + q) * rows + lo
                            rng = pl.ds(pl.multiple_of(start, 8), size)
                            total = ins[keep][rng].astype(F32) + ins[recv][rng].astype(F32)
                            ref[at:at + size] = total.astype(BF)

        def done(outs):
            for flow, move in zip(self.flows, moves):
                flow.keep = outs[move[5]]
                flow.axes.remove(move[0])
                flow.order.pop(0)

        return kernel, done


class Join:
    def __init__(self, top, low, high):
        self.top, self.low, self.high = top, low, high
        self.rows = low.rows

    def plan(self, take_in, give):
        low, high = self.low, self.high
        refs = [take_in(low.keep), take_in(low.recv.array), take_in(high.keep),
                take_in(high.recv.array)]
        held = give(fixed(low.keep.shape, BF))
        place = give.send(self.top, self.rows, self)
        slot = BITS + self.top - 1
        rows = self.rows

        def kernel(s_ref, ins, outs, sends):
            dst, base = sends(place)
            part = lambda n, flow: (ins[refs[n]][...].astype(F32) + ins[refs[n + 1]][
                flow.recv.start:flow.recv.start + rows].astype(F32))
            a, b = part(0, low), part(2, high)
            upper = s_ref[slot] == 1
            outs[held][...] = jnp.where(upper, b, a).astype(BF)
            dst[base:base + rows] = jnp.where(upper, a, b).astype(BF)

        def done(outs):
            self.keep = outs[held]

        return kernel, done


class Small:
    def __init__(self, links, value, order):
        self.keep, self.order = value, list(order)
        self.recv = Part(links.swap(value, 0), 0)

    def plan(self, take_in, give):
        a, b = take_in(self.keep), take_in(self.recv.array)
        first, wide = self.recv.start, self.recv.array.dtype == F32
        rows, cols = self.keep.shape
        half = cols // 2
        total = give(fixed(self.keep.shape, F32))
        place = give.send(self.order.pop(0), 4 * rows, self) if self.order else None

        def kernel(s_ref, ins, outs, sends):
            if wide:
                came = ins[b][...]
            else:
                part = lambda n: ins[b][first + n:first + n + 2 * rows].astype(F32)
                both = part(0) + part(2 * rows)
                came = jnp.concatenate([both[:rows], both[rows:]], axis=1)
            added = ins[a][...] + came
            outs[total][...] = added
            if place is not None:
                dst, base = sends(place)
                stacked = jnp.concatenate([added[:, :half], added[:, half:]], axis=0)
                high = stacked.astype(BF)
                dst[base:base + 2 * rows] = high
                dst[base + 2 * rows:base + 4 * rows] = (stacked - high.astype(F32)).astype(BF)

        def done(outs):
            self.keep = outs[total]
            if place is None:
                self.recv = None

        return kernel, done


class Finish:
    def __init__(self, flows, shapes, write):
        self.flows, self.shapes, self.write = flows, shapes, write

    def plan(self, take_in, give):
        refs = [(take_in(f.keep), take_in(f.recv.array), f.recv.start, f.rows) for f in self.flows]
        results = [give(fixed(shape, F32)) for shape in self.shapes]

        def kernel(s_ref, ins, outs, sends):
            rows = jnp.concatenate(
                [ins[k][...].astype(F32) + ins[r][first:first + n].astype(F32)
                 for k, r, first, n in refs], axis=0)
            self.write(rows, *[outs[n] for n in results])

        def done(outs):
            self.result = [outs[n] for n in results]

        return kernel, done


class Carry:
    def __init__(self, *values):
        self.values = values

    def plan(self, take_in, give):
        anywhere = pl.BlockSpec(memory_space=pltpu.HBM)
        at = []
        for v in self.values:
            n = give((jax.ShapeDtypeStruct(v.shape, v.dtype), anywhere))
            give.aliases[take_in(v, anywhere)] = n
            at.append(n)

        def done(outs):
            self.values = [outs[n] for n in at]

        return lambda *refs: None, done


class Gives:
    def __init__(self):
        self.outs, self.sizes, self.takers, self.aliases = [], {}, [], {}

    def __call__(self, spec):
        self.outs.append(spec)
        return len(self.outs) - 1

    def send(self, axis, rows, taker):
        start = self.sizes.get(axis, 0)
        self.sizes[axis] = start + rows
        self.takers.append((axis, start, taker))
        return axis, start


def advance(run, links, *items):
    args, ins, index = [], [], {}

    def take_in(array, spec=None):
        if id(array) not in index:
            index[id(array)] = len(args)
            args.append(array)
            ins.append(spec or whole(array.shape))
        return index[id(array)]

    give = Gives()
    plans = [item.plan(take_in, give) for item in items]
    n_out = len(give.outs)
    axes = sorted(give.sizes, key=lambda a: 0 if a == "y" else a)
    outs = give.outs + [fixed((give.sizes[a], args[0].shape[-1]), BF) for a in axes]

    def kernel(s_ref, *refs):
        in_refs, out_refs = refs[:len(args)], refs[len(args):]
        sends = lambda place: (out_refs[n_out + axes.index(place[0])], place[1])
        for part, _ in plans:
            part(s_ref, in_refs, out_refs, sends)

    done = run(kernel, "add", (1,), ins, outs, [], args, 0,
               {1 + a: b for a, b in give.aliases.items()})
    came = {a: links.swap(done[n_out + n], a) for n, a in enumerate(axes)}
    for axis, start, taker in give.takers:
        taker.recv = Part(came[axis], start)
    for _, take in plans:
        take(done)


class Deal:
    def __init__(self, links, pairs, axes, orders, cuts):
        self.links, self.axes, self.orders, self.cuts = links, axes, orders, cuts
        self.keeps = [k for k, _ in pairs]
        self.sends = [x for _, x in pairs]
        self.rows, self.cols = self.keeps[0].shape[-2:]

    def start(self, sends):
        self.recvs = [self.links.swap(x, 0) for x in sends]

    def spans(self, c):
        lo, hi = self.cuts[c], self.cuts[c + 1]
        for n in range(2):
            a, b = max(lo - n * self.rows, 0), min(hi - n * self.rows, self.rows)
            if a < b:
                yield n, a, b

    def add(self, run, steps):
        n = len(self.axes)
        lead = (2,) * n
        rows, cols = self.rows, self.cols
        firsts = [self.axes.index(o[0]) for o in self.orders]
        others = [a for a in range(n) if a not in firsts]
        split = max(steps >> len(others), 1)
        width = cols // split
        count = 2 ** len(others) * split

        def at(i):
            places, rest = [0] * n, i // split
            for a in reversed(others):
                places[a] = rest % 2
                rest = rest // 2
            return places, i % split

        block = tuple(1 if a in others else 2 for a in range(n))

        def read(i, s):
            places, col = at(i)
            return (*places, 0, col)

        def write(first):
            def index(i, s):
                places, col = at(i)
                return (*places[:first], *places[first + 1:], 0, col)
            return index

        args = [a.reshape(lead + (rows, cols)) for a in self.keeps + self.recvs]
        ins = [pl.BlockSpec(block + (rows, width), read)] * 4
        outs, slots = [], []
        for c, first in enumerate(firsts):
            size = self.cuts[c + 1] - self.cuts[c]
            shape = lead[1:] + (size, cols)
            less = block[:first] + block[first + 1:]
            outs += [out(shape, BF, less + (size, width), write(first))] * 2
            axis = self.axes[first]
            slots.append(Y if axis == "y" else BITS + axis - 1)

        def kernel(s_ref, *refs):
            held, sent = refs[4::2], refs[5::2]

            for c, first in enumerate(firsts):
                bit = s_ref[slots[c]]
                row = 0
                for m, a, b in self.spans(c):
                    keep, recv = refs[m], refs[2 + m]
                    for dst, side in ((held[c], bit), (sent[c], 1 - bit)):
                        pick = tuple(side if d == first else slice(None) for d in range(n))
                        pick += (slice(a, b), slice(None))
                        total = keep[pick].astype(F32) + recv[pick].astype(F32)
                        to = (slice(None),) * (n - 1) + (slice(row, row + b - a),)
                        dst[to] = total.astype(BF)
                    row += b - a

        def take(*done):
            self.chains = []
            for c, order in enumerate(self.orders):
                axes = [a for a in self.axes if a != order[0]]
                recv = self.links.swap(done[2 * c + 1], order[0])
                size = self.cuts[c + 1] - self.cuts[c]
                flow = Flow(axes, order[1:], size)
                flow.keep, flow.recv = done[2 * c].reshape(-1, self.cols), Part(
                    recv.reshape(-1, self.cols), 0)
                self.chains.append(flow)

        done = run(kernel, "deal", (count,), ins, outs, [], args, 0)
        take(*done)


def angle_parts(rows, width):
    fine = 32
    frequency = jnp.exp(
        jnp.arange(0, width, 2).astype(F32) * (-math.log(10000.0) / width))
    coarse = (fine * (rows // fine - 1 - jnp.arange(rows // fine))).astype(F32)
    near = (fine - 1 - jnp.arange(fine)).astype(F32)
    a, b = coarse[:, None] * frequency[None, :], near[:, None] * frequency[None, :]
    return (jnp.sin(a), jnp.cos(a), jnp.sin(b), jnp.cos(b))


def body(tokens, memory, compressed, cotangent, seg_len, mem_fill, cmem_fill, w_qkv, w_rel, w_out,
         w_up, w_down, w_comp, norm_gain1, norm_gain2, bias_content, bias_position, bias_up):
    streams = tokens.shape[0]
    assert streams == 1
    links = Links()
    n_dp, top = links.n_dp, links.top
    seg, width = tokens.shape[1:]
    mem, comp = memory.shape[1], compressed.shape[1]
    start = comp + mem
    keys = start + seg
    squeezed_rows = mem // 3
    scale = (width // H) ** (-0.5)
    current, recent, distant = tokens[0], memory[0], compressed[0]
    seg_length = seg_len[0]
    core, x, z = links.bit(0), links.bit(1), links.bit(2)
    run = Steps(jnp.stack(
        [links.y, core, seg_length, mem_fill[0], cmem_fill[0], core * 2 + z,
         core * 2 + x] + [links.bit(n) for n in range(1, top + 1)]).astype(jnp.int32))
    gain1, gain2 = norm_gain1.reshape(1, -1), norm_gain2.reshape(1, -1)

    swap = links.swap
    near_parts = lambda value: (value, swap(value, 0))
    p_rel, p_a, p_b = pack_first(run, w_qkv, w_rel)
    rel, a, b = swap(p_rel, "y"), swap(p_a, "y"), swap(p_b, "y")
    normed = norm_hidden(run, distant, recent, current, gain1)
    rel_far = swap(rel, 2)
    p_c, p_d, p_up, p_down = pack_rest(run, w_out, w_up, w_down, w_comp)
    c, d = swap(p_c, "y"), swap(p_d, "y")
    table, groups = constants(run, recent, angle_parts(keys, width), squeezed_rows)
    rel, = order(run, (rel, rel_far, 2))
    rel_parts = near_parts(rel)
    a_far, b_far = swap(a, 2), swap(b, 1)
    pos = project_position(run, table, w_rel, rel_parts)
    a, b = order(run, (a, a_far, 2), (b, b_far, 1))
    a_parts, b_parts = near_parts(a), near_parts(b)
    p_up, p_down = follow(run, p_up, p_down)
    up, down = swap(p_up, "y"), swap(p_down, "y")
    kv, qc, qp, probe, w_full = project_qkv(
        run, normed, w_qkv, a_parts, b_parts, bias_content, bias_position, seg, scale)
    c, d = follow(run, c, d)
    c_far, d_far = swap(c, 2), swap(d, 1)
    p0, m0 = attention(run, qc, qp, kv, pos, comp, mem, 0)
    c, d = order(run, (c, c_far, 2), (d, d_far, 1))
    c_parts, d_parts = near_parts(c), near_parts(d)
    p1, m1 = attention(run, qc, qp, kv, pos, comp, mem, 1)
    up, down = follow(run, up, down)
    up_far, down_far = swap(up, 2), swap(down, 1)
    squeezed, squeezed_low, ck, cv = squeeze(run, groups, w_comp, c_parts, d_parts, w_full, gain1)
    gck, gcv = reconstruct(run, probe, kv, ck, cv, mem)
    up, down = order(run, (up, up_far, 2), (down, down_far, 1))
    up_parts, down_parts = near_parts(up), near_parts(down)
    comp_keep, comp_send = grad_comp(run, squeezed, gck, gcv, w_full, gain1, groups, n_dp)

    attended, second, w_out_full = mix_out(run, current, (m0, m1), w_out, d_parts, gain2)
    far = list(range(3, top + 1))
    names, under = ["y"] + list(range(top, 0, -1)), ["y"] + list(range(top - 1, 0, -1))
    turns = lambda rest: [[1, "y", 2] + rest, ["y", 2, 1] + rest, [2, 1, "y"] + rest]
    of_comp = Source(links, comp_keep, comp_send, names, [[2, 1, "y"] + far])
    advance(run, links, of_comp)
    (act, grad_attended, grad_mix, up_keep, up_send, down_keep, down_send, sum_bias, sum_gain2
     ) = feed_forward(run, second, cotangent[0], attended, w_up, up_parts, w_down, down_parts,
                      bias_up.reshape(1, -1), gain2, w_out_full, n_dp)
    inner = bias_up.shape[0]
    rows, half = inner // n_dp, width // 2
    flat = lambda a: a.reshape(2, n_dp // 2, rows, half)
    third = max(2 * rows * 11 // 32 // 16 * 16, 8)
    deal = Deal(
        links, [(flat(up_keep), flat(up_send)), (flat(down_keep), flat(down_send))], names,
        turns(far), (0, third, 2 * third, 2 * rows))
    carry = Carry(*deal.sends)
    advance(run, links, *of_comp.flows, carry)
    deal.start(carry.values)

    chunk = width // n_dp

    def write_ffn(rows, up, down):
        size = rows.shape[0] // 2
        up[...] = rows[:size].T
        for n in range(inner // (2 * half)):
            down[n * half:(n + 1) * half] = rows[size + n * chunk:size + (n + 1) * chunk].T

    def write_comp(rows, grad):
        for t in range(3):
            grad[t] = rows[t * chunk:(t + 1) * chunk].T

    def write_rest(rows, qkv, rel, ow):
        tap = lambda t: rows[t * chunk:(t + 1) * chunk].T
        qkv[0], qkv[1], qkv[2] = tap(2), tap(0), tap(1)
        rel[...], ow[...] = tap(3), tap(4)

    waiting = lambda *flows: [f for f in flows if f.order]
    back = functools.partial(attention_back, run, (p0, p1), (m0, m1), grad_mix, qc, qp, kv, pos, start, scale)
    grads = lambda turned, gq, half: projection_grads(
        run, turned, gq, grad_attended, normed, table, (m0, m1), w_full, n_dp, half)
    gq0, gk0, gv0, gpos0, content0, position0 = back(0)
    advance(run, links, *of_comp.flows)
    deal.add(run, 4)
    keep_0, send_0, gain_0 = grads((gk0, gv0, gpos0), gq0, 0)
    gq1, gk1, gv1, gpos1, content1, position1 = back(1)
    carry = Carry(send_0)
    advance(run, links, *deal.chains, *of_comp.flows, carry)
    early = Source(links, keep_0, carry.values[0], under, turns(far[:-1]))
    keep_1, send_1, gain_1 = grads((gk1, gv1, gpos1), gq1, 1)
    carry = Carry(send_1)
    comp_end = Finish(of_comp.flows, [(3, half, chunk)], write_comp)
    comp_left = list(waiting(*of_comp.flows))
    held = [Carry(f.recv.array) for f in of_comp.flows if not comp_left]
    advance(run, links, *deal.chains, *comp_left, early, carry, *held)
    for flow, kept in zip(of_comp.flows, held):
        flow.recv = Part(kept.values[0], flow.recv.start)
    late = Source(links, keep_1, carry.values[0], under, turns(far[:-1]))
    row = lambda a, b: jnp.concatenate([a, b], axis=1)
    small = Small(links, jnp.concatenate(
        [(gain_0 + gain_1) / gain1, sum_gain2, row(content0, content1), row(position0, position1),
         sum_bias.reshape(-1, width)], axis=0), ["y", 1, 2] + far)
    new_memory = lax.dynamic_slice_in_dim(
        jnp.concatenate([recent, current], axis=0), seg_length, mem, 0)
    new_compressed = lax.dynamic_slice_in_dim(
        jnp.concatenate([distant, squeezed_low[:squeezed_rows]], axis=0), seg_length // 3, comp, 0)
    output = layer_output(run, act, attended, w_down, down_parts)
    advance(run, links, *waiting(*deal.chains, *comp_left), late, small)
    grad_rows = grad_tokens(run, (gk0, gk1), (gv0, gv1), (gq0, gq1), current, grad_attended,
                            w_full, gain1)
    while any(f.order for f in late.flows):
        advance(run, links, *waiting(*deal.chains, *comp_left, *early.flows, *late.flows),
                small)
        if not comp_left and comp_end.flows[0].recv is not None and not hasattr(comp_end, 'result'):
            advance(run, links, comp_end)
    ends = [Join(top, a, b) for a, b in zip(early.flows, late.flows)]
    of_ffn = Finish(deal.chains, [(half, rows), (inner // 2, chunk)], write_ffn)
    advance(run, links, *ends, small, of_ffn, *([comp_end] if comp_left else []))
    rest = Finish(ends, [(3, half, chunk), (half, chunk), (half, chunk)], write_rest)
    advance(run, links, rest, small)
    assert small.recv is None
    (grad_up, grad_down), (grad_comp_,) = of_ffn.result, comp_end.result
    grad_qkv, grad_rel, grad_out = rest.result

    at = links.dp * 2 + links.y
    each, each_up = width // (2 * n_dp), bias_up.shape[0] // (2 * n_dp)
    vec = lax.dynamic_slice(small.keep[:4], (0, at * each), (4, each))
    vec_up = lax.dynamic_slice_in_dim(small.keep[4:].reshape(-1), at * each_up, each_up)
    return (output[None], grad_rows[None], new_memory[None], new_compressed[None],
            grad_qkv, grad_rel, grad_out,
            grad_up, grad_down, grad_comp_, vec[0], vec[1], vec[2], vec[3], vec_up)


def solution(mesh):
    rows = P(("dp", "fsdp"), None, None)
    one = P(("dp", "fsdp"))
    return jax.shard_map(
        body,
        mesh=mesh,
        in_specs=(rows, rows, rows, rows, one, one, one, P(None, "fsdp", None), P("fsdp", None),
                  P("fsdp", None), P("fsdp", None), P("fsdp", None), P(None, "fsdp", None), P(),
                  P(), P(), P(), P()),
        out_specs=(rows, rows, rows, rows, P(None, "fsdp", "dp"), P("fsdp", "dp"),
                   P("fsdp", "dp"), P("fsdp", "dp"), P("fsdp", "dp"), P(None, "fsdp", "dp"), one,
                   one, one, one, one),
        check_vma=False,
    )
```
